32 devices in a mesh: dp: 8 (over z, x), tensor: 4 (over y, core).
Axes of the slice: x: 2, y: 2, z: 4, core: 2. Of those that a mesh axis runs over, the one named last changes fastest.
Arguments:
- block_input: bfloat16 [16384, 768], P(('dp', 'tensor')), may hold values from -6 to 6
- out_grad: bfloat16 [16384, 768], P(('dp', 'tensor')), may hold values from -6 to 6
- w_qkv: bfloat16 [3, 768, 768], P(None, 'dp', 'tensor'), may hold values from -0.21875 to 0.21875
- w_out: bfloat16 [768, 768], P('tensor', 'dp'), may hold values from -0.875 to 0.875
- rel_table: float32 [32, 12], replicated, may hold values from -4 to 4
- gain_attn: float32 [768], replicated, may hold values from 0.5 to 1.5
- gain_moe: float32 [768], replicated, may hold values from 0.5 to 1.5
- w_router: bfloat16 [768, 8], replicated, may hold values from -0.15917969 to 0.15917969
- w_up: bfloat16 [8, 3072, 768], P('dp', 'tensor'), may hold values from -0.21875 to 0.21875
- w_down: bfloat16 [8, 3072, 768], P('dp', 'tensor'), may hold values from -0.21875 to 0.21875
- routes: int32 [16384, 2], P(('dp', 'tensor')), may hold values from 0 to 7, all different within a row
- segments: int32 [16, 1024], P('dp'), may hold values from 0 to 510, as said below
- padding: int32 [16, 1024], P('dp'), may hold values from 0 to 1, as said below
- rel_bucket: int32 [1024], replicated, may hold values from 0 to 31, as said below
Outputs:
- block_output: float32 [16384, 768], P(('dp', 'tensor'))
- input_grad: float32 [16384, 768], P(('dp', 'tensor'))
- w_qkv_grad: float32 [3, 768, 768], P(None, 'dp', 'tensor')
- w_out_grad: float32 [768, 768], P('tensor', 'dp')
- rel_table_grad: float32 [32, 12], replicated
- gain_attn_grad: float32 [768], replicated
- gain_moe_grad: float32 [768], replicated
- w_router_grad: float32 [768, 8], replicated
- w_up_grad: float32 [8, 3072, 768], P('dp', 'tensor')
- w_down_grad: float32 [8, 3072, 768], P('dp', 'tensor')
The draws below stay inside these ranges and needn't reach their ends.
Inputs may be any that keep to these rules, and one draw needn't show every extreme that they name: `segments`: along a sequence the ids never fall; places 1024 // 4 to 768 belong to one document; the first document has id 0 and the last one, which holds at least place 1024 - 1, has id 1024 // 2 - 2. `padding`: each sequence is ones followed by at most 128 zeros. `rel_bucket`: distance 0 has bucket 0, buckets never fall with distance, distance 1024 - 1 has bucket 32 - 1. `routes`: A token's two experts differ.
All inputs are finite; a program needn't handle non-finite values.
Results may differ from the reference program's by a relative error of at most 0.015.
Values may be sent and summed in bfloat16 or wider, within the bound.
A program may use at most 256 MiB of HBM per device.

```python
import math
import jax
import jax.numpy as jnp
from jax import lax

D = 768
H = 12
DH = 64
FF = 3072
NB = 32
WINDOW = 1024
L = 1024
EXPERTS = 8
INNER = 768
SEQS = 16
TOKENS = 16384
TOK_DEV = 512
CAPACITY = 160
SLOTS = 5120


def draw_segments(key, part):
    key = jax.random.fold_in(key, 11)
    cuts = jax.random.randint(key, (SEQS, L), 0, max(4, L // 16))
    places = jnp.arange(L, dtype=jnp.int32)[None, :]
    starts = (cuts == 0) & (places > 0) & ((places < L // 4) | (places > 3 * L // 4)) | (places == L - 1)
    counted = jnp.cumsum(starts.astype(jnp.int32), axis=1).astype(jnp.int32)
    final = counted[:, L - 1:L]
    return jnp.where(counted == final, L // 2 - 2, counted).astype(jnp.int32)


def draw_padding(key, part):
    key = jax.random.fold_in(key, 23)
    tails = jax.random.randint(key, (SEQS, 1), 0, L // 8 + 1)
    places = jnp.arange(L, dtype=jnp.int32)[None, :]
    return (places < L - tails).astype(jnp.int32)


def draw_rel_bucket(key, part):
    key = jax.random.fold_in(key, 37)
    places = jnp.arange(L, dtype=jnp.int32)
    picks = jax.random.randint(key, (L,), 0, max(2, L // NB))
    stepped = ((places > 0) & (picks == 0)).astype(jnp.int32)
    grown = jnp.minimum(jnp.cumsum(stepped), NB - 1)
    return jnp.where(places == L - 1, NB - 1, grown).astype(jnp.int32)


def block_scale(stream_key, shape, cuts, low, top_value):
    loudness, own = 1.0, jax.random.fold_in(stream_key, 6)
    for position, shards_of in cuts:
        heights = jnp.exp(jax.random.uniform(jax.random.fold_in(own, position), (shards_of,), jnp.float32, low / len(cuts), top_value / len(cuts)))
        loudness = loudness * jnp.repeat(heights, shape[position] // shards_of).reshape([-1 if axis == position else 1 for axis in range(len(shape))])
    return loudness


def choose_distinct(own_key, rows, amount, top, lift):
    order = jax.random.permutation(jax.random.fold_in(own_key, 1), amount)
    favour = order
    for power in range(3):
        favour = favour * favour // amount
    favour = favour * lift // amount
    chance = jax.random.randint(jax.random.fold_in(own_key, 2), (rows, amount), 0, 4096) + favour
    sure = jax.random.permutation(jax.random.fold_in(own_key, 3), rows)[jnp.arange(amount) % rows]
    chance = jnp.where(jnp.arange(rows)[:, None] == sure[None, :], 1 << 14, chance)
    priority = chance * amount + jnp.arange(amount)
    return lax.top_k(priority.astype(jnp.int32), top)[1].astype(jnp.int32)


def scatter_about(own_key, dims, width, limit, split=(), held_as=jnp.bfloat16):
    factor_of = block_scale(own_key, dims, split, -0.22, 0.18) if split else 1.0
    result = jax.random.normal(own_key, dims, jnp.float32) * width * factor_of
    return jnp.minimum(jnp.maximum(result, -limit), limit).astype(held_as)


def setup_inputs(seed: int = 0) -> dict:
    key_of = jax.random.split(jax.random.key(seed), 15)
    return {
        "block_input": scatter_about(key_of[0], (TOKENS, D), 1.0, 6.0, ((0, 32),)),
        "out_grad": scatter_about(key_of[1], (TOKENS, D), 1.0, 6.0, ((0, 32),)),
        "w_qkv": scatter_about(key_of[2], (3, D, INNER), D ** -0.5, 0.21875, ((1, 8), (2, 4))),
        "w_out": scatter_about(key_of[3], (INNER, D), (INNER // 16) ** -0.5, 0.875, ((0, 4), (1, 8))),
        "rel_table": scatter_about(key_of[4], (NB, H), 1.0, 4.0, (), jnp.float32),
        "gain_attn": jnp.clip(1.0 + 0.1 * jax.random.normal(key_of[5], (D,), jnp.float32), 0.5, 1.5),
        "gain_moe": jnp.clip(1.0 + 0.1 * jax.random.normal(key_of[6], (D,), jnp.float32), 0.5, 1.5),
        "w_router": scatter_about(key_of[7], (D, EXPERTS), 0.027, 0.15917969),
        "w_up": scatter_about(key_of[8], (EXPERTS, FF, D), D ** -0.5, 0.21875, ((0, 8), (1, 4))),
        "w_down": scatter_about(key_of[9], (EXPERTS, FF, D), (FF // 4) ** -0.5, 0.21875, ((0, 8), (1, 4))),
        "routes": choose_distinct(key_of[10], TOKENS, EXPERTS, 2, 2048),
        "segments": draw_segments(jax.random.fold_in(key_of[14], 71), 0),
        "padding": draw_padding(jax.random.fold_in(key_of[14], 71), 0),
        "rel_bucket": draw_rel_bucket(jax.random.fold_in(key_of[14], 71), 0),
    }


@jax.custom_vjp
def low(v):
    return lax.optimization_barrier(v.astype(jnp.bfloat16)).astype(jnp.float32)

@jax.custom_vjp
def low_back(v):
    return v

def low_keep(v):
    return (low(v), None)

def low_pass(kept, grad):
    return (grad,)

def back_keep(v):
    return (v, None)

def back_low(kept, grad):
    return (low(grad),)
low.defvjp(low_keep, low_pass)
low_back.defvjp(back_keep, back_low)
EPSILON = 1e-06
NEGATIVE = -1e+30
HIGHEST = lax.Precision.HIGHEST

def norm_rows(values, gain):
    return values * lax.rsqrt(lax.optimization_barrier(jnp.mean(values * values, axis=-1, keepdims=True)) + EPSILON) * gain

def slot_places(routes, padding):
    live_mask = padding.reshape(TOKENS)
    expert_ids = jnp.arange(EXPERTS, dtype=jnp.int32)
    sources = TOKENS // TOK_DEV
    usable = live_mask[:, None] == 1
    first_hot = ((routes[:, 0:1] == expert_ids[None, :]) & usable).astype(jnp.int32).reshape(sources, TOK_DEV, EXPERTS)
    second_hot = ((routes[:, 1:2] == expert_ids[None, :]) & usable).astype(jnp.int32).reshape(sources, TOK_DEV, EXPERTS)
    first_before = jnp.cumsum(first_hot, axis=1) - first_hot
    second_before = jnp.cumsum(second_hot, axis=1) - second_hot + lax.optimization_barrier(jnp.sum(first_hot, axis=1, keepdims=True))
    first_place = lax.optimization_barrier(jnp.sum(first_before * first_hot, axis=2)).reshape(TOKENS)
    second_place = lax.optimization_barrier(jnp.sum(second_before * second_hot, axis=2)).reshape(TOKENS)
    return (live_mask, first_place, second_place)

def reference(block_input, out_grad, w_qkv, w_out, rel_table, gain_attn, gain_moe, w_router, w_up, w_down, routes, segments, padding, rel_bucket):
    live_mask, first_place, second_place = slot_places(routes, padding)
    token_ids = jnp.arange(TOKENS, dtype=jnp.int32)
    anchor = token_ids // TOK_DEV
    first_keep = (live_mask == 1) & (first_place < CAPACITY)
    second_keep = (live_mask == 1) & (second_place < CAPACITY)
    first_slot = anchor * CAPACITY + jnp.minimum(first_place, CAPACITY - 1)
    second_slot = anchor * CAPACITY + jnp.minimum(second_place, CAPACITY - 1)
    spare = EXPERTS * SLOTS
    first_flat = jnp.where(first_keep, routes[:, 0] * SLOTS + first_slot, spare)
    second_flat = jnp.where(second_keep, routes[:, 1] * SLOTS + second_slot, spare)
    slot_owner = jnp.zeros((spare + 1,), jnp.int32).at[first_flat].set(token_ids).at[second_flat].set(token_ids)
    filled = jnp.zeros((spare + 1,), jnp.float32).at[first_flat].set(1.0).at[second_flat].set(1.0)
    slot_owner = slot_owner[:spare].reshape(EXPERTS, SLOTS)
    filled = filled[:spare].reshape(EXPERTS, SLOTS)
    live_float = live_mask.astype(jnp.float32)
    places = jnp.arange(L, dtype=jnp.int32)
    gap_table = places[:, None] - places[None, :]
    bucket_table = rel_bucket[jnp.maximum(gap_table, 0)]
    causal = (gap_table >= 0) & (gap_table < WINDOW)
    diagonal = gap_table == 0
    score_scale = 1.0 / math.sqrt(DH)

    def forward(x_in, qkv_w, out_w, table, gain_a, gain_m, router_w, up_w, down_w):
        attn_norm = low(norm_rows(x_in, gain_a))
        qkv_all = low(low_back(jnp.einsum('nd,cdf->cnf', attn_norm, qkv_w, precision=HIGHEST)))
        rel_bias = jnp.transpose(table[bucket_table], (2, 0, 1))

        def attend(carry, pieces):
            queries, keys_in, values_in, seg_row, pad_row = pieces
            allowed = (seg_row[:, None] == seg_row[None, :]) & causal & ((pad_row[None, :] == 1) | diagonal)
            scores = jnp.einsum('ihd,jhd->hij', queries, keys_in, precision=HIGHEST) * score_scale + rel_bias
            scores = jnp.where(allowed[None], low_back(scores), NEGATIVE)
            probs = low(jax.nn.softmax(scores, axis=-1))
            return (carry, jnp.einsum('hij,jhd->ihd', probs, values_in, precision=HIGHEST))
        shaped = qkv_all.reshape(3, SEQS, L, H, DH)
        _, heads_out = lax.scan(jax.checkpoint(attend), jnp.zeros((), jnp.float32), (shaped[0], shaped[1], shaped[2], segments, padding))
        heads_out = low(low_back(heads_out.reshape(TOKENS, INNER)))
        attn_out = low_back(jnp.dot(heads_out, out_w, precision=HIGHEST))
        middle = x_in + attn_out
        moe_norm = low(norm_rows(middle, gain_m))
        logits = low_back(jnp.dot(moe_norm, router_w, precision=HIGHEST))
        first_logit = jnp.take_along_axis(logits, routes[:, 0:1], axis=1)[:, 0]
        second_logit = jnp.take_along_axis(logits, routes[:, 1:2], axis=1)[:, 0]
        first_gate = jax.nn.sigmoid(first_logit - second_logit) * live_float
        second_gate = jax.nn.sigmoid(second_logit - first_logit) * live_float

        def expert(pieces):
            up_one, down_one, owner_one, filled_one = pieces
            rows_in = low_back(moe_norm[owner_one]) * filled_one[:, None]
            pre_act = low_back(jnp.dot(rows_in, up_one.T, precision=HIGHEST))
            activated = low(jax.nn.gelu(pre_act))
            return low_back(low(jnp.dot(activated, down_one, precision=HIGHEST)))
        produced = lax.map(jax.checkpoint(expert), (up_w, down_w, slot_owner, filled))
        first_rows = jnp.where(first_keep[:, None], produced[routes[:, 0], first_slot], 0.0)
        second_rows = jnp.where(second_keep[:, None], produced[routes[:, 1], second_slot], 0.0)
        return middle + first_gate[:, None] * first_rows + second_gate[:, None] * second_rows
    block_output, pull = jax.vjp(forward, block_input.astype(jnp.float32), w_qkv.astype(jnp.float32), w_out.astype(jnp.float32), rel_table, gain_attn, gain_moe, w_router.astype(jnp.float32), w_up.astype(jnp.float32), w_down.astype(jnp.float32))
    grads = pull(out_grad.astype(jnp.float32))
    return (block_output, grads[0], grads[1], grads[2], grads[3], grads[4], grads[5], grads[6], grads[7], grads[8])
```

```python
import functools
import math

import jax
import jax.numpy as jnp
from jax import lax
from jax.experimental import pallas as pl
from jax.experimental.pallas import tpu as pltpu
from jax.sharding import PartitionSpec as P

NB = 32
EPSILON = 1e-06
HIGHEST = lax.Precision.HIGHEST
DH = 64
NEGATIVE = -1e30
QB = 256
NT = (((1,), (1,)), ((), ()))
TN = (((0,), (0,)), ((), ()))
NN = (((1,), (0,)), ((), ()))


def mm(a, b, dims):
    return lax.dot_general(a, b, dims, preferred_element_type=jnp.float32)


def build_bias(line_ref, tiles, heads, blocks):
    for h in range(heads):
        for d in range(blocks):
            piece = line_ref[h : h + 1, d * QB : d * QB + 2 * QB]
            wide = jnp.broadcast_to(piece, (QB, 2 * QB))
            turned = pltpu.roll(wide, 0, 1, stride=1, stride_axis=0)
            tiles[h, d] = turned[:, QB:]


def score_block(keys, query, tiles, h, qb, segk_ref, segq_ref):
    raw = mm(keys, query, NT)
    q_seg = segq_ref[0, :, qb * QB : (qb + 1) * QB]
    parts = []
    for kb in range(qb + 1):
        k_seg = segk_ref[0, kb * QB : (kb + 1) * QB, :]
        same = k_seg == q_seg
        if kb == qb:
            row = lax.broadcasted_iota(jnp.int32, (QB, QB), 0)
            col = lax.broadcasted_iota(jnp.int32, (QB, QB), 1)
            same = same | (row == col)
        parts.append(
            jnp.where(same, raw[kb * QB : (kb + 1) * QB] + tiles[h, qb - kb], NEGATIVE)
        )
    return parts


def attend_kernel(heads, blocks, line_ref, segk_ref, segq_ref, rows_ref, w_ref,
                  qkv_ref, out_ref, lse_ref, tiles):
    @pl.when(pl.program_id(0) == 0)
    def _():
        build_bias(line_ref, tiles, heads, blocks)

    for c in range(3):
        qkv_ref[c] = mm(rows_ref[...], w_ref[c], NN).astype(jnp.bfloat16)
    scale = 1.0 / math.sqrt(DH)
    for qb in range(blocks):
        nk = (qb + 1) * QB
        lower = qb * QB
        turned = []
        for h in range(heads):
            cols = slice(h * DH, (h + 1) * DH)
            query = (qkv_ref[0, lower : lower + QB, cols].astype(jnp.float32) * scale).astype(jnp.bfloat16)
            parts = score_block(qkv_ref[1, 0:nk, cols], query, tiles, h, qb, segk_ref, segq_ref)
            peak = functools.reduce(jnp.maximum, [jnp.max(x, axis=0, keepdims=True) for x in parts])
            probs = [jnp.exp(x - peak) for x in parts]
            total = functools.reduce(jnp.add, [jnp.sum(x, axis=0, keepdims=True) for x in probs])
            mixed = functools.reduce(jnp.add, [
                mm(qkv_ref[2, kb * QB : (kb + 1) * QB, cols], x.astype(jnp.bfloat16), TN)
                for kb, x in enumerate(probs)])
            turned.append(mixed / total)
            lse_ref[0, h : h + 1, lower : lower + QB] = peak + jnp.log(total)
        out_ref[lower : lower + QB, :] = jnp.concatenate(turned, axis=0).T.astype(jnp.bfloat16)


def attend(line, segk, segq, rows, w):
    seqs, _, seq_len = segq.shape
    heads = line.shape[0]
    inner = heads * DH
    blocks = seq_len // QB
    width = rows.shape[1]
    return pl.pallas_call(
        functools.partial(attend_kernel, heads, blocks),
        grid=(seqs,),
        in_specs=[
            pl.BlockSpec(line.shape, lambda s: (0, 0)),
            pl.BlockSpec((1, seq_len, 1), lambda s: (s, 0, 0)),
            pl.BlockSpec((1, 1, seq_len), lambda s: (s, 0, 0)),
            pl.BlockSpec((seq_len, width), lambda s: (s, 0)),
            pl.BlockSpec(w.shape, lambda s: (0, 0, 0)),
        ],
        out_specs=[
            pl.BlockSpec((3, seq_len, inner), lambda s: (0, s, 0)),
            pl.BlockSpec((seq_len, inner), lambda s: (s, 0)),
            pl.BlockSpec((1, heads, seq_len), lambda s: (s, 0, 0)),
        ],
        out_shape=[
            jax.ShapeDtypeStruct((3, seqs * seq_len, inner), jnp.bfloat16),
            jax.ShapeDtypeStruct((seqs * seq_len, inner), jnp.bfloat16),
            jax.ShapeDtypeStruct((seqs, heads, seq_len), jnp.float32),
        ],
        scratch_shapes=[pltpu.VMEM((heads, blocks, QB, QB), jnp.float32)],
        compiler_params=pltpu.CompilerParams(vmem_limit_bytes=48 << 20),
        cost_estimate=pl.CostEstimate(flops=10_000_000_000, bytes_accessed=10 << 20, transcendentals=4_000_000),
        name="attend",
    )(line, segk, segq, rows, w)


def attend_back_kernel(heads, blocks, seqs, line_ref, segk_ref, segq_ref, rows_ref, w_ref,
                       qkv_ref, og_ref, lse_ref,
                       norm_ref, wg_ref, lg_ref, tiles, sums, kg, vg, dq):
    step = pl.program_id(0)

    @pl.when(step == 0)
    def _():
        build_bias(line_ref, tiles, heads, blocks)
        sums[...] = jnp.zeros_like(sums)
        wg_ref[...] = jnp.zeros_like(wg_ref)

    scale = 1.0 / math.sqrt(DH)
    for h in range(heads):
        cols = slice(h * DH, (h + 1) * DH)
        kg[...] = jnp.zeros_like(kg)
        vg[...] = jnp.zeros_like(vg)
        for qb in range(blocks):
            nk = (qb + 1) * QB
            lower = qb * QB
            query = (qkv_ref[0, lower : lower + QB, cols].astype(jnp.float32) * scale).astype(jnp.bfloat16)
            grad = og_ref[lower : lower + QB, cols]
            lse = lse_ref[0, h : h + 1, lower : lower + QB]
            parts = score_block(qkv_ref[1, 0:nk, cols], query, tiles, h, qb, segk_ref, segq_ref)
            probs = [jnp.exp(x - lse) for x in parts]
            pg = mm(qkv_ref[2, 0:nk, cols], grad, NT)
            pgs = [pg[kb * QB : (kb + 1) * QB] for kb in range(qb + 1)]
            delta = functools.reduce(jnp.add, [jnp.sum(p * g, axis=0, keepdims=True) for p, g in zip(probs, pgs)])
            dqt = jnp.zeros((DH, QB), jnp.float32)
            for kb in range(qb + 1):
                rows = slice(kb * QB, (kb + 1) * QB)
                sg = (probs[kb] * (pgs[kb] - delta)).astype(jnp.bfloat16)
                sums[h, qb - kb] += sg.astype(jnp.float32)
                vg[rows] += mm(probs[kb].astype(jnp.bfloat16), grad, NN)
                kg[rows] += mm(sg, query, NN)
                dqt = dqt + mm(qkv_ref[1, rows, cols], sg, TN)
            dq[lower : lower + QB, h * DH : (h + 1) * DH] = (dqt * scale).T.astype(jnp.bfloat16)
        inner = heads * DH
        dq[:, inner + h * DH : inner + (h + 1) * DH] = kg[...].astype(jnp.bfloat16)
        dq[:, 2 * inner + h * DH : 2 * inner + (h + 1) * DH] = vg[...].astype(jnp.bfloat16)
    inner = heads * DH
    total = jnp.zeros(norm_ref.shape, jnp.float32)
    for c in range(3):
        piece = dq[:, c * inner : (c + 1) * inner]
        wg_ref[c] += mm(rows_ref[...], piece, TN)
        total = total + mm(piece, w_ref[c], NT)
    norm_ref[...] = total.astype(norm_ref.dtype)

    @pl.when(step == seqs - 1)
    def _():
        for h in range(heads):
            for d in range(blocks):
                lg_ref[h * blocks + d] = fold_tile(sums, h, d)


def fold_tile(sums, h, d):
    blank = jnp.zeros((8, QB), jnp.float32)
    total = jnp.zeros((8, 2 * QB), jnp.float32)
    for g in range(QB // 8):
        piece = jnp.concatenate([sums[h, d, 8 * g : 8 * g + 8, :], blank], axis=1)
        total = total + (piece if g == 0 else pltpu.roll(piece, 2 * QB - 8 * g, 1))
    return total


def lines_of(folded, heads, blocks):
    moved = sum(jnp.roll(folded[:, s, :], -s, axis=1) for s in range(8))
    moved = moved.reshape(heads, blocks, 2, QB)
    ahead = jnp.concatenate([moved[:, 1:, 1], jnp.zeros((heads, 1, QB), jnp.float32)], axis=1)
    return (moved[:, :, 0] + ahead).reshape(heads, blocks * QB)


def attend_back(line, segk, segq, rows, w, qkv, og, lse):
    seqs, _, seq_len = segq.shape
    heads = line.shape[0]
    inner = heads * DH
    blocks = seq_len // QB
    width = rows.shape[1]
    return pl.pallas_call(
        functools.partial(attend_back_kernel, heads, blocks, seqs),
        grid=(seqs,),
        in_specs=[
            pl.BlockSpec(line.shape, lambda s: (0, 0)),
            pl.BlockSpec((1, seq_len, 1), lambda s: (s, 0, 0)),
            pl.BlockSpec((1, 1, seq_len), lambda s: (s, 0, 0)),
            pl.BlockSpec((seq_len, width), lambda s: (s, 0)),
            pl.BlockSpec(w.shape, lambda s: (0, 0, 0)),
            pl.BlockSpec((3, seq_len, inner), lambda s: (0, s, 0)),
            pl.BlockSpec((seq_len, inner), lambda s: (s, 0)),
            pl.BlockSpec((1, heads, seq_len), lambda s: (s, 0, 0)),
        ],
        out_specs=[
            pl.BlockSpec((seq_len, width), lambda s: (s, 0)),
            pl.BlockSpec(w.shape, lambda s: (0, 0, 0)),
            pl.BlockSpec((heads * blocks, 8, 2 * QB), lambda s: (0, 0, 0)),
        ],
        out_shape=[
            jax.ShapeDtypeStruct((seqs * seq_len, width), jnp.bfloat16),
            jax.ShapeDtypeStruct(w.shape, jnp.float32),
            jax.ShapeDtypeStruct((heads * blocks, 8, 2 * QB), jnp.float32),
        ],
        scratch_shapes=[
            pltpu.VMEM((heads, blocks, QB, QB), jnp.float32),
            pltpu.VMEM((heads, blocks, QB, QB), jnp.float32),
            pltpu.VMEM((seq_len, DH), jnp.float32),
            pltpu.VMEM((seq_len, DH), jnp.float32),
            pltpu.VMEM((seq_len, 3 * inner), jnp.bfloat16),
        ],
        compiler_params=pltpu.CompilerParams(vmem_limit_bytes=48 << 20),
        cost_estimate=pl.CostEstimate(flops=20_000_000_000, bytes_accessed=16 << 20, transcendentals=4_000_000),
        name="attend_back",
    )(line, segk, segq, rows, w, qkv, og, lse)


def mask_inputs(segments, padding):
    keyed = jnp.where(padding == 1, segments, -1)
    return keyed[:, :, None], segments[:, None, :]


def line_of(by_distance):
    return jnp.concatenate([jnp.full((by_distance.shape[0], QB), NEGATIVE, jnp.float32), by_distance], axis=1)


FT = 512
ROOT_2_PI = math.sqrt(2.0 / math.pi)


def gelu_pair(x):
    square = x * x
    t = jnp.tanh(ROOT_2_PI * x * (1.0 + 0.044715 * square))
    half = 0.5 * (1.0 + t)
    slope = half + 0.5 * x * (1.0 - t * t) * (ROOT_2_PI * (1.0 + 3 * 0.044715 * square))
    return x * half, slope


def expert_kernel(steps, x_ref, g_ref, up_ref, down_ref, act_ref, pre_ref, back_ref, dot_ref, total, dots):
    step = pl.program_id(0)

    @pl.when(step == 0)
    def _():
        total[...] = jnp.zeros_like(total)
        dots[...] = jnp.zeros_like(dots)

    rows = x_ref.shape[0]
    chunk = 256
    for lower in range(0, rows, chunk):
        part = slice(lower, lower + chunk)
        pre = mm(x_ref[part], up_ref[...], NT)
        out_side = mm(g_ref[part], down_ref[...], NT)
        act, slope = gelu_pair(pre)
        low = act.astype(jnp.bfloat16)
        act_ref[part] = low
        product = low.astype(jnp.float32) * out_side
        dots[part] += sum(product[:, k : k + 128] for k in range(0, FT, 128))
        back = (out_side * slope).astype(jnp.bfloat16)
        pre_ref[part] = back
        total[part] += mm(back, up_ref[...], NN)

    @pl.when(step == steps - 1)
    def _():
        back_ref[...] = total[...].astype(jnp.bfloat16)
        dot_ref[...] = lax.dot_general(
            jnp.ones((8, 128), jnp.float32), dots[...], NT,
            precision=HIGHEST, preferred_element_type=jnp.float32)


def expert_first(x, g, up, down):
    rows, width = x.shape
    hidden = up.shape[0]
    steps = hidden // FT
    whole = lambda f: (0, 0)
    return pl.pallas_call(
        functools.partial(expert_kernel, steps),
        grid=(steps,),
        in_specs=[
            pl.BlockSpec((rows, width), whole),
            pl.BlockSpec((rows, width), whole),
            pl.BlockSpec((FT, width), lambda f: (f, 0)),
            pl.BlockSpec((FT, width), lambda f: (f, 0)),
        ],
        out_specs=[
            pl.BlockSpec((rows, FT), lambda f: (0, f)),
            pl.BlockSpec((rows, FT), lambda f: (0, f)),
            pl.BlockSpec((rows, width), whole),
            pl.BlockSpec((8, rows), whole),
        ],
        out_shape=[
            jax.ShapeDtypeStruct((rows, hidden), jnp.bfloat16),
            jax.ShapeDtypeStruct((rows, hidden), jnp.bfloat16),
            jax.ShapeDtypeStruct((rows, width), jnp.bfloat16),
            jax.ShapeDtypeStruct((8, rows), jnp.float32),
        ],
        scratch_shapes=[
            pltpu.VMEM((rows, width), jnp.float32),
            pltpu.VMEM((rows, 128), jnp.float32),
        ],
        compiler_params=pltpu.CompilerParams(vmem_limit_bytes=48 << 20),
        cost_estimate=pl.CostEstimate(
            flops=6 * rows * width * hidden, bytes_accessed=32 << 20, transcendentals=rows * hidden),
        name="expert_first",
    )(x, g, up, down)


def expert_late_kernel(steps, x_ref, g_ref, gate_ref, act_ref, pre_ref, down_ref,
                       out_ref, up_grad_ref, down_grad_ref, total, x_gated, g_gated):
    step = pl.program_id(0)

    @pl.when(step == 0)
    def _():
        total[...] = jnp.zeros_like(total)
        gate = gate_ref[...]
        x_gated[...] = (x_ref[...].astype(jnp.float32) * gate).astype(jnp.bfloat16)
        g_gated[...] = (g_ref[...].astype(jnp.float32) * gate).astype(jnp.bfloat16)

    up_grad_ref[...] = mm(pre_ref[...], x_gated[...], TN).astype(up_grad_ref.dtype)
    down_grad_ref[...] = mm(act_ref[...], g_gated[...], TN).astype(down_grad_ref.dtype)
    total[...] += mm(act_ref[...], down_ref[...], NN)

    @pl.when(step == steps - 1)
    def _():
        out_ref[...] = total[...].astype(jnp.bfloat16)


def expert_late(x, g, gate, act, pre, down):
    rows, width = x.shape
    hidden = down.shape[0]
    steps = hidden // FT
    whole = lambda f: (0, 0)
    tile = pl.BlockSpec((FT, width), lambda f: (f, 0))
    return pl.pallas_call(
        functools.partial(expert_late_kernel, steps),
        grid=(steps,),
        in_specs=[
            pl.BlockSpec((rows, width), whole),
            pl.BlockSpec((rows, width), whole),
            pl.BlockSpec((rows, 1), whole),
            pl.BlockSpec((rows, FT), lambda f: (0, f)),
            pl.BlockSpec((rows, FT), lambda f: (0, f)),
            tile,
        ],
        out_specs=[pl.BlockSpec((rows, width), whole), tile, tile],
        out_shape=[
            jax.ShapeDtypeStruct((rows, width), jnp.bfloat16),
            jax.ShapeDtypeStruct((hidden, width), jnp.bfloat16),
            jax.ShapeDtypeStruct((hidden, width), jnp.bfloat16),
        ],
        scratch_shapes=[
            pltpu.VMEM((rows, width), jnp.float32),
            pltpu.VMEM((rows, width), jnp.bfloat16),
            pltpu.VMEM((rows, width), jnp.bfloat16),
        ],
        compiler_params=pltpu.CompilerParams(vmem_limit_bytes=48 << 20),
        cost_estimate=pl.CostEstimate(
            flops=6 * rows * width * hidden, bytes_accessed=32 << 20, transcendentals=0),
        name="expert_late",
    )(x, g, gate, act, pre, down)


def norm_rows(values, gain):
    return values * lax.rsqrt(jnp.mean(values * values, axis=-1, keepdims=True) + EPSILON) * gain


def norm_back(values, gain, grad):
    r = lax.rsqrt(jnp.mean(values * values, axis=-1, keepdims=True) + EPSILON)
    u = values * r
    du = grad * gain
    return r * (du - u * jnp.mean(du * u, axis=-1, keepdims=True)), grad * u


def body(
    block_input,
    out_grad,
    w_qkv,
    w_out,
    rel_table,
    gain_attn,
    gain_moe,
    w_router,
    w_up,
    w_down,
    routes,
    segments,
    padding,
    rel_bucket,
):
    tensor_pos = lax.axis_index("tensor")
    rows_local, width = block_input.shape
    seq_len = segments.shape[1]
    expert_count = w_router.shape[1]
    capacity = (10 * rows_local + 4 * expert_count - 1) // (4 * expert_count)
    slots = expert_count * capacity
    x_float = block_input.astype(jnp.float32)
    grad_float = out_grad.astype(jnp.float32)

    attn_norm = norm_rows(x_float, gain_attn).astype(jnp.bfloat16)
    seq_rows = lax.all_gather(attn_norm, "tensor", axis=0, tiled=True)
    qkv_full = lax.all_gather(w_qkv, "dp", axis=1, tiled=True)
    out_rows = lax.all_gather(w_out, "dp", axis=1, tiled=True)
    out_full = lax.all_gather(out_rows, "tensor", axis=0, tiled=True)
    up_full = lax.all_gather(w_up[0], "tensor", axis=0, tiled=True)
    down_full = lax.all_gather(w_down[0], "tensor", axis=0, tiled=True)

    live_mask = lax.dynamic_slice_in_dim(padding.reshape(-1), tensor_pos * rows_local, rows_local)
    live_float = live_mask.astype(jnp.float32)
    expert_ids = jnp.arange(expert_count, dtype=jnp.int32)
    pick_first = routes[:, 0:1] == expert_ids[None, :]
    pick_second = routes[:, 1:2] == expert_ids[None, :]
    usable = live_mask[:, None] == 1
    first_hot = (pick_first & usable).astype(jnp.int32)
    second_hot = (pick_second & usable).astype(jnp.int32)
    first_place = jnp.sum((jnp.cumsum(first_hot, axis=0) - first_hot) * first_hot, axis=1)
    second_before = (
        jnp.cumsum(second_hot, axis=0) - second_hot + jnp.sum(first_hot, axis=0, keepdims=True)
    )
    second_place = jnp.sum(second_before * second_hot, axis=1)
    first_slot = jnp.where(
        (live_mask == 1) & (first_place < capacity), routes[:, 0] * capacity + first_place, -1
    )
    second_slot = jnp.where(
        (live_mask == 1) & (second_place < capacity), routes[:, 1] * capacity + second_place, -1
    )
    slot_ids = jnp.arange(slots, dtype=jnp.int32)
    select_first = slot_ids[:, None] == first_slot[None, :]
    select_second = slot_ids[:, None] == second_slot[None, :]
    select_both = (select_first | select_second).astype(jnp.bfloat16)
    select_first_low = select_first.astype(jnp.bfloat16)
    select_second_low = select_second.astype(jnp.bfloat16)

    def to_experts(rows):
        return lax.all_to_all(rows, "dp", split_axis=0, concat_axis=0, tiled=True)

    grad_rows = jnp.dot(select_both, out_grad, preferred_element_type=jnp.float32)
    sent_grads = to_experts(grad_rows.astype(jnp.bfloat16).reshape(expert_count, capacity, width))
    sent_grads = sent_grads.reshape(slots, width)

    heads = qkv_full.shape[2] // DH
    inner = heads * DH
    table_local = lax.dynamic_slice_in_dim(rel_table, tensor_pos * heads, heads, 1)
    bucket_hot = (rel_bucket[:, None] == jnp.arange(NB, dtype=jnp.int32)[None, :]).astype(jnp.float32)
    line = line_of(jnp.dot(bucket_hot, table_local, precision=HIGHEST).T)
    segk, segq = mask_inputs(segments, padding)
    qkv_low, heads_low, lse = attend(line, segk, segq, seq_rows, qkv_full)
    heads_own = lax.all_to_all(heads_low, "tensor", split_axis=0, concat_axis=1, tiled=True)

    middle = x_float + jnp.dot(heads_own, out_full, preferred_element_type=jnp.float32)
    moe_low = norm_rows(middle, gain_moe).astype(jnp.bfloat16)
    rows_out = jnp.dot(select_both, moe_low, preferred_element_type=jnp.float32)
    sent_rows = to_experts(rows_out.astype(jnp.bfloat16).reshape(expert_count, capacity, width))
    sent_rows = sent_rows.reshape(slots, width)
    logits = jnp.dot(moe_low, w_router, preferred_element_type=jnp.float32)
    first_logit = jnp.sum(jnp.where(pick_first, logits, 0.0), axis=1)
    second_logit = jnp.sum(jnp.where(pick_second, logits, 0.0), axis=1)
    first_gate = jax.nn.sigmoid(first_logit - second_logit) * live_float
    second_gate = jax.nn.sigmoid(second_logit - first_logit) * live_float
    slot_gate = jnp.sum(
        jnp.where(select_first, first_gate[None, :], 0.0)
        + jnp.where(select_second, second_gate[None, :], 0.0),
        axis=1,
    )
    sent_gates = to_experts(slot_gate.reshape(expert_count, capacity)).reshape(slots, 1)

    act, pre_grad, back, dots = expert_first(sent_rows, sent_grads, up_full, down_full)
    returned_grad = to_experts(back.reshape(expert_count, capacity, width)).reshape(slots, width)
    slot_dots = to_experts(dots[0].reshape(expert_count, capacity)).reshape(slots)
    produced, up_part, down_part = expert_late(
        sent_rows, sent_grads, sent_gates, act, pre_grad, down_full
    )
    returned = to_experts(produced.reshape(expert_count, capacity, width)).reshape(slots, width)
    w_up_grad = lax.psum_scatter(up_part, "tensor", scatter_dimension=0, tiled=True)
    w_down_grad = lax.psum_scatter(down_part, "tensor", scatter_dimension=0, tiled=True)

    first_dot = jnp.sum(jnp.where(select_first, slot_dots[:, None], 0.0), axis=0)
    second_dot = jnp.sum(jnp.where(select_second, slot_dots[:, None], 0.0), axis=0)
    coefficient = first_gate * second_gate * (first_dot - second_dot)
    logit_grad = (
        jnp.where(pick_first, coefficient[:, None], 0.0)
        - jnp.where(pick_second, coefficient[:, None], 0.0)
    ).astype(jnp.bfloat16)
    router_grad = jnp.einsum("nd,ne->de", moe_low, logit_grad, preferred_element_type=jnp.float32)

    def gated(rows):
        first_rows = jnp.einsum("st,sd->td", select_first_low, rows, preferred_element_type=jnp.float32)
        second_rows = jnp.einsum("st,sd->td", select_second_low, rows, preferred_element_type=jnp.float32)
        return first_gate[:, None] * first_rows + second_gate[:, None] * second_rows

    moe_norm_grad = (
        jnp.einsum("ne,de->nd", logit_grad, w_router, preferred_element_type=jnp.float32)
        + gated(returned_grad)
    )
    middle_back, gain_moe_rows = norm_back(middle, gain_moe, moe_norm_grad)
    middle_grad = grad_float + middle_back
    gain_moe_grad = jnp.sum(gain_moe_rows, axis=0)
    attn_grad = middle_grad.astype(jnp.bfloat16)
    heads_grad = jnp.einsum("nd,fd->nf", attn_grad, out_full, preferred_element_type=jnp.float32)
    heads_grad = lax.all_to_all(
        heads_grad.astype(jnp.bfloat16), "tensor", split_axis=1, concat_axis=0, tiled=True
    )
    out_part = jnp.einsum("nf,nd->fd", heads_own, attn_grad, preferred_element_type=jnp.float32)
    out_part = lax.psum_scatter(out_part.astype(jnp.bfloat16), "tensor", scatter_dimension=0, tiled=True)
    w_out_grad = lax.psum_scatter(out_part.astype(jnp.float32), "dp", scatter_dimension=1, tiled=True)
    gain_moe_grad, router_grad = lax.psum((gain_moe_grad, router_grad), ("dp", "tensor"))

    norm_part, qkv_part, folded = attend_back(
        line, segk, segq, seq_rows, qkv_full, qkv_low, heads_grad, lse
    )
    attn_norm_grad = lax.psum_scatter(norm_part, "tensor", scatter_dimension=0, tiled=True)
    input_back, gain_attn_rows = norm_back(x_float, gain_attn, attn_norm_grad.astype(jnp.float32))
    input_grad = middle_grad + input_back
    gain_attn_grad = jnp.sum(gain_attn_rows, axis=0)
    w_qkv_grad = lax.psum_scatter(qkv_part, "dp", scatter_dimension=1, tiled=True)
    line_grad = lines_of(folded, heads, seq_len // QB)
    table_part = jnp.dot(bucket_hot.T, line_grad.T, precision=HIGHEST)
    table_whole = lax.dynamic_update_slice(
        jnp.zeros(rel_table.shape, jnp.float32), table_part, (0, tensor_pos * heads)
    )
    gain_attn_grad, table_whole = lax.psum((gain_attn_grad, table_whole), ("dp", "tensor"))
    block_output = middle + gated(returned)
    return (
        block_output,
        input_grad,
        w_qkv_grad,
        w_out_grad,
        table_whole,
        gain_attn_grad,
        gain_moe_grad,
        router_grad,
        w_up_grad.astype(jnp.float32)[None],
        w_down_grad.astype(jnp.float32)[None],
    )


def solution(mesh):
    in_specs = (
        P(("dp", "tensor"), None),
        P(("dp", "tensor"), None),
        P(None, "dp", "tensor"),
        P("tensor", "dp"),
        P(),
        P(),
        P(),
        P(),
        P("dp", "tensor", None),
        P("dp", "tensor", None),
        P(("dp", "tensor"), None),
        P("dp", None),
        P("dp", None),
        P(),
    )
    out_specs = (
        P(("dp", "tensor"), None),
        P(("dp", "tensor"), None),
        P(None, "dp", "tensor"),
        P("tensor", "dp"),
        P(),
        P(),
        P(),
        P(),
        P("dp", "tensor", None),
        P("dp", "tensor", None),
    )
    return jax.shard_map(body, mesh=mesh, in_specs=in_specs, out_specs=out_specs, check_vma=False)
```

```python
import functools
import math

import jax
import jax.numpy as jnp
from jax import lax
from jax.experimental import pallas as pl
from jax.experimental.pallas import tpu as pltpu
from jax.sharding import PartitionSpec as P

NB = 32
EPSILON = 1e-06
HIGHEST = lax.Precision.HIGHEST
DH = 64
NEGATIVE = -1e30
QB = 256
NT = (((1,), (1,)), ((), ()))
TN = (((0,), (0,)), ((), ()))
NN = (((1,), (0,)), ((), ()))


def mm(a, b, dims):
    return lax.dot_general(a, b, dims, preferred_element_type=jnp.float32)


def build_bias(line_ref, tiles, heads, blocks):
    for h in range(heads):
        for d in range(blocks):
            piece = line_ref[h : h + 1, d * QB : d * QB + 2 * QB]
            wide = jnp.broadcast_to(piece, (QB, 2 * QB))
            turned = pltpu.roll(wide, 0, 1, stride=1, stride_axis=0)
            tiles[h, d] = turned[:, QB:]


def score_block(keys, query, tiles, h, qb, segk_ref, segq_ref):
    raw = mm(keys, query, NT)
    q_seg = segq_ref[:, qb * QB : (qb + 1) * QB]
    parts = []
    for kb in range(qb + 1):
        k_seg = segk_ref[kb * QB : (kb + 1) * QB, :]
        same = k_seg == q_seg
        if kb == qb:
            row = lax.broadcasted_iota(jnp.int32, (QB, QB), 0)
            col = lax.broadcasted_iota(jnp.int32, (QB, QB), 1)
            same = same | (row == col)
        parts.append(
            jnp.where(same, raw[kb * QB : (kb + 1) * QB] + tiles[h, qb - kb], NEGATIVE)
        )
    return parts


def attend_back_kernel(heads, blocks, seqs, line_ref, segk_ref, segq_ref, rows_ref, w_ref,
                       qkv_ref, og_ref, lse_ref,
                       norm_ref, wg_ref, lg_ref, tiles, sums, kg, vg, dq):
    step = pl.program_id(0)

    @pl.when(step == 0)
    def _():
        build_bias(line_ref, tiles, heads, blocks)
        sums[...] = jnp.zeros_like(sums)
        wg_ref[...] = jnp.zeros_like(wg_ref)

    scale = 1.0 / math.sqrt(DH)
    for h in range(heads):
        cols = slice(h * DH, (h + 1) * DH)
        kg[...] = jnp.zeros_like(kg)
        vg[...] = jnp.zeros_like(vg)
        for qb in range(blocks):
            nk = (qb + 1) * QB
            lower = qb * QB
            query = (qkv_ref[0, 0, lower : lower + QB, cols].astype(jnp.float32) * scale).astype(jnp.bfloat16)
            grad = og_ref[lower : lower + QB, cols]
            lse = lse_ref[0, h : h + 1, lower : lower + QB]
            parts = score_block(qkv_ref[0, 1, 0:nk, cols], query, tiles, h, qb, segk_ref.at[0], segq_ref.at[0])
            probs = [jnp.exp(x - lse) for x in parts]
            pg = mm(qkv_ref[0, 2, 0:nk, cols], grad, NT)
            pgs = [pg[kb * QB : (kb + 1) * QB] for kb in range(qb + 1)]
            delta = functools.reduce(jnp.add, [jnp.sum(p * g, axis=0, keepdims=True) for p, g in zip(probs, pgs)])
            dqt = jnp.zeros((DH, QB), jnp.float32)
            for kb in range(qb + 1):
                rows = slice(kb * QB, (kb + 1) * QB)
                sg = (probs[kb] * (pgs[kb] - delta)).astype(jnp.bfloat16)
                sums[h, qb - kb] += sg.astype(jnp.float32)
                vg[rows] += mm(probs[kb].astype(jnp.bfloat16), grad, NN)
                kg[rows] += mm(sg, query, NN)
                dqt = dqt + mm(qkv_ref[0, 1, rows, cols], sg, TN)
            dq[lower : lower + QB, h * DH : (h + 1) * DH] = (dqt * scale).T.astype(jnp.bfloat16)
        inner = heads * DH
        dq[:, inner + h * DH : inner + (h + 1) * DH] = kg[...].astype(jnp.bfloat16)
        dq[:, 2 * inner + h * DH : 2 * inner + (h + 1) * DH] = vg[...].astype(jnp.bfloat16)
    inner = heads * DH
    total = jnp.zeros(norm_ref.shape, jnp.float32)
    for c in range(3):
        piece = dq[:, c * inner : (c + 1) * inner]
        wg_ref[c] += mm(rows_ref[...], piece, TN)
        total = total + mm(piece, w_ref[c], NT)
    norm_ref[...] = total.astype(norm_ref.dtype)

    @pl.when(step == seqs - 1)
    def _():
        for h in range(heads):
            for d in range(blocks):
                lg_ref[h * blocks + d] = fold_tile(sums, h, d)


def fold_tile(sums, h, d):
    blank = jnp.zeros((8, QB), jnp.float32)
    total = jnp.zeros((8, 2 * QB), jnp.float32)
    for g in range(QB // 8):
        piece = jnp.concatenate([sums[h, d, 8 * g : 8 * g + 8, :], blank], axis=1)
        total = total + (piece if g == 0 else pltpu.roll(piece, 2 * QB - 8 * g, 1))
    return total


def lines_of(folded, heads, blocks):
    moved = sum(jnp.roll(folded[:, s, :], -s, axis=1) for s in range(8))
    moved = moved.reshape(heads, blocks, 2, QB)
    ahead = jnp.concatenate([moved[:, 1:, 1], jnp.zeros((heads, 1, QB), jnp.float32)], axis=1)
    return (moved[:, :, 0] + ahead).reshape(heads, blocks * QB)


def attend_back(line, segk, segq, rows, w, qkv, og, lse):
    seqs, _, seq_len = segq.shape
    heads = line.shape[0]
    inner = heads * DH
    blocks = seq_len // QB
    width = rows.shape[1]
    return pl.pallas_call(
        functools.partial(attend_back_kernel, heads, blocks, seqs),
        grid=(seqs,),
        in_specs=[
            pl.BlockSpec(line.shape, lambda s: (0, 0)),
            pl.BlockSpec((1, seq_len, 1), lambda s: (s, 0, 0)),
            pl.BlockSpec((1, 1, seq_len), lambda s: (s, 0, 0)),
            pl.BlockSpec((seq_len, width), lambda s: (s, 0)),
            pl.BlockSpec(w.shape, lambda s: (0, 0, 0)),
            pl.BlockSpec((1, 3, seq_len, inner), lambda s: (s, 0, 0, 0)),
            pl.BlockSpec((seq_len, inner), lambda s: (s, 0)),
            pl.BlockSpec((1, heads, seq_len), lambda s: (s, 0, 0)),
        ],
        out_specs=[
            pl.BlockSpec((seq_len, width), lambda s: (s, 0)),
            pl.BlockSpec(w.shape, lambda s: (0, 0, 0)),
            pl.BlockSpec((heads * blocks, 8, 2 * QB), lambda s: (0, 0, 0)),
        ],
        out_shape=[
            jax.ShapeDtypeStruct((seqs * seq_len, width), jnp.bfloat16),
            jax.ShapeDtypeStruct(w.shape, jnp.float32),
            jax.ShapeDtypeStruct((heads * blocks, 8, 2 * QB), jnp.float32),
        ],
        scratch_shapes=[
            pltpu.VMEM((heads, blocks, QB, QB), jnp.float32),
            pltpu.VMEM((heads, blocks, QB, QB), jnp.float32),
            pltpu.VMEM((seq_len, DH), jnp.float32),
            pltpu.VMEM((seq_len, DH), jnp.float32),
            pltpu.VMEM((seq_len, 3 * inner), jnp.bfloat16),
        ],
        compiler_params=pltpu.CompilerParams(vmem_limit_bytes=48 << 20),
        cost_estimate=pl.CostEstimate(flops=20_000_000_000, bytes_accessed=16 << 20, transcendentals=4_000_000),
        name="attend_back",
    )(line, segk, segq, rows, w, qkv, og, lse)


def mask_inputs(segments, padding):
    keyed = jnp.where(padding == 1, segments, -1)
    return keyed[:, :, None], segments[:, None, :]


def line_of(by_distance):
    return jnp.concatenate([jnp.full((by_distance.shape[0], QB), NEGATIVE, jnp.float32), by_distance], axis=1)


MESH = pl.DeviceIdType.MESH


def remote(src, dst, send, recv, axis, place):
    return pltpu.make_async_remote_copy(
        src_ref=src, dst_ref=dst, send_sem=send, recv_sem=recv, device_id={axis: place}, device_id_type=MESH
    )


def each_peer(count, step):
    if count <= 8:
        for r in range(1, count):
            step(r)
    else:
        def one(r, carry):
            step(r)
            return carry
        lax.fori_loop(1, count, one, 0)


def greet(dp_count, tensor_count):
    barrier = pltpu.get_barrier_semaphore()
    dp, tp = lax.axis_index("dp"), lax.axis_index("tensor")
    for r in range(1, tensor_count):
        pl.semaphore_signal(barrier, inc=1, device_id={"tensor": lax.rem(tp + r, tensor_count)}, device_id_type=MESH)

    def signal(r):
        pl.semaphore_signal(barrier, inc=1, device_id={"dp": lax.rem(dp + r, dp_count)}, device_id_type=MESH)
    each_peer(dp_count, signal)
    return lambda: pl.semaphore_wait(barrier, tensor_count - 1 + dp_count - 1)


def place_pairs(routes_ref, live_ref, experts, capacity, cap_rows):
    tokens = live_ref.shape[1]
    live = live_ref[...] == 1
    ids = lax.broadcasted_iota(jnp.int32, (experts, tokens), 0)
    row = lax.broadcasted_iota(jnp.int32, (tokens, tokens), 0)
    col = lax.broadcasted_iota(jnp.int32, (tokens, tokens), 1)
    before = (row < col).astype(jnp.float32).astype(jnp.bfloat16)
    slots = []
    base = jnp.zeros((experts, 1), jnp.float32)
    for k in range(2):
        route = routes_ref[k : k + 1, :]
        hot = jnp.where((ids == route) & live, 1.0, 0.0)
        count = mm(hot.astype(jnp.bfloat16), before, NN) + base
        place = jnp.sum(count * hot, axis=0, keepdims=True).astype(jnp.int32)
        slots.append(jnp.where(live & (place < capacity), route * cap_rows + place, -1))
        base = base + jnp.sum(hot, axis=1, keepdims=True)
    return slots


def chosen(first, second, expert, cap_rows):
    ids = lax.broadcasted_iota(jnp.int32, (cap_rows, first.shape[1]), 0) + expert * cap_rows
    return jnp.where((ids == first) | (ids == second), 1.0, 0.0).astype(jnp.bfloat16)


def attend_sequence(heads, blocks, seq, line_tiles, segk_ref, segq_ref, qkv, heads_out, lse_ref):
    scale = 1.0 / math.sqrt(DH)
    for qb in range(blocks):
        nk = (qb + 1) * QB
        lower = qb * QB
        turned = []
        for h in range(heads):
            cols = slice(h * DH, (h + 1) * DH)
            query = (qkv[seq, 0, lower : lower + QB, cols].astype(jnp.float32) * scale).astype(jnp.bfloat16)
            parts = score_block(qkv[seq, 1, 0:nk, cols], query, line_tiles, h, qb, segk_ref.at[seq], segq_ref.at[seq])
            peak = functools.reduce(jnp.maximum, [jnp.max(x, axis=0, keepdims=True) for x in parts])
            probs = [jnp.exp(x - peak) for x in parts]
            total = functools.reduce(jnp.add, [jnp.sum(x, axis=0, keepdims=True) for x in probs])
            mixed = functools.reduce(jnp.add, [
                mm(qkv[seq, 2, kb * QB : (kb + 1) * QB, cols], x.astype(jnp.bfloat16), TN)
                for kb, x in enumerate(probs)])
            turned.append(mixed / total)
            lse_ref[seq, h : h + 1, lower : lower + QB] = peak + jnp.log(total)
        mixed = jnp.concatenate(turned, axis=0).T.astype(jnp.bfloat16)
        half = blocks // 2
        heads_out[seq * 2 + qb // half, (qb % half) * QB : (qb % half + 1) * QB, :] = mixed


def front_kernel(sizes, x_ref, gain_ref, w_ref, grad_ref, routes_ref, live_ref, line_ref, segk_ref, segq_ref,
                 rows, w_all, qkv, lse_ref, heads_all, slots_ref, cot,
                 tiles, heads_out, cot_send,
                 far_send, far_recv, w_send, w_recv, cot_s, cot_r, head_send, head_recv, local_sem):
    dp_count, tensor_count, experts, capacity, cap_rows, heads, blocks, gather_w = sizes
    dp, tp = lax.axis_index("dp"), lax.axis_index("tensor")
    sib, opp = tp + 1 - 2 * lax.rem(tp, 2), lax.rem(tp + 2, tensor_count)
    wait_barrier = greet(dp_count, tensor_count)

    x = x_ref[...].astype(jnp.float32)
    r = lax.rsqrt(jnp.mean(x * x, axis=-1, keepdims=True) + EPSILON)
    rows[tp] = (x * r * gain_ref[...]).astype(jnp.bfloat16)
    wait_barrier()

    half = rows.shape[1] // 2
    parts = [pl.ds(0, half), pl.ds(half, half)]
    far = [remote(rows.at[tp, p], rows.at[tp, p], far_send.at[k], far_recv.at[k], "tensor", opp) for k, p in enumerate(parts)]
    near = remote(rows.at[tp], rows.at[tp], far_send.at[2], far_recv.at[2], "tensor", sib)
    onward = [remote(rows.at[opp, p], rows.at[opp, p], far_send.at[3 + k], far_recv.at[3 + k], "tensor", sib) for k, p in enumerate(parts)]
    for c in far:
        c.start()
    near.start()

    def w_copy(r):
        return remote(w_ref, w_all.at[:, dp], w_send.at[r], w_recv.at[r], "dp", lax.rem(dp + r, dp_count))
    if gather_w:
        each_peer(dp_count, lambda r: w_copy(r).start())
        own_w = pltpu.make_async_copy(w_ref, w_all.at[:, dp], local_sem.at[0])
        own_w.start()

    first, second = place_pairs(routes_ref, live_ref, experts, capacity, cap_rows)
    slots_ref[0:1, :] = first
    slots_ref[1:2, :] = second

    def cot_copy(r):
        to = lax.rem(dp + r, dp_count)
        return remote(cot_send.at[to], cot.at[dp], cot_s.at[r], cot_r.at[r], "dp", to)

    def cot_fill(r):
        to = lax.rem(dp + r, dp_count)
        cot_send[to] = mm(chosen(first, second, to, cap_rows), grad_ref[...], NN).astype(jnp.bfloat16)

    def cot_go(r):
        cot_fill(r)
        cot_copy(r).start()
    each_peer(dp_count, cot_go)
    cot_fill(0)
    own_cot = pltpu.make_async_copy(cot_send.at[dp], cot.at[dp], local_sem.at[1])
    own_cot.start()

    build_bias(line_ref, tiles, heads, blocks)
    if gather_w:
        own_w.wait()
        each_peer(dp_count, lambda r: w_copy(r).wait_recv())
    near.wait_recv()

    width = rows.shape[2]
    own_seq = tp // 2
    inner = heads * DH

    def project(seq):
        tokens = rows[pl.ds(seq * 2, 2)].reshape(2 * rows.shape[1], width)
        for c in range(3):
            weight = w_all[c].reshape(width, inner) if gather_w else w_ref[c]
            qkv[seq, c] = mm(tokens, weight, NN).astype(jnp.bfloat16)

    def head_copy(k, to):
        return remote(heads_out.at[to], heads_all.at[tp], head_send.at[k], head_recv.at[k], "tensor", to)

    project(own_seq)
    for k in range(2):
        far[k].wait_recv()
        onward[k].start()
    attend_sequence(heads, blocks, own_seq, tiles, segk_ref, segq_ref, qkv, heads_out, lse_ref)
    head_copy(0, sib).start()
    heads_all[tp] = heads_out[tp]
    for k in range(2):
        onward[k].wait_recv()
    other = 1 - own_seq
    project(other)
    attend_sequence(heads, blocks, other, tiles, segk_ref, segq_ref, qkv, heads_out, lse_ref)
    across = lax.rem(sib + 2, tensor_count)
    head_copy(1, opp).start()
    head_copy(2, across).start()

    own_cot.wait()
    each_peer(dp_count, lambda r: cot_copy(r).wait())
    if gather_w:
        each_peer(dp_count, lambda r: w_copy(r).wait_send())
    for c in far + [near] + onward:
        c.wait_send()
    head_copy(0, sib).wait()
    head_copy(1, opp).wait()
    head_copy(2, across).wait()


def front(sizes, x, gain, w, grad, routes_t, live_row, line, segk, segq):
    dp_count, tensor_count, experts, capacity, cap_rows, heads, blocks, gather_w = sizes
    tokens, width = x.shape
    seq_len = blocks * QB
    seqs = tensor_count * tokens // seq_len
    inner = heads * DH
    vmem = pl.BlockSpec(memory_space=pltpu.VMEM)
    return pl.pallas_call(
        functools.partial(front_kernel, sizes),
        in_specs=[vmem] * 9,
        out_specs=[vmem] * 7,
        out_shape=[
            jax.ShapeDtypeStruct((tensor_count, tokens, width), jnp.bfloat16),
            jax.ShapeDtypeStruct((3, dp_count, width // dp_count, inner) if gather_w else (3, 8, 128), jnp.bfloat16),
            jax.ShapeDtypeStruct((seqs, 3, seq_len, inner), jnp.bfloat16),
            jax.ShapeDtypeStruct((seqs, heads, seq_len), jnp.float32),
            jax.ShapeDtypeStruct((tensor_count, tokens, inner), jnp.bfloat16),
            jax.ShapeDtypeStruct((8, tokens), jnp.int32),
            jax.ShapeDtypeStruct((experts, cap_rows, width), jnp.bfloat16),
        ],
        scratch_shapes=[
            pltpu.VMEM((heads, blocks, QB, QB), jnp.float32),
            pltpu.VMEM((tensor_count, tokens, inner), jnp.bfloat16),
            pltpu.VMEM((experts, cap_rows, width), jnp.bfloat16),
            pltpu.SemaphoreType.DMA((5,)),
            pltpu.SemaphoreType.DMA((5,)),
            pltpu.SemaphoreType.DMA((dp_count,)),
            pltpu.SemaphoreType.DMA((dp_count,)),
            pltpu.SemaphoreType.DMA((dp_count,)),
            pltpu.SemaphoreType.DMA((dp_count,)),
            pltpu.SemaphoreType.DMA((3,)),
            pltpu.SemaphoreType.DMA((3,)),
            pltpu.SemaphoreType.DMA((2,)),
        ],
        compiler_params=pltpu.CompilerParams(
            vmem_limit_bytes=56 << 20, collective_id=1, has_side_effects=True),
        cost_estimate=pl.CostEstimate(flops=20_000_000_000, bytes_accessed=20 << 20, transcendentals=4_000_000),
        name="front",
    )(x, gain, w, grad, routes_t, live_row, line, segk, segq)


FT = 512
ROOT_2_PI = math.sqrt(2.0 / math.pi)


def gelu_pair(x):
    square = x * x
    t = jnp.tanh(ROOT_2_PI * x * (1.0 + 0.044715 * square))
    half = 0.5 * (1.0 + t)
    slope = half + 0.5 * x * (1.0 - t * t) * (ROOT_2_PI * (1.0 + 3 * 0.044715 * square))
    return x * half, slope


def expert_kernel(steps, x_ref, g_ref, up_ref, down_ref, act_ref, pre_ref, back_ref, dot_ref, total, dots):
    step = pl.program_id(0)

    @pl.when(step == 0)
    def _():
        total[...] = jnp.zeros_like(total)
        dots[...] = jnp.zeros_like(dots)

    rows = x_ref.shape[0]
    chunk = 256
    for lower in range(0, rows, chunk):
        part = slice(lower, lower + chunk)
        pre = mm(x_ref[part], up_ref[...], NT)
        out_side = mm(g_ref[part], down_ref[...], NT)
        act, slope = gelu_pair(pre)
        low = act.astype(jnp.bfloat16)
        act_ref[part] = low
        product = low.astype(jnp.float32) * out_side
        dots[part] += sum(product[:, k : k + 128] for k in range(0, FT, 128))
        back = (out_side * slope).astype(jnp.bfloat16)
        pre_ref[part] = back
        total[part] += mm(back, up_ref[...], NN)

    @pl.when(step == steps - 1)
    def _():
        back_ref[...] = total[...].astype(jnp.bfloat16)
        dot_ref[...] = lax.dot_general(
            jnp.ones((8, 128), jnp.float32), dots[...], NT,
            precision=HIGHEST, preferred_element_type=jnp.float32)


def expert_first(x, g, up, down):
    rows, width = x.shape
    hidden = up.shape[0]
    steps = hidden // FT
    whole = lambda f: (0, 0)
    return pl.pallas_call(
        functools.partial(expert_kernel, steps),
        grid=(steps,),
        in_specs=[
            pl.BlockSpec((rows, width), whole),
            pl.BlockSpec((rows, width), whole),
            pl.BlockSpec((FT, width), lambda f: (f, 0)),
            pl.BlockSpec((FT, width), lambda f: (f, 0)),
        ],
        out_specs=[
            pl.BlockSpec((rows, FT), lambda f: (0, f)),
            pl.BlockSpec((rows, FT), lambda f: (0, f)),
            pl.BlockSpec((rows, width), whole),
            pl.BlockSpec((8, rows), whole),
        ],
        out_shape=[
            jax.ShapeDtypeStruct((rows, hidden), jnp.bfloat16),
            jax.ShapeDtypeStruct((rows, hidden), jnp.bfloat16),
            jax.ShapeDtypeStruct((rows, width), jnp.bfloat16),
            jax.ShapeDtypeStruct((8, rows), jnp.float32),
        ],
        scratch_shapes=[
            pltpu.VMEM((rows, width), jnp.float32),
            pltpu.VMEM((rows, 128), jnp.float32),
        ],
        compiler_params=pltpu.CompilerParams(vmem_limit_bytes=48 << 20),
        cost_estimate=pl.CostEstimate(
            flops=6 * rows * width * hidden, bytes_accessed=32 << 20, transcendentals=rows * hidden),
        name="expert_first",
    )(x, g, up, down)


def expert_late_kernel(steps, x_ref, g_ref, gate_ref, act_ref, pre_ref, down_ref,
                       out_ref, up_grad_ref, down_grad_ref, total, x_gated, g_gated):
    step = pl.program_id(0)

    @pl.when(step == 0)
    def _():
        total[...] = jnp.zeros_like(total)
        gate = gate_ref[...]
        x_gated[...] = (x_ref[...].astype(jnp.float32) * gate).astype(jnp.bfloat16)
        g_gated[...] = (g_ref[...].astype(jnp.float32) * gate).astype(jnp.bfloat16)

    up_grad_ref[...] = mm(pre_ref[...], x_gated[...], TN).astype(up_grad_ref.dtype)
    down_grad_ref[...] = mm(act_ref[...], g_gated[...], TN).astype(down_grad_ref.dtype)
    total[...] += mm(act_ref[...], down_ref[...], NN)

    @pl.when(step == steps - 1)
    def _():
        out_ref[...] = total[...].astype(jnp.bfloat16)


def expert_late(x, g, gate, act, pre, down):
    rows, width = x.shape
    hidden = down.shape[0]
    steps = hidden // FT
    whole = lambda f: (0, 0)
    tile = pl.BlockSpec((FT, width), lambda f: (f, 0))
    return pl.pallas_call(
        functools.partial(expert_late_kernel, steps),
        grid=(steps,),
        in_specs=[
            pl.BlockSpec((rows, width), whole),
            pl.BlockSpec((rows, width), whole),
            pl.BlockSpec((rows, 1), whole),
            pl.BlockSpec((rows, FT), lambda f: (0, f)),
            pl.BlockSpec((rows, FT), lambda f: (0, f)),
            tile,
        ],
        out_specs=[pl.BlockSpec((rows, width), whole), tile, tile],
        out_shape=[
            jax.ShapeDtypeStruct((rows, width), jnp.bfloat16),
            jax.ShapeDtypeStruct((hidden, width), jnp.bfloat16),
            jax.ShapeDtypeStruct((hidden, width), jnp.bfloat16),
        ],
        scratch_shapes=[
            pltpu.VMEM((rows, width), jnp.float32),
            pltpu.VMEM((rows, width), jnp.bfloat16),
            pltpu.VMEM((rows, width), jnp.bfloat16),
        ],
        compiler_params=pltpu.CompilerParams(vmem_limit_bytes=48 << 20),
        cost_estimate=pl.CostEstimate(
            flops=6 * rows * width * hidden, bytes_accessed=32 << 20, transcendentals=0),
        name="expert_late",
    )(x, g, gate, act, pre, down)


def norm_rows(values, gain):
    return values * lax.rsqrt(jnp.mean(values * values, axis=-1, keepdims=True) + EPSILON) * gain


def norm_back(values, gain, grad):
    r = lax.rsqrt(jnp.mean(values * values, axis=-1, keepdims=True) + EPSILON)
    u = values * r
    du = grad * gain
    return r * (du - u * jnp.mean(du * u, axis=-1, keepdims=True)), grad * u


def body(
    block_input,
    out_grad,
    w_qkv,
    w_out,
    rel_table,
    gain_attn,
    gain_moe,
    w_router,
    w_up,
    w_down,
    routes,
    segments,
    padding,
    rel_bucket,
):
    tensor_pos = lax.axis_index("tensor")
    rows_local, width = block_input.shape
    seq_len = segments.shape[1]
    expert_count = w_router.shape[1]
    capacity = (10 * rows_local + 4 * expert_count - 1) // (4 * expert_count)
    x_float = block_input.astype(jnp.float32)
    grad_float = out_grad.astype(jnp.float32)

    dp_count, tensor_count = lax.axis_size("dp"), lax.axis_size("tensor")
    cap_rows = -(-capacity // 16) * 16
    slots = expert_count * cap_rows
    heads = w_qkv.shape[2] // DH
    gather_w = w_qkv.shape[1] % 16 == 0
    sizes = (dp_count, tensor_count, expert_count, capacity, cap_rows, heads, seq_len // QB, gather_w)

    out_rows = lax.all_gather(w_out, "dp", axis=1, tiled=True)
    out_full = lax.all_gather(out_rows, "tensor", axis=0, tiled=True)
    up_full = lax.all_gather(w_up[0], "tensor", axis=0, tiled=True)
    down_full = lax.all_gather(w_down[0], "tensor", axis=0, tiled=True)

    live_mask = lax.dynamic_slice_in_dim(padding.reshape(-1), tensor_pos * rows_local, rows_local)
    live_float = live_mask.astype(jnp.float32)
    table_local = lax.dynamic_slice_in_dim(rel_table, tensor_pos * heads, heads, 1)
    bucket_hot = (rel_bucket[:, None] == jnp.arange(NB, dtype=jnp.int32)[None, :]).astype(jnp.float32)
    line = line_of(jnp.dot(bucket_hot, table_local, precision=HIGHEST).T)
    segk, segq = mask_inputs(segments, padding)
    qkv_weight = w_qkv if gather_w else lax.all_gather(w_qkv, "dp", axis=1, tiled=True)
    seq_rows, qkv_full, qkv_low, lse, heads_all, slot_rows, cot = front(
        sizes, block_input, gain_attn[None], qkv_weight, out_grad, routes.T, live_mask[None], line, segk, segq
    )
    sent_grads = cot.reshape(slots, width)
    seq_rows = seq_rows.reshape(tensor_count * rows_local, width)
    qkv_full = qkv_full.reshape(3, width, heads * DH) if gather_w else qkv_weight
    heads_own = jnp.moveaxis(heads_all, 0, 1).reshape(rows_local, -1)

    expert_ids = jnp.arange(expert_count, dtype=jnp.int32)
    pick_first = routes[:, 0:1] == expert_ids[None, :]
    pick_second = routes[:, 1:2] == expert_ids[None, :]
    slot_ids = jnp.arange(slots, dtype=jnp.int32)
    select_first = slot_ids[:, None] == slot_rows[0][None, :]
    select_second = slot_ids[:, None] == slot_rows[1][None, :]
    select_both = (select_first | select_second).astype(jnp.bfloat16)
    select_first_low = select_first.astype(jnp.bfloat16)
    select_second_low = select_second.astype(jnp.bfloat16)

    def to_experts(rows):
        return lax.all_to_all(rows, "dp", split_axis=0, concat_axis=0, tiled=True)

    middle = x_float + jnp.dot(heads_own, out_full, preferred_element_type=jnp.float32)
    moe_low = norm_rows(middle, gain_moe).astype(jnp.bfloat16)
    rows_out = jnp.dot(select_both, moe_low, preferred_element_type=jnp.float32)
    sent_rows = to_experts(rows_out.astype(jnp.bfloat16).reshape(expert_count, cap_rows, width))
    sent_rows = sent_rows.reshape(slots, width)
    logits = jnp.dot(moe_low, w_router, preferred_element_type=jnp.float32)
    first_logit = jnp.sum(jnp.where(pick_first, logits, 0.0), axis=1)
    second_logit = jnp.sum(jnp.where(pick_second, logits, 0.0), axis=1)
    first_gate = jax.nn.sigmoid(first_logit - second_logit) * live_float
    second_gate = jax.nn.sigmoid(second_logit - first_logit) * live_float
    slot_gate = jnp.sum(
        jnp.where(select_first, first_gate[None, :], 0.0)
        + jnp.where(select_second, second_gate[None, :], 0.0),
        axis=1,
    )
    sent_gates = to_experts(slot_gate.reshape(expert_count, cap_rows)).reshape(slots, 1)

    act, pre_grad, back, dots = expert_first(sent_rows, sent_grads, up_full, down_full)
    returned_grad = to_experts(back.reshape(expert_count, cap_rows, width)).reshape(slots, width)
    slot_dots = to_experts(dots[0].reshape(expert_count, cap_rows)).reshape(slots)
    produced, up_part, down_part = expert_late(
        sent_rows, sent_grads, sent_gates, act, pre_grad, down_full
    )
    returned = to_experts(produced.reshape(expert_count, cap_rows, width)).reshape(slots, width)
    w_up_grad = lax.psum_scatter(up_part, "tensor", scatter_dimension=0, tiled=True)
    w_down_grad = lax.psum_scatter(down_part, "tensor", scatter_dimension=0, tiled=True)

    first_dot = jnp.sum(jnp.where(select_first, slot_dots[:, None], 0.0), axis=0)
    second_dot = jnp.sum(jnp.where(select_second, slot_dots[:, None], 0.0), axis=0)
    coefficient = first_gate * second_gate * (first_dot - second_dot)
    logit_grad = (
        jnp.where(pick_first, coefficient[:, None], 0.0)
        - jnp.where(pick_second, coefficient[:, None], 0.0)
    ).astype(jnp.bfloat16)
    router_grad = jnp.einsum("nd,ne->de", moe_low, logit_grad, preferred_element_type=jnp.float32)

    def gated(rows):
        first_rows = jnp.einsum("st,sd->td", select_first_low, rows, preferred_element_type=jnp.float32)
        second_rows = jnp.einsum("st,sd->td", select_second_low, rows, preferred_element_type=jnp.float32)
        return first_gate[:, None] * first_rows + second_gate[:, None] * second_rows

    moe_norm_grad = (
        jnp.einsum("ne,de->nd", logit_grad, w_router, preferred_element_type=jnp.float32)
        + gated(returned_grad)
    )
    middle_back, gain_moe_rows = norm_back(middle, gain_moe, moe_norm_grad)
    middle_grad = grad_float + middle_back
    gain_moe_grad = jnp.sum(gain_moe_rows, axis=0)
    attn_grad = middle_grad.astype(jnp.bfloat16)
    heads_grad = jnp.einsum("nd,fd->nf", attn_grad, out_full, preferred_element_type=jnp.float32)
    heads_grad = lax.all_to_all(
        heads_grad.astype(jnp.bfloat16), "tensor", split_axis=1, concat_axis=0, tiled=True
    )
    out_part = jnp.einsum("nf,nd->fd", heads_own, attn_grad, preferred_element_type=jnp.float32)
    out_part = lax.psum_scatter(out_part.astype(jnp.bfloat16), "tensor", scatter_dimension=0, tiled=True)
    w_out_grad = lax.psum_scatter(out_part.astype(jnp.float32), "dp", scatter_dimension=1, tiled=True)
    gain_moe_grad, router_grad = lax.psum((gain_moe_grad, router_grad), ("dp", "tensor"))

    norm_part, qkv_part, folded = attend_back(
        line, segk, segq, seq_rows, qkv_full, qkv_low, heads_grad, lse
    )
    attn_norm_grad = lax.psum_scatter(norm_part, "tensor", scatter_dimension=0, tiled=True)
    input_back, gain_attn_rows = norm_back(x_float, gain_attn, attn_norm_grad.astype(jnp.float32))
    input_grad = middle_grad + input_back
    gain_attn_grad = jnp.sum(gain_attn_rows, axis=0)
    w_qkv_grad = lax.psum_scatter(qkv_part, "dp", scatter_dimension=1, tiled=True)
    line_grad = lines_of(folded, heads, seq_len // QB)
    table_part = jnp.dot(bucket_hot.T, line_grad.T, precision=HIGHEST)
    table_whole = lax.dynamic_update_slice(
        jnp.zeros(rel_table.shape, jnp.float32), table_part, (0, tensor_pos * heads)
    )
    gain_attn_grad, table_whole = lax.psum((gain_attn_grad, table_whole), ("dp", "tensor"))
    block_output = middle + gated(returned)
    return (
        block_output,
        input_grad,
        w_qkv_grad,
        w_out_grad,
        table_whole,
        gain_attn_grad,
        gain_moe_grad,
        router_grad,
        w_up_grad.astype(jnp.float32)[None],
        w_down_grad.astype(jnp.float32)[None],
    )


def solution(mesh):
    in_specs = (
        P(("dp", "tensor"), None),
        P(("dp", "tensor"), None),
        P(None, "dp", "tensor"),
        P("tensor", "dp"),
        P(),
        P(),
        P(),
        P(),
        P("dp", "tensor", None),
        P("dp", "tensor", None),
        P(("dp", "tensor"), None),
        P("dp", None),
        P("dp", None),
        P(),
    )
    out_specs = (
        P(("dp", "tensor"), None),
        P(("dp", "tensor"), None),
        P(None, "dp", "tensor"),
        P("tensor", "dp"),
        P(),
        P(),
        P(),
        P(),
        P("dp", "tensor", None),
        P("dp", "tensor", None),
    )
    return jax.shard_map(body, mesh=mesh, in_specs=in_specs, out_specs=out_specs, check_vma=False)
```

```python
import functools
import math

import jax
import jax.numpy as jnp
from jax import lax
from jax.experimental import pallas as pl
from jax.experimental.pallas import tpu as pltpu
from jax.sharding import PartitionSpec as P

NB = 32
EPSILON = 1e-06
HIGHEST = lax.Precision.HIGHEST
DH = 64
NEGATIVE = -1e30
QB = 256
NT = (((1,), (1,)), ((), ()))
TN = (((0,), (0,)), ((), ()))
NN = (((1,), (0,)), ((), ()))


def mm(a, b, dims):
    return lax.dot_general(a, b, dims, preferred_element_type=jnp.float32)


def build_bias(line_ref, tiles, heads, blocks):
    for h in range(heads):
        for d in range(blocks):
            piece = line_ref[h : h + 1, d * QB : d * QB + 2 * QB]
            wide = jnp.broadcast_to(piece, (QB, 2 * QB))
            turned = pltpu.roll(wide, 0, 1, stride=1, stride_axis=0)
            tiles[h, d] = turned[:, QB:]


def score_block(keys, query, tiles, h, qb, segk_ref, segq_ref):
    raw = mm(keys, query, NT)
    q_seg = segq_ref[:, qb * QB : (qb + 1) * QB]
    parts = []
    for kb in range(qb + 1):
        k_seg = segk_ref[kb * QB : (kb + 1) * QB, :]
        same = k_seg == q_seg
        if kb == qb:
            row = lax.broadcasted_iota(jnp.int32, (QB, QB), 0)
            col = lax.broadcasted_iota(jnp.int32, (QB, QB), 1)
            same = same | (row == col)
        parts.append(
            jnp.where(same, raw[kb * QB : (kb + 1) * QB] + tiles[h, qb - kb], NEGATIVE)
        )
    return parts


def attend_kernel(heads, blocks, line_ref, segk_ref, segq_ref, rows_ref, w_ref,
                  qkv_ref, out_ref, lse_ref, tiles):
    @pl.when(pl.program_id(0) == 0)
    def _():
        build_bias(line_ref, tiles, heads, blocks)

    for c in range(3):
        qkv_ref[c] = mm(rows_ref[...], w_ref[c], NN).astype(jnp.bfloat16)
    scale = 1.0 / math.sqrt(DH)
    for qb in range(blocks):
        nk = (qb + 1) * QB
        lower = qb * QB
        turned = []
        for h in range(heads):
            cols = slice(h * DH, (h + 1) * DH)
            query = (qkv_ref[0, lower : lower + QB, cols].astype(jnp.float32) * scale).astype(jnp.bfloat16)
            parts = score_block(qkv_ref[1, 0:nk, cols], query, tiles, h, qb, segk_ref.at[0], segq_ref.at[0])
            peak = functools.reduce(jnp.maximum, [jnp.max(x, axis=0, keepdims=True) for x in parts])
            probs = [jnp.exp(x - peak) for x in parts]
            total = functools.reduce(jnp.add, [jnp.sum(x, axis=0, keepdims=True) for x in probs])
            mixed = functools.reduce(jnp.add, [
                mm(qkv_ref[2, kb * QB : (kb + 1) * QB, cols], x.astype(jnp.bfloat16), TN)
                for kb, x in enumerate(probs)])
            turned.append(mixed / total)
            lse_ref[0, h : h + 1, lower : lower + QB] = peak + jnp.log(total)
        out_ref[lower : lower + QB, :] = jnp.concatenate(turned, axis=0).T.astype(jnp.bfloat16)


def attend(line, segk, segq, rows, w):
    seqs, _, seq_len = segq.shape
    heads = line.shape[0]
    inner = heads * DH
    blocks = seq_len // QB
    width = rows.shape[1]
    return pl.pallas_call(
        functools.partial(attend_kernel, heads, blocks),
        grid=(seqs,),
        in_specs=[
            pl.BlockSpec(line.shape, lambda s: (0, 0)),
            pl.BlockSpec((1, seq_len, 1), lambda s: (s, 0, 0)),
            pl.BlockSpec((1, 1, seq_len), lambda s: (s, 0, 0)),
            pl.BlockSpec((seq_len, width), lambda s: (s, 0)),
            pl.BlockSpec(w.shape, lambda s: (0, 0, 0)),
        ],
        out_specs=[
            pl.BlockSpec((3, seq_len, inner), lambda s: (0, s, 0)),
            pl.BlockSpec((seq_len, inner), lambda s: (s, 0)),
            pl.BlockSpec((1, heads, seq_len), lambda s: (s, 0, 0)),
        ],
        out_shape=[
            jax.ShapeDtypeStruct((3, seqs * seq_len, inner), jnp.bfloat16),
            jax.ShapeDtypeStruct((seqs * seq_len, inner), jnp.bfloat16),
            jax.ShapeDtypeStruct((seqs, heads, seq_len), jnp.float32),
        ],
        scratch_shapes=[pltpu.VMEM((heads, blocks, QB, QB), jnp.float32)],
        compiler_params=pltpu.CompilerParams(vmem_limit_bytes=48 << 20),
        cost_estimate=pl.CostEstimate(flops=10_000_000_000, bytes_accessed=10 << 20, transcendentals=4_000_000),
        name="attend",
    )(line, segk, segq, rows, w)


def attend_back_kernel(heads, blocks, seqs, line_ref, segk_ref, segq_ref, rows_ref, w_ref,
                       qkv_ref, og_ref, lse_ref,
                       norm_ref, wg_ref, lg_ref, tiles, sums, kg, vg, dq):
    step = pl.program_id(0)

    @pl.when(step == 0)
    def _():
        build_bias(line_ref, tiles, heads, blocks)
        sums[...] = jnp.zeros_like(sums)
        wg_ref[...] = jnp.zeros_like(wg_ref)

    scale = 1.0 / math.sqrt(DH)
    for h in range(heads):
        cols = slice(h * DH, (h + 1) * DH)
        kg[...] = jnp.zeros_like(kg)
        vg[...] = jnp.zeros_like(vg)
        for qb in range(blocks):
            nk = (qb + 1) * QB
            lower = qb * QB
            query = (qkv_ref[0, lower : lower + QB, cols].astype(jnp.float32) * scale).astype(jnp.bfloat16)
            grad = og_ref[lower : lower + QB, cols]
            lse = lse_ref[0, h : h + 1, lower : lower + QB]
            parts = score_block(qkv_ref[1, 0:nk, cols], query, tiles, h, qb, segk_ref.at[0], segq_ref.at[0])
            probs = [jnp.exp(x - lse) for x in parts]
            pg = mm(qkv_ref[2, 0:nk, cols], grad, NT)
            pgs = [pg[kb * QB : (kb + 1) * QB] for kb in range(qb + 1)]
            delta = functools.reduce(jnp.add, [jnp.sum(p * g, axis=0, keepdims=True) for p, g in zip(probs, pgs)])
            dqt = jnp.zeros((DH, QB), jnp.float32)
            for kb in range(qb + 1):
                rows = slice(kb * QB, (kb + 1) * QB)
                sg = (probs[kb] * (pgs[kb] - delta)).astype(jnp.bfloat16)
                sums[h, qb - kb] += sg.astype(jnp.float32)
                vg[rows] += mm(probs[kb].astype(jnp.bfloat16), grad, NN)
                kg[rows] += mm(sg, query, NN)
                dqt = dqt + mm(qkv_ref[1, rows, cols], sg, TN)
            dq[lower : lower + QB, h * DH : (h + 1) * DH] = (dqt * scale).T.astype(jnp.bfloat16)
        inner = heads * DH
        dq[:, inner + h * DH : inner + (h + 1) * DH] = kg[...].astype(jnp.bfloat16)
        dq[:, 2 * inner + h * DH : 2 * inner + (h + 1) * DH] = vg[...].astype(jnp.bfloat16)
    inner = heads * DH
    total = jnp.zeros(norm_ref.shape, jnp.float32)
    for c in range(3):
        piece = dq[:, c * inner : (c + 1) * inner]
        wg_ref[c] += mm(rows_ref[...], piece, TN)
        total = total + mm(piece, w_ref[c], NT)
    norm_ref[...] = total.astype(norm_ref.dtype)

    @pl.when(step == seqs - 1)
    def _():
        for h in range(heads):
            for d in range(blocks):
                lg_ref[h * blocks + d] = fold_tile(sums, h, d)


def fold_tile(sums, h, d):
    blank = jnp.zeros((8, QB), jnp.float32)
    total = jnp.zeros((8, 2 * QB), jnp.float32)
    for g in range(QB // 8):
        piece = jnp.concatenate([sums[h, d, 8 * g : 8 * g + 8, :], blank], axis=1)
        total = total + (piece if g == 0 else pltpu.roll(piece, 2 * QB - 8 * g, 1))
    return total


def lines_of(folded, heads, blocks):
    moved = sum(jnp.roll(folded[:, s, :], -s, axis=1) for s in range(8))
    moved = moved.reshape(heads, blocks, 2, QB)
    ahead = jnp.concatenate([moved[:, 1:, 1], jnp.zeros((heads, 1, QB), jnp.float32)], axis=1)
    return (moved[:, :, 0] + ahead).reshape(heads, blocks * QB)


def attend_back(line, segk, segq, rows, w, qkv, og, lse):
    seqs, _, seq_len = segq.shape
    heads = line.shape[0]
    inner = heads * DH
    blocks = seq_len // QB
    width = rows.shape[1]
    return pl.pallas_call(
        functools.partial(attend_back_kernel, heads, blocks, seqs),
        grid=(seqs,),
        in_specs=[
            pl.BlockSpec(line.shape, lambda s: (0, 0)),
            pl.BlockSpec((1, seq_len, 1), lambda s: (s, 0, 0)),
            pl.BlockSpec((1, 1, seq_len), lambda s: (s, 0, 0)),
            pl.BlockSpec((seq_len, width), lambda s: (s, 0)),
            pl.BlockSpec(w.shape, lambda s: (0, 0, 0)),
            pl.BlockSpec((3, seq_len, inner), lambda s: (0, s, 0)),
            pl.BlockSpec((seq_len, inner), lambda s: (s, 0)),
            pl.BlockSpec((1, heads, seq_len), lambda s: (s, 0, 0)),
        ],
        out_specs=[
            pl.BlockSpec((seq_len, width), lambda s: (s, 0)),
            pl.BlockSpec(w.shape, lambda s: (0, 0, 0)),
            pl.BlockSpec((heads * blocks, 8, 2 * QB), lambda s: (0, 0, 0)),
        ],
        out_shape=[
            jax.ShapeDtypeStruct((seqs * seq_len, width), jnp.bfloat16),
            jax.ShapeDtypeStruct(w.shape, jnp.float32),
            jax.ShapeDtypeStruct((heads * blocks, 8, 2 * QB), jnp.float32),
        ],
        scratch_shapes=[
            pltpu.VMEM((heads, blocks, QB, QB), jnp.float32),
            pltpu.VMEM((heads, blocks, QB, QB), jnp.float32),
            pltpu.VMEM((seq_len, DH), jnp.float32),
            pltpu.VMEM((seq_len, DH), jnp.float32),
            pltpu.VMEM((seq_len, 3 * inner), jnp.bfloat16),
        ],
        compiler_params=pltpu.CompilerParams(vmem_limit_bytes=48 << 20),
        cost_estimate=pl.CostEstimate(flops=20_000_000_000, bytes_accessed=16 << 20, transcendentals=4_000_000),
        name="attend_back",
    )(line, segk, segq, rows, w, qkv, og, lse)


def mask_inputs(segments, padding):
    keyed = jnp.where(padding == 1, segments, -1)
    return keyed[:, :, None], segments[:, None, :]


def line_of(by_distance):
    return jnp.concatenate([jnp.full((by_distance.shape[0], QB), NEGATIVE, jnp.float32), by_distance], axis=1)


FT = 512
ROOT_2_PI = math.sqrt(2.0 / math.pi)


def gelu_pair(x):
    square = x * x
    t = jnp.tanh(ROOT_2_PI * x * (1.0 + 0.044715 * square))
    half = 0.5 * (1.0 + t)
    slope = half + 0.5 * x * (1.0 - t * t) * (ROOT_2_PI * (1.0 + 3 * 0.044715 * square))
    return x * half, slope


def expert_kernel(steps, x_ref, g_ref, up_ref, down_ref, act_ref, pre_ref, back_ref, dot_ref, total, dots):
    step = pl.program_id(0)

    @pl.when(step == 0)
    def _():
        total[...] = jnp.zeros_like(total)
        dots[...] = jnp.zeros_like(dots)

    rows = x_ref.shape[0]
    chunk = 256
    for lower in range(0, rows, chunk):
        part = slice(lower, lower + chunk)
        pre = mm(x_ref[part], up_ref[...], NT)
        out_side = mm(g_ref[part], down_ref[...], NT)
        act, slope = gelu_pair(pre)
        low = act.astype(jnp.bfloat16)
        act_ref[part] = low
        product = low.astype(jnp.float32) * out_side
        dots[part] += sum(product[:, k : k + 128] for k in range(0, FT, 128))
        back = (out_side * slope).astype(jnp.bfloat16)
        pre_ref[part] = back
        total[part] += mm(back, up_ref[...], NN)

    @pl.when(step == steps - 1)
    def _():
        back_ref[...] = total[...].astype(jnp.bfloat16)
        dot_ref[...] = lax.dot_general(
            jnp.ones((8, 128), jnp.float32), dots[...], NT,
            precision=HIGHEST, preferred_element_type=jnp.float32)


def expert_first(x, g, up, down):
    rows, width = x.shape
    hidden = up.shape[0]
    steps = hidden // FT
    whole = lambda f: (0, 0)
    return pl.pallas_call(
        functools.partial(expert_kernel, steps),
        grid=(steps,),
        in_specs=[
            pl.BlockSpec((rows, width), whole),
            pl.BlockSpec((rows, width), whole),
            pl.BlockSpec((FT, width), lambda f: (f, 0)),
            pl.BlockSpec((FT, width), lambda f: (f, 0)),
        ],
        out_specs=[
            pl.BlockSpec((rows, FT), lambda f: (0, f)),
            pl.BlockSpec((rows, FT), lambda f: (0, f)),
            pl.BlockSpec((rows, width), whole),
            pl.BlockSpec((8, rows), whole),
        ],
        out_shape=[
            jax.ShapeDtypeStruct((rows, hidden), jnp.bfloat16),
            jax.ShapeDtypeStruct((rows, hidden), jnp.bfloat16),
            jax.ShapeDtypeStruct((rows, width), jnp.bfloat16),
            jax.ShapeDtypeStruct((8, rows), jnp.float32),
        ],
        scratch_shapes=[
            pltpu.VMEM((rows, width), jnp.float32),
            pltpu.VMEM((rows, 128), jnp.float32),
        ],
        compiler_params=pltpu.CompilerParams(vmem_limit_bytes=48 << 20),
        cost_estimate=pl.CostEstimate(
            flops=6 * rows * width * hidden, bytes_accessed=32 << 20, transcendentals=rows * hidden),
        name="expert_first",
    )(x, g, up, down)


def expert_late_kernel(steps, x_ref, g_ref, gate_ref, act_ref, pre_ref, down_ref,
                       out_ref, up_grad_ref, down_grad_ref, total, x_gated, g_gated):
    step = pl.program_id(0)

    @pl.when(step == 0)
    def _():
        total[...] = jnp.zeros_like(total)
        gate = gate_ref[...]
        x_gated[...] = (x_ref[...].astype(jnp.float32) * gate).astype(jnp.bfloat16)
        g_gated[...] = (g_ref[...].astype(jnp.float32) * gate).astype(jnp.bfloat16)

    up_grad_ref[...] = mm(pre_ref[...], x_gated[...], TN).astype(up_grad_ref.dtype)
    down_grad_ref[...] = mm(act_ref[...], g_gated[...], TN).astype(down_grad_ref.dtype)
    total[...] += mm(act_ref[...], down_ref[...], NN)

    @pl.when(step == steps - 1)
    def _():
        out_ref[...] = total[...].astype(jnp.bfloat16)


def expert_late(x, g, gate, act, pre, down):
    rows, width = x.shape
    hidden = down.shape[0]
    steps = hidden // FT
    whole = lambda f: (0, 0)
    tile = pl.BlockSpec((FT, width), lambda f: (f, 0))
    return pl.pallas_call(
        functools.partial(expert_late_kernel, steps),
        grid=(steps,),
        in_specs=[
            pl.BlockSpec((rows, width), whole),
            pl.BlockSpec((rows, width), whole),
            pl.BlockSpec((rows, 1), whole),
            pl.BlockSpec((rows, FT), lambda f: (0, f)),
            pl.BlockSpec((rows, FT), lambda f: (0, f)),
            tile,
        ],
        out_specs=[pl.BlockSpec((rows, width), whole), tile, tile],
        out_shape=[
            jax.ShapeDtypeStruct((rows, width), jnp.bfloat16),
            jax.ShapeDtypeStruct((hidden, width), jnp.bfloat16),
            jax.ShapeDtypeStruct((hidden, width), jnp.bfloat16),
        ],
        scratch_shapes=[
            pltpu.VMEM((rows, width), jnp.float32),
            pltpu.VMEM((rows, width), jnp.bfloat16),
            pltpu.VMEM((rows, width), jnp.bfloat16),
        ],
        compiler_params=pltpu.CompilerParams(vmem_limit_bytes=48 << 20),
        cost_estimate=pl.CostEstimate(
            flops=6 * rows * width * hidden, bytes_accessed=32 << 20, transcendentals=0),
        name="expert_late",
    )(x, g, gate, act, pre, down)


MESH = pl.DeviceIdType.MESH
VMEM_LIMIT = 60 << 20


def remote(src, dst, send, recv, axis, place):
    return pltpu.make_async_remote_copy(
        src_ref=src, dst_ref=dst, send_sem=send, recv_sem=recv, device_id={axis: place}, device_id_type=MESH
    )


def each_peer(count, step, start=1):
    if count <= 8:
        for r in range(start, count):
            step(r)
    else:
        def one(r, carry):
            step(r)
            return carry
        lax.fori_loop(start, count, one, 0)


def greet(dp_count, tensor_count):
    barrier = pltpu.get_barrier_semaphore()
    dp, tp = lax.axis_index("dp"), lax.axis_index("tensor")
    for r in range(1, tensor_count):
        pl.semaphore_signal(barrier, inc=1, device_id={"tensor": lax.rem(tp + r, tensor_count)}, device_id_type=MESH)

    def signal(r):
        pl.semaphore_signal(barrier, inc=1, device_id={"dp": lax.rem(dp + r, dp_count)}, device_id_type=MESH)
    each_peer(dp_count, signal)
    return lambda: pl.semaphore_wait(barrier, tensor_count - 1 + dp_count - 1)


def partners(tensor_count):
    tp = lax.axis_index("tensor")
    sib = tp + 1 - 2 * lax.rem(tp, 2)
    return tp, sib, lax.rem(tp + 2, tensor_count), lax.rem(sib + 2, tensor_count)


def place_pairs(routes_ref, live_ref, experts, capacity, cap_rows):
    tokens = live_ref.shape[1]
    live = live_ref[...] == 1
    ids = lax.broadcasted_iota(jnp.int32, (experts, tokens), 0)
    row = lax.broadcasted_iota(jnp.int32, (tokens, tokens), 0)
    col = lax.broadcasted_iota(jnp.int32, (tokens, tokens), 1)
    before = (row < col).astype(jnp.float32).astype(jnp.bfloat16)
    slots = []
    base = jnp.zeros((experts, 1), jnp.float32)
    for k in range(2):
        route = routes_ref[k : k + 1, :]
        hot = jnp.where((ids == route) & live, 1.0, 0.0)
        count = mm(hot.astype(jnp.bfloat16), before, NN) + base
        place = jnp.sum(count * hot, axis=0, keepdims=True).astype(jnp.int32)
        slots.append(jnp.where(live & (place < capacity), route * cap_rows + place, -1))
        base = base + jnp.sum(hot, axis=1, keepdims=True)
    return slots


def chosen(first, second, expert, cap_rows):
    ids = lax.broadcasted_iota(jnp.int32, (cap_rows, first.shape[1]), 0) + expert * cap_rows
    return jnp.where((ids == first) | (ids == second), 1.0, 0.0).astype(jnp.bfloat16)


def attend_sequence(heads, blocks, seq, line_tiles, segk_ref, segq_ref, qkv, heads_out, lse_ref):
    scale = 1.0 / math.sqrt(DH)
    for qb in range(blocks):
        nk = (qb + 1) * QB
        lower = qb * QB
        turned = []
        for h in range(heads):
            cols = slice(h * DH, (h + 1) * DH)
            query = (qkv[seq, 0, lower : lower + QB, cols].astype(jnp.float32) * scale).astype(jnp.bfloat16)
            parts = score_block(qkv[seq, 1, 0:nk, cols], query, line_tiles, h, qb, segk_ref.at[seq], segq_ref.at[seq])
            peak = functools.reduce(jnp.maximum, [jnp.max(x, axis=0, keepdims=True) for x in parts])
            probs = [jnp.exp(x - peak) for x in parts]
            total = functools.reduce(jnp.add, [jnp.sum(x, axis=0, keepdims=True) for x in probs])
            mixed = functools.reduce(jnp.add, [
                mm(qkv[seq, 2, kb * QB : (kb + 1) * QB, cols], x.astype(jnp.bfloat16), TN)
                for kb, x in enumerate(probs)])
            turned.append(mixed / total)
            lse_ref[seq, h : h + 1, lower : lower + QB] = peak + jnp.log(total)
        mixed = jnp.concatenate(turned, axis=0).T.astype(jnp.bfloat16)
        half = blocks // 2
        heads_out[seq * 2 + qb // half, (qb % half) * QB : (qb % half + 1) * QB, :] = mixed


def front_kernel(sizes, x_ref, gain_ref, w_ref, outw_ref, down_ref, grad_ref, routes_ref, live_ref, line_ref,
                 segk_ref, segq_ref,
                 rows, w_all, outw_all, down_all, qkv, lse_ref, heads_all, slots_ref, cot,
                 tiles, heads_out, cot_send,
                 far_send, far_recv, w_send, w_recv, o_send, o_recv, ot_send, ot_recv,
                 dn_send, dn_recv, cot_s, cot_r, head_send, head_recv, local_sem):
    dp_count, tensor_count, experts, capacity, cap_rows, heads, blocks, gather_w = sizes
    dp = lax.axis_index("dp")
    tp, sib, opp, across = partners(tensor_count)
    wait_barrier = greet(dp_count, tensor_count)

    x = x_ref[...].astype(jnp.float32)
    r = lax.rsqrt(jnp.mean(x * x, axis=-1, keepdims=True) + EPSILON)
    rows[tp] = (x * r * gain_ref[...]).astype(jnp.bfloat16)
    wait_barrier()

    half = rows.shape[1] // 2
    parts = [pl.ds(0, half), pl.ds(half, half)]
    far = [remote(rows.at[tp, p], rows.at[tp, p], far_send.at[k], far_recv.at[k], "tensor", opp) for k, p in enumerate(parts)]
    near = remote(rows.at[tp], rows.at[tp], far_send.at[2], far_recv.at[2], "tensor", sib)
    onward = [remote(rows.at[opp, p], rows.at[opp, p], far_send.at[3 + k], far_recv.at[3 + k], "tensor", sib) for k, p in enumerate(parts)]
    for c in far:
        c.start()
    near.start()

    def w_copy(r):
        return remote(w_ref, w_all.at[:, dp], w_send.at[r], w_recv.at[r], "dp", lax.rem(dp + r, dp_count))

    def o_copy(r):
        return remote(outw_ref, outw_all.at[tp, dp], o_send.at[r], o_recv.at[r], "dp", lax.rem(dp + r, dp_count))

    def ot_copy(k, to):
        return remote(outw_all.at[tp], outw_all.at[tp], ot_send.at[k], ot_recv.at[k], "tensor", to)
    if gather_w:
        each_peer(dp_count, lambda r: w_copy(r).start())
        each_peer(dp_count, lambda r: o_copy(r).start())
        own_w = pltpu.make_async_copy(w_ref, w_all.at[:, dp], local_sem.at[0])
        own_w.start()
        own_o = pltpu.make_async_copy(outw_ref, outw_all.at[tp, dp], local_sem.at[2])
        own_o.start()

    first, second = place_pairs(routes_ref, live_ref, experts, capacity, cap_rows)
    slots_ref[0:1, :] = first
    slots_ref[1:2, :] = second

    def cot_copy(r):
        to = lax.rem(dp + r, dp_count)
        return remote(cot_send.at[to], cot.at[dp], cot_s.at[r], cot_r.at[r], "dp", to)

    def cot_fill(r):
        to = lax.rem(dp + r, dp_count)
        cot_send[to] = mm(chosen(first, second, to, cap_rows), grad_ref[...], NN).astype(jnp.bfloat16)

    def cot_go(r):
        cot_fill(r)
        cot_copy(r).start()
    each_peer(dp_count, cot_go)
    cot_fill(0)
    own_cot = pltpu.make_async_copy(cot_send.at[dp], cot.at[dp], local_sem.at[1])
    own_cot.start()

    build_bias(line_ref, tiles, heads, blocks)
    if gather_w:
        own_w.wait()
        each_peer(dp_count, lambda r: w_copy(r).wait_recv())
    near.wait_recv()

    width = rows.shape[2]
    own_seq = tp // 2
    inner = heads * DH

    def project(seq):
        tokens = rows[pl.ds(seq * 2, 2)].reshape(2 * rows.shape[1], width)
        for c in range(3):
            weight = w_all[c].reshape(width, inner) if gather_w else w_ref[c]
            qkv[seq, c] = mm(tokens, weight, NN).astype(jnp.bfloat16)

    def head_copy(k, to):
        return remote(heads_out.at[to], heads_all.at[tp], head_send.at[k], head_recv.at[k], "tensor", to)

    own_down = pltpu.make_async_copy(down_ref, down_all.at[tp], local_sem.at[3])
    down_far = remote(down_ref, down_all.at[tp], dn_send.at[0], dn_recv.at[0], "tensor", opp)
    down_near = remote(down_ref, down_all.at[tp], dn_send.at[1], dn_recv.at[1], "tensor", sib)
    down_on = remote(down_all.at[opp], down_all.at[opp], dn_send.at[2], dn_recv.at[2], "tensor", sib)

    project(own_seq)
    for k in range(2):
        far[k].wait_recv()
        onward[k].start()
    own_down.start()
    down_far.start()
    down_near.start()
    attend_sequence(heads, blocks, own_seq, tiles, segk_ref, segq_ref, qkv, heads_out, lse_ref)
    head_copy(0, sib).start()
    heads_all[tp] = heads_out[tp]
    for k in range(2):
        onward[k].wait_recv()
    other = 1 - own_seq
    project(other)
    if gather_w:
        own_o.wait()
        each_peer(dp_count, lambda r: o_copy(r).wait_recv())
        for k, to in enumerate((sib, opp, across)):
            ot_copy(k, to).start()
    attend_sequence(heads, blocks, other, tiles, segk_ref, segq_ref, qkv, heads_out, lse_ref)
    head_copy(1, opp).start()
    head_copy(2, across).start()

    down_far.wait_recv()
    down_on.start()
    own_cot.wait()
    own_down.wait()
    each_peer(dp_count, lambda r: cot_copy(r).wait())
    if gather_w:
        each_peer(dp_count, lambda r: w_copy(r).wait_send())
        each_peer(dp_count, lambda r: o_copy(r).wait_send())
        for k, to in enumerate((sib, opp, across)):
            ot_copy(k, to).wait()
    for c in far + [near] + onward:
        c.wait_send()
    head_copy(0, sib).wait()
    head_copy(1, opp).wait()
    head_copy(2, across).wait()
    down_far.wait_send()
    down_near.wait()
    down_on.wait()


def sems(*counts):
    out = []
    for n in counts:
        out += [pltpu.SemaphoreType.DMA((n,)), pltpu.SemaphoreType.DMA((n,))]
    return out


def front(sizes, x, gain, w, outw, down, grad, routes_t, live_row, line, segk, segq):
    dp_count, tensor_count, experts, capacity, cap_rows, heads, blocks, gather_w = sizes
    tokens, width = x.shape
    seq_len = blocks * QB
    seqs = tensor_count * tokens // seq_len
    inner = heads * DH
    vmem = pl.BlockSpec(memory_space=pltpu.VMEM)
    anywhere = pl.BlockSpec(memory_space=pl.ANY)
    share = width // dp_count
    return pl.pallas_call(
        functools.partial(front_kernel, sizes),
        in_specs=[vmem] * 4 + [anywhere] + [vmem] * 6,
        out_specs=[vmem] * 3 + [anywhere] + [vmem] * 4 + [anywhere],
        out_shape=[
            jax.ShapeDtypeStruct((tensor_count, tokens, width), jnp.bfloat16),
            jax.ShapeDtypeStruct((3, dp_count, share, inner) if gather_w else (3, 8, 16, 128), jnp.bfloat16),
            jax.ShapeDtypeStruct((tensor_count, dp_count, share, inner) if gather_w else (3, 8, 16, 128), jnp.bfloat16),
            jax.ShapeDtypeStruct((tensor_count,) + down.shape, jnp.bfloat16),
            jax.ShapeDtypeStruct((seqs, 3, seq_len, inner), jnp.bfloat16),
            jax.ShapeDtypeStruct((seqs, heads, seq_len), jnp.float32),
            jax.ShapeDtypeStruct((tensor_count, tokens, inner), jnp.bfloat16),
            jax.ShapeDtypeStruct((8, tokens), jnp.int32),
            jax.ShapeDtypeStruct((experts, cap_rows, width), jnp.bfloat16),
        ],
        scratch_shapes=[
            pltpu.VMEM((heads, blocks, QB, QB), jnp.float32),
            pltpu.VMEM((tensor_count, tokens, inner), jnp.bfloat16),
            pltpu.VMEM((experts, cap_rows, width), jnp.bfloat16),
        ] + sems(5, dp_count, dp_count, 3, 3, dp_count, 3) + [pltpu.SemaphoreType.DMA((4,))],
        compiler_params=pltpu.CompilerParams(
            vmem_limit_bytes=VMEM_LIMIT, collective_id=1, has_side_effects=True),
        cost_estimate=pl.CostEstimate(flops=20_000_000_000, bytes_accessed=20 << 20, transcendentals=4_000_000),
        name="front",
    )(x, gain, w, outw, down, grad, routes_t, live_row, line, segk, segq)


def to_row(column, lanes):
    n = column.shape[0]
    row = lax.broadcasted_iota(jnp.int32, (n, lanes), 0)
    col = lax.broadcasted_iota(jnp.int32, (n, lanes), 1)
    return jnp.sum(jnp.where(row == col, column, 0.0), axis=0, keepdims=True)


def to_column(row_values, n):
    lanes = row_values.shape[1]
    row = lax.broadcasted_iota(jnp.int32, (n, lanes), 0)
    col = lax.broadcasted_iota(jnp.int32, (n, lanes), 1)
    return jnp.sum(jnp.where(row == col, row_values, 0.0), axis=1, keepdims=True)


def gate_map(first, second, gate_first, gate_second, expert, cap_rows):
    ids = lax.broadcasted_iota(jnp.int32, (cap_rows, first.shape[1]), 0) + expert * cap_rows
    return jnp.where(ids == first, gate_first, jnp.where(ids == second, gate_second, 0.0))


def gated_rows(weights, rows):
    high = weights.astype(jnp.bfloat16)
    low = (weights - high.astype(jnp.float32)).astype(jnp.bfloat16)
    return mm(high, rows, TN) + mm(low, rows, TN)


def middle_kernel(sizes, x_ref, grad_ref, heads_ref, outw_ref, gain_ref, router_ref, routes_ref, live_ref,
                  slots_ref, cot_ref, up_ref, down_ref,
                  up_part, down_part, produced, middle, middle_grad, heads_grad, out_part, stats, gates,
                  up, down, g_rows, x_rows, x_send, act, side, back_send, back, gate_send, gate_rows,
                  dot_send, dot_rows, total, moe_low, stage,
                  up_s, up_r, x_s, x_r, b_s, b_r, g_s, g_r, d_s, d_r, load_sem, stage_sem):
    dp_count, tensor_count, experts, capacity, cap_rows, heads, blocks, gather_w = sizes
    dp = lax.axis_index("dp")
    tp, sib, opp, across = partners(tensor_count)
    hidden = up.shape[1]
    tokens, width = x_ref.shape
    lanes = gate_send.shape[2]
    wait_barrier = greet(dp_count, tensor_count)

    load_g = pltpu.make_async_copy(cot_ref, g_rows, load_sem.at[0])
    load_down = pltpu.make_async_copy(down_ref, down, load_sem.at[1])
    load_up = pltpu.make_async_copy(up_ref, up.at[tp], load_sem.at[2])
    load_g.start()
    load_down.start()
    load_up.start()

    mixed = x_ref[...].astype(jnp.float32)
    for t in range(tensor_count):
        mixed = mixed + mm(heads_ref[t], outw_ref[t], NT)
    middle[...] = mixed
    r = lax.rsqrt(jnp.mean(mixed * mixed, axis=-1, keepdims=True) + EPSILON)
    moe_low[...] = (mixed * r * gain_ref[...]).astype(jnp.bfloat16)
    first, second = slots_ref[0:1, :], slots_ref[1:2, :]
    wait_barrier()

    def x_copy(r):
        to = lax.rem(dp + r, dp_count)
        return remote(x_send.at[to], x_rows.at[dp], x_s.at[r], x_r.at[r], "dp", to)

    def x_go(r):
        to = lax.rem(dp + r, dp_count)
        x_send[to] = mm(chosen(first, second, to, cap_rows), moe_low[...], NN).astype(jnp.bfloat16)
        x_copy(r).start()
    each_peer(dp_count, x_go)
    x_rows[dp] = mm(chosen(first, second, dp, cap_rows), moe_low[...], NN).astype(jnp.bfloat16)

    up_far = remote(up_ref, up.at[tp], up_s.at[0], up_r.at[0], "tensor", opp)
    up_near = remote(up_ref, up.at[tp], up_s.at[1], up_r.at[1], "tensor", sib)
    up_on = remote(up.at[opp], up.at[opp], up_s.at[2], up_r.at[2], "tensor", sib)
    up_far.start()
    up_near.start()

    ids = lax.broadcasted_iota(jnp.int32, (experts, tokens), 0)
    pick_first, pick_second = ids == routes_ref[0:1, :], ids == routes_ref[1:2, :]
    live = (live_ref[...] == 1).astype(jnp.float32)
    logits = mm(router_ref[...], moe_low[...], NT)
    gap = jnp.sum(jnp.where(pick_first, logits, 0.0) - jnp.where(pick_second, logits, 0.0), axis=0, keepdims=True)
    gate_first = live / (1.0 + jnp.exp(-gap))
    gate_second = live / (1.0 + jnp.exp(gap))
    gates[0:1, :] = gate_first
    gates[1:2, :] = gate_second

    def gate_copy(r):
        to = lax.rem(dp + r, dp_count)
        return remote(gate_send.at[to], gate_rows.at[dp], g_s.at[r], g_r.at[r], "dp", to)

    def gate_fill(r):
        to = lax.rem(dp + r, dp_count)
        column = jnp.sum(gate_map(first, second, gate_first, gate_second, to, cap_rows), axis=1, keepdims=True)
        return jnp.broadcast_to(to_row(column, lanes), (8, lanes))

    def gate_go(r):
        gate_send[lax.rem(dp + r, dp_count)] = gate_fill(r)
        gate_copy(r).start()
    each_peer(dp_count, gate_go)
    gate_rows[dp] = gate_fill(0)

    load_g.wait()
    load_down.wait()
    slots = experts * cap_rows
    block = slots // 4

    def side_block(k, carry):
        part = pl.ds(pl.multiple_of(k * block, 16), block)
        here = g_rows[pl.ds(k * (experts // 4), experts // 4)].reshape(block, width)
        for t in range(tensor_count):
            side[part, t * hidden : (t + 1) * hidden] = mm(here, down[t], NT).astype(jnp.bfloat16)
        return carry
    lax.fori_loop(0, 4, side_block, 0)

    load_up.wait()
    up_far.wait_recv()
    up_on.start()
    up_near.wait_recv()
    up_on.wait_recv()

    def back_copy(r):
        to = lax.rem(dp - r + dp_count, dp_count)
        return remote(back_send.at[to], back.at[dp], b_s.at[r], b_r.at[r], "dp", to)

    def dot_copy(r):
        to = lax.rem(dp - r + dp_count, dp_count)
        return remote(dot_send.at[to], dot_rows.at[dp], d_s.at[r], d_r.at[r], "dp", to)

    group = max(1, min(dp_count, 320 // cap_rows))

    def first_pass(step, carry):
        rounds = [step * group + k for k in range(group)]
        froms = [lax.rem(dp - r + dp_count, dp_count) for r in rounds]
        for k, r in enumerate(rounds):
            if k == 0:
                @pl.when(r > 0)
                def _():
                    x_copy(r).wait_recv()
            else:
                x_copy(r).wait_recv()
        here = jnp.concatenate([x_rows[s] for s in froms], axis=0)
        total_back = jnp.zeros((group * cap_rows, width), jnp.float32)
        dots = jnp.zeros((group * cap_rows, 128), jnp.float32)
        for t in range(tensor_count):
            cols = slice(t * hidden, (t + 1) * hidden)
            pre = mm(here, up[t], NT)
            value, slope = gelu_pair(pre)
            low = value.astype(jnp.bfloat16)
            places = [pl.ds(pl.multiple_of(s * cap_rows, 16), cap_rows) for s in froms]
            beside = jnp.concatenate([side[p, cols] for p in places], axis=0).astype(jnp.float32)
            product = low.astype(jnp.float32) * beside
            dots = dots + sum(product[:, k : k + 128] for k in range(0, hidden, 128))
            grad = (beside * slope).astype(jnp.bfloat16)
            for k, p in enumerate(places):
                piece = slice(k * cap_rows, (k + 1) * cap_rows)
                act[p, cols] = low[piece]
                side[p, cols] = grad[piece]
            total_back = total_back + mm(grad, up[t], NN)
        column = jnp.sum(dots, axis=1, keepdims=True)
        for k, (r, s) in enumerate(zip(rounds, froms)):
            piece = slice(k * cap_rows, (k + 1) * cap_rows)
            low = total_back[piece].astype(jnp.bfloat16)
            line = jnp.broadcast_to(to_row(column[piece], lanes), (8, lanes))

            def send():
                back_send[s] = low
                dot_send[s] = line
                back_copy(r).start()
                dot_copy(r).start()

            def keep():
                back[dp] = low
                dot_rows[dp] = line
            if k == 0:
                pl.when(r > 0)(send)
                pl.when(r == 0)(keep)
            else:
                send()
        return carry
    lax.fori_loop(0, dp_count // group, first_pass, 0)

    each_peer(dp_count, lambda r: gate_copy(r).wait_recv())

    def gate_rows_in(s, carry):
        column = to_column(gate_rows[s, 0:1, :], cap_rows)
        x_rows[s] = (x_rows[s].astype(jnp.float32) * column).astype(jnp.bfloat16)
        g_rows[s] = (g_rows[s].astype(jnp.float32) * column).astype(jnp.bfloat16)
        return carry
    lax.fori_loop(0, experts, gate_rows_in, 0)

    def late_pass(t, carry):
        cols = pl.ds(pl.multiple_of(t * hidden, 128), hidden)
        for k, (left, right, out) in enumerate(((act, g_rows, down_part), (side, x_rows, up_part))):
            whole = right[...].reshape(slots, width)

            def put():
                return pltpu.make_async_copy(stage.at[k], out.at[t], stage_sem.at[k])

            @pl.when(t > 0)
            def _():
                put().wait()
            stage[k] = mm(left[:, cols], whole, TN).astype(jnp.bfloat16)
            put().start()
        return carry
    lax.fori_loop(0, tensor_count, late_pass, 0)

    def produce(k, carry):
        part = pl.ds(pl.multiple_of(k * block, 16), block)
        out = jnp.zeros((block, width), jnp.float32)
        for t in range(tensor_count):
            out = out + mm(act[part, t * hidden : (t + 1) * hidden], down[t], NN)
        produced[part, :] = out.astype(jnp.bfloat16)
        return carry
    lax.fori_loop(0, 4, produce, 0)

    total[...] = jnp.zeros_like(total)

    def combine(r, carry):
        dot_first, dot_second = carry
        e = lax.rem(dp + r, dp_count)

        @pl.when(r > 0)
        def _():
            back_copy(r).wait_recv()
            dot_copy(r).wait_recv()
        weights = gate_map(first, second, gate_first, gate_second, e, cap_rows)
        total[...] += gated_rows(weights, back[e])
        column = to_column(dot_rows[e, 0:1, :], cap_rows)
        ids = lax.broadcasted_iota(jnp.int32, (cap_rows, tokens), 0) + e * cap_rows
        dot_first = dot_first + jnp.sum(jnp.where(ids == first, column, 0.0), axis=0, keepdims=True)
        dot_second = dot_second + jnp.sum(jnp.where(ids == second, column, 0.0), axis=0, keepdims=True)
        return dot_first, dot_second
    zero_row = jnp.zeros((1, tokens), jnp.float32)
    dot_first, dot_second = lax.fori_loop(0, dp_count, combine, (zero_row, zero_row))

    change = gate_first * gate_second * (dot_first - dot_second)
    logit_grad = (jnp.where(pick_first, change, 0.0) - jnp.where(pick_second, change, 0.0)).astype(jnp.bfloat16)
    norm_grad = total[...] + mm(logit_grad, router_ref[...], TN)
    mixed = middle[...]
    r = lax.rsqrt(jnp.mean(mixed * mixed, axis=-1, keepdims=True) + EPSILON)
    u = mixed * r
    du = norm_grad * gain_ref[...]
    grad = grad_ref[...].astype(jnp.float32) + r * (du - u * jnp.mean(du * u, axis=-1, keepdims=True))
    middle_grad[...] = grad
    low = grad.astype(jnp.bfloat16)
    for t in range(tensor_count):
        heads_grad[t] = mm(low, outw_ref[t], NN).astype(jnp.bfloat16)
        out_part[t] = mm(low, heads_ref[t], TN).astype(jnp.bfloat16)
    stats[0:8, :] = jnp.broadcast_to(jnp.sum(norm_grad * u, axis=0, keepdims=True), (8, width))
    stats[8:, :] = mm(logit_grad, moe_low[...], NN)

    for k in range(2):
        out = (down_part, up_part)[k]
        pltpu.make_async_copy(stage.at[k], out.at[tensor_count - 1], stage_sem.at[k]).wait()
    up_far.wait_send()
    up_near.wait_send()
    up_on.wait_send()

    def drain(r):
        x_copy(r).wait_send()
        gate_copy(r).wait_send()
        back_copy(r).wait_send()
        dot_copy(r).wait_send()
    each_peer(dp_count, drain)


def middle_pass(sizes, x, grad, heads_all, outw, gain, router_t, routes_t, live_row, slot_rows, cot, up, down_all):
    dp_count, tensor_count, experts, capacity, cap_rows, heads, blocks, gather_w = sizes
    tokens, width = x.shape
    inner = heads * DH
    hidden = up.shape[0]
    slots = experts * cap_rows
    lanes = -(-cap_rows // 128) * 128
    vmem = pl.BlockSpec(memory_space=pltpu.VMEM)
    anywhere = pl.BlockSpec(memory_space=pl.ANY)
    shape = jax.ShapeDtypeStruct
    low = jnp.bfloat16
    return pl.pallas_call(
        functools.partial(middle_kernel, sizes),
        in_specs=[vmem] * 9 + [anywhere] * 3,
        out_specs=[anywhere] * 2 + [vmem] * 7,
        out_shape=[
            shape((tensor_count, hidden, width), low),
            shape((tensor_count, hidden, width), low),
            shape((slots, width), low),
            shape((tokens, width), jnp.float32),
            shape((tokens, width), jnp.float32),
            shape((tensor_count, tokens, inner), low),
            shape((tensor_count, width, inner), low),
            shape((8 + experts, width), jnp.float32),
            shape((8, tokens), jnp.float32),
        ],
        scratch_shapes=[
            pltpu.VMEM((tensor_count, hidden, width), low),
            pltpu.VMEM((tensor_count, hidden, width), low),
            pltpu.VMEM((experts, cap_rows, width), low),
            pltpu.VMEM((experts, cap_rows, width), low),
            pltpu.VMEM((experts, cap_rows, width), low),
            pltpu.VMEM((slots, tensor_count * hidden), low),
            pltpu.VMEM((slots, tensor_count * hidden), low),
            pltpu.VMEM((experts, cap_rows, width), low),
            pltpu.VMEM((experts, cap_rows, width), low),
            pltpu.VMEM((experts, 8, lanes), jnp.float32),
            pltpu.VMEM((experts, 8, lanes), jnp.float32),
            pltpu.VMEM((experts, 8, lanes), jnp.float32),
            pltpu.VMEM((experts, 8, lanes), jnp.float32),
            pltpu.VMEM((tokens, width), jnp.float32),
            pltpu.VMEM((tokens, width), low),
            pltpu.VMEM((2, hidden, width), low),
        ] + sems(3, dp_count, dp_count, dp_count, dp_count)
        + [pltpu.SemaphoreType.DMA((3,)), pltpu.SemaphoreType.DMA((2,))],
        compiler_params=pltpu.CompilerParams(
            vmem_limit_bytes=VMEM_LIMIT, collective_id=2, has_side_effects=True),
        cost_estimate=pl.CostEstimate(
            flops=12 * slots * width * hidden * tensor_count, bytes_accessed=40 << 20, transcendentals=4_000_000),
        name="middle_pass",
    )(x, grad, heads_all, outw, gain, router_t, routes_t, live_row, slot_rows, cot, up, down_all)


def attend_back_sequence(heads, blocks, seq, tiles, sums, segk_ref, segq_ref, qkv, grads, lse_ref, kg, vg, dq, between):
    scale = 1.0 / math.sqrt(DH)
    inner = heads * DH
    half = blocks // 2
    for h in range(heads):
        cols = slice(h * DH, (h + 1) * DH)
        kg[...] = jnp.zeros_like(kg)
        vg[...] = jnp.zeros_like(vg)
        for qb in range(blocks):
            nk = (qb + 1) * QB
            lower = qb * QB
            query = (qkv[seq, 0, lower : lower + QB, cols].astype(jnp.float32) * scale).astype(jnp.bfloat16)
            grad = grads[seq * 2 + qb // half, (qb % half) * QB : (qb % half + 1) * QB, cols]
            lse = lse_ref[seq, h : h + 1, lower : lower + QB]
            parts = score_block(qkv[seq, 1, 0:nk, cols], query, tiles, h, qb, segk_ref.at[seq], segq_ref.at[seq])
            probs = [jnp.exp(x - lse) for x in parts]
            pg = mm(qkv[seq, 2, 0:nk, cols], grad, NT)
            pgs = [pg[kb * QB : (kb + 1) * QB] for kb in range(qb + 1)]
            delta = functools.reduce(jnp.add, [jnp.sum(p * g, axis=0, keepdims=True) for p, g in zip(probs, pgs)])
            dqt = jnp.zeros((DH, QB), jnp.float32)
            for kb in range(qb + 1):
                rows = slice(kb * QB, (kb + 1) * QB)
                sg = (probs[kb] * (pgs[kb] - delta)).astype(jnp.bfloat16)
                sums[h, qb - kb] += sg.astype(jnp.float32)
                vg[rows] += mm(probs[kb].astype(jnp.bfloat16), grad, NN)
                kg[rows] += mm(sg, query, NN)
                dqt = dqt + mm(qkv[seq, 1, rows, cols], sg, TN)
            dq[lower : lower + QB, h * DH : (h + 1) * DH] = (dqt * scale).T.astype(jnp.bfloat16)
        dq[:, inner + h * DH : inner + (h + 1) * DH] = kg[...].astype(jnp.bfloat16)
        dq[:, 2 * inner + h * DH : 2 * inner + (h + 1) * DH] = vg[...].astype(jnp.bfloat16)
        between(h)


def fold_lines(sums, h, blocks):
    moved = []
    for d in range(blocks):
        folded = fold_tile(sums, h, d)
        line = folded[0:1, :]
        for s in range(1, 8):
            line = line + pltpu.roll(folded[s : s + 1, :], 2 * QB - s, 1)
        moved.append(line)
    out = []
    for d in range(blocks):
        piece = moved[d][:, :QB]
        if d + 1 < blocks:
            piece = piece + moved[d + 1][:, QB:]
        out.append(piece)
    return jnp.concatenate(out, axis=1)


def two_stage_start(send, land, s_sem, r_sem, tensor_count):
    tp = lax.axis_index("tensor")
    copies = []
    for r in range(1, tensor_count):
        copies.append(remote(send, land.at[r - 1], s_sem.at[r], r_sem.at[r], "tensor", lax.rem(tp + r, tensor_count)))
    for c in copies:
        c.start()
    return copies


def last_kernel(sizes, x_ref, gain_ref, middle_ref, mgrad_ref, hgrad_ref, rows, w_ref, qkv, lse_ref, line_ref,
                segk_ref, segq_ref, produced_ref, slots_ref, gates_ref, early_ref, bucket_ref,
                out_ref, input_grad_ref, wgrad_ref, early_out, late_out,
                tiles, sums, kg, vg, dq, grads, landed, npart, near_land, far_land, pair, wsum, wsend, wland,
                early_land, early_mid, early_dp, late, late_land, late_mid, late_dp, total,
                h_s, h_r, p_s, p_r, n_s, n_r, w_s, w_r, et_s, et_r, ed_s, ed_r, lt_s, lt_r, ld_s, ld_r):
    dp_count, tensor_count, experts, capacity, cap_rows, heads, blocks, gather_w = sizes
    dp = lax.axis_index("dp")
    tp, sib, opp, across = partners(tensor_count)
    tokens, width = x_ref.shape
    inner = heads * DH
    wait_barrier = greet(dp_count, tensor_count)
    build_bias(line_ref, tiles, heads, blocks)
    sums[...] = jnp.zeros_like(sums)
    own_seq = tp // 2
    other = 1 - own_seq
    wait_barrier()

    def h_copy(k, to):
        return remote(hgrad_ref.at[to], grads.at[tp], h_s.at[k], h_r.at[k], "tensor", to)
    h_copy(0, opp).start()
    h_copy(1, across).start()
    h_copy(2, sib).start()
    grads[tp] = hgrad_ref[tp]

    def p_copy(r):
        to = lax.rem(dp - r + dp_count, dp_count)
        return remote(produced_ref.at[to], landed.at[dp], p_s.at[r], p_r.at[r], "dp", to)
    each_peer(dp_count, lambda r: p_copy(r).start())
    landed[dp] = produced_ref[dp]

    early = two_stage_start(early_ref, early_land, et_s, et_r, tensor_count)

    def early_copy(r):
        return remote(early_mid, early_dp.at[r], ed_s.at[r], ed_r.at[r], "dp", lax.rem(dp + r, dp_count))

    h_copy(0, opp).wait_recv()
    h_copy(1, across).wait_recv()

    def n_copy(k, src, dst, to):
        return remote(src, dst, n_s.at[k], n_r.at[k], "tensor", to)
    pair_near = n_copy(0, npart.at[across], near_land.at[0], sib)
    pair_far = n_copy(1, pair, far_land, opp)
    own_near = n_copy(2, npart.at[sib], near_land.at[1], sib)

    def nothing(h):
        pass

    def project(seq, fresh):
        here = rows[pl.ds(seq * 2, 2)].reshape(2 * tokens, width)
        norm = jnp.zeros((2 * tokens, width), jnp.float32)
        for c in range(3):
            piece = dq[:, c * inner : (c + 1) * inner]
            weight = w_ref[c].reshape(width, inner)
            part = mm(here, piece, TN)
            wsum[c] = part if fresh else wsum[c] + part
            norm = norm + mm(piece, weight, NT)
        column = jnp.sum(norm * here.astype(jnp.float32), axis=0, keepdims=True)
        low = norm.astype(jnp.bfloat16)
        npart[seq * 2] = low[:tokens]
        npart[seq * 2 + 1] = low[tokens:]
        return column

    attend_back_sequence(heads, blocks, other, tiles, sums, segk_ref, segq_ref, qkv, grads, lse_ref, kg, vg, dq, nothing)
    gain_row = project(other, True)
    pair_near.start()

    def between(h):
        if h == 0:
            pair_near.wait_recv()
            pair[...] = (npart[opp].astype(jnp.float32) + near_land[0].astype(jnp.float32)).astype(jnp.bfloat16)
            pair_far.start()
            for c in early:
                c.wait_recv()
            early_mid[...] = early_ref[...] + early_land[0] + early_land[1] + early_land[2]
            each_peer(dp_count, lambda r: early_copy(r).start())

    h_copy(2, sib).wait_recv()
    attend_back_sequence(heads, blocks, own_seq, tiles, sums, segk_ref, segq_ref, qkv, grads, lse_ref, kg, vg, dq, between)
    gain_row = gain_row + project(own_seq, False)
    own_near.start()

    def w_copy(r):
        to = lax.rem(dp + r, dp_count)
        return remote(wsend.at[to], wland.at[r], w_s.at[r], w_r.at[r], "dp", to)
    share = width // dp_count
    for to in range(dp_count):
        for c in range(3):
            wsend[to, c] = wsum[c, to * share : (to + 1) * share, :].astype(jnp.bfloat16)
    each_peer(dp_count, lambda r: w_copy(r).start())

    gain_row = gain_row / gain_ref[...]
    late[...] = jnp.zeros_like(late)
    for k in range(width // 128):
        late[k : k + 1, :] = gain_row[:, k * 128 : (k + 1) * 128]
    buckets = late.shape[0] - 8
    ids = lax.broadcasted_iota(jnp.int32, (buckets, bucket_ref.shape[1]), 0)
    hot = ids == bucket_ref[...]
    lane = lax.broadcasted_iota(jnp.int32, (buckets, 128), 1)
    table = jnp.zeros((buckets, 128), jnp.float32)
    for h in range(heads):
        column = jnp.sum(jnp.where(hot, fold_lines(sums, h, blocks), 0.0), axis=1, keepdims=True)
        table = table + jnp.where(lane == tp * heads + h, column, 0.0)
    late[8:, :] = table
    late_first = two_stage_start(late, late_land, lt_s, lt_r, tensor_count)

    def late_copy(r):
        return remote(late_mid, late_dp.at[r], ld_s.at[r], ld_r.at[r], "dp", lax.rem(dp + r, dp_count))

    each_peer(dp_count, lambda r: early_copy(r).wait_recv())
    summed = early_mid[...]
    for r in range(1, dp_count):
        summed = summed + early_dp[r]
    early_out[...] = summed

    for c in late_first:
        c.wait_recv()
    late_mid[...] = late[...] + late_land[0] + late_land[1] + late_land[2]
    each_peer(dp_count, lambda r: late_copy(r).start())

    first, second = slots_ref[0:1, :], slots_ref[1:2, :]
    gate_first, gate_second = gates_ref[0:1, :], gates_ref[1:2, :]
    total[...] = middle_ref[...]

    def combine(r, carry):
        e = lax.rem(dp + r, dp_count)

        @pl.when(r > 0)
        def _():
            p_copy(r).wait_recv()
        total[...] += gated_rows(gate_map(first, second, gate_first, gate_second, e, cap_rows), landed[e])
        return carry
    lax.fori_loop(0, dp_count, combine, 0)
    out_ref[...] = total[...]

    own_near.wait_recv()
    pair_far.wait_recv()
    norm_grad = npart[tp].astype(jnp.float32) + near_land[1].astype(jnp.float32) + far_land[...].astype(jnp.float32)
    x = x_ref[...].astype(jnp.float32)
    r = lax.rsqrt(jnp.mean(x * x, axis=-1, keepdims=True) + EPSILON)
    u = x * r
    du = norm_grad * gain_ref[...]
    input_grad_ref[...] = mgrad_ref[...] + r * (du - u * jnp.mean(du * u, axis=-1, keepdims=True))

    each_peer(dp_count, lambda r: w_copy(r).wait_recv())
    for c in range(3):
        part = wsum[c, pl.ds(pl.multiple_of(dp * share, 8), share), :]
        for r in range(1, dp_count):
            part = part + wland[r, c].astype(jnp.float32)
        wgrad_ref[c] = part

    each_peer(dp_count, lambda r: late_copy(r).wait_recv())
    summed = late_mid[...]
    for r in range(1, dp_count):
        summed = summed + late_dp[r]
    late_out[...] = summed

    for c in early + late_first + [pair_near, pair_far, own_near, h_copy(0, opp), h_copy(1, across), h_copy(2, sib)]:
        c.wait_send()

    def drain(r):
        p_copy(r).wait_send()
        early_copy(r).wait_send()
        w_copy(r).wait_send()
        late_copy(r).wait_send()
    each_peer(dp_count, drain)


def last_pass(sizes, x, gain, middle, middle_grad, heads_grad, rows, w, qkv, lse, line, segk, segq, produced,
              slot_rows, gates, early, bucket_row):
    dp_count, tensor_count, experts, capacity, cap_rows, heads, blocks, gather_w = sizes
    tokens, width = x.shape
    inner = heads * DH
    seq_len = blocks * QB
    share = width // dp_count
    vmem = pl.BlockSpec(memory_space=pltpu.VMEM)
    shape = jax.ShapeDtypeStruct
    low, full = jnp.bfloat16, jnp.float32
    late = 8 + NB
    return pl.pallas_call(
        functools.partial(last_kernel, sizes),
        in_specs=[vmem] * 17,
        out_specs=[vmem] * 5,
        out_shape=[
            shape((tokens, width), full),
            shape((tokens, width), full),
            shape((3, share, inner), full),
            shape(early.shape, full),
            shape((late, 128), full),
        ],
        scratch_shapes=[
            pltpu.VMEM((heads, blocks, QB, QB), full),
            pltpu.VMEM((heads, blocks, QB, QB), full),
            pltpu.VMEM((seq_len, DH), full),
            pltpu.VMEM((seq_len, DH), full),
            pltpu.VMEM((seq_len, 3 * inner), low),
            pltpu.VMEM((tensor_count, tokens, inner), low),
            pltpu.VMEM((experts, cap_rows, width), low),
            pltpu.VMEM((tensor_count, tokens, width), low),
            pltpu.VMEM((2, tokens, width), low),
            pltpu.VMEM((tokens, width), low),
            pltpu.VMEM((tokens, width), low),
            pltpu.VMEM((3, width, inner), full),
            pltpu.VMEM((dp_count, 3, share, inner), low),
            pltpu.VMEM((dp_count, 3, share, inner), low),
            pltpu.VMEM((tensor_count - 1,) + early.shape, full),
            pltpu.VMEM(early.shape, full),
            pltpu.VMEM((dp_count,) + early.shape, full),
            pltpu.VMEM((late, 128), full),
            pltpu.VMEM((tensor_count - 1, late, 128), full),
            pltpu.VMEM((late, 128), full),
            pltpu.VMEM((dp_count, late, 128), full),
            pltpu.VMEM((tokens, width), full),
        ] + sems(3, dp_count, 3, dp_count, tensor_count, dp_count, tensor_count, dp_count),
        compiler_params=pltpu.CompilerParams(
            vmem_limit_bytes=VMEM_LIMIT, collective_id=3, has_side_effects=True),
        cost_estimate=pl.CostEstimate(flops=30_000_000_000, bytes_accessed=30 << 20, transcendentals=4_000_000),
        name="last_pass",
    )(x, gain, middle, middle_grad, heads_grad, rows, w, qkv, lse, line, segk, segq, produced, slot_rows, gates,
      early, bucket_row)


def norm_rows(values, gain):
    return values * lax.rsqrt(jnp.mean(values * values, axis=-1, keepdims=True) + EPSILON) * gain


def norm_back(values, gain, grad):
    r = lax.rsqrt(jnp.mean(values * values, axis=-1, keepdims=True) + EPSILON)
    u = values * r
    du = grad * gain
    return r * (du - u * jnp.mean(du * u, axis=-1, keepdims=True)), grad * u


def plain_body(
    block_input,
    out_grad,
    w_qkv,
    w_out,
    rel_table,
    gain_attn,
    gain_moe,
    w_router,
    w_up,
    w_down,
    routes,
    segments,
    padding,
    rel_bucket,
):
    tensor_pos = lax.axis_index("tensor")
    rows_local, width = block_input.shape
    seq_len = segments.shape[1]
    expert_count = w_router.shape[1]
    capacity = (10 * rows_local + 4 * expert_count - 1) // (4 * expert_count)
    slots = expert_count * capacity
    x_float = block_input.astype(jnp.float32)
    grad_float = out_grad.astype(jnp.float32)

    attn_norm = norm_rows(x_float, gain_attn).astype(jnp.bfloat16)
    seq_rows = lax.all_gather(attn_norm, "tensor", axis=0, tiled=True)
    qkv_full = lax.all_gather(w_qkv, "dp", axis=1, tiled=True)
    out_rows = lax.all_gather(w_out, "dp", axis=1, tiled=True)
    out_full = lax.all_gather(out_rows, "tensor", axis=0, tiled=True)
    up_full = lax.all_gather(w_up[0], "tensor", axis=0, tiled=True)
    down_full = lax.all_gather(w_down[0], "tensor", axis=0, tiled=True)

    live_mask = lax.dynamic_slice_in_dim(padding.reshape(-1), tensor_pos * rows_local, rows_local)
    live_float = live_mask.astype(jnp.float32)
    expert_ids = jnp.arange(expert_count, dtype=jnp.int32)
    pick_first = routes[:, 0:1] == expert_ids[None, :]
    pick_second = routes[:, 1:2] == expert_ids[None, :]
    usable = live_mask[:, None] == 1
    first_hot = (pick_first & usable).astype(jnp.int32)
    second_hot = (pick_second & usable).astype(jnp.int32)
    first_place = jnp.sum((jnp.cumsum(first_hot, axis=0) - first_hot) * first_hot, axis=1)
    second_before = (
        jnp.cumsum(second_hot, axis=0) - second_hot + jnp.sum(first_hot, axis=0, keepdims=True)
    )
    second_place = jnp.sum(second_before * second_hot, axis=1)
    first_slot = jnp.where(
        (live_mask == 1) & (first_place < capacity), routes[:, 0] * capacity + first_place, -1
    )
    second_slot = jnp.where(
        (live_mask == 1) & (second_place < capacity), routes[:, 1] * capacity + second_place, -1
    )
    slot_ids = jnp.arange(slots, dtype=jnp.int32)
    select_first = slot_ids[:, None] == first_slot[None, :]
    select_second = slot_ids[:, None] == second_slot[None, :]
    select_both = (select_first | select_second).astype(jnp.bfloat16)
    select_first_low = select_first.astype(jnp.bfloat16)
    select_second_low = select_second.astype(jnp.bfloat16)

    def to_experts(rows):
        return lax.all_to_all(rows, "dp", split_axis=0, concat_axis=0, tiled=True)

    grad_rows = jnp.dot(select_both, out_grad, preferred_element_type=jnp.float32)
    sent_grads = to_experts(grad_rows.astype(jnp.bfloat16).reshape(expert_count, capacity, width))
    sent_grads = sent_grads.reshape(slots, width)

    heads = qkv_full.shape[2] // DH
    inner = heads * DH
    table_local = lax.dynamic_slice_in_dim(rel_table, tensor_pos * heads, heads, 1)
    bucket_hot = (rel_bucket[:, None] == jnp.arange(NB, dtype=jnp.int32)[None, :]).astype(jnp.float32)
    line = line_of(jnp.dot(bucket_hot, table_local, precision=HIGHEST).T)
    segk, segq = mask_inputs(segments, padding)
    qkv_low, heads_low, lse = attend(line, segk, segq, seq_rows, qkv_full)
    heads_own = lax.all_to_all(heads_low, "tensor", split_axis=0, concat_axis=1, tiled=True)

    middle = x_float + jnp.dot(heads_own, out_full, preferred_element_type=jnp.float32)
    moe_low = norm_rows(middle, gain_moe).astype(jnp.bfloat16)
    rows_out = jnp.dot(select_both, moe_low, preferred_element_type=jnp.float32)
    sent_rows = to_experts(rows_out.astype(jnp.bfloat16).reshape(expert_count, capacity, width))
    sent_rows = sent_rows.reshape(slots, width)
    logits = jnp.dot(moe_low, w_router, preferred_element_type=jnp.float32)
    first_logit = jnp.sum(jnp.where(pick_first, logits, 0.0), axis=1)
    second_logit = jnp.sum(jnp.where(pick_second, logits, 0.0), axis=1)
    first_gate = jax.nn.sigmoid(first_logit - second_logit) * live_float
    second_gate = jax.nn.sigmoid(second_logit - first_logit) * live_float
    slot_gate = jnp.sum(
        jnp.where(select_first, first_gate[None, :], 0.0)
        + jnp.where(select_second, second_gate[None, :], 0.0),
        axis=1,
    )
    sent_gates = to_experts(slot_gate.reshape(expert_count, capacity)).reshape(slots, 1)

    act, pre_grad, back, dots = expert_first(sent_rows, sent_grads, up_full, down_full)
    returned_grad = to_experts(back.reshape(expert_count, capacity, width)).reshape(slots, width)
    slot_dots = to_experts(dots[0].reshape(expert_count, capacity)).reshape(slots)
    produced, up_part, down_part = expert_late(
        sent_rows, sent_grads, sent_gates, act, pre_grad, down_full
    )
    returned = to_experts(produced.reshape(expert_count, capacity, width)).reshape(slots, width)
    w_up_grad = lax.psum_scatter(up_part, "tensor", scatter_dimension=0, tiled=True)
    w_down_grad = lax.psum_scatter(down_part, "tensor", scatter_dimension=0, tiled=True)

    first_dot = jnp.sum(jnp.where(select_first, slot_dots[:, None], 0.0), axis=0)
    second_dot = jnp.sum(jnp.where(select_second, slot_dots[:, None], 0.0), axis=0)
    coefficient = first_gate * second_gate * (first_dot - second_dot)
    logit_grad = (
        jnp.where(pick_first, coefficient[:, None], 0.0)
        - jnp.where(pick_second, coefficient[:, None], 0.0)
    ).astype(jnp.bfloat16)
    router_grad = jnp.einsum("nd,ne->de", moe_low, logit_grad, preferred_element_type=jnp.float32)

    def gated(rows):
        first_rows = jnp.einsum("st,sd->td", select_first_low, rows, preferred_element_type=jnp.float32)
        second_rows = jnp.einsum("st,sd->td", select_second_low, rows, preferred_element_type=jnp.float32)
        return first_gate[:, None] * first_rows + second_gate[:, None] * second_rows

    moe_norm_grad = (
        jnp.einsum("ne,de->nd", logit_grad, w_router, preferred_element_type=jnp.float32)
        + gated(returned_grad)
    )
    middle_back, gain_moe_rows = norm_back(middle, gain_moe, moe_norm_grad)
    middle_grad = grad_float + middle_back
    gain_moe_grad = jnp.sum(gain_moe_rows, axis=0)
    attn_grad = middle_grad.astype(jnp.bfloat16)
    heads_grad = jnp.einsum("nd,fd->nf", attn_grad, out_full, preferred_element_type=jnp.float32)
    heads_grad = lax.all_to_all(
        heads_grad.astype(jnp.bfloat16), "tensor", split_axis=1, concat_axis=0, tiled=True
    )
    out_part = jnp.einsum("nf,nd->fd", heads_own, attn_grad, preferred_element_type=jnp.float32)
    out_part = lax.psum_scatter(out_part.astype(jnp.bfloat16), "tensor", scatter_dimension=0, tiled=True)
    w_out_grad = lax.psum_scatter(out_part.astype(jnp.float32), "dp", scatter_dimension=1, tiled=True)
    gain_moe_grad, router_grad = lax.psum((gain_moe_grad, router_grad), ("dp", "tensor"))

    norm_part, qkv_part, folded = attend_back(
        line, segk, segq, seq_rows, qkv_full, qkv_low, heads_grad, lse
    )
    attn_norm_grad = lax.psum_scatter(norm_part, "tensor", scatter_dimension=0, tiled=True)
    input_back, gain_attn_rows = norm_back(x_float, gain_attn, attn_norm_grad.astype(jnp.float32))
    input_grad = middle_grad + input_back
    gain_attn_grad = jnp.sum(gain_attn_rows, axis=0)
    w_qkv_grad = lax.psum_scatter(qkv_part, "dp", scatter_dimension=1, tiled=True)
    line_grad = lines_of(folded, heads, seq_len // QB)
    table_part = jnp.dot(bucket_hot.T, line_grad.T, precision=HIGHEST)
    table_whole = lax.dynamic_update_slice(
        jnp.zeros(rel_table.shape, jnp.float32), table_part, (0, tensor_pos * heads)
    )
    gain_attn_grad, table_whole = lax.psum((gain_attn_grad, table_whole), ("dp", "tensor"))
    block_output = middle + gated(returned)
    return (
        block_output,
        input_grad,
        w_qkv_grad,
        w_out_grad,
        table_whole,
        gain_attn_grad,
        gain_moe_grad,
        router_grad,
        w_up_grad.astype(jnp.float32)[None],
        w_down_grad.astype(jnp.float32)[None],
    )


def fused_body(
    block_input,
    out_grad,
    w_qkv,
    w_out,
    rel_table,
    gain_attn,
    gain_moe,
    w_router,
    w_up,
    w_down,
    routes,
    segments,
    padding,
    rel_bucket,
):
    tensor_pos = lax.axis_index("tensor")
    dp_count, tensor_count = lax.axis_size("dp"), lax.axis_size("tensor")
    rows_local, width = block_input.shape
    seq_len = segments.shape[1]
    heads = w_qkv.shape[2] // DH
    capacity = slot_capacity(rows_local, w_router.shape[1])
    expert_count = w_router.shape[1]
    sizes = (dp_count, tensor_count, expert_count, capacity, capacity, heads, seq_len // QB, True)

    live_row = lax.dynamic_slice_in_dim(padding.reshape(-1), tensor_pos * rows_local, rows_local)[None]
    routes_t = routes.T
    table_local = lax.dynamic_slice_in_dim(rel_table, tensor_pos * heads, heads, 1)
    bucket_hot = (rel_bucket[:, None] == jnp.arange(NB, dtype=jnp.int32)[None, :]).astype(jnp.float32)
    line = line_of(jnp.dot(bucket_hot, table_local, precision=HIGHEST).T)
    segk, segq = mask_inputs(segments, padding)
    rows, w_all, outw, down_all, qkv, lse, heads_all, slot_rows, cot = front(
        sizes, block_input, gain_attn[None], w_qkv, w_out.T, w_down[0], out_grad, routes_t, live_row, line, segk, segq
    )
    outw = outw.reshape(tensor_count, width, -1)
    up_part, down_part, produced, middle, middle_grad, heads_grad, out_part, early, gates = middle_pass(
        sizes, block_input, out_grad, heads_all, outw, gain_moe[None], w_router.T, routes_t, live_row,
        slot_rows, cot, w_up[0], down_all
    )

    def scattered(part):
        return lax.psum_scatter(part, "tensor", scatter_dimension=0, tiled=False)
    w_up_grad = scattered(up_part)
    w_down_grad = scattered(down_part)
    w_out_grad = lax.psum_scatter(scattered(out_part).astype(jnp.float32), "dp", scatter_dimension=0, tiled=True)
    block_output, input_grad, w_qkv_grad, early, late = last_pass(
        sizes, block_input, gain_attn[None], middle, middle_grad, heads_grad, rows, w_all, qkv, lse, line, segk, segq,
        produced.reshape(expert_count, capacity, width), slot_rows, gates, early, rel_bucket[None]
    )
    return (
        block_output,
        input_grad,
        w_qkv_grad,
        w_out_grad.T,
        late[8:, : rel_table.shape[1]],
        late[: width // 128].reshape(width),
        early[0],
        early[8:].T,
        w_up_grad.astype(jnp.float32)[None],
        w_down_grad.astype(jnp.float32)[None],
    )


def slot_capacity(tokens, experts):
    return (10 * tokens + 4 * experts - 1) // (4 * experts)


def body(*args):
    block_input, w_qkv, w_router = args[0], args[2], args[7]
    capacity = slot_capacity(block_input.shape[0], w_router.shape[1])
    fits = capacity % 16 == 0 and w_qkv.shape[1] % 16 == 0 and block_input.shape[1] <= 1024
    return fused_body(*args) if fits else plain_body(*args)


def solution(mesh):
    in_specs = (
        P(("dp", "tensor"), None),
        P(("dp", "tensor"), None),
        P(None, "dp", "tensor"),
        P("tensor", "dp"),
        P(),
        P(),
        P(),
        P(),
        P("dp", "tensor", None),
        P("dp", "tensor", None),
        P(("dp", "tensor"), None),
        P("dp", None),
        P("dp", None),
        P(),
    )
    out_specs = (
        P(("dp", "tensor"), None),
        P(("dp", "tensor"), None),
        P(None, "dp", "tensor"),
        P("tensor", "dp"),
        P(),
        P(),
        P(),
        P(),
        P("dp", "tensor", None),
        P("dp", "tensor", None),
    )
    return jax.shard_map(body, mesh=mesh, in_specs=in_specs, out_specs=out_specs, check_vma=False)
```

```python
import functools
import math

import jax
import jax.numpy as jnp
from jax import lax
from jax.experimental import pallas as pl
from jax.experimental.pallas import tpu as pltpu
from jax.sharding import PartitionSpec as P

NB = 32
EPSILON = 1e-06
HIGHEST = lax.Precision.HIGHEST
DH = 64
NEGATIVE = -1e30
QB = 256
NT = (((1,), (1,)), ((), ()))
TN = (((0,), (0,)), ((), ()))
NN = (((1,), (0,)), ((), ()))


def mm(a, b, dims):
    return lax.dot_general(a, b, dims, preferred_element_type=jnp.float32)


def build_bias(line_ref, tiles, heads, blocks):
    for h in range(heads):
        for d in range(blocks):
            piece = line_ref[h : h + 1, d * QB : d * QB + 2 * QB]
            wide = jnp.broadcast_to(piece, (QB, 2 * QB))
            turned = pltpu.roll(wide, 0, 1, stride=1, stride_axis=0)
            tiles[h, d] = turned[:, QB:]


def score_block(keys, query, tiles, h, qb, segk_ref, segq_ref):
    raw = mm(keys, query, NT)
    q_seg = segq_ref[:, qb * QB : (qb + 1) * QB]
    parts = []
    for kb in range(qb + 1):
        k_seg = segk_ref[kb * QB : (kb + 1) * QB, :]
        same = k_seg == q_seg
        if kb == qb:
            row = lax.broadcasted_iota(jnp.int32, (QB, QB), 0)
            col = lax.broadcasted_iota(jnp.int32, (QB, QB), 1)
            same = same | (row == col)
        parts.append(
            jnp.where(same, raw[kb * QB : (kb + 1) * QB] + tiles[h, qb - kb], NEGATIVE)
        )
    return parts


def attend_kernel(heads, blocks, line_ref, segk_ref, segq_ref, rows_ref, w_ref,
                  qkv_ref, out_ref, lse_ref, tiles):
    @pl.when(pl.program_id(0) == 0)
    def _():
        build_bias(line_ref, tiles, heads, blocks)

    for c in range(3):
        qkv_ref[c] = mm(rows_ref[...], w_ref[c], NN).astype(jnp.bfloat16)
    scale = 1.0 / math.sqrt(DH)
    for qb in range(blocks):
        nk = (qb + 1) * QB
        lower = qb * QB
        turned = []
        for h in range(heads):
            cols = slice(h * DH, (h + 1) * DH)
            query = (qkv_ref[0, lower : lower + QB, cols].astype(jnp.float32) * scale).astype(jnp.bfloat16)
            parts = score_block(qkv_ref[1, 0:nk, cols], query, tiles, h, qb, segk_ref.at[0], segq_ref.at[0])
            peak = functools.reduce(jnp.maximum, [jnp.max(x, axis=0, keepdims=True) for x in parts])
            probs = [jnp.exp(x - peak) for x in parts]
            total = functools.reduce(jnp.add, [jnp.sum(x, axis=0, keepdims=True) for x in probs])
            mixed = functools.reduce(jnp.add, [
                mm(qkv_ref[2, kb * QB : (kb + 1) * QB, cols], x.astype(jnp.bfloat16), TN)
                for kb, x in enumerate(probs)])
            turned.append(mixed / total)
            lse_ref[0, h : h + 1, lower : lower + QB] = peak + jnp.log(total)
        out_ref[lower : lower + QB, :] = jnp.concatenate(turned, axis=0).T.astype(jnp.bfloat16)


def attend(line, segk, segq, rows, w):
    seqs, _, seq_len = segq.shape
    heads = line.shape[0]
    inner = heads * DH
    blocks = seq_len // QB
    width = rows.shape[1]
    return pl.pallas_call(
        functools.partial(attend_kernel, heads, blocks),
        grid=(seqs,),
        in_specs=[
            pl.BlockSpec(line.shape, lambda s: (0, 0)),
            pl.BlockSpec((1, seq_len, 1), lambda s: (s, 0, 0)),
            pl.BlockSpec((1, 1, seq_len), lambda s: (s, 0, 0)),
            pl.BlockSpec((seq_len, width), lambda s: (s, 0)),
            pl.BlockSpec(w.shape, lambda s: (0, 0, 0)),
        ],
        out_specs=[
            pl.BlockSpec((3, seq_len, inner), lambda s: (0, s, 0)),
            pl.BlockSpec((seq_len, inner), lambda s: (s, 0)),
            pl.BlockSpec((1, heads, seq_len), lambda s: (s, 0, 0)),
        ],
        out_shape=[
            jax.ShapeDtypeStruct((3, seqs * seq_len, inner), jnp.bfloat16),
            jax.ShapeDtypeStruct((seqs * seq_len, inner), jnp.bfloat16),
            jax.ShapeDtypeStruct((seqs, heads, seq_len), jnp.float32),
        ],
        scratch_shapes=[pltpu.VMEM((heads, blocks, QB, QB), jnp.float32)],
        compiler_params=pltpu.CompilerParams(vmem_limit_bytes=48 << 20),
        cost_estimate=pl.CostEstimate(flops=10_000_000_000, bytes_accessed=10 << 20, transcendentals=4_000_000),
        name="attend",
    )(line, segk, segq, rows, w)


def attend_back_kernel(heads, blocks, seqs, line_ref, segk_ref, segq_ref, rows_ref, w_ref,
                       qkv_ref, og_ref, lse_ref,
                       norm_ref, wg_ref, lg_ref, tiles, sums, kg, vg, dq):
    step = pl.program_id(0)

    @pl.when(step == 0)
    def _():
        build_bias(line_ref, tiles, heads, blocks)
        sums[...] = jnp.zeros_like(sums)
        wg_ref[...] = jnp.zeros_like(wg_ref)

    scale = 1.0 / math.sqrt(DH)
    for h in range(heads):
        cols = slice(h * DH, (h + 1) * DH)
        kg[...] = jnp.zeros_like(kg)
        vg[...] = jnp.zeros_like(vg)
        for qb in range(blocks):
            nk = (qb + 1) * QB
            lower = qb * QB
            query = (qkv_ref[0, lower : lower + QB, cols].astype(jnp.float32) * scale).astype(jnp.bfloat16)
            grad = og_ref[lower : lower + QB, cols]
            lse = lse_ref[0, h : h + 1, lower : lower + QB]
            parts = score_block(qkv_ref[1, 0:nk, cols], query, tiles, h, qb, segk_ref.at[0], segq_ref.at[0])
            probs = [jnp.exp(x - lse) for x in parts]
            pg = mm(qkv_ref[2, 0:nk, cols], grad, NT)
            pgs = [pg[kb * QB : (kb + 1) * QB] for kb in range(qb + 1)]
            delta = functools.reduce(jnp.add, [jnp.sum(p * g, axis=0, keepdims=True) for p, g in zip(probs, pgs)])
            dqt = jnp.zeros((DH, QB), jnp.float32)
            for kb in range(qb + 1):
                rows = slice(kb * QB, (kb + 1) * QB)
                sg = (probs[kb] * (pgs[kb] - delta)).astype(jnp.bfloat16)
                sums[h, qb - kb] += sg.astype(jnp.float32)
                vg[rows] += mm(probs[kb].astype(jnp.bfloat16), grad, NN)
                kg[rows] += mm(sg, query, NN)
                dqt = dqt + mm(qkv_ref[1, rows, cols], sg, TN)
            dq[lower : lower + QB, h * DH : (h + 1) * DH] = (dqt * scale).T.astype(jnp.bfloat16)
        inner = heads * DH
        dq[:, inner + h * DH : inner + (h + 1) * DH] = kg[...].astype(jnp.bfloat16)
        dq[:, 2 * inner + h * DH : 2 * inner + (h + 1) * DH] = vg[...].astype(jnp.bfloat16)
    inner = heads * DH
    total = jnp.zeros(norm_ref.shape, jnp.float32)
    for c in range(3):
        piece = dq[:, c * inner : (c + 1) * inner]
        wg_ref[c] += mm(rows_ref[...], piece, TN)
        total = total + mm(piece, w_ref[c], NT)
    norm_ref[...] = total.astype(norm_ref.dtype)

    @pl.when(step == seqs - 1)
    def _():
        for h in range(heads):
            for d in range(blocks):
                lg_ref[h * blocks + d] = fold_tile(sums, h, d)


def fold_tile(sums, h, d):
    blank = jnp.zeros((8, QB), jnp.float32)
    total = jnp.zeros((8, 2 * QB), jnp.float32)
    for g in range(QB // 8):
        piece = jnp.concatenate([sums[h, d, 8 * g : 8 * g + 8, :], blank], axis=1)
        total = total + (piece if g == 0 else pltpu.roll(piece, 2 * QB - 8 * g, 1))
    return total


def lines_of(folded, heads, blocks):
    moved = sum(jnp.roll(folded[:, s, :], -s, axis=1) for s in range(8))
    moved = moved.reshape(heads, blocks, 2, QB)
    ahead = jnp.concatenate([moved[:, 1:, 1], jnp.zeros((heads, 1, QB), jnp.float32)], axis=1)
    return (moved[:, :, 0] + ahead).reshape(heads, blocks * QB)


def attend_back(line, segk, segq, rows, w, qkv, og, lse):
    seqs, _, seq_len = segq.shape
    heads = line.shape[0]
    inner = heads * DH
    blocks = seq_len // QB
    width = rows.shape[1]
    return pl.pallas_call(
        functools.partial(attend_back_kernel, heads, blocks, seqs),
        grid=(seqs,),
        in_specs=[
            pl.BlockSpec(line.shape, lambda s: (0, 0)),
            pl.BlockSpec((1, seq_len, 1), lambda s: (s, 0, 0)),
            pl.BlockSpec((1, 1, seq_len), lambda s: (s, 0, 0)),
            pl.BlockSpec((seq_len, width), lambda s: (s, 0)),
            pl.BlockSpec(w.shape, lambda s: (0, 0, 0)),
            pl.BlockSpec((3, seq_len, inner), lambda s: (0, s, 0)),
            pl.BlockSpec((seq_len, inner), lambda s: (s, 0)),
            pl.BlockSpec((1, heads, seq_len), lambda s: (s, 0, 0)),
        ],
        out_specs=[
            pl.BlockSpec((seq_len, width), lambda s: (s, 0)),
            pl.BlockSpec(w.shape, lambda s: (0, 0, 0)),
            pl.BlockSpec((heads * blocks, 8, 2 * QB), lambda s: (0, 0, 0)),
        ],
        out_shape=[
            jax.ShapeDtypeStruct((seqs * seq_len, width), jnp.bfloat16),
            jax.ShapeDtypeStruct(w.shape, jnp.float32),
            jax.ShapeDtypeStruct((heads * blocks, 8, 2 * QB), jnp.float32),
        ],
        scratch_shapes=[
            pltpu.VMEM((heads, blocks, QB, QB), jnp.float32),
            pltpu.VMEM((heads, blocks, QB, QB), jnp.float32),
            pltpu.VMEM((seq_len, DH), jnp.float32),
            pltpu.VMEM((seq_len, DH), jnp.float32),
            pltpu.VMEM((seq_len, 3 * inner), jnp.bfloat16),
        ],
        compiler_params=pltpu.CompilerParams(vmem_limit_bytes=48 << 20),
        cost_estimate=pl.CostEstimate(flops=20_000_000_000, bytes_accessed=16 << 20, transcendentals=4_000_000),
        name="attend_back",
    )(line, segk, segq, rows, w, qkv, og, lse)


def mask_inputs(segments, padding):
    keyed = jnp.where(padding == 1, segments, -1)
    return keyed[:, :, None], segments[:, None, :]


def line_of(by_distance):
    return jnp.concatenate([jnp.full((by_distance.shape[0], QB), NEGATIVE, jnp.float32), by_distance], axis=1)


FT = 512
ROOT_2_PI = math.sqrt(2.0 / math.pi)


def gelu_pair(x):
    square = x * x
    t = jnp.tanh(ROOT_2_PI * x * (1.0 + 0.044715 * square))
    half = 0.5 * (1.0 + t)
    slope = half + 0.5 * x * (1.0 - t * t) * (ROOT_2_PI * (1.0 + 3 * 0.044715 * square))
    return x * half, slope


def expert_kernel(steps, x_ref, g_ref, up_ref, down_ref, act_ref, pre_ref, back_ref, dot_ref, total, dots):
    step = pl.program_id(0)

    @pl.when(step == 0)
    def _():
        total[...] = jnp.zeros_like(total)
        dots[...] = jnp.zeros_like(dots)

    rows = x_ref.shape[0]
    chunk = 256
    for lower in range(0, rows, chunk):
        part = slice(lower, lower + chunk)
        pre = mm(x_ref[part], up_ref[...], NT)
        out_side = mm(g_ref[part], down_ref[...], NT)
        act, slope = gelu_pair(pre)
        low = act.astype(jnp.bfloat16)
        act_ref[part] = low
        product = low.astype(jnp.float32) * out_side
        dots[part] += sum(product[:, k : k + 128] for k in range(0, FT, 128))
        back = (out_side * slope).astype(jnp.bfloat16)
        pre_ref[part] = back
        total[part] += mm(back, up_ref[...], NN)

    @pl.when(step == steps - 1)
    def _():
        back_ref[...] = total[...].astype(jnp.bfloat16)
        dot_ref[...] = lax.dot_general(
            jnp.ones((8, 128), jnp.float32), dots[...], NT,
            precision=HIGHEST, preferred_element_type=jnp.float32)


def expert_first(x, g, up, down):
    rows, width = x.shape
    hidden = up.shape[0]
    steps = hidden // FT
    whole = lambda f: (0, 0)
    return pl.pallas_call(
        functools.partial(expert_kernel, steps),
        grid=(steps,),
        in_specs=[
            pl.BlockSpec((rows, width), whole),
            pl.BlockSpec((rows, width), whole),
            pl.BlockSpec((FT, width), lambda f: (f, 0)),
            pl.BlockSpec((FT, width), lambda f: (f, 0)),
        ],
        out_specs=[
            pl.BlockSpec((rows, FT), lambda f: (0, f)),
            pl.BlockSpec((rows, FT), lambda f: (0, f)),
            pl.BlockSpec((rows, width), whole),
            pl.BlockSpec((8, rows), whole),
        ],
        out_shape=[
            jax.ShapeDtypeStruct((rows, hidden), jnp.bfloat16),
            jax.ShapeDtypeStruct((rows, hidden), jnp.bfloat16),
            jax.ShapeDtypeStruct((rows, width), jnp.bfloat16),
            jax.ShapeDtypeStruct((8, rows), jnp.float32),
        ],
        scratch_shapes=[
            pltpu.VMEM((rows, width), jnp.float32),
            pltpu.VMEM((rows, 128), jnp.float32),
        ],
        compiler_params=pltpu.CompilerParams(vmem_limit_bytes=48 << 20),
        cost_estimate=pl.CostEstimate(
            flops=6 * rows * width * hidden, bytes_accessed=32 << 20, transcendentals=rows * hidden),
        name="expert_first",
    )(x, g, up, down)


def expert_late_kernel(steps, x_ref, g_ref, gate_ref, act_ref, pre_ref, down_ref,
                       out_ref, up_grad_ref, down_grad_ref, total, x_gated, g_gated):
    step = pl.program_id(0)

    @pl.when(step == 0)
    def _():
        total[...] = jnp.zeros_like(total)
        gate = gate_ref[...]
        x_gated[...] = (x_ref[...].astype(jnp.float32) * gate).astype(jnp.bfloat16)
        g_gated[...] = (g_ref[...].astype(jnp.float32) * gate).astype(jnp.bfloat16)

    up_grad_ref[...] = mm(pre_ref[...], x_gated[...], TN).astype(up_grad_ref.dtype)
    down_grad_ref[...] = mm(act_ref[...], g_gated[...], TN).astype(down_grad_ref.dtype)
    total[...] += mm(act_ref[...], down_ref[...], NN)

    @pl.when(step == steps - 1)
    def _():
        out_ref[...] = total[...].astype(jnp.bfloat16)


def expert_late(x, g, gate, act, pre, down):
    rows, width = x.shape
    hidden = down.shape[0]
    steps = hidden // FT
    whole = lambda f: (0, 0)
    tile = pl.BlockSpec((FT, width), lambda f: (f, 0))
    return pl.pallas_call(
        functools.partial(expert_late_kernel, steps),
        grid=(steps,),
        in_specs=[
            pl.BlockSpec((rows, width), whole),
            pl.BlockSpec((rows, width), whole),
            pl.BlockSpec((rows, 1), whole),
            pl.BlockSpec((rows, FT), lambda f: (0, f)),
            pl.BlockSpec((rows, FT), lambda f: (0, f)),
            tile,
        ],
        out_specs=[pl.BlockSpec((rows, width), whole), tile, tile],
        out_shape=[
            jax.ShapeDtypeStruct((rows, width), jnp.bfloat16),
            jax.ShapeDtypeStruct((hidden, width), jnp.bfloat16),
            jax.ShapeDtypeStruct((hidden, width), jnp.bfloat16),
        ],
        scratch_shapes=[
            pltpu.VMEM((rows, width), jnp.float32),
            pltpu.VMEM((rows, width), jnp.bfloat16),
            pltpu.VMEM((rows, width), jnp.bfloat16),
        ],
        compiler_params=pltpu.CompilerParams(vmem_limit_bytes=48 << 20),
        cost_estimate=pl.CostEstimate(
            flops=6 * rows * width * hidden, bytes_accessed=32 << 20, transcendentals=0),
        name="expert_late",
    )(x, g, gate, act, pre, down)


MESH = pl.DeviceIdType.MESH
VMEM_LIMIT = 61 << 20


def remote(src, dst, send, recv, axis, place):
    return pltpu.make_async_remote_copy(
        src_ref=src, dst_ref=dst, send_sem=send, recv_sem=recv, device_id={axis: place}, device_id_type=MESH
    )


def each_peer(count, step, start=1):
    if count <= 8:
        for r in range(start, count):
            step(r)
    else:
        def one(r, carry):
            step(r)
            return carry
        lax.fori_loop(start, count, one, 0)


def greet(dp_count, tensor_count):
    barrier = pltpu.get_barrier_semaphore()
    dp, tp = lax.axis_index("dp"), lax.axis_index("tensor")
    for r in range(1, tensor_count):
        pl.semaphore_signal(barrier, inc=1, device_id={"tensor": lax.rem(tp + r, tensor_count)}, device_id_type=MESH)

    def signal(r):
        pl.semaphore_signal(barrier, inc=1, device_id={"dp": lax.rem(dp + r, dp_count)}, device_id_type=MESH)
    each_peer(dp_count, signal)
    return lambda: pl.semaphore_wait(barrier, tensor_count - 1 + dp_count - 1)


def partners(tensor_count):
    tp = lax.axis_index("tensor")
    sib = tp + 1 - 2 * lax.rem(tp, 2)
    return tp, sib, lax.rem(tp + 2, tensor_count), lax.rem(sib + 2, tensor_count)


def place_pairs(routes_ref, live_ref, experts, capacity, cap_rows):
    tokens = live_ref.shape[1]
    live = live_ref[...] == 1
    ids = lax.broadcasted_iota(jnp.int32, (experts, tokens), 0)
    row = lax.broadcasted_iota(jnp.int32, (tokens, tokens), 0)
    col = lax.broadcasted_iota(jnp.int32, (tokens, tokens), 1)
    before = (row < col).astype(jnp.float32).astype(jnp.bfloat16)
    slots = []
    base = jnp.zeros((experts, 1), jnp.float32)
    for k in range(2):
        route = routes_ref[k : k + 1, :]
        hot = jnp.where((ids == route) & live, 1.0, 0.0)
        count = mm(hot.astype(jnp.bfloat16), before, NN) + base
        place = jnp.sum(count * hot, axis=0, keepdims=True).astype(jnp.int32)
        slots.append(jnp.where(live & (place < capacity), route * cap_rows + place, -1))
        base = base + jnp.sum(hot, axis=1, keepdims=True)
    return slots


def chosen(first, second, expert, cap_rows):
    ids = lax.broadcasted_iota(jnp.int32, (cap_rows, first.shape[1]), 0) + expert * cap_rows
    return jnp.where((ids == first) | (ids == second), 1.0, 0.0).astype(jnp.bfloat16)


def attend_sequence(heads, blocks, seq, line_tiles, segk_ref, segq_ref, qkv, heads_out, lse_ref):
    scale = 1.0 / math.sqrt(DH)
    inner = heads * DH
    half = blocks // 2
    for qb in range(blocks):
        nk = (qb + 1) * QB
        lower = qb * QB
        for h in range(heads):
            cols = [slice(c * inner + h * DH, c * inner + (h + 1) * DH) for c in range(3)]
            query = (qkv[seq, lower : lower + QB, cols[0]].astype(jnp.float32) * scale).astype(jnp.bfloat16)
            parts = score_block(qkv[seq, 0:nk, cols[1]], query, line_tiles, h, qb, segk_ref.at[seq], segq_ref.at[seq])
            peak = functools.reduce(jnp.maximum, [jnp.max(x, axis=0, keepdims=True) for x in parts])
            probs = [jnp.exp(x - peak) for x in parts]
            total = functools.reduce(jnp.add, [jnp.sum(x, axis=0, keepdims=True) for x in probs])
            mixed = functools.reduce(jnp.add, [
                mm(qkv[seq, kb * QB : (kb + 1) * QB, cols[2]], x.astype(jnp.bfloat16), TN)
                for kb, x in enumerate(probs)])
            heads_out[seq * 2 + qb // half, h * DH : (h + 1) * DH, (qb % half) * QB : (qb % half + 1) * QB] = (
                mixed / total).astype(jnp.bfloat16)
            lse_ref[seq, h : h + 1, lower : lower + QB] = peak + jnp.log(total)


def front_kernel(sizes, x_ref, gain_ref, w_ref, outw_ref, down_ref, grad_ref, routes_ref, live_ref, line_ref,
                 segk_ref, segq_ref,
                 rows, w_all, outw_all, down_all, qkv, lse_ref, heads_all, slots_ref, cot,
                 tiles, heads_out, cot_send,
                 far_send, far_recv, w_send, w_recv, o_send, o_recv, ot_send, ot_recv,
                 dn_send, dn_recv, cot_s, cot_r, head_send, head_recv, local_sem):
    dp_count, tensor_count, experts, capacity, cap_rows, heads, blocks, gather_w = sizes
    dp = lax.axis_index("dp")
    tp, sib, opp, across = partners(tensor_count)
    wait_barrier = greet(dp_count, tensor_count)

    x = x_ref[...].astype(jnp.float32)
    r = lax.rsqrt(jnp.mean(x * x, axis=-1, keepdims=True) + EPSILON)
    rows[tp] = (x * r * gain_ref[...]).astype(jnp.bfloat16)
    wait_barrier()

    half = rows.shape[1] // 2
    parts = [pl.ds(0, half), pl.ds(half, half)]
    far = [remote(rows.at[tp, p], rows.at[tp, p], far_send.at[k], far_recv.at[k], "tensor", opp) for k, p in enumerate(parts)]
    near = remote(rows.at[tp], rows.at[tp], far_send.at[2], far_recv.at[2], "tensor", sib)
    onward = [remote(rows.at[opp, p], rows.at[opp, p], far_send.at[3 + k], far_recv.at[3 + k], "tensor", sib) for k, p in enumerate(parts)]
    for c in far:
        c.start()
    near.start()

    def w_copy(r):
        return remote(w_ref, w_all.at[dp], w_send.at[r], w_recv.at[r], "dp", lax.rem(dp + r, dp_count))

    def o_copy(r):
        return remote(outw_ref, outw_all.at[tp, dp], o_send.at[r], o_recv.at[r], "dp", lax.rem(dp + r, dp_count))

    def ot_copy(k, to):
        return remote(outw_all.at[tp], outw_all.at[tp], ot_send.at[k], ot_recv.at[k], "tensor", to)
    if gather_w:
        each_peer(dp_count, lambda r: w_copy(r).start())
        each_peer(dp_count, lambda r: o_copy(r).start())
        own_w = pltpu.make_async_copy(w_ref, w_all.at[dp], local_sem.at[0])
        own_w.start()
        own_o = pltpu.make_async_copy(outw_ref, outw_all.at[tp, dp], local_sem.at[2])
        own_o.start()

    first, second = place_pairs(routes_ref, live_ref, experts, capacity, cap_rows)
    slots_ref[0:1, :] = first
    slots_ref[1:2, :] = second

    def cot_copy(r):
        to = lax.rem(dp + r, dp_count)
        return remote(cot_send.at[to], cot.at[dp], cot_s.at[r], cot_r.at[r], "dp", to)

    def cot_fill(r):
        to = lax.rem(dp + r, dp_count)
        cot_send[to] = mm(chosen(first, second, to, cap_rows), grad_ref[...], NN).astype(jnp.bfloat16)

    each_peer(dp_count, cot_fill)
    cot_fill(0)
    own_cot = pltpu.make_async_copy(cot_send.at[dp], cot.at[dp], local_sem.at[1])
    own_cot.start()

    build_bias(line_ref, tiles, heads, blocks)
    if gather_w:
        own_w.wait()
        each_peer(dp_count, lambda r: w_copy(r).wait_recv())
    each_peer(dp_count, lambda r: cot_copy(r).start())
    near.wait_recv()

    width = rows.shape[2]
    own_seq = tp // 2
    inner = heads * DH

    def project(seq):
        tokens = rows[pl.ds(seq * 2, 2)].reshape(2 * rows.shape[1], width)
        weight = w_all[...].reshape(width, w_all.shape[2])
        qkv[seq] = mm(tokens, weight, NN).astype(jnp.bfloat16)

    def head_copy(k, to):
        return remote(heads_out.at[to], heads_all.at[tp], head_send.at[k], head_recv.at[k], "tensor", to)

    own_down = pltpu.make_async_copy(down_ref, down_all.at[tp], local_sem.at[3])
    down_far = remote(down_ref, down_all.at[tp], dn_send.at[0], dn_recv.at[0], "tensor", opp)
    down_near = remote(down_ref, down_all.at[tp], dn_send.at[1], dn_recv.at[1], "tensor", sib)
    down_on = remote(down_all.at[opp], down_all.at[opp], dn_send.at[2], dn_recv.at[2], "tensor", sib)

    project(own_seq)
    for k in range(2):
        far[k].wait_recv()
        onward[k].start()
    own_down.start()
    down_far.start()
    down_near.start()
    attend_sequence(heads, blocks, own_seq, tiles, segk_ref, segq_ref, qkv, heads_out, lse_ref)
    head_copy(0, sib).start()
    heads_all[tp] = heads_out[tp]
    for k in range(2):
        onward[k].wait_recv()
    other = 1 - own_seq
    project(other)
    if gather_w:
        own_o.wait()
        each_peer(dp_count, lambda r: o_copy(r).wait_recv())
        for k, to in enumerate((sib, opp, across)):
            ot_copy(k, to).start()
    attend_sequence(heads, blocks, other, tiles, segk_ref, segq_ref, qkv, heads_out, lse_ref)
    head_copy(1, opp).start()
    head_copy(2, across).start()

    down_far.wait_recv()
    down_on.start()
    own_cot.wait()
    own_down.wait()
    each_peer(dp_count, lambda r: cot_copy(r).wait())
    if gather_w:
        each_peer(dp_count, lambda r: w_copy(r).wait_send())
        each_peer(dp_count, lambda r: o_copy(r).wait_send())
        for k, to in enumerate((sib, opp, across)):
            ot_copy(k, to).wait()
    for c in far + [near] + onward:
        c.wait_send()
    head_copy(0, sib).wait()
    head_copy(1, opp).wait()
    head_copy(2, across).wait()
    down_far.wait_send()
    down_near.wait()
    down_on.wait()


def sems(*counts):
    out = []
    for n in counts:
        out += [pltpu.SemaphoreType.DMA((n,)), pltpu.SemaphoreType.DMA((n,))]
    return out


def front(sizes, x, gain, w, outw, down, grad, routes_t, live_row, line, segk, segq):
    dp_count, tensor_count, experts, capacity, cap_rows, heads, blocks, gather_w = sizes
    tokens, width = x.shape
    seq_len = blocks * QB
    seqs = tensor_count * tokens // seq_len
    inner = heads * DH
    vmem = pl.BlockSpec(memory_space=pltpu.VMEM)
    anywhere = pl.BlockSpec(memory_space=pl.ANY)
    return pl.pallas_call(
        functools.partial(front_kernel, sizes),
        in_specs=[vmem] * 4 + [anywhere] + [vmem] * 6,
        out_specs=[vmem] * 3 + [anywhere] + [vmem] * 4 + [anywhere],
        out_shape=[
            jax.ShapeDtypeStruct((tensor_count, tokens, width), jnp.bfloat16),
            jax.ShapeDtypeStruct((dp_count,) + w.shape, jnp.bfloat16),
            jax.ShapeDtypeStruct((tensor_count, dp_count) + outw.shape, jnp.bfloat16),
            jax.ShapeDtypeStruct((tensor_count,) + down.shape, jnp.bfloat16),
            jax.ShapeDtypeStruct((seqs, seq_len, w.shape[1]), jnp.bfloat16),
            jax.ShapeDtypeStruct((seqs, heads, seq_len), jnp.float32),
            jax.ShapeDtypeStruct((tensor_count, inner, tokens), jnp.bfloat16),
            jax.ShapeDtypeStruct((8, tokens), jnp.int32),
            jax.ShapeDtypeStruct((experts, cap_rows, width), jnp.bfloat16),
        ],
        scratch_shapes=[
            pltpu.VMEM((heads, blocks, QB, QB), jnp.float32),
            pltpu.VMEM((tensor_count, inner, tokens), jnp.bfloat16),
            pltpu.VMEM((experts, cap_rows, width), jnp.bfloat16),
        ] + sems(5, dp_count, dp_count, 3, 3, dp_count, 3) + [pltpu.SemaphoreType.DMA((4,))],
        compiler_params=pltpu.CompilerParams(
            vmem_limit_bytes=VMEM_LIMIT, collective_id=1, has_side_effects=True),
        cost_estimate=pl.CostEstimate(flops=20_000_000_000, bytes_accessed=20 << 20, transcendentals=4_000_000),
        name="front",
    )(x, gain, w, outw, down, grad, routes_t, live_row, line, segk, segq)


def to_row(column, lanes):
    n = column.shape[0]
    row = lax.broadcasted_iota(jnp.int32, (n, lanes), 0)
    col = lax.broadcasted_iota(jnp.int32, (n, lanes), 1)
    return jnp.sum(jnp.where(row == col, column, 0.0), axis=0, keepdims=True)


def to_column(row_values, n):
    lanes = row_values.shape[1]
    row = lax.broadcasted_iota(jnp.int32, (n, lanes), 0)
    col = lax.broadcasted_iota(jnp.int32, (n, lanes), 1)
    return jnp.sum(jnp.where(row == col, row_values, 0.0), axis=1, keepdims=True)


def gate_map(first, second, gate_first, gate_second, expert, cap_rows):
    ids = lax.broadcasted_iota(jnp.int32, (cap_rows, first.shape[1]), 0) + expert * cap_rows
    return jnp.where(ids == first, gate_first, jnp.where(ids == second, gate_second, 0.0))


def gated_rows(weights, rows):
    high = weights.astype(jnp.bfloat16)
    low = (weights - high.astype(jnp.float32)).astype(jnp.bfloat16)
    return mm(high, rows, TN) + mm(low, rows, TN)


def middle_kernel(sizes, x_ref, grad_ref, heads_ref, outw_ref, gain_ref, router_ref, routes_ref, live_ref,
                  slots_ref, cot_ref, up_ref, down_ref,
                  up_pair, up_own, down_grad, produced, middle, middle_grad, heads_grad, out_part, stats, gates,
                  up, down, g_rows, x_rows, act, side, back_send, back, gate_send, gate_rows,
                  dot_send, dot_rows, put_rows, moe_low, stage, down_pair, down_own, down_land, heads_low,
                  up_s, up_r, x_s, x_r, b_s, b_r, g_s, g_r, d_s, d_r, a_s, a_r, load_sem):
    dp_count, tensor_count, experts, capacity, cap_rows, heads, blocks, gather_w = sizes
    dp = lax.axis_index("dp")
    tp, sib, opp, across = partners(tensor_count)
    hidden = up.shape[1]
    x_send = produced
    total = middle_grad
    tokens, width = x_ref.shape
    lanes = gate_send.shape[2]
    wait_barrier = greet(dp_count, tensor_count)

    load_g = pltpu.make_async_copy(cot_ref, g_rows, load_sem.at[0])
    load_down = pltpu.make_async_copy(down_ref, down, load_sem.at[1])
    load_up = pltpu.make_async_copy(up_ref, up.at[tp], load_sem.at[2])
    load_g.start()
    load_down.start()
    load_up.start()

    mixed = x_ref[...].astype(jnp.float32)
    inner = heads * DH
    for t in range(tensor_count):
        heads_low[t] = heads_ref[t].T
        mixed = mixed + mm(heads_low[t], outw_ref[t][:, :inner], NT)
    middle[...] = mixed
    r = lax.rsqrt(jnp.mean(mixed * mixed, axis=-1, keepdims=True) + EPSILON)
    moe_low[...] = (mixed * r * gain_ref[...]).astype(jnp.bfloat16)
    first, second = slots_ref[0:1, :], slots_ref[1:2, :]
    wait_barrier()

    def x_copy(r):
        to = lax.rem(dp + r, dp_count)
        return remote(x_send.at[to], x_rows.at[dp], x_s.at[r], x_r.at[r], "dp", to)

    def x_go(r):
        to = lax.rem(dp + r, dp_count)
        x_send[to] = mm(chosen(first, second, to, cap_rows), moe_low[...], NN).astype(jnp.bfloat16)
        x_copy(r).start()
    each_peer(dp_count, x_go)
    x_rows[dp] = mm(chosen(first, second, dp, cap_rows), moe_low[...], NN).astype(jnp.bfloat16)

    up_far = remote(up_ref, up.at[tp], up_s.at[0], up_r.at[0], "tensor", opp)
    up_near = remote(up_ref, up.at[tp], up_s.at[1], up_r.at[1], "tensor", sib)
    up_on = remote(up.at[opp], up.at[opp], up_s.at[2], up_r.at[2], "tensor", sib)
    up_far.start()
    up_near.start()

    ids = lax.broadcasted_iota(jnp.int32, (experts, tokens), 0)
    pick_first, pick_second = ids == routes_ref[0:1, :], ids == routes_ref[1:2, :]
    live = (live_ref[...] == 1).astype(jnp.float32)
    logits = mm(router_ref[...], moe_low[...], NT)
    gap = jnp.sum(jnp.where(pick_first, logits, 0.0) - jnp.where(pick_second, logits, 0.0), axis=0, keepdims=True)
    gate_first = live / (1.0 + jnp.exp(-gap))
    gate_second = live / (1.0 + jnp.exp(gap))
    gates[0:1, :] = gate_first
    gates[1:2, :] = gate_second

    def gate_copy(r):
        to = lax.rem(dp + r, dp_count)
        return remote(gate_send.at[to], gate_rows.at[dp], g_s.at[r], g_r.at[r], "dp", to)

    def gate_fill(r):
        to = lax.rem(dp + r, dp_count)
        column = jnp.sum(gate_map(first, second, gate_first, gate_second, to, cap_rows), axis=1, keepdims=True)
        return jnp.broadcast_to(to_row(column, lanes), (8, lanes))

    def gate_go(r):
        gate_send[lax.rem(dp + r, dp_count)] = gate_fill(r)
        gate_copy(r).start()
    each_peer(dp_count, gate_go)
    gate_rows[dp] = gate_fill(0)

    load_g.wait()
    load_down.wait()
    slots = experts * cap_rows
    block = slots // 4

    def side_block(k, carry):
        part = pl.ds(pl.multiple_of(k * block, 16), block)
        here = g_rows[pl.ds(k * (experts // 4), experts // 4)].reshape(block, width)
        for t in range(tensor_count):
            side[part, t * hidden : (t + 1) * hidden] = mm(here, down[t], NT).astype(jnp.bfloat16)
        return carry
    lax.fori_loop(0, 4, side_block, 0)

    load_up.wait()
    up_far.wait_recv()
    up_on.start()
    up_near.wait_recv()
    up_on.wait_recv()

    def back_copy(r):
        to = lax.rem(dp - r + dp_count, dp_count)
        return remote(back_send.at[to], back.at[dp], b_s.at[r], b_r.at[r], "dp", to)

    def dot_copy(r):
        to = lax.rem(dp - r + dp_count, dp_count)
        return remote(dot_send.at[to], dot_rows.at[dp], d_s.at[r], d_r.at[r], "dp", to)

    group = max(1, min(dp_count, 320 // cap_rows))

    def first_pass(step, carry):
        rounds = [step * group + k for k in range(group)]
        froms = [lax.rem(dp - r + dp_count, dp_count) for r in rounds]
        for k, r in enumerate(rounds):
            if k == 0:
                @pl.when(r > 0)
                def _():
                    x_copy(r).wait_recv()
            else:
                x_copy(r).wait_recv()
        here = jnp.concatenate([x_rows[s] for s in froms], axis=0)
        total_back = jnp.zeros((group * cap_rows, width), jnp.float32)
        dots = jnp.zeros((group * cap_rows, 128), jnp.float32)
        for t in range(tensor_count):
            cols = slice(t * hidden, (t + 1) * hidden)
            pre = mm(here, up[t], NT)
            value, slope = gelu_pair(pre)
            low = value.astype(jnp.bfloat16)
            places = [pl.ds(pl.multiple_of(s * cap_rows, 16), cap_rows) for s in froms]
            beside = jnp.concatenate([side[p, cols] for p in places], axis=0).astype(jnp.float32)
            product = low.astype(jnp.float32) * beside
            dots = dots + sum(product[:, k : k + 128] for k in range(0, hidden, 128))
            grad = (beside * slope).astype(jnp.bfloat16)
            for k, p in enumerate(places):
                piece = slice(k * cap_rows, (k + 1) * cap_rows)
                act[p, cols] = low[piece]
                side[p, cols] = grad[piece]
            total_back = total_back + mm(grad, up[t], NN)
        column = jnp.sum(dots, axis=1, keepdims=True)
        for k, (r, s) in enumerate(zip(rounds, froms)):
            piece = slice(k * cap_rows, (k + 1) * cap_rows)
            low = total_back[piece].astype(jnp.bfloat16)
            line = jnp.broadcast_to(to_row(column[piece], lanes), (8, lanes))

            def send():
                back_send[s] = low
                dot_send[s] = line
                back_copy(r).start()
                dot_copy(r).start()

            def keep():
                back[dp] = low
                dot_rows[dp] = line
            if k == 0:
                pl.when(r > 0)(send)
                pl.when(r == 0)(keep)
            else:
                send()
        return carry
    lax.fori_loop(0, dp_count // group, first_pass, 0)

    each_peer(dp_count, lambda r: gate_copy(r).wait_recv())

    def gate_rows_in(s, carry):
        column = to_column(gate_rows[s, 0:1, :], cap_rows)
        x_rows[s] = (x_rows[s].astype(jnp.float32) * column).astype(jnp.bfloat16)
        g_rows[s] = (g_rows[s].astype(jnp.float32) * column).astype(jnp.bfloat16)
        return carry
    lax.fori_loop(0, experts, gate_rows_in, 0)

    each_peer(dp_count, lambda r: x_copy(r).wait_send())
    lands = ((down_pair, down_own), (up_pair, up_own))
    aside = [remote(stage.at[k], lands[k][n], a_s.at[2 * k + n], a_r.at[2 * k + n], "tensor", sib)
             for k in range(2) for n in range(2)]
    down_far = remote(down_pair, down_land, a_s.at[4], a_r.at[4], "tensor", opp)
    piece = hidden // 2
    for n, t in enumerate((across, sib, opp, tp)):
        for k, (left, right) in enumerate(((act, g_rows), (side, x_rows))):
            if n == 1:
                aside[2 * k].wait_send()
            if n >= 2:
                aside[2 * k + n - 2].wait_recv()
            for m in range(2):
                cols = pl.ds(pl.multiple_of(t * hidden + m * piece, 128), piece)
                part = pl.ds(m * piece, piece)
                tile = mm(left[:, cols], right[...].reshape(slots, width), TN)
                if n < 2:
                    stage[k, part, :] = tile.astype(jnp.bfloat16)
                else:
                    land = lands[k][n - 2]
                    land[part, :] = (tile + land[part, :].astype(jnp.float32)).astype(jnp.bfloat16)
            if n < 2:
                aside[2 * k + n].start()
            elif n == 2 and k == 0:
                down_far.start()

    def produce(k, carry):
        part = pl.ds(pl.multiple_of(k * block, 16), block)
        out = jnp.zeros((block, width), jnp.float32)
        for t in range(tensor_count):
            out = out + mm(act[part, t * hidden : (t + 1) * hidden], down[t], NN)
        out = out.astype(jnp.bfloat16)
        for e in range(experts // 4):
            produced[k * (experts // 4) + e] = out[e * cap_rows : (e + 1) * cap_rows]
        return carry
    lax.fori_loop(0, 4, produce, 0)

    total[...] = jnp.zeros_like(total)

    def combine(r, carry):
        dot_first, dot_second = carry
        e = lax.rem(dp + r, dp_count)

        @pl.when(r > 0)
        def _():
            back_copy(r).wait_recv()
            dot_copy(r).wait_recv()
        weights = gate_map(first, second, gate_first, gate_second, e, cap_rows)
        total[...] += gated_rows(weights, back[e])
        column = to_column(dot_rows[e, 0:1, :], cap_rows)
        ids = lax.broadcasted_iota(jnp.int32, (cap_rows, tokens), 0) + e * cap_rows
        dot_first = dot_first + jnp.sum(jnp.where(ids == first, column, 0.0), axis=0, keepdims=True)
        dot_second = dot_second + jnp.sum(jnp.where(ids == second, column, 0.0), axis=0, keepdims=True)
        return dot_first, dot_second
    zero_row = jnp.zeros((1, tokens), jnp.float32)
    dot_first, dot_second = lax.fori_loop(0, dp_count, combine, (zero_row, zero_row))

    change = gate_first * gate_second * (dot_first - dot_second)
    logit_grad = (jnp.where(pick_first, change, 0.0) - jnp.where(pick_second, change, 0.0)).astype(jnp.bfloat16)
    norm_grad = total[...] + mm(logit_grad, router_ref[...], TN)
    mixed = middle[...]
    r = lax.rsqrt(jnp.mean(mixed * mixed, axis=-1, keepdims=True) + EPSILON)
    u = mixed * r
    du = norm_grad * gain_ref[...]
    grad = grad_ref[...].astype(jnp.float32) + r * (du - u * jnp.mean(du * u, axis=-1, keepdims=True))
    middle_grad[...] = grad
    low = grad.astype(jnp.bfloat16)
    for t in range(tensor_count):
        heads_grad[t] = mm(low, outw_ref[t][:, :inner], NN).T.astype(jnp.bfloat16)
        out_part[t] = mm(heads_low[t], low, TN).astype(jnp.bfloat16)
    stats[0:8, :] = jnp.broadcast_to(jnp.sum(norm_grad * u, axis=0, keepdims=True), (8, width))
    stats[8:, :] = mm(logit_grad, moe_low[...], NN)

    down_far.wait_recv()
    strip = put_rows.shape[1]

    def put_copy(k):
        return pltpu.make_async_copy(
            put_rows.at[k % 2], down_grad.at[pl.ds(k * strip, strip)], load_sem.at[3 + k % 2])
    for k in range(hidden // strip):
        part = pl.ds(k * strip, strip)
        if k >= 2:
            put_copy(k - 2).wait()
        put_rows[k % 2] = down_own[part, :].astype(jnp.float32) + down_land[part, :].astype(jnp.float32)
        put_copy(k).start()
    for k in range(hidden // strip - 2, hidden // strip):
        put_copy(k).wait()
    down_far.wait_send()
    for k in range(2):
        aside[2 * k + 1].wait_send()
    up_far.wait_send()
    up_near.wait_send()
    up_on.wait_send()

    def drain(r):
        gate_copy(r).wait_send()
        back_copy(r).wait_send()
        dot_copy(r).wait_send()
    each_peer(dp_count, drain)


def middle_pass(sizes, x, grad, heads_all, outw, gain, router_t, routes_t, live_row, slot_rows, cot, up, down_all):
    dp_count, tensor_count, experts, capacity, cap_rows, heads, blocks, gather_w = sizes
    tokens, width = x.shape
    inner = heads * DH
    hidden = up.shape[0]
    slots = experts * cap_rows
    lanes = -(-cap_rows // 128) * 128
    vmem = pl.BlockSpec(memory_space=pltpu.VMEM)
    anywhere = pl.BlockSpec(memory_space=pl.ANY)
    shape = jax.ShapeDtypeStruct
    low = jnp.bfloat16
    return pl.pallas_call(
        functools.partial(middle_kernel, sizes),
        in_specs=[vmem] * 9 + [anywhere] * 3,
        out_specs=[vmem] * 2 + [anywhere] + [vmem] * 7,
        out_shape=[
            shape((hidden, width), low),
            shape((hidden, width), low),
            shape((hidden, width), jnp.float32),
            shape((experts, cap_rows, width), low),
            shape((tokens, width), jnp.float32),
            shape((tokens, width), jnp.float32),
            shape((tensor_count, inner, tokens), low),
            shape((tensor_count, inner, width), low),
            shape((8 + experts, width), jnp.float32),
            shape((8, tokens), jnp.float32),
        ],
        scratch_shapes=[
            pltpu.VMEM((tensor_count, hidden, width), low),
            pltpu.VMEM((tensor_count, hidden, width), low),
            pltpu.VMEM((experts, cap_rows, width), low),
            pltpu.VMEM((experts, cap_rows, width), low),
            pltpu.VMEM((slots, tensor_count * hidden), low),
            pltpu.VMEM((slots, tensor_count * hidden), low),
            pltpu.VMEM((experts, cap_rows, width), low),
            pltpu.VMEM((experts, cap_rows, width), low),
            pltpu.VMEM((experts, 8, lanes), jnp.float32),
            pltpu.VMEM((experts, 8, lanes), jnp.float32),
            pltpu.VMEM((experts, 8, lanes), jnp.float32),
            pltpu.VMEM((experts, 8, lanes), jnp.float32),
            pltpu.VMEM((2, 96, width), jnp.float32),
            pltpu.VMEM((tokens, width), low),
            pltpu.VMEM((2, hidden, width), low),
            pltpu.VMEM((hidden, width), low),
            pltpu.VMEM((hidden, width), low),
            pltpu.VMEM((hidden, width), low),
            pltpu.VMEM((tensor_count, tokens, inner), low),
        ] + sems(3, dp_count, dp_count, dp_count, dp_count, 5) + [pltpu.SemaphoreType.DMA((5,))],
        compiler_params=pltpu.CompilerParams(
            vmem_limit_bytes=VMEM_LIMIT, collective_id=2, has_side_effects=True),
        cost_estimate=pl.CostEstimate(
            flops=12 * slots * width * hidden * tensor_count, bytes_accessed=40 << 20, transcendentals=4_000_000),
        name="middle_pass",
    )(x, grad, heads_all, outw, gain, router_t, routes_t, live_row, slot_rows, cot, up, down_all)


def attend_back_sequence(heads, blocks, seq, tiles, sums, segk_ref, segq_ref, qkv, grads, lse_ref, kg, vg, dq, between):
    scale = 1.0 / math.sqrt(DH)
    inner = heads * DH
    half = blocks // 2
    for h in range(heads):
        cols, kcols, vcols = [slice(c * inner + h * DH, c * inner + (h + 1) * DH) for c in range(3)]
        kg[...] = jnp.zeros_like(kg)
        vg[...] = jnp.zeros_like(vg)
        for qb in range(blocks):
            nk = (qb + 1) * QB
            lower = qb * QB
            query = (qkv[seq, lower : lower + QB, cols].astype(jnp.float32) * scale).astype(jnp.bfloat16)
            grad = grads[seq * 2 + qb // half, cols, (qb % half) * QB : (qb % half + 1) * QB]
            lse = lse_ref[seq, h : h + 1, lower : lower + QB]
            parts = score_block(qkv[seq, 0:nk, kcols], query, tiles, h, qb, segk_ref.at[seq], segq_ref.at[seq])
            probs = [jnp.exp(x - lse) for x in parts]
            pg = mm(qkv[seq, 0:nk, vcols], grad, NN)
            pgs = [pg[kb * QB : (kb + 1) * QB] for kb in range(qb + 1)]
            delta = functools.reduce(jnp.add, [jnp.sum(p * g, axis=0, keepdims=True) for p, g in zip(probs, pgs)])
            dqt = jnp.zeros((DH, QB), jnp.float32)
            for kb in range(qb + 1):
                rows = slice(kb * QB, (kb + 1) * QB)
                sg = (probs[kb] * (pgs[kb] - delta)).astype(jnp.bfloat16)
                sums[h, qb - kb] += sg.astype(jnp.float32)
                vg[rows] += mm(probs[kb].astype(jnp.bfloat16), grad, NT)
                kg[rows] += mm(sg, query, NN)
                dqt = dqt + mm(qkv[seq, rows, kcols], sg, TN)
            dq[lower : lower + QB, h * DH : (h + 1) * DH] = (dqt * scale).T.astype(jnp.bfloat16)
        dq[:, inner + h * DH : inner + (h + 1) * DH] = kg[...].astype(jnp.bfloat16)
        dq[:, 2 * inner + h * DH : 2 * inner + (h + 1) * DH] = vg[...].astype(jnp.bfloat16)
        between(h)


def fold_lines(sums, h, blocks):
    moved = []
    for d in range(blocks):
        folded = fold_tile(sums, h, d)
        line = folded[0:1, :]
        for s in range(1, 8):
            line = line + pltpu.roll(folded[s : s + 1, :], 2 * QB - s, 1)
        moved.append(line)
    out = []
    for d in range(blocks):
        piece = moved[d][:, :QB]
        if d + 1 < blocks:
            piece = piece + moved[d + 1][:, QB:]
        out.append(piece)
    return jnp.concatenate(out, axis=1)


def two_stage_start(send, land, s_sem, r_sem, tensor_count):
    tp = lax.axis_index("tensor")
    copies = []
    for r in range(1, tensor_count):
        copies.append(remote(send, land.at[r - 1], s_sem.at[r], r_sem.at[r], "tensor", lax.rem(tp + r, tensor_count)))
    for c in copies:
        c.start()
    return copies


def last_kernel(sizes, x_ref, gain_ref, middle_ref, mgrad_ref, hgrad_ref, rows, w_ref, qkv, lse_ref, line_ref,
                segk_ref, segq_ref, produced_ref, slots_ref, gates_ref, early_ref, bucket_ref,
                out_part, up_pair, up_own,
                out_ref, input_grad_ref, wgrad_ref, early_out, late_out, ograd_ref, up_grad,
                tiles, sums, kg, vg, dq, grads, landed, npart, near_land, far_land, pair, wsum, wsend, wland,
                early_land, early_mid, early_dp, late, late_land, late_mid, late_dp, total,
                up_land, out_land, out_pair, out_far, osend, oland,
                h_s, h_r, p_s, p_r, n_s, n_r, w_s, w_r, et_s, et_r, ed_s, ed_r, lt_s, lt_r, ld_s, ld_r, o_s, o_r, od_s, od_r):
    dp_count, tensor_count, experts, capacity, cap_rows, heads, blocks, gather_w = sizes
    dp = lax.axis_index("dp")
    tp, sib, opp, across = partners(tensor_count)
    tokens, width = x_ref.shape
    inner = heads * DH
    wait_barrier = greet(dp_count, tensor_count)
    build_bias(line_ref, tiles, heads, blocks)
    sums[...] = jnp.zeros_like(sums)
    dq[...] = jnp.zeros_like(dq)
    own_seq = tp // 2
    other = 1 - own_seq
    wait_barrier()

    def h_copy(k, to):
        return remote(hgrad_ref.at[to], grads.at[tp], h_s.at[k], h_r.at[k], "tensor", to)
    h_copy(0, opp).start()
    h_copy(1, across).start()
    h_copy(2, sib).start()
    grads[tp] = hgrad_ref[tp]

    def p_copy(r):
        to = lax.rem(dp - r + dp_count, dp_count)
        return remote(produced_ref.at[to], landed.at[dp], p_s.at[r], p_r.at[r], "dp", to)
    each_peer(dp_count, lambda r: p_copy(r).start())
    landed[dp] = produced_ref[dp]

    early = two_stage_start(early_ref, early_land, et_s, et_r, tensor_count)

    def early_copy(r):
        return remote(early_mid, early_dp.at[r], ed_s.at[r], ed_r.at[r], "dp", lax.rem(dp + r, dp_count))

    out_near = [remote(out_part.at[t], out_land.at[k], o_s.at[k], o_r.at[k], "tensor", sib)
                for k, t in enumerate((across, sib))]
    out_across = remote(out_pair, out_far, o_s.at[2], o_r.at[2], "tensor", opp)
    up_across = remote(up_pair, up_land, o_s.at[3], o_r.at[3], "tensor", opp)
    for c in out_near:
        c.start()

    def o_copy(r):
        to = lax.rem(dp + r, dp_count)
        return remote(osend.at[to], oland.at[r], od_s.at[r], od_r.at[r], "dp", to)

    h_copy(0, opp).wait_recv()
    h_copy(1, across).wait_recv()
    out_near[0].wait_recv()
    out_pair[...] = (out_part[opp].astype(jnp.float32) + out_land[0].astype(jnp.float32)).astype(jnp.bfloat16)
    out_across.start()
    up_across.start()

    def n_copy(k, src, dst, to):
        return remote(src, dst, n_s.at[k], n_r.at[k], "tensor", to)
    pair_near = n_copy(0, npart.at[across], near_land.at[0], sib)
    pair_far = n_copy(1, pair, far_land, opp)
    own_near = n_copy(2, npart.at[sib], near_land.at[1], sib)

    def nothing(h):
        pass

    def project(seq, fresh):
        here = rows[pl.ds(seq * 2, 2)].reshape(2 * tokens, width)
        part = mm(here, dq[...], TN)
        wsum[...] = part if fresh else wsum[...] + part
        norm = mm(dq[...], w_ref[...].reshape(width, w_ref.shape[2]), NT)
        column = jnp.sum(norm * here.astype(jnp.float32), axis=0, keepdims=True)
        low = norm.astype(jnp.bfloat16)
        npart[seq * 2] = low[:tokens]
        npart[seq * 2 + 1] = low[tokens:]
        return column

    attend_back_sequence(heads, blocks, other, tiles, sums, segk_ref, segq_ref, qkv, grads, lse_ref, kg, vg, dq, nothing)
    out_across.wait_recv()
    out_near[1].wait_recv()
    out_whole = out_part[tp].astype(jnp.float32) + out_land[1].astype(jnp.float32) + out_far[...].astype(jnp.float32)
    out_whole = out_whole.T.astype(jnp.bfloat16)
    share = width // dp_count
    osend[:, :, inner:] = jnp.zeros((dp_count, share, osend.shape[2] - inner), jnp.bfloat16)
    for to in range(dp_count):
        osend[to, :, :inner] = out_whole[to * share : (to + 1) * share]
    each_peer(dp_count, lambda r: o_copy(r).start())
    gain_row = project(other, True)
    pair_near.start()

    def between(h):
        if h == 0:
            pair_near.wait_recv()
            pair[...] = (npart[opp].astype(jnp.float32) + near_land[0].astype(jnp.float32)).astype(jnp.bfloat16)
            pair_far.start()
            for c in early:
                c.wait_recv()
            early_mid[...] = early_ref[...] + early_land[0] + early_land[1] + early_land[2]
            each_peer(dp_count, lambda r: early_copy(r).start())

    h_copy(2, sib).wait_recv()
    attend_back_sequence(heads, blocks, own_seq, tiles, sums, segk_ref, segq_ref, qkv, grads, lse_ref, kg, vg, dq, between)
    gain_row = gain_row + project(own_seq, False)
    own_near.start()

    def w_copy(r):
        to = lax.rem(dp + r, dp_count)
        return remote(wsend.at[to], wland.at[r], w_s.at[r], w_r.at[r], "dp", to)
    for to in range(dp_count):
        wsend[to] = wsum[to * share : (to + 1) * share, :].astype(jnp.bfloat16)
    each_peer(dp_count, lambda r: w_copy(r).start())

    gain_row = gain_row / gain_ref[...]
    late[...] = jnp.zeros_like(late)
    for k in range(width // 128):
        late[k : k + 1, :] = gain_row[:, k * 128 : (k + 1) * 128]
    buckets = late.shape[0] - 8
    ids = lax.broadcasted_iota(jnp.int32, (buckets, bucket_ref.shape[1]), 0)
    hot = ids == bucket_ref[...]
    lane = lax.broadcasted_iota(jnp.int32, (buckets, 128), 1)
    table = jnp.zeros((buckets, 128), jnp.float32)
    for h in range(heads):
        column = jnp.sum(jnp.where(hot, fold_lines(sums, h, blocks), 0.0), axis=1, keepdims=True)
        table = table + jnp.where(lane == tp * heads + h, column, 0.0)
    late[8:, :] = table
    late_first = two_stage_start(late, late_land, lt_s, lt_r, tensor_count)

    def late_copy(r):
        return remote(late_mid, late_dp.at[r], ld_s.at[r], ld_r.at[r], "dp", lax.rem(dp + r, dp_count))

    each_peer(dp_count, lambda r: early_copy(r).wait_recv())
    summed = early_mid[...]
    for r in range(1, dp_count):
        summed = summed + early_dp[r]
    early_out[...] = summed

    for c in late_first:
        c.wait_recv()
    late_mid[...] = late[...] + late_land[0] + late_land[1] + late_land[2]
    each_peer(dp_count, lambda r: late_copy(r).start())

    each_peer(dp_count, lambda r: o_copy(r).wait_recv())
    part = osend[dp].astype(jnp.float32)
    for r in range(1, dp_count):
        part = part + oland[r].astype(jnp.float32)
    ograd_ref[...] = part

    first, second = slots_ref[0:1, :], slots_ref[1:2, :]
    gate_first, gate_second = gates_ref[0:1, :], gates_ref[1:2, :]
    total[...] = middle_ref[...]

    def combine(r, carry):
        e = lax.rem(dp + r, dp_count)

        @pl.when(r > 0)
        def _():
            p_copy(r).wait_recv()
        total[...] += gated_rows(gate_map(first, second, gate_first, gate_second, e, cap_rows), landed[e])
        return carry
    lax.fori_loop(0, dp_count, combine, 0)
    out_ref[...] = total[...]

    up_across.wait_recv()
    up_grad[...] = up_own[...].astype(jnp.float32) + up_land[...].astype(jnp.float32)

    own_near.wait_recv()
    pair_far.wait_recv()
    norm_grad = npart[tp].astype(jnp.float32) + near_land[1].astype(jnp.float32) + far_land[...].astype(jnp.float32)
    x = x_ref[...].astype(jnp.float32)
    r = lax.rsqrt(jnp.mean(x * x, axis=-1, keepdims=True) + EPSILON)
    u = x * r
    du = norm_grad * gain_ref[...]
    input_grad_ref[...] = mgrad_ref[...] + r * (du - u * jnp.mean(du * u, axis=-1, keepdims=True))

    each_peer(dp_count, lambda r: w_copy(r).wait_recv())
    part = wsum[pl.ds(pl.multiple_of(dp * share, 8), share), :]
    for r in range(1, dp_count):
        part = part + wland[r].astype(jnp.float32)
    wgrad_ref[...] = part

    each_peer(dp_count, lambda r: late_copy(r).wait_recv())
    summed = late_mid[...]
    for r in range(1, dp_count):
        summed = summed + late_dp[r]
    late_out[...] = summed

    for c in early + late_first + out_near + [out_across, up_across, pair_near, pair_far, own_near, h_copy(0, opp), h_copy(1, across), h_copy(2, sib)]:
        c.wait_send()

    def drain(r):
        p_copy(r).wait_send()
        o_copy(r).wait_send()
        early_copy(r).wait_send()
        w_copy(r).wait_send()
        late_copy(r).wait_send()
    each_peer(dp_count, drain)


def last_pass(sizes, x, gain, middle, middle_grad, heads_grad, rows, w, qkv, lse, line, segk, segq, produced,
              slot_rows, gates, early, bucket_row, out_part, up_pair, up_own):
    dp_count, tensor_count, experts, capacity, cap_rows, heads, blocks, gather_w = sizes
    tokens, width = x.shape
    inner = heads * DH
    seq_len = blocks * QB
    share = width // dp_count
    vmem = pl.BlockSpec(memory_space=pltpu.VMEM)
    shape = jax.ShapeDtypeStruct
    low, full = jnp.bfloat16, jnp.float32
    late = 8 + NB
    packed = w.shape[2]
    spread = -(-inner // 128) * 128
    return pl.pallas_call(
        functools.partial(last_kernel, sizes),
        in_specs=[vmem] * 20,
        out_specs=[vmem] * 7,
        out_shape=[
            shape((tokens, width), full),
            shape((tokens, width), full),
            shape((share, packed), full),
            shape(early.shape, full),
            shape((late, 128), full),
            shape((share, spread), full),
            shape(up_own.shape, full),
        ],
        scratch_shapes=[
            pltpu.VMEM((heads, blocks, QB, QB), full),
            pltpu.VMEM((heads, blocks, QB, QB), full),
            pltpu.VMEM((seq_len, DH), full),
            pltpu.VMEM((seq_len, DH), full),
            pltpu.VMEM((seq_len, packed), low),
            pltpu.VMEM((tensor_count, inner, tokens), low),
            pltpu.VMEM((experts, cap_rows, width), low),
            pltpu.VMEM((tensor_count, tokens, width), low),
            pltpu.VMEM((2, tokens, width), low),
            pltpu.VMEM((tokens, width), low),
            pltpu.VMEM((tokens, width), low),
            pltpu.VMEM((width, packed), full),
            pltpu.VMEM((dp_count, share, packed), low),
            pltpu.VMEM((dp_count, share, packed), low),
            pltpu.VMEM((tensor_count - 1,) + early.shape, full),
            pltpu.VMEM(early.shape, full),
            pltpu.VMEM((dp_count,) + early.shape, full),
            pltpu.VMEM((late, 128), full),
            pltpu.VMEM((tensor_count - 1, late, 128), full),
            pltpu.VMEM((late, 128), full),
            pltpu.VMEM((dp_count, late, 128), full),
            pltpu.VMEM((tokens, width), full),
            pltpu.VMEM(up_own.shape, low),
            pltpu.VMEM((2, inner, width), low),
            pltpu.VMEM((inner, width), low),
            pltpu.VMEM((inner, width), low),
            pltpu.VMEM((dp_count, share, spread), low),
            pltpu.VMEM((dp_count, share, spread), low),
        ] + sems(3, dp_count, 3, dp_count, tensor_count, dp_count, tensor_count, dp_count, 4, dp_count),
        compiler_params=pltpu.CompilerParams(
            vmem_limit_bytes=VMEM_LIMIT, collective_id=3, has_side_effects=True),
        cost_estimate=pl.CostEstimate(flops=30_000_000_000, bytes_accessed=30 << 20, transcendentals=4_000_000),
        name="last_pass",
    )(x, gain, middle, middle_grad, heads_grad, rows, w, qkv, lse, line, segk, segq, produced, slot_rows, gates,
      early, bucket_row, out_part, up_pair, up_own)


def norm_rows(values, gain):
    return values * lax.rsqrt(jnp.mean(values * values, axis=-1, keepdims=True) + EPSILON) * gain


def norm_back(values, gain, grad):
    r = lax.rsqrt(jnp.mean(values * values, axis=-1, keepdims=True) + EPSILON)
    u = values * r
    du = grad * gain
    return r * (du - u * jnp.mean(du * u, axis=-1, keepdims=True)), grad * u


def plain_body(
    block_input,
    out_grad,
    w_qkv,
    w_out,
    rel_table,
    gain_attn,
    gain_moe,
    w_router,
    w_up,
    w_down,
    routes,
    segments,
    padding,
    rel_bucket,
):
    tensor_pos = lax.axis_index("tensor")
    rows_local, width = block_input.shape
    seq_len = segments.shape[1]
    expert_count = w_router.shape[1]
    capacity = (10 * rows_local + 4 * expert_count - 1) // (4 * expert_count)
    slots = expert_count * capacity
    x_float = block_input.astype(jnp.float32)
    grad_float = out_grad.astype(jnp.float32)

    attn_norm = norm_rows(x_float, gain_attn).astype(jnp.bfloat16)
    seq_rows = lax.all_gather(attn_norm, "tensor", axis=0, tiled=True)
    qkv_full = lax.all_gather(w_qkv, "dp", axis=1, tiled=True)
    out_rows = lax.all_gather(w_out, "dp", axis=1, tiled=True)
    out_full = lax.all_gather(out_rows, "tensor", axis=0, tiled=True)
    up_full = lax.all_gather(w_up[0], "tensor", axis=0, tiled=True)
    down_full = lax.all_gather(w_down[0], "tensor", axis=0, tiled=True)

    live_mask = lax.dynamic_slice_in_dim(padding.reshape(-1), tensor_pos * rows_local, rows_local)
    live_float = live_mask.astype(jnp.float32)
    expert_ids = jnp.arange(expert_count, dtype=jnp.int32)
    pick_first = routes[:, 0:1] == expert_ids[None, :]
    pick_second = routes[:, 1:2] == expert_ids[None, :]
    usable = live_mask[:, None] == 1
    first_hot = (pick_first & usable).astype(jnp.int32)
    second_hot = (pick_second & usable).astype(jnp.int32)
    first_place = jnp.sum((jnp.cumsum(first_hot, axis=0) - first_hot) * first_hot, axis=1)
    second_before = (
        jnp.cumsum(second_hot, axis=0) - second_hot + jnp.sum(first_hot, axis=0, keepdims=True)
    )
    second_place = jnp.sum(second_before * second_hot, axis=1)
    first_slot = jnp.where(
        (live_mask == 1) & (first_place < capacity), routes[:, 0] * capacity + first_place, -1
    )
    second_slot = jnp.where(
        (live_mask == 1) & (second_place < capacity), routes[:, 1] * capacity + second_place, -1
    )
    slot_ids = jnp.arange(slots, dtype=jnp.int32)
    select_first = slot_ids[:, None] == first_slot[None, :]
    select_second = slot_ids[:, None] == second_slot[None, :]
    select_both = (select_first | select_second).astype(jnp.bfloat16)
    select_first_low = select_first.astype(jnp.bfloat16)
    select_second_low = select_second.astype(jnp.bfloat16)

    def to_experts(rows):
        return lax.all_to_all(rows, "dp", split_axis=0, concat_axis=0, tiled=True)

    grad_rows = jnp.dot(select_both, out_grad, preferred_element_type=jnp.float32)
    sent_grads = to_experts(grad_rows.astype(jnp.bfloat16).reshape(expert_count, capacity, width))
    sent_grads = sent_grads.reshape(slots, width)

    heads = qkv_full.shape[2] // DH
    inner = heads * DH
    table_local = lax.dynamic_slice_in_dim(rel_table, tensor_pos * heads, heads, 1)
    bucket_hot = (rel_bucket[:, None] == jnp.arange(NB, dtype=jnp.int32)[None, :]).astype(jnp.float32)
    line = line_of(jnp.dot(bucket_hot, table_local, precision=HIGHEST).T)
    segk, segq = mask_inputs(segments, padding)
    qkv_low, heads_low, lse = attend(line, segk, segq, seq_rows, qkv_full)
    heads_own = lax.all_to_all(heads_low, "tensor", split_axis=0, concat_axis=1, tiled=True)

    middle = x_float + jnp.dot(heads_own, out_full, preferred_element_type=jnp.float32)
    moe_low = norm_rows(middle, gain_moe).astype(jnp.bfloat16)
    rows_out = jnp.dot(select_both, moe_low, preferred_element_type=jnp.float32)
    sent_rows = to_experts(rows_out.astype(jnp.bfloat16).reshape(expert_count, capacity, width))
    sent_rows = sent_rows.reshape(slots, width)
    logits = jnp.dot(moe_low, w_router, preferred_element_type=jnp.float32)
    first_logit = jnp.sum(jnp.where(pick_first, logits, 0.0), axis=1)
    second_logit = jnp.sum(jnp.where(pick_second, logits, 0.0), axis=1)
    first_gate = jax.nn.sigmoid(first_logit - second_logit) * live_float
    second_gate = jax.nn.sigmoid(second_logit - first_logit) * live_float
    slot_gate = jnp.sum(
        jnp.where(select_first, first_gate[None, :], 0.0)
        + jnp.where(select_second, second_gate[None, :], 0.0),
        axis=1,
    )
    sent_gates = to_experts(slot_gate.reshape(expert_count, capacity)).reshape(slots, 1)

    act, pre_grad, back, dots = expert_first(sent_rows, sent_grads, up_full, down_full)
    returned_grad = to_experts(back.reshape(expert_count, capacity, width)).reshape(slots, width)
    slot_dots = to_experts(dots[0].reshape(expert_count, capacity)).reshape(slots)
    produced, up_part, down_part = expert_late(
        sent_rows, sent_grads, sent_gates, act, pre_grad, down_full
    )
    returned = to_experts(produced.reshape(expert_count, capacity, width)).reshape(slots, width)
    w_up_grad = lax.psum_scatter(up_part, "tensor", scatter_dimension=0, tiled=True)
    w_down_grad = lax.psum_scatter(down_part, "tensor", scatter_dimension=0, tiled=True)

    first_dot = jnp.sum(jnp.where(select_first, slot_dots[:, None], 0.0), axis=0)
    second_dot = jnp.sum(jnp.where(select_second, slot_dots[:, None], 0.0), axis=0)
    coefficient = first_gate * second_gate * (first_dot - second_dot)
    logit_grad = (
        jnp.where(pick_first, coefficient[:, None], 0.0)
        - jnp.where(pick_second, coefficient[:, None], 0.0)
    ).astype(jnp.bfloat16)
    router_grad = jnp.einsum("nd,ne->de", moe_low, logit_grad, preferred_element_type=jnp.float32)

    def gated(rows):
        first_rows = jnp.einsum("st,sd->td", select_first_low, rows, preferred_element_type=jnp.float32)
        second_rows = jnp.einsum("st,sd->td", select_second_low, rows, preferred_element_type=jnp.float32)
        return first_gate[:, None] * first_rows + second_gate[:, None] * second_rows

    moe_norm_grad = (
        jnp.einsum("ne,de->nd", logit_grad, w_router, preferred_element_type=jnp.float32)
        + gated(returned_grad)
    )
    middle_back, gain_moe_rows = norm_back(middle, gain_moe, moe_norm_grad)
    middle_grad = grad_float + middle_back
    gain_moe_grad = jnp.sum(gain_moe_rows, axis=0)
    attn_grad = middle_grad.astype(jnp.bfloat16)
    heads_grad = jnp.einsum("nd,fd->nf", attn_grad, out_full, preferred_element_type=jnp.float32)
    heads_grad = lax.all_to_all(
        heads_grad.astype(jnp.bfloat16), "tensor", split_axis=1, concat_axis=0, tiled=True
    )
    out_part = jnp.einsum("nf,nd->fd", heads_own, attn_grad, preferred_element_type=jnp.float32)
    out_part = lax.psum_scatter(out_part.astype(jnp.bfloat16), "tensor", scatter_dimension=0, tiled=True)
    w_out_grad = lax.psum_scatter(out_part.astype(jnp.float32), "dp", scatter_dimension=1, tiled=True)
    gain_moe_grad, router_grad = lax.psum((gain_moe_grad, router_grad), ("dp", "tensor"))

    norm_part, qkv_part, folded = attend_back(
        line, segk, segq, seq_rows, qkv_full, qkv_low, heads_grad, lse
    )
    attn_norm_grad = lax.psum_scatter(norm_part, "tensor", scatter_dimension=0, tiled=True)
    input_back, gain_attn_rows = norm_back(x_float, gain_attn, attn_norm_grad.astype(jnp.float32))
    input_grad = middle_grad + input_back
    gain_attn_grad = jnp.sum(gain_attn_rows, axis=0)
    w_qkv_grad = lax.psum_scatter(qkv_part, "dp", scatter_dimension=1, tiled=True)
    line_grad = lines_of(folded, heads, seq_len // QB)
    table_part = jnp.dot(bucket_hot.T, line_grad.T, precision=HIGHEST)
    table_whole = lax.dynamic_update_slice(
        jnp.zeros(rel_table.shape, jnp.float32), table_part, (0, tensor_pos * heads)
    )
    gain_attn_grad, table_whole = lax.psum((gain_attn_grad, table_whole), ("dp", "tensor"))
    block_output = middle + gated(returned)
    return (
        block_output,
        input_grad,
        w_qkv_grad,
        w_out_grad,
        table_whole,
        gain_attn_grad,
        gain_moe_grad,
        router_grad,
        w_up_grad.astype(jnp.float32)[None],
        w_down_grad.astype(jnp.float32)[None],
    )


def fused_body(
    block_input,
    out_grad,
    w_qkv,
    w_out,
    rel_table,
    gain_attn,
    gain_moe,
    w_router,
    w_up,
    w_down,
    routes,
    segments,
    padding,
    rel_bucket,
):
    tensor_pos = lax.axis_index("tensor")
    dp_count, tensor_count = lax.axis_size("dp"), lax.axis_size("tensor")
    rows_local, width = block_input.shape
    seq_len = segments.shape[1]
    heads = w_qkv.shape[2] // DH
    capacity = slot_capacity(rows_local, w_router.shape[1])
    expert_count = w_router.shape[1]
    sizes = (dp_count, tensor_count, expert_count, capacity, capacity, heads, seq_len // QB, True)

    live_row = lax.dynamic_slice_in_dim(padding.reshape(-1), tensor_pos * rows_local, rows_local)[None]
    routes_t = routes.T
    table_local = lax.dynamic_slice_in_dim(rel_table, tensor_pos * heads, heads, 1)
    bucket_hot = (rel_bucket[:, None] == jnp.arange(NB, dtype=jnp.int32)[None, :]).astype(jnp.float32)
    line = line_of(jnp.dot(bucket_hot, table_local, precision=HIGHEST).T)
    segk, segq = mask_inputs(segments, padding)
    share, inner = w_qkv.shape[1:]
    w_packed = jnp.moveaxis(w_qkv, 0, 1).reshape(share, 3 * inner)
    w_packed = jnp.pad(w_packed, ((0, 0), (0, -3 * inner % 128)))
    w_out_turned = jnp.pad(w_out.T, ((0, 0), (0, -inner % 128)))
    rows, w_all, outw, down_all, qkv, lse, heads_all, slot_rows, cot = front(
        sizes, block_input, gain_attn[None], w_packed, w_out_turned, w_down[0], out_grad, routes_t, live_row, line, segk, segq
    )
    outw = outw.reshape(tensor_count, width, -1)
    up_pair, up_own, w_down_grad, produced, middle, middle_grad, heads_grad, out_part, early, gates = middle_pass(
        sizes, block_input, out_grad, heads_all, outw, gain_moe[None], w_router.T, routes_t, live_row,
        slot_rows, cot, w_up[0], down_all
    )

    block_output, input_grad, w_qkv_grad, early, late, w_out_grad, w_up_grad = last_pass(
        sizes, block_input, gain_attn[None], middle, middle_grad, heads_grad, rows, w_all, qkv, lse, line, segk, segq,
        produced, slot_rows, gates, early, rel_bucket[None], out_part, up_pair, up_own
    )
    return (
        block_output,
        input_grad,
        jnp.moveaxis(w_qkv_grad[:, : 3 * inner].reshape(share, 3, inner), 1, 0),
        w_out_grad[:, :inner].T,
        late[8:, : rel_table.shape[1]],
        late[: width // 128].reshape(width),
        early[0],
        early[8:].T,
        w_up_grad[None],
        w_down_grad[None],
    )


def slot_capacity(tokens, experts):
    return (10 * tokens + 4 * experts - 1) // (4 * experts)


def body(*args):
    block_input, w_qkv, w_router = args[0], args[2], args[7]
    capacity = slot_capacity(block_input.shape[0], w_router.shape[1])
    fits = capacity % 16 == 0 and w_qkv.shape[1] % 16 == 0 and block_input.shape[1] <= 1024
    return fused_body(*args) if fits else plain_body(*args)


def solution(mesh):
    in_specs = (
        P(("dp", "tensor"), None),
        P(("dp", "tensor"), None),
        P(None, "dp", "tensor"),
        P("tensor", "dp"),
        P(),
        P(),
        P(),
        P(),
        P("dp", "tensor", None),
        P("dp", "tensor", None),
        P(("dp", "tensor"), None),
        P("dp", None),
        P("dp", None),
        P(),
    )
    out_specs = (
        P(("dp", "tensor"), None),
        P(("dp", "tensor"), None),
        P(None, "dp", "tensor"),
        P("tensor", "dp"),
        P(),
        P(),
        P(),
        P(),
        P("dp", "tensor", None),
        P("dp", "tensor", None),
    )
    return jax.shard_map(body, mesh=mesh, in_specs=in_specs, out_specs=out_specs, check_vma=False)
```

```python
import functools
import math

import jax
import jax.numpy as jnp
from jax import lax
from jax.experimental import pallas as pl
from jax.experimental.pallas import tpu as pltpu
from jax.sharding import PartitionSpec as P

NB = 32
EPSILON = 1e-06
HIGHEST = lax.Precision.HIGHEST
DH = 64
NEGATIVE = -1e30
QB = 256
NT = (((1,), (1,)), ((), ()))
TN = (((0,), (0,)), ((), ()))
NN = (((1,), (0,)), ((), ()))


def mm(a, b, dims):
    return lax.dot_general(a, b, dims, preferred_element_type=jnp.float32)


def build_bias(line_ref, tiles, heads, blocks):
    for h in range(heads):
        for d in range(blocks):
            piece = line_ref[h : h + 1, d * QB : d * QB + 2 * QB]
            wide = jnp.broadcast_to(piece, (QB, 2 * QB))
            turned = pltpu.roll(wide, 0, 1, stride=1, stride_axis=0)
            tiles[h, d] = turned[:, QB:]


def score_block(keys, query, tiles, h, qb, segk_ref, segq_ref):
    raw = mm(keys, query, NT)
    q_seg = segq_ref[:, qb * QB : (qb + 1) * QB]
    parts = []
    for kb in range(qb + 1):
        k_seg = segk_ref[kb * QB : (kb + 1) * QB, :]
        same = k_seg == q_seg
        if kb == qb:
            row = lax.broadcasted_iota(jnp.int32, (QB, QB), 0)
            col = lax.broadcasted_iota(jnp.int32, (QB, QB), 1)
            same = same | (row == col)
        parts.append(
            jnp.where(same, raw[kb * QB : (kb + 1) * QB] + tiles[h, qb - kb], NEGATIVE)
        )
    return parts


def attend_kernel(heads, blocks, line_ref, segk_ref, segq_ref, rows_ref, w_ref,
                  qkv_ref, out_ref, lse_ref, tiles):
    @pl.when(pl.program_id(0) == 0)
    def _():
        build_bias(line_ref, tiles, heads, blocks)

    for c in range(3):
        qkv_ref[c] = mm(rows_ref[...], w_ref[c], NN).astype(jnp.bfloat16)
    scale = 1.0 / math.sqrt(DH)
    for qb in range(blocks):
        nk = (qb + 1) * QB
        lower = qb * QB
        turned = []
        for h in range(heads):
            cols = slice(h * DH, (h + 1) * DH)
            query = (qkv_ref[0, lower : lower + QB, cols].astype(jnp.float32) * scale).astype(jnp.bfloat16)
            parts = score_block(qkv_ref[1, 0:nk, cols], query, tiles, h, qb, segk_ref.at[0], segq_ref.at[0])
            peak = functools.reduce(jnp.maximum, [jnp.max(x, axis=0, keepdims=True) for x in parts])
            probs = [jnp.exp(x - peak) for x in parts]
            total = functools.reduce(jnp.add, [jnp.sum(x, axis=0, keepdims=True) for x in probs])
            mixed = functools.reduce(jnp.add, [
                mm(qkv_ref[2, kb * QB : (kb + 1) * QB, cols], x.astype(jnp.bfloat16), TN)
                for kb, x in enumerate(probs)])
            turned.append(mixed / total)
            lse_ref[0, h : h + 1, lower : lower + QB] = peak + jnp.log(total)
        out_ref[lower : lower + QB, :] = jnp.concatenate(turned, axis=0).T.astype(jnp.bfloat16)


def attend(line, segk, segq, rows, w):
    seqs, _, seq_len = segq.shape
    heads = line.shape[0]
    inner = heads * DH
    blocks = seq_len // QB
    width = rows.shape[1]
    return pl.pallas_call(
        functools.partial(attend_kernel, heads, blocks),
        grid=(seqs,),
        in_specs=[
            pl.BlockSpec(line.shape, lambda s: (0, 0)),
            pl.BlockSpec((1, seq_len, 1), lambda s: (s, 0, 0)),
            pl.BlockSpec((1, 1, seq_len), lambda s: (s, 0, 0)),
            pl.BlockSpec((seq_len, width), lambda s: (s, 0)),
            pl.BlockSpec(w.shape, lambda s: (0, 0, 0)),
        ],
        out_specs=[
            pl.BlockSpec((3, seq_len, inner), lambda s: (0, s, 0)),
            pl.BlockSpec((seq_len, inner), lambda s: (s, 0)),
            pl.BlockSpec((1, heads, seq_len), lambda s: (s, 0, 0)),
        ],
        out_shape=[
            jax.ShapeDtypeStruct((3, seqs * seq_len, inner), jnp.bfloat16),
            jax.ShapeDtypeStruct((seqs * seq_len, inner), jnp.bfloat16),
            jax.ShapeDtypeStruct((seqs, heads, seq_len), jnp.float32),
        ],
        scratch_shapes=[pltpu.VMEM((heads, blocks, QB, QB), jnp.float32)],
        compiler_params=pltpu.CompilerParams(vmem_limit_bytes=48 << 20),
        cost_estimate=pl.CostEstimate(flops=10_000_000_000, bytes_accessed=10 << 20, transcendentals=4_000_000),
        name="attend",
    )(line, segk, segq, rows, w)


def attend_back_kernel(heads, blocks, seqs, line_ref, segk_ref, segq_ref, rows_ref, w_ref,
                       qkv_ref, og_ref, lse_ref,
                       norm_ref, wg_ref, lg_ref, tiles, sums, kg, vg, dq):
    step = pl.program_id(0)

    @pl.when(step == 0)
    def _():
        build_bias(line_ref, tiles, heads, blocks)
        sums[...] = jnp.zeros_like(sums)
        wg_ref[...] = jnp.zeros_like(wg_ref)

    scale = 1.0 / math.sqrt(DH)
    for h in range(heads):
        cols = slice(h * DH, (h + 1) * DH)
        kg[...] = jnp.zeros_like(kg)
        vg[...] = jnp.zeros_like(vg)
        for qb in range(blocks):
            nk = (qb + 1) * QB
            lower = qb * QB
            query = (qkv_ref[0, lower : lower + QB, cols].astype(jnp.float32) * scale).astype(jnp.bfloat16)
            grad = og_ref[lower : lower + QB, cols]
            lse = lse_ref[0, h : h + 1, lower : lower + QB]
            parts = score_block(qkv_ref[1, 0:nk, cols], query, tiles, h, qb, segk_ref.at[0], segq_ref.at[0])
            probs = [jnp.exp(x - lse) for x in parts]
            pg = mm(qkv_ref[2, 0:nk, cols], grad, NT)
            pgs = [pg[kb * QB : (kb + 1) * QB] for kb in range(qb + 1)]
            delta = functools.reduce(jnp.add, [jnp.sum(p * g, axis=0, keepdims=True) for p, g in zip(probs, pgs)])
            dqt = jnp.zeros((DH, QB), jnp.float32)
            for kb in range(qb + 1):
                rows = slice(kb * QB, (kb + 1) * QB)
                sg = (probs[kb] * (pgs[kb] - delta)).astype(jnp.bfloat16)
                sums[h, qb - kb] += sg.astype(jnp.float32)
                vg[rows] += mm(probs[kb].astype(jnp.bfloat16), grad, NN)
                kg[rows] += mm(sg, query, NN)
                dqt = dqt + mm(qkv_ref[1, rows, cols], sg, TN)
            dq[lower : lower + QB, h * DH : (h + 1) * DH] = (dqt * scale).T.astype(jnp.bfloat16)
        inner = heads * DH
        dq[:, inner + h * DH : inner + (h + 1) * DH] = kg[...].astype(jnp.bfloat16)
        dq[:, 2 * inner + h * DH : 2 * inner + (h + 1) * DH] = vg[...].astype(jnp.bfloat16)
    inner = heads * DH
    total = jnp.zeros(norm_ref.shape, jnp.float32)
    for c in range(3):
        piece = dq[:, c * inner : (c + 1) * inner]
        wg_ref[c] += mm(rows_ref[...], piece, TN)
        total = total + mm(piece, w_ref[c], NT)
    norm_ref[...] = total.astype(norm_ref.dtype)

    @pl.when(step == seqs - 1)
    def _():
        for h in range(heads):
            for d in range(blocks):
                lg_ref[h * blocks + d] = fold_tile(sums, h, d)


def fold_tile(sums, h, d):
    blank = jnp.zeros((8, QB), jnp.float32)
    total = jnp.zeros((8, 2 * QB), jnp.float32)
    for g in range(QB // 8):
        piece = jnp.concatenate([sums[h, d, 8 * g : 8 * g + 8, :], blank], axis=1)
        total = total + (piece if g == 0 else pltpu.roll(piece, 2 * QB - 8 * g, 1))
    return total


def lines_of(folded, heads, blocks):
    moved = sum(jnp.roll(folded[:, s, :], -s, axis=1) for s in range(8))
    moved = moved.reshape(heads, blocks, 2, QB)
    ahead = jnp.concatenate([moved[:, 1:, 1], jnp.zeros((heads, 1, QB), jnp.float32)], axis=1)
    return (moved[:, :, 0] + ahead).reshape(heads, blocks * QB)


def attend_back(line, segk, segq, rows, w, qkv, og, lse):
    seqs, _, seq_len = segq.shape
    heads = line.shape[0]
    inner = heads * DH
    blocks = seq_len // QB
    width = rows.shape[1]
    return pl.pallas_call(
        functools.partial(attend_back_kernel, heads, blocks, seqs),
        grid=(seqs,),
        in_specs=[
            pl.BlockSpec(line.shape, lambda s: (0, 0)),
            pl.BlockSpec((1, seq_len, 1), lambda s: (s, 0, 0)),
            pl.BlockSpec((1, 1, seq_len), lambda s: (s, 0, 0)),
            pl.BlockSpec((seq_len, width), lambda s: (s, 0)),
            pl.BlockSpec(w.shape, lambda s: (0, 0, 0)),
            pl.BlockSpec((3, seq_len, inner), lambda s: (0, s, 0)),
            pl.BlockSpec((seq_len, inner), lambda s: (s, 0)),
            pl.BlockSpec((1, heads, seq_len), lambda s: (s, 0, 0)),
        ],
        out_specs=[
            pl.BlockSpec((seq_len, width), lambda s: (s, 0)),
            pl.BlockSpec(w.shape, lambda s: (0, 0, 0)),
            pl.BlockSpec((heads * blocks, 8, 2 * QB), lambda s: (0, 0, 0)),
        ],
        out_shape=[
            jax.ShapeDtypeStruct((seqs * seq_len, width), jnp.bfloat16),
            jax.ShapeDtypeStruct(w.shape, jnp.float32),
            jax.ShapeDtypeStruct((heads * blocks, 8, 2 * QB), jnp.float32),
        ],
        scratch_shapes=[
            pltpu.VMEM((heads, blocks, QB, QB), jnp.float32),
            pltpu.VMEM((heads, blocks, QB, QB), jnp.float32),
            pltpu.VMEM((seq_len, DH), jnp.float32),
            pltpu.VMEM((seq_len, DH), jnp.float32),
            pltpu.VMEM((seq_len, 3 * inner), jnp.bfloat16),
        ],
        compiler_params=pltpu.CompilerParams(vmem_limit_bytes=48 << 20),
        cost_estimate=pl.CostEstimate(flops=20_000_000_000, bytes_accessed=16 << 20, transcendentals=4_000_000),
        name="attend_back",
    )(line, segk, segq, rows, w, qkv, og, lse)


def mask_inputs(segments, padding):
    keyed = jnp.where(padding == 1, segments, -1)
    return keyed[:, :, None], segments[:, None, :]


def line_of(by_distance):
    return jnp.concatenate([jnp.full((by_distance.shape[0], QB), NEGATIVE, jnp.float32), by_distance], axis=1)


FT = 512
ROOT_2_PI = math.sqrt(2.0 / math.pi)


def gelu_pair(x):
    square = x * x
    t = jnp.tanh(ROOT_2_PI * x * (1.0 + 0.044715 * square))
    half = 0.5 * (1.0 + t)
    slope = half + 0.5 * x * (1.0 - t * t) * (ROOT_2_PI * (1.0 + 3 * 0.044715 * square))
    return x * half, slope


def expert_kernel(steps, x_ref, g_ref, up_ref, down_ref, act_ref, pre_ref, back_ref, dot_ref, total, dots):
    step = pl.program_id(0)

    @pl.when(step == 0)
    def _():
        total[...] = jnp.zeros_like(total)
        dots[...] = jnp.zeros_like(dots)

    rows = x_ref.shape[0]
    chunk = 256
    for lower in range(0, rows, chunk):
        part = slice(lower, lower + chunk)
        pre = mm(x_ref[part], up_ref[...], NT)
        out_side = mm(g_ref[part], down_ref[...], NT)
        act, slope = gelu_pair(pre)
        low = act.astype(jnp.bfloat16)
        act_ref[part] = low
        product = low.astype(jnp.float32) * out_side
        dots[part] += sum(product[:, k : k + 128] for k in range(0, FT, 128))
        back = (out_side * slope).astype(jnp.bfloat16)
        pre_ref[part] = back
        total[part] += mm(back, up_ref[...], NN)

    @pl.when(step == steps - 1)
    def _():
        back_ref[...] = total[...].astype(jnp.bfloat16)
        dot_ref[...] = lax.dot_general(
            jnp.ones((8, 128), jnp.float32), dots[...], NT,
            precision=HIGHEST, preferred_element_type=jnp.float32)


def expert_first(x, g, up, down):
    rows, width = x.shape
    hidden = up.shape[0]
    steps = hidden // FT
    whole = lambda f: (0, 0)
    return pl.pallas_call(
        functools.partial(expert_kernel, steps),
        grid=(steps,),
        in_specs=[
            pl.BlockSpec((rows, width), whole),
            pl.BlockSpec((rows, width), whole),
            pl.BlockSpec((FT, width), lambda f: (f, 0)),
            pl.BlockSpec((FT, width), lambda f: (f, 0)),
        ],
        out_specs=[
            pl.BlockSpec((rows, FT), lambda f: (0, f)),
            pl.BlockSpec((rows, FT), lambda f: (0, f)),
            pl.BlockSpec((rows, width), whole),
            pl.BlockSpec((8, rows), whole),
        ],
        out_shape=[
            jax.ShapeDtypeStruct((rows, hidden), jnp.bfloat16),
            jax.ShapeDtypeStruct((rows, hidden), jnp.bfloat16),
            jax.ShapeDtypeStruct((rows, width), jnp.bfloat16),
            jax.ShapeDtypeStruct((8, rows), jnp.float32),
        ],
        scratch_shapes=[
            pltpu.VMEM((rows, width), jnp.float32),
            pltpu.VMEM((rows, 128), jnp.float32),
        ],
        compiler_params=pltpu.CompilerParams(vmem_limit_bytes=48 << 20),
        cost_estimate=pl.CostEstimate(
            flops=6 * rows * width * hidden, bytes_accessed=32 << 20, transcendentals=rows * hidden),
        name="expert_first",
    )(x, g, up, down)


def expert_late_kernel(steps, x_ref, g_ref, gate_ref, act_ref, pre_ref, down_ref,
                       out_ref, up_grad_ref, down_grad_ref, total, x_gated, g_gated):
    step = pl.program_id(0)

    @pl.when(step == 0)
    def _():
        total[...] = jnp.zeros_like(total)
        gate = gate_ref[...]
        x_gated[...] = (x_ref[...].astype(jnp.float32) * gate).astype(jnp.bfloat16)
        g_gated[...] = (g_ref[...].astype(jnp.float32) * gate).astype(jnp.bfloat16)

    up_grad_ref[...] = mm(pre_ref[...], x_gated[...], TN).astype(up_grad_ref.dtype)
    down_grad_ref[...] = mm(act_ref[...], g_gated[...], TN).astype(down_grad_ref.dtype)
    total[...] += mm(act_ref[...], down_ref[...], NN)

    @pl.when(step == steps - 1)
    def _():
        out_ref[...] = total[...].astype(jnp.bfloat16)


def expert_late(x, g, gate, act, pre, down):
    rows, width = x.shape
    hidden = down.shape[0]
    steps = hidden // FT
    whole = lambda f: (0, 0)
    tile = pl.BlockSpec((FT, width), lambda f: (f, 0))
    return pl.pallas_call(
        functools.partial(expert_late_kernel, steps),
        grid=(steps,),
        in_specs=[
            pl.BlockSpec((rows, width), whole),
            pl.BlockSpec((rows, width), whole),
            pl.BlockSpec((rows, 1), whole),
            pl.BlockSpec((rows, FT), lambda f: (0, f)),
            pl.BlockSpec((rows, FT), lambda f: (0, f)),
            tile,
        ],
        out_specs=[pl.BlockSpec((rows, width), whole), tile, tile],
        out_shape=[
            jax.ShapeDtypeStruct((rows, width), jnp.bfloat16),
            jax.ShapeDtypeStruct((hidden, width), jnp.bfloat16),
            jax.ShapeDtypeStruct((hidden, width), jnp.bfloat16),
        ],
        scratch_shapes=[
            pltpu.VMEM((rows, width), jnp.float32),
            pltpu.VMEM((rows, width), jnp.bfloat16),
            pltpu.VMEM((rows, width), jnp.bfloat16),
        ],
        compiler_params=pltpu.CompilerParams(vmem_limit_bytes=48 << 20),
        cost_estimate=pl.CostEstimate(
            flops=6 * rows * width * hidden, bytes_accessed=32 << 20, transcendentals=0),
        name="expert_late",
    )(x, g, gate, act, pre, down)


MESH = pl.DeviceIdType.MESH
VMEM_LIMIT = 61 << 20


def remote(src, dst, send, recv, axis, place):
    return pltpu.make_async_remote_copy(
        src_ref=src, dst_ref=dst, send_sem=send, recv_sem=recv, device_id={axis: place}, device_id_type=MESH
    )


def each_peer(count, step, start=1):
    if count <= 8:
        for r in range(start, count):
            step(r)
    else:
        def one(r, carry):
            step(r)
            return carry
        lax.fori_loop(start, count, one, 0)


def peer(r):
    return jnp.bitwise_xor(lax.axis_index("dp"), r)


def greet(dp_count, tensor_count):
    barrier = pltpu.get_barrier_semaphore()
    dp, tp = lax.axis_index("dp"), lax.axis_index("tensor")
    for r in range(1, tensor_count):
        pl.semaphore_signal(barrier, inc=1, device_id={"tensor": lax.rem(tp + r, tensor_count)}, device_id_type=MESH)

    def signal(r):
        pl.semaphore_signal(barrier, inc=1, device_id={"dp": peer(r)}, device_id_type=MESH)
    each_peer(dp_count, signal)
    return lambda: pl.semaphore_wait(barrier, tensor_count - 1 + dp_count - 1)


def partners(tensor_count):
    tp = lax.axis_index("tensor")
    sib = tp + 1 - 2 * lax.rem(tp, 2)
    return tp, sib, lax.rem(tp + 2, tensor_count), lax.rem(sib + 2, tensor_count)


def place_pairs(routes_ref, live, experts, capacity, cap_rows):
    tokens = live.shape[1]
    live = live == 1
    ids = lax.broadcasted_iota(jnp.int32, (experts, tokens), 0)
    row = lax.broadcasted_iota(jnp.int32, (tokens, tokens), 0)
    col = lax.broadcasted_iota(jnp.int32, (tokens, tokens), 1)
    before = (row < col).astype(jnp.float32).astype(jnp.bfloat16)
    slots = []
    base = jnp.zeros((experts, 1), jnp.float32)
    for k in range(2):
        route = routes_ref[k : k + 1, :]
        hot = jnp.where((ids == route) & live, 1.0, 0.0)
        count = mm(hot.astype(jnp.bfloat16), before, NN) + base
        place = jnp.sum(count * hot, axis=0, keepdims=True).astype(jnp.int32)
        slots.append(jnp.where(live & (place < capacity), route * cap_rows + place, -1))
        base = base + jnp.sum(hot, axis=1, keepdims=True)
    return slots


def chosen(first, second, expert, cap_rows):
    ids = lax.broadcasted_iota(jnp.int32, (cap_rows, first.shape[1]), 0) + expert * cap_rows
    return jnp.where((ids == first) | (ids == second), 1.0, 0.0).astype(jnp.bfloat16)


def attend_sequence(heads, blocks, seq, line_tiles, segk_ref, segq_ref, qkv, heads_out, lse_ref):
    scale = 1.0 / math.sqrt(DH)
    inner = heads * DH
    half = blocks // 2
    for qb in range(blocks):
        nk = (qb + 1) * QB
        lower = qb * QB
        for h in range(heads):
            cols = [slice(c * inner + h * DH, c * inner + (h + 1) * DH) for c in range(3)]
            query = (qkv[seq, lower : lower + QB, cols[0]].astype(jnp.float32) * scale).astype(jnp.bfloat16)
            parts = score_block(qkv[seq, 0:nk, cols[1]], query, line_tiles, h, qb, segk_ref.at[seq], segq_ref.at[pl.ds(seq, 1)])
            peak = functools.reduce(jnp.maximum, [jnp.max(x, axis=0, keepdims=True) for x in parts])
            probs = [jnp.exp(x - peak) for x in parts]
            total = functools.reduce(jnp.add, [jnp.sum(x, axis=0, keepdims=True) for x in probs])
            mixed = functools.reduce(jnp.add, [
                mm(qkv[seq, kb * QB : (kb + 1) * QB, cols[2]], x.astype(jnp.bfloat16), TN)
                for kb, x in enumerate(probs)])
            heads_out[seq * 2 + qb // half, h * DH : (h + 1) * DH, (qb % half) * QB : (qb % half + 1) * QB] = (
                mixed / total).astype(jnp.bfloat16)
            lse_ref[seq, h : h + 1, lower : lower + QB] = peak + jnp.log(total)


def packed_gather(own_ref, all_ref, send, recv, dp_count):
    dp = lax.axis_index("dp")
    side = peer(1)
    columns = dp_count // 2
    near = remote(own_ref, all_ref.at[dp], send.at[0], recv.at[0], "dp", side)
    out = [remote(own_ref, all_ref.at[dp], send.at[k], recv.at[k], "dp", peer(2 * k))
           for k in range(1, columns)]
    onward = []
    for k in range(1, columns):
        src = peer(2 * k)
        n = columns - 1 + k
        onward.append(remote(all_ref.at[src], all_ref.at[src], send.at[n], recv.at[n], "dp", side))
    return near, out, onward


def prepare(heads, tp, table_ref, bucket_ref, segments_ref, padding_ref, line_ref, segk_ref):
    buckets, length = table_ref.shape[0], bucket_ref.shape[1]
    ids = lax.broadcasted_iota(jnp.int32, (buckets, length), 0)
    hot = ids == bucket_ref[...]
    lane = lax.broadcasted_iota(jnp.int32, table_ref.shape, 1)
    for h in range(heads):
        column = jnp.sum(jnp.where(lane == tp * heads + h, table_ref[...], 0.0), axis=1, keepdims=True)
        line_ref[h : h + 1, :QB] = jnp.full((1, QB), NEGATIVE, jnp.float32)
        line_ref[h : h + 1, QB:] = jnp.sum(jnp.where(hot, column, 0.0), axis=0, keepdims=True)
    keyed = jnp.where(padding_ref[...] == 1, segments_ref[...], -1).astype(jnp.float32)
    for s in range(keyed.shape[0]):
        for k in range(length // QB):
            piece = keyed[s : s + 1, k * QB : (k + 1) * QB]
            segk_ref[s, k * QB : (k + 1) * QB, :] = to_column(piece, QB).astype(jnp.int32)


def front_kernel(sizes, x_ref, gain_ref, w_ref, outw_ref, down_ref, grad_ref, routes_ref, segments_ref, padding_ref,
                 table_ref, bucket_ref,
                 rows, w_all, outw_all, down_all, qkv, lse_ref, heads_all, slots_ref, cot, line_ref, segk_ref,
                 tiles, heads_out, cot_send, w_own,
                 far_send, far_recv, w_send, w_recv, ot_send, ot_recv,
                 dn_send, dn_recv, cot_s, cot_r, head_send, head_recv, local_sem):
    dp_count, tensor_count, experts, capacity, cap_rows, heads, blocks, gather_w = sizes
    dp = lax.axis_index("dp")
    tp, sib, opp, across = partners(tensor_count)
    wait_barrier = greet(dp_count, tensor_count)
    inner = heads * DH
    for c in range(3):
        w_own[:, c * inner : (c + 1) * inner] = w_ref[c]
    w_own[:, 3 * inner :] = outw_ref[...].T

    x = x_ref[...].astype(jnp.float32)
    r = lax.rsqrt(jnp.mean(x * x, axis=-1, keepdims=True) + EPSILON)
    rows[tp] = (x * r * gain_ref[...]).astype(jnp.bfloat16)
    wait_barrier()

    half = rows.shape[1] // 2
    parts = [pl.ds(0, half), pl.ds(half, half)]
    far = [remote(rows.at[tp, p], rows.at[tp, p], far_send.at[k], far_recv.at[k], "tensor", opp) for k, p in enumerate(parts)]
    near = remote(rows.at[tp], rows.at[tp], far_send.at[2], far_recv.at[2], "tensor", sib)
    onward = [remote(rows.at[opp, p], rows.at[opp, p], far_send.at[3 + k], far_recv.at[3 + k], "tensor", sib) for k, p in enumerate(parts)]
    for c in far:
        c.start()
    near.start()

    w_near, w_out, w_on = packed_gather(w_own, w_all, w_send, w_recv, dp_count)
    for c in w_out:
        c.start()
    w_near.start()
    w_all[dp] = w_own[...]

    tokens = x_ref.shape[0]
    live = padding_ref[pl.ds(tp // 2, 1), pl.ds(pl.multiple_of(lax.rem(tp, 2) * tokens, 128), tokens)]
    first, second = place_pairs(routes_ref, live, experts, capacity, cap_rows)
    slots_ref[0:1, :] = first
    slots_ref[1:2, :] = second

    def cot_copy(r):
        to = peer(r)
        return remote(cot_send.at[to], cot.at[dp], cot_s.at[r], cot_r.at[r], "dp", to)

    def cot_fill(r):
        to = peer(r)
        cot_send[to] = mm(chosen(first, second, to, cap_rows), grad_ref[...], NN).astype(jnp.bfloat16)

    each_peer(dp_count, cot_fill)
    cot_fill(0)
    own_cot = pltpu.make_async_copy(cot_send.at[dp], cot.at[dp], local_sem.at[1])
    own_cot.start()

    each_peer(dp_count, lambda r: cot_copy(r).start())
    prepare(heads, tp, table_ref, bucket_ref, segments_ref, padding_ref, line_ref, segk_ref)
    build_bias(line_ref, tiles, heads, blocks)
    for c, on in zip(w_out, w_on):
        c.wait_recv()
        on.start()
    w_near.wait_recv()
    for c in w_on:
        c.wait_recv()
    near.wait_recv()

    width = rows.shape[2]
    own_seq = tp // 2
    packed = qkv.shape[2]

    def project(seq):
        tokens = rows[pl.ds(seq * 2, 2)].reshape(2 * rows.shape[1], width)
        weight = w_all[...].reshape(width, w_all.shape[2])[:, :packed]
        qkv[seq] = mm(tokens, weight, NN).astype(jnp.bfloat16)

    def head_copy(k, to):
        return remote(heads_out.at[to], heads_all.at[tp], head_send.at[k], head_recv.at[k], "tensor", to)

    part = pl.ds(0, down_ref.shape[0] // 2)
    down_far = remote(down_ref.at[part], down_all.at[tp, part], dn_send.at[0], dn_recv.at[0], "tensor", opp)
    down_near = remote(down_ref, down_all.at[tp], dn_send.at[1], dn_recv.at[1], "tensor", sib)
    down_on = remote(down_all.at[opp, part], down_all.at[opp, part], dn_send.at[2], dn_recv.at[2], "tensor", sib)

    project(own_seq)
    outw_all[tp] = w_all[...].reshape(width, w_all.shape[2])[:, 3 * inner :].T
    ot_far = remote(outw_all.at[tp], outw_all.at[tp], ot_send.at[0], ot_recv.at[0], "tensor", opp)
    ot_near = remote(outw_all.at[tp], outw_all.at[tp], ot_send.at[1], ot_recv.at[1], "tensor", sib)
    ot_on = remote(outw_all.at[opp], outw_all.at[opp], ot_send.at[2], ot_recv.at[2], "tensor", sib)
    for k in range(2):
        far[k].wait_recv()
        onward[k].start()
    ot_far.start()
    ot_near.start()
    down_far.start()
    down_near.start()
    attend_sequence(heads, blocks, own_seq, tiles, segk_ref, segments_ref, qkv, heads_out, lse_ref)
    head_copy(0, sib).start()
    heads_all[tp] = heads_out[tp]
    for k in range(2):
        onward[k].wait_recv()
    other = 1 - own_seq
    project(other)
    attend_sequence(heads, blocks, other, tiles, segk_ref, segments_ref, qkv, heads_out, lse_ref)
    ot_far.wait_recv()
    ot_on.start()
    head_copy(1, opp).start()
    head_copy(2, across).start()

    down_far.wait_recv()
    down_on.start()
    own_cot.wait()
    each_peer(dp_count, lambda r: cot_copy(r).wait())
    ot_on.wait()
    ot_near.wait()
    ot_far.wait_send()
    for c in [w_near] + w_out + w_on:
        c.wait_send()
    for c in far + [near] + onward:
        c.wait_send()
    head_copy(0, sib).wait()
    head_copy(1, opp).wait()
    head_copy(2, across).wait()
    down_far.wait_send()
    down_near.wait()
    down_on.wait()


def sems(*counts):
    out = []
    for n in counts:
        out += [pltpu.SemaphoreType.DMA((n,)), pltpu.SemaphoreType.DMA((n,))]
    return out


def front(sizes, x, gain, w, outw, down, grad, routes_t, segments, padding, table, bucket):
    dp_count, tensor_count, experts, capacity, cap_rows, heads, blocks, gather_w = sizes
    tokens, width = x.shape
    seq_len = blocks * QB
    seqs = tensor_count * tokens // seq_len
    inner = heads * DH
    packed = -(-3 * inner // 128) * 128
    vmem = pl.BlockSpec(memory_space=pltpu.VMEM)
    anywhere = pl.BlockSpec(memory_space=pl.ANY)
    shape = jax.ShapeDtypeStruct
    low = jnp.bfloat16
    return pl.pallas_call(
        functools.partial(front_kernel, sizes),
        in_specs=[vmem] * 4 + [anywhere] + [vmem] * 6,
        out_specs=[vmem] * 3 + [anywhere] + [vmem] * 4 + [anywhere] + [vmem] * 2,
        out_shape=[
            shape((tensor_count, tokens, width), low),
            shape((dp_count, w.shape[1], 4 * inner), low),
            shape((tensor_count, inner, width), low),
            shape((tensor_count,) + down.shape, low),
            shape((seqs, seq_len, packed), low),
            shape((seqs, heads, seq_len), jnp.float32),
            shape((tensor_count, inner, tokens), low),
            shape((8, tokens), jnp.int32),
            shape((experts, cap_rows, width), low),
            shape((heads, QB + seq_len), jnp.float32),
            shape((seqs, seq_len, 1), jnp.int32),
        ],
        scratch_shapes=[
            pltpu.VMEM((heads, blocks, QB, QB), jnp.float32),
            pltpu.VMEM((tensor_count, inner, tokens), low),
            pltpu.VMEM((experts, cap_rows, width), low),
            pltpu.VMEM((w.shape[1], 4 * inner), low),
        ] + sems(5, dp_count, 3, 3, dp_count, 3) + [pltpu.SemaphoreType.DMA((3,))],
        compiler_params=pltpu.CompilerParams(
            vmem_limit_bytes=VMEM_LIMIT, collective_id=1, has_side_effects=True),
        cost_estimate=pl.CostEstimate(flops=20_000_000_000, bytes_accessed=20 << 20, transcendentals=4_000_000),
        name="front",
    )(x, gain, w, outw, down, grad, routes_t, segments, padding, table, bucket)


def to_row(column, lanes):
    n = column.shape[0]
    row = lax.broadcasted_iota(jnp.int32, (n, lanes), 0)
    col = lax.broadcasted_iota(jnp.int32, (n, lanes), 1)
    return jnp.sum(jnp.where(row == col, column, 0.0), axis=0, keepdims=True)


def to_column(row_values, n):
    lanes = row_values.shape[1]
    row = lax.broadcasted_iota(jnp.int32, (n, lanes), 0)
    col = lax.broadcasted_iota(jnp.int32, (n, lanes), 1)
    return jnp.sum(jnp.where(row == col, row_values, 0.0), axis=1, keepdims=True)


def gate_map(first, second, gate_first, gate_second, expert, cap_rows):
    ids = lax.broadcasted_iota(jnp.int32, (cap_rows, first.shape[1]), 0) + expert * cap_rows
    return jnp.where(ids == first, gate_first, jnp.where(ids == second, gate_second, 0.0))


def gated_rows(weights, rows):
    high = weights.astype(jnp.bfloat16)
    low = (weights - high.astype(jnp.float32)).astype(jnp.bfloat16)
    return mm(high, rows, TN) + mm(low, rows, TN)


def middle_kernel(sizes, x_ref, grad_ref, heads_ref, outw_ref, gain_ref, router_ref, routes_ref, padding_ref,
                  slots_ref, cot_ref, up_ref, down_own_ref, down_ref,
                  up_pair, up_own, down_own, down_land, produced, middle, middle_grad, heads_grad, out_part, stats, gates,
                  up, down, g_rows, x_rows, act, side, back_send, back, gate_send, gate_rows,
                  dot_send, dot_rows, moe_low, stage, down_pair,
                  up_s, up_r, x_s, x_r, b_s, b_r, g_s, g_r, d_s, d_r, a_s, a_r, load_sem):
    dp_count, tensor_count, experts, capacity, cap_rows, heads, blocks, gather_w = sizes
    dp = lax.axis_index("dp")
    tp, sib, opp, across = partners(tensor_count)
    hidden = up.shape[1]
    x_send = produced
    total = middle_grad
    tokens, width = x_ref.shape
    lanes = gate_send.shape[2]
    wait_barrier = greet(dp_count, tensor_count)

    load_g = pltpu.make_async_copy(cot_ref, g_rows, load_sem.at[0])
    early, late = pl.ds(0, hidden // 2), pl.ds(hidden // 2, hidden // 2)
    load_down = [
        pltpu.make_async_copy(down_own_ref, down.at[tp], load_sem.at[1]),
        pltpu.make_async_copy(down_ref.at[sib], down.at[sib], load_sem.at[5]),
        pltpu.make_async_copy(down_ref.at[opp, early], down.at[opp, early], load_sem.at[6]),
        pltpu.make_async_copy(down_ref.at[across, early], down.at[across, early], load_sem.at[7]),
    ]
    load_up = pltpu.make_async_copy(up_ref, up.at[tp], load_sem.at[2])
    load_g.start()
    for c in load_down:
        c.start()
    load_up.start()

    mixed = x_ref[...].astype(jnp.float32)
    for t in range(tensor_count):
        mixed = mixed + mm(heads_ref[t], outw_ref[t], TN)
    middle[...] = mixed
    r = lax.rsqrt(jnp.mean(mixed * mixed, axis=-1, keepdims=True) + EPSILON)
    moe_low[...] = (mixed * r * gain_ref[...]).astype(jnp.bfloat16)
    first, second = slots_ref[0:1, :], slots_ref[1:2, :]
    wait_barrier()

    rest_far = remote(down_own_ref.at[late], down.at[tp, late], up_s.at[3], up_r.at[3], "tensor", opp)
    rest_on = remote(down.at[opp, late], down.at[opp, late], up_s.at[4], up_r.at[4], "tensor", sib)
    up_far = remote(up_ref, up.at[tp], up_s.at[0], up_r.at[0], "tensor", opp)
    up_near = remote(up_ref, up.at[tp], up_s.at[1], up_r.at[1], "tensor", sib)
    up_on = remote(up.at[opp], up.at[opp], up_s.at[2], up_r.at[2], "tensor", sib)
    rest_far.start()
    up_far.start()
    up_near.start()

    def x_copy(r):
        to = peer(r)
        return remote(x_send.at[to], x_rows.at[dp], x_s.at[r], x_r.at[r], "dp", to)

    def x_go(r):
        to = peer(r)
        x_send[to] = mm(chosen(first, second, to, cap_rows), moe_low[...], NN).astype(jnp.bfloat16)
        x_copy(r).start()
    each_peer(dp_count, x_go)
    x_rows[dp] = mm(chosen(first, second, dp, cap_rows), moe_low[...], NN).astype(jnp.bfloat16)


    ids = lax.broadcasted_iota(jnp.int32, (experts, tokens), 0)
    pick_first, pick_second = ids == routes_ref[0:1, :], ids == routes_ref[1:2, :]
    live = padding_ref[pl.ds(tp // 2, 1), pl.ds(pl.multiple_of(lax.rem(tp, 2) * tokens, 128), tokens)]
    live = (live == 1).astype(jnp.float32)
    logits = mm(router_ref[...], moe_low[...], NT)
    gap = jnp.sum(jnp.where(pick_first, logits, 0.0) - jnp.where(pick_second, logits, 0.0), axis=0, keepdims=True)
    gate_first = live / (1.0 + jnp.exp(-gap))
    gate_second = live / (1.0 + jnp.exp(gap))
    gates[0:1, :] = gate_first
    gates[1:2, :] = gate_second

    def gate_copy(r):
        to = peer(r)
        return remote(gate_send.at[to], gate_rows.at[dp], g_s.at[r], g_r.at[r], "dp", to)

    def gate_fill(r):
        to = peer(r)
        column = jnp.sum(gate_map(first, second, gate_first, gate_second, to, cap_rows), axis=1, keepdims=True)
        return jnp.broadcast_to(to_row(column, lanes), (8, lanes))

    def gate_go(r):
        gate_send[peer(r)] = gate_fill(r)
        gate_copy(r).start()
    each_peer(dp_count, gate_go)
    gate_rows[dp] = gate_fill(0)

    load_g.wait()
    rest_far.wait_recv()
    rest_on.start()
    for c in load_down:
        c.wait()
    rest_on.wait_recv()
    slots = experts * cap_rows
    block = slots // 4

    def side_block(k, carry):
        part = pl.ds(pl.multiple_of(k * block, 16), block)
        here = g_rows[pl.ds(k * (experts // 4), experts // 4)].reshape(block, width)
        for t in range(tensor_count):
            side[part, t * hidden : (t + 1) * hidden] = mm(here, down[t], NT).astype(jnp.bfloat16)
        return carry
    lax.fori_loop(0, 4, side_block, 0)

    load_up.wait()
    up_far.wait_recv()
    up_on.start()
    up_near.wait_recv()
    up_on.wait_recv()

    def back_copy(r):
        to = peer(r)
        return remote(back_send.at[to], back.at[dp], b_s.at[r], b_r.at[r], "dp", to)

    def dot_copy(r):
        to = peer(r)
        return remote(dot_send.at[to], dot_rows.at[dp], d_s.at[r], d_r.at[r], "dp", to)

    group = max(1, min(dp_count, 320 // cap_rows))

    def first_pass(step, carry):
        rounds = [step * group + k for k in range(group)]
        froms = [peer(r) for r in rounds]
        for k, r in enumerate(rounds):
            if k == 0:
                @pl.when(r > 0)
                def _():
                    x_copy(r).wait_recv()
            else:
                x_copy(r).wait_recv()
        here = jnp.concatenate([x_rows[s] for s in froms], axis=0)
        total_back = jnp.zeros((group * cap_rows, width), jnp.float32)
        dots = jnp.zeros((group * cap_rows, 128), jnp.float32)
        for t in range(tensor_count):
            cols = slice(t * hidden, (t + 1) * hidden)
            pre = mm(here, up[t], NT)
            value, slope = gelu_pair(pre)
            low = value.astype(jnp.bfloat16)
            places = [pl.ds(pl.multiple_of(s * cap_rows, 16), cap_rows) for s in froms]
            beside = jnp.concatenate([side[p, cols] for p in places], axis=0).astype(jnp.float32)
            product = low.astype(jnp.float32) * beside
            dots = dots + sum(product[:, k : k + 128] for k in range(0, hidden, 128))
            grad = (beside * slope).astype(jnp.bfloat16)
            for k, p in enumerate(places):
                piece = slice(k * cap_rows, (k + 1) * cap_rows)
                act[p, cols] = low[piece]
                side[p, cols] = grad[piece]
            total_back = total_back + mm(grad, up[t], NN)
        column = jnp.sum(dots, axis=1, keepdims=True)
        for k, (r, s) in enumerate(zip(rounds, froms)):
            piece = slice(k * cap_rows, (k + 1) * cap_rows)
            low = total_back[piece].astype(jnp.bfloat16)
            line = jnp.broadcast_to(to_row(column[piece], lanes), (8, lanes))

            def send():
                back_send[s] = low
                dot_send[s] = line
                back_copy(r).start()
                dot_copy(r).start()

            def keep():
                back[dp] = low
                dot_rows[dp] = line
            if k == 0:
                pl.when(r > 0)(send)
                pl.when(r == 0)(keep)
            else:
                send()
        return carry
    lax.fori_loop(0, dp_count // group, first_pass, 0)

    each_peer(dp_count, lambda r: gate_copy(r).wait_recv())

    def gate_rows_in(s, carry):
        column = to_column(gate_rows[s, 0:1, :], cap_rows)
        x_rows[s] = (x_rows[s].astype(jnp.float32) * column).astype(jnp.bfloat16)
        g_rows[s] = (g_rows[s].astype(jnp.float32) * column).astype(jnp.bfloat16)
        return carry
    lax.fori_loop(0, experts, gate_rows_in, 0)

    each_peer(dp_count, lambda r: x_copy(r).wait_send())
    lands = ((down_pair, down_own), (up_pair, up_own))
    aside = [remote(stage.at[k], lands[k][n], a_s.at[2 * k + n], a_r.at[2 * k + n], "tensor", sib)
             for k in range(2) for n in range(2)]
    down_far = remote(down_pair, down_land, a_s.at[4], a_r.at[4], "tensor", opp)
    piece = hidden // 2
    for n, t in enumerate((across, sib, opp, tp)):
        for k, (left, right) in enumerate(((act, g_rows), (side, x_rows))):
            if n == 1:
                aside[2 * k].wait_send()
            if n >= 2:
                aside[2 * k + n - 2].wait_recv()
            for m in range(2):
                cols = pl.ds(pl.multiple_of(t * hidden + m * piece, 128), piece)
                part = pl.ds(m * piece, piece)
                tile = mm(left[:, cols], right[...].reshape(slots, width), TN)
                if n < 2:
                    stage[k, part, :] = tile.astype(jnp.bfloat16)
                else:
                    land = lands[k][n - 2]
                    land[part, :] = (tile + land[part, :].astype(jnp.float32)).astype(jnp.bfloat16)
            if n < 2:
                aside[2 * k + n].start()
            elif n == 2 and k == 0:
                down_far.start()

    def produce(k, carry):
        part = pl.ds(pl.multiple_of(k * block, 16), block)
        out = jnp.zeros((block, width), jnp.float32)
        for t in range(tensor_count):
            out = out + mm(act[part, t * hidden : (t + 1) * hidden], down[t], NN)
        out = out.astype(jnp.bfloat16)
        for e in range(experts // 4):
            produced[k * (experts // 4) + e] = out[e * cap_rows : (e + 1) * cap_rows]
        return carry
    lax.fori_loop(0, 4, produce, 0)

    total[...] = jnp.zeros_like(total)

    def combine(r, carry):
        dot_first, dot_second = carry
        e = peer(r)

        @pl.when(r > 0)
        def _():
            back_copy(r).wait_recv()
            dot_copy(r).wait_recv()
        weights = gate_map(first, second, gate_first, gate_second, e, cap_rows)
        total[...] += gated_rows(weights, back[e])
        column = to_column(dot_rows[e, 0:1, :], cap_rows)
        ids = lax.broadcasted_iota(jnp.int32, (cap_rows, tokens), 0) + e * cap_rows
        dot_first = dot_first + jnp.sum(jnp.where(ids == first, column, 0.0), axis=0, keepdims=True)
        dot_second = dot_second + jnp.sum(jnp.where(ids == second, column, 0.0), axis=0, keepdims=True)
        return dot_first, dot_second
    zero_row = jnp.zeros((1, tokens), jnp.float32)
    dot_first, dot_second = lax.fori_loop(0, dp_count, combine, (zero_row, zero_row))

    change = gate_first * gate_second * (dot_first - dot_second)
    logit_grad = (jnp.where(pick_first, change, 0.0) - jnp.where(pick_second, change, 0.0)).astype(jnp.bfloat16)
    norm_grad = total[...] + mm(logit_grad, router_ref[...], TN)
    mixed = middle[...]
    r = lax.rsqrt(jnp.mean(mixed * mixed, axis=-1, keepdims=True) + EPSILON)
    u = mixed * r
    du = norm_grad * gain_ref[...]
    grad = grad_ref[...].astype(jnp.float32) + r * (du - u * jnp.mean(du * u, axis=-1, keepdims=True))
    middle_grad[...] = grad
    low = grad.astype(jnp.bfloat16)
    for t in range(tensor_count):
        heads_grad[t] = mm(outw_ref[t], low, NT).astype(jnp.bfloat16)
        out_part[t] = mm(heads_ref[t], low, NN).astype(jnp.bfloat16)
    stats[0:8, :] = jnp.broadcast_to(jnp.sum(norm_grad * u, axis=0, keepdims=True), (8, width))
    stats[8:, :] = mm(logit_grad, moe_low[...], NN)

    down_far.wait_recv()
    down_far.wait_send()
    for k in range(2):
        aside[2 * k + 1].wait_send()
    up_far.wait_send()
    rest_far.wait_send()
    rest_on.wait_send()
    up_near.wait_send()
    up_on.wait_send()

    def drain(r):
        gate_copy(r).wait_send()
        back_copy(r).wait_send()
        dot_copy(r).wait_send()
    each_peer(dp_count, drain)


def middle_pass(sizes, x, grad, heads_all, outw, gain, router_t, routes_t, padding, slot_rows, cot, up, down, down_all):
    dp_count, tensor_count, experts, capacity, cap_rows, heads, blocks, gather_w = sizes
    tokens, width = x.shape
    inner = heads * DH
    hidden = up.shape[0]
    slots = experts * cap_rows
    lanes = -(-cap_rows // 128) * 128
    vmem = pl.BlockSpec(memory_space=pltpu.VMEM)
    anywhere = pl.BlockSpec(memory_space=pl.ANY)
    shape = jax.ShapeDtypeStruct
    low = jnp.bfloat16
    return pl.pallas_call(
        functools.partial(middle_kernel, sizes),
        in_specs=[vmem] * 9 + [anywhere] * 4,
        out_specs=[vmem] * 11,
        out_shape=[
            shape((hidden, width), low),
            shape((hidden, width), low),
            shape((hidden, width), low),
            shape((hidden, width), low),
            shape((experts, cap_rows, width), low),
            shape((tokens, width), jnp.float32),
            shape((tokens, width), jnp.float32),
            shape((tensor_count, inner, tokens), low),
            shape((tensor_count, inner, width), low),
            shape((8 + experts, width), jnp.float32),
            shape((8, tokens), jnp.float32),
        ],
        scratch_shapes=[
            pltpu.VMEM((tensor_count, hidden, width), low),
            pltpu.VMEM((tensor_count, hidden, width), low),
            pltpu.VMEM((experts, cap_rows, width), low),
            pltpu.VMEM((experts, cap_rows, width), low),
            pltpu.VMEM((slots, tensor_count * hidden), low),
            pltpu.VMEM((slots, tensor_count * hidden), low),
            pltpu.VMEM((experts, cap_rows, width), low),
            pltpu.VMEM((experts, cap_rows, width), low),
            pltpu.VMEM((experts, 8, lanes), jnp.float32),
            pltpu.VMEM((experts, 8, lanes), jnp.float32),
            pltpu.VMEM((experts, 8, lanes), jnp.float32),
            pltpu.VMEM((experts, 8, lanes), jnp.float32),
            pltpu.VMEM((tokens, width), low),
            pltpu.VMEM((2, hidden, width), low),
            pltpu.VMEM((hidden, width), low),
        ] + sems(5, dp_count, dp_count, dp_count, dp_count, 5) + [pltpu.SemaphoreType.DMA((8,))],
        compiler_params=pltpu.CompilerParams(
            vmem_limit_bytes=VMEM_LIMIT, collective_id=2, has_side_effects=True),
        cost_estimate=pl.CostEstimate(
            flops=12 * slots * width * hidden * tensor_count, bytes_accessed=40 << 20, transcendentals=4_000_000),
        name="middle_pass",
    )(x, grad, heads_all, outw, gain, router_t, routes_t, padding, slot_rows, cot, up, down, down_all)


def attend_back_sequence(heads, blocks, seq, tiles, sums, segk_ref, segq_ref, qkv, grads, lse_ref, kg, vg, dq, between):
    scale = 1.0 / math.sqrt(DH)
    inner = heads * DH
    half = blocks // 2
    for h in range(heads):
        cols, kcols, vcols = [slice(c * inner + h * DH, c * inner + (h + 1) * DH) for c in range(3)]
        kg[...] = jnp.zeros_like(kg)
        vg[...] = jnp.zeros_like(vg)
        for qb in range(blocks):
            nk = (qb + 1) * QB
            lower = qb * QB
            query = (qkv[seq, lower : lower + QB, cols].astype(jnp.float32) * scale).astype(jnp.bfloat16)
            grad = grads[seq * 2 + qb // half, cols, (qb % half) * QB : (qb % half + 1) * QB]
            lse = lse_ref[seq, h : h + 1, lower : lower + QB]
            parts = score_block(qkv[seq, 0:nk, kcols], query, tiles, h, qb, segk_ref.at[seq], segq_ref.at[pl.ds(seq, 1)])
            probs = [jnp.exp(x - lse) for x in parts]
            pg = mm(qkv[seq, 0:nk, vcols], grad, NN)
            pgs = [pg[kb * QB : (kb + 1) * QB] for kb in range(qb + 1)]
            delta = functools.reduce(jnp.add, [jnp.sum(p * g, axis=0, keepdims=True) for p, g in zip(probs, pgs)])
            dqt = jnp.zeros((DH, QB), jnp.float32)
            for kb in range(qb + 1):
                rows = slice(kb * QB, (kb + 1) * QB)
                sg = (probs[kb] * (pgs[kb] - delta)).astype(jnp.bfloat16)
                sums[h, qb - kb] += sg.astype(jnp.float32)
                vg[rows] += mm(probs[kb].astype(jnp.bfloat16), grad, NT)
                kg[rows] += mm(sg, query, NN)
                dqt = dqt + mm(qkv[seq, rows, kcols], sg, TN)
            dq[lower : lower + QB, h * DH : (h + 1) * DH] = (dqt * scale).T.astype(jnp.bfloat16)
        dq[:, inner + h * DH : inner + (h + 1) * DH] = kg[...].astype(jnp.bfloat16)
        dq[:, 2 * inner + h * DH : 2 * inner + (h + 1) * DH] = vg[...].astype(jnp.bfloat16)
        between(h)


def fold_lines(sums, h, blocks):
    moved = []
    for d in range(blocks):
        folded = fold_tile(sums, h, d)
        line = folded[0:1, :]
        for s in range(1, 8):
            line = line + pltpu.roll(folded[s : s + 1, :], 2 * QB - s, 1)
        moved.append(line)
    out = []
    for d in range(blocks):
        piece = moved[d][:, :QB]
        if d + 1 < blocks:
            piece = piece + moved[d + 1][:, QB:]
        out.append(piece)
    return jnp.concatenate(out, axis=1)


def two_stage_start(send, land, s_sem, r_sem, tensor_count):
    tp = lax.axis_index("tensor")
    copies = []
    for r in range(1, tensor_count):
        copies.append(remote(send, land.at[r - 1], s_sem.at[r], r_sem.at[r], "tensor", lax.rem(tp + r, tensor_count)))
    for c in copies:
        c.start()
    return copies


def last_kernel(sizes, x_ref, gain_ref, middle_ref, mgrad_ref, hgrad_ref, rows, w_ref, qkv, lse_ref, line_ref,
                segk_ref, segq_ref, produced_ref, slots_ref, gates_ref, early_ref, bucket_ref,
                out_part, up_pair,
                out_ref, input_grad_ref, wgrad_ref, early_out, late_out, up_land,
                tiles, sums, kg, vg, dq, grads, landed, npart, near_land, far_land, pair, wsum, wsend, wland,
                early_land, early_mid, early_dp, late, late_land, late_mid, late_dp, total,
                out_land, out_pair, out_far,
                h_s, h_r, p_s, p_r, n_s, n_r, w_s, w_r, et_s, et_r, ed_s, ed_r, lt_s, lt_r, ld_s, ld_r, o_s, o_r):
    dp_count, tensor_count, experts, capacity, cap_rows, heads, blocks, gather_w = sizes
    dp = lax.axis_index("dp")
    tp, sib, opp, across = partners(tensor_count)
    tokens, width = x_ref.shape
    inner = heads * DH
    wait_barrier = greet(dp_count, tensor_count)
    build_bias(line_ref, tiles, heads, blocks)
    sums[...] = jnp.zeros_like(sums)
    dq[...] = jnp.zeros_like(dq)
    own_seq = tp // 2
    other = 1 - own_seq
    wait_barrier()

    def h_copy(k, to):
        return remote(hgrad_ref.at[to], grads.at[tp], h_s.at[k], h_r.at[k], "tensor", to)
    h_copy(0, opp).start()
    h_copy(1, across).start()
    h_copy(2, sib).start()
    grads[tp] = hgrad_ref[tp]

    def p_copy(r):
        to = peer(r)
        return remote(produced_ref.at[to], landed.at[dp], p_s.at[r], p_r.at[r], "dp", to)
    each_peer(dp_count, lambda r: p_copy(r).start())
    landed[dp] = produced_ref[dp]

    early = two_stage_start(early_ref.at[pl.ds(8, experts)], early_land, et_s, et_r, tensor_count)

    def early_copy(r):
        return remote(early_mid, early_dp.at[r], ed_s.at[r], ed_r.at[r], "dp", peer(r))

    out_near = [remote(out_part.at[t], out_land.at[k], o_s.at[k], o_r.at[k], "tensor", sib)
                for k, t in enumerate((across, sib))]
    out_across = remote(out_pair, out_far, o_s.at[2], o_r.at[2], "tensor", opp)
    up_across = remote(up_pair, up_land, o_s.at[3], o_r.at[3], "tensor", opp)
    for c in out_near:
        c.start()

    h_copy(0, opp).wait_recv()
    h_copy(1, across).wait_recv()
    out_near[0].wait_recv()
    out_pair[...] = (out_part[opp].astype(jnp.float32) + out_land[0].astype(jnp.float32)).astype(jnp.bfloat16)
    out_across.start()
    up_across.start()

    def n_copy(k, src, dst, to):
        return remote(src, dst, n_s.at[k], n_r.at[k], "tensor", to)
    pair_near = n_copy(0, npart.at[across], near_land.at[0], sib)
    pair_far = n_copy(1, pair, far_land, opp)
    own_near = n_copy(2, npart.at[sib], near_land.at[1], sib)

    def nothing(h):
        pass

    def project(seq, fresh):
        here = rows[pl.ds(seq * 2, 2)].reshape(2 * tokens, width)
        packed = dq.shape[1]
        part = mm(here, dq[...], TN)
        wsum[:, :packed] = part if fresh else wsum[:, :packed] + part
        norm = mm(dq[...], w_ref[...].reshape(width, w_ref.shape[2])[:, :packed], NT)
        column = jnp.sum(norm * here.astype(jnp.float32), axis=0, keepdims=True)
        low = norm.astype(jnp.bfloat16)
        npart[seq * 2] = low[:tokens]
        npart[seq * 2 + 1] = low[tokens:]
        return column

    attend_back_sequence(heads, blocks, other, tiles, sums, segk_ref, segq_ref, qkv, grads, lse_ref, kg, vg, dq, nothing)
    out_across.wait_recv()
    out_near[1].wait_recv()
    out_whole = out_part[tp].astype(jnp.float32) + out_land[1].astype(jnp.float32) + out_far[...].astype(jnp.float32)
    out_far[...] = out_whole.astype(jnp.bfloat16)
    gain_row = project(other, True)
    pair_near.start()

    def between(h):
        if h == 0:
            pair_near.wait_recv()
            pair[...] = (npart[opp].astype(jnp.float32) + near_land[0].astype(jnp.float32)).astype(jnp.bfloat16)
            pair_far.start()
            for c in early:
                c.wait_recv()
            early_mid[...] = early_ref[8:, :] + early_land[0] + early_land[1] + early_land[2]
            each_peer(dp_count, lambda r: early_copy(r).start())

    h_copy(2, sib).wait_recv()
    attend_back_sequence(heads, blocks, own_seq, tiles, sums, segk_ref, segq_ref, qkv, grads, lse_ref, kg, vg, dq, between)
    gain_row = gain_row + project(own_seq, False)
    own_near.start()

    wsum[:, 3 * inner :] = out_far[...].astype(jnp.float32).T
    share = width // dp_count
    side = peer(1)
    columns = dp_count // 2

    def share_rows(d):
        return pl.ds(pl.multiple_of(d * share, 8), share)

    def side_copy(k):
        return remote(wsend.at[k], wland.at[k], w_s.at[k], w_r.at[k], "dp", side)

    def column_copy(k):
        n = columns + k
        return remote(wsend.at[n], wland.at[n], w_s.at[n], w_r.at[n], "dp", peer(2 * k))
    for k in range(columns):
        wsend[k] = wsum[share_rows(jnp.bitwise_xor(side, 2 * k)), :].astype(jnp.bfloat16)
        side_copy(k).start()

    gain_row = gain_row / gain_ref[...]
    late[...] = jnp.zeros_like(late)
    for k in range(width // 128):
        late[k : k + 1, :] = gain_row[:, k * 128 : (k + 1) * 128]
        late[8 + k : 9 + k, :] = early_ref[0:1, k * 128 : (k + 1) * 128]
    buckets = late.shape[0] - 16
    ids = lax.broadcasted_iota(jnp.int32, (buckets, bucket_ref.shape[1]), 0)
    hot = ids == bucket_ref[...]
    lane = lax.broadcasted_iota(jnp.int32, (buckets, 128), 1)
    table = jnp.zeros((buckets, 128), jnp.float32)
    for h in range(heads):
        column = jnp.sum(jnp.where(hot, fold_lines(sums, h, blocks), 0.0), axis=1, keepdims=True)
        table = table + jnp.where(lane == tp * heads + h, column, 0.0)
    late[16:, :] = table
    late_first = two_stage_start(late, late_land, lt_s, lt_r, tensor_count)

    def late_copy(r):
        return remote(late_mid, late_dp.at[r], ld_s.at[r], ld_r.at[r], "dp", peer(r))

    for k in range(1, columns):
        side_copy(k).wait_recv()
        mine = wsum[share_rows(peer(2 * k)), :]
        wsend[columns + k] = (mine + wland[k].astype(jnp.float32)).astype(jnp.bfloat16)
        column_copy(k).start()

    each_peer(dp_count, lambda r: early_copy(r).wait_recv())
    summed = early_mid[...]
    for r in range(1, dp_count):
        summed = summed + early_dp[r]
    early_out[...] = summed

    for c in late_first:
        c.wait_recv()
    late_mid[...] = late[...] + late_land[0] + late_land[1] + late_land[2]
    each_peer(dp_count, lambda r: late_copy(r).start())

    first, second = slots_ref[0:1, :], slots_ref[1:2, :]
    gate_first, gate_second = gates_ref[0:1, :], gates_ref[1:2, :]
    total[...] = middle_ref[...]

    def combine(r, carry):
        e = peer(r)

        @pl.when(r > 0)
        def _():
            p_copy(r).wait_recv()
        total[...] += gated_rows(gate_map(first, second, gate_first, gate_second, e, cap_rows), landed[e])
        return carry
    lax.fori_loop(0, dp_count, combine, 0)
    out_ref[...] = total[...]

    up_across.wait_recv()

    own_near.wait_recv()
    pair_far.wait_recv()
    norm_grad = npart[tp].astype(jnp.float32) + near_land[1].astype(jnp.float32) + far_land[...].astype(jnp.float32)
    x = x_ref[...].astype(jnp.float32)
    r = lax.rsqrt(jnp.mean(x * x, axis=-1, keepdims=True) + EPSILON)
    u = x * r
    du = norm_grad * gain_ref[...]
    input_grad_ref[...] = mgrad_ref[...] + r * (du - u * jnp.mean(du * u, axis=-1, keepdims=True))

    side_copy(0).wait_recv()
    part = wsum[share_rows(dp), :] + wland[0].astype(jnp.float32)
    for k in range(1, columns):
        column_copy(k).wait_recv()
        part = part + wland[columns + k].astype(jnp.float32)
    wgrad_ref[...] = part

    each_peer(dp_count, lambda r: late_copy(r).wait_recv())
    summed = late_mid[...]
    for r in range(1, dp_count):
        summed = summed + late_dp[r]
    late_out[...] = summed

    for c in early + late_first + out_near + [out_across, up_across, pair_near, pair_far, own_near, h_copy(0, opp), h_copy(1, across), h_copy(2, sib)]:
        c.wait_send()

    def drain(r):
        p_copy(r).wait_send()
        early_copy(r).wait_send()
        late_copy(r).wait_send()
    each_peer(dp_count, drain)
    for k in range(columns):
        side_copy(k).wait_send()
        if k:
            column_copy(k).wait_send()


def last_pass(sizes, x, gain, middle, middle_grad, heads_grad, rows, w, qkv, lse, line, segk, segq, produced,
              slot_rows, gates, early, bucket_row, out_part, up_pair):
    dp_count, tensor_count, experts, capacity, cap_rows, heads, blocks, gather_w = sizes
    tokens, width = x.shape
    inner = heads * DH
    seq_len = blocks * QB
    share = width // dp_count
    vmem = pl.BlockSpec(memory_space=pltpu.VMEM)
    shape = jax.ShapeDtypeStruct
    low, full = jnp.bfloat16, jnp.float32
    late = 16 + NB
    packed = qkv.shape[2]
    return pl.pallas_call(
        functools.partial(last_kernel, sizes),
        in_specs=[vmem] * 19,
        out_specs=[vmem] * 6,
        out_shape=[
            shape((tokens, width), full),
            shape((tokens, width), full),
            shape((share, w.shape[2]), full),
            shape((experts, width), full),
            shape((late, 128), full),
            shape(up_pair.shape, low),
        ],
        scratch_shapes=[
            pltpu.VMEM((heads, blocks, QB, QB), full),
            pltpu.VMEM((heads, blocks, QB, QB), full),
            pltpu.VMEM((seq_len, DH), full),
            pltpu.VMEM((seq_len, DH), full),
            pltpu.VMEM((seq_len, packed), low),
            pltpu.VMEM((tensor_count, inner, tokens), low),
            pltpu.VMEM((experts, cap_rows, width), low),
            pltpu.VMEM((tensor_count, tokens, width), low),
            pltpu.VMEM((2, tokens, width), low),
            pltpu.VMEM((tokens, width), low),
            pltpu.VMEM((tokens, width), low),
            pltpu.VMEM((width, w.shape[2]), full),
            pltpu.VMEM((dp_count, share, w.shape[2]), low),
            pltpu.VMEM((dp_count, share, w.shape[2]), low),
            pltpu.VMEM((tensor_count - 1, experts, width), full),
            pltpu.VMEM((experts, width), full),
            pltpu.VMEM((dp_count, experts, width), full),
            pltpu.VMEM((late, 128), full),
            pltpu.VMEM((tensor_count - 1, late, 128), full),
            pltpu.VMEM((late, 128), full),
            pltpu.VMEM((dp_count, late, 128), full),
            pltpu.VMEM((tokens, width), full),
            pltpu.VMEM((2, inner, width), low),
            pltpu.VMEM((inner, width), low),
            pltpu.VMEM((inner, width), low),
        ] + sems(3, dp_count, 3, dp_count, tensor_count, dp_count, tensor_count, dp_count, 4),
        compiler_params=pltpu.CompilerParams(
            vmem_limit_bytes=VMEM_LIMIT, collective_id=3, has_side_effects=True),
        cost_estimate=pl.CostEstimate(flops=30_000_000_000, bytes_accessed=30 << 20, transcendentals=4_000_000),
        name="last_pass",
    )(x, gain, middle, middle_grad, heads_grad, rows, w, qkv, lse, line, segk, segq, produced, slot_rows, gates,
      early, bucket_row, out_part, up_pair)


def finish_kernel(out_ref, input_grad_ref, wgrad_ref, early_ref, late_ref, up_own, up_land, down_own, down_land,
                  out, input_grad, w_qkv_grad, w_out_grad, table, gain_attn, gain_moe, router, up_grad, down_grad):
    out[...] = out_ref[...]
    input_grad[...] = input_grad_ref[...]
    up_grad[...] = up_own[...].astype(jnp.float32) + up_land[...].astype(jnp.float32)
    down_grad[...] = down_own[...].astype(jnp.float32) + down_land[...].astype(jnp.float32)

    @pl.when(pl.program_id(0) == 0)
    def _():
        inner = w_qkv_grad.shape[2]
        for c in range(3):
            w_qkv_grad[c] = wgrad_ref[:, c * inner : (c + 1) * inner]
        w_out_grad[...] = wgrad_ref[:, 3 * inner :].T
        table[...] = late_ref[16:, : table.shape[1]]
        for k in range(gain_attn.shape[1] // 128):
            gain_attn[:, k * 128 : (k + 1) * 128] = late_ref[k : k + 1, :]
            gain_moe[:, k * 128 : (k + 1) * 128] = late_ref[8 + k : 9 + k, :]
        router[...] = early_ref[...].T


def finish(heads_total, out, input_grad, wgrad, early, late, up_own, up_land, down_own, down_land):
    steps = 4
    tokens, width = out.shape
    share = wgrad.shape[0]
    inner = wgrad.shape[1] // 4
    hidden = up_own.shape[0]
    full = jnp.float32
    shape = jax.ShapeDtypeStruct

    def rows(n):
        return pl.BlockSpec((n // steps, width), lambda s: (s, 0))

    def whole(*dims):
        return pl.BlockSpec(dims, lambda s: (0,) * len(dims))
    return pl.pallas_call(
        finish_kernel,
        grid=(steps,),
        in_specs=[rows(tokens), rows(tokens), whole(*wgrad.shape), whole(*early.shape), whole(*late.shape)]
        + [rows(hidden)] * 4,
        out_specs=[rows(tokens), rows(tokens), whole(3, share, inner), whole(inner, share), whole(NB, heads_total),
                   whole(1, width), whole(1, width), whole(width, early.shape[0]), rows(hidden), rows(hidden)],
        out_shape=[shape((tokens, width), full), shape((tokens, width), full), shape((3, share, inner), full),
                   shape((inner, share), full), shape((NB, heads_total), full), shape((1, width), full),
                   shape((1, width), full), shape((width, early.shape[0]), full), shape((hidden, width), full),
                   shape((hidden, width), full)],
        cost_estimate=pl.CostEstimate(flops=0, bytes_accessed=16 << 20, transcendentals=0),
        name="finish",
    )(out, input_grad, wgrad, early, late, up_own, up_land, down_own, down_land)


def norm_rows(values, gain):
    return values * lax.rsqrt(jnp.mean(values * values, axis=-1, keepdims=True) + EPSILON) * gain


def norm_back(values, gain, grad):
    r = lax.rsqrt(jnp.mean(values * values, axis=-1, keepdims=True) + EPSILON)
    u = values * r
    du = grad * gain
    return r * (du - u * jnp.mean(du * u, axis=-1, keepdims=True)), grad * u


def plain_body(
    block_input,
    out_grad,
    w_qkv,
    w_out,
    rel_table,
    gain_attn,
    gain_moe,
    w_router,
    w_up,
    w_down,
    routes,
    segments,
    padding,
    rel_bucket,
):
    tensor_pos = lax.axis_index("tensor")
    rows_local, width = block_input.shape
    seq_len = segments.shape[1]
    expert_count = w_router.shape[1]
    capacity = (10 * rows_local + 4 * expert_count - 1) // (4 * expert_count)
    slots = expert_count * capacity
    x_float = block_input.astype(jnp.float32)
    grad_float = out_grad.astype(jnp.float32)

    attn_norm = norm_rows(x_float, gain_attn).astype(jnp.bfloat16)
    seq_rows = lax.all_gather(attn_norm, "tensor", axis=0, tiled=True)
    qkv_full = lax.all_gather(w_qkv, "dp", axis=1, tiled=True)
    out_rows = lax.all_gather(w_out, "dp", axis=1, tiled=True)
    out_full = lax.all_gather(out_rows, "tensor", axis=0, tiled=True)
    up_full = lax.all_gather(w_up[0], "tensor", axis=0, tiled=True)
    down_full = lax.all_gather(w_down[0], "tensor", axis=0, tiled=True)

    live_mask = lax.dynamic_slice_in_dim(padding.reshape(-1), tensor_pos * rows_local, rows_local)
    live_float = live_mask.astype(jnp.float32)
    expert_ids = jnp.arange(expert_count, dtype=jnp.int32)
    pick_first = routes[:, 0:1] == expert_ids[None, :]
    pick_second = routes[:, 1:2] == expert_ids[None, :]
    usable = live_mask[:, None] == 1
    first_hot = (pick_first & usable).astype(jnp.int32)
    second_hot = (pick_second & usable).astype(jnp.int32)
    first_place = jnp.sum((jnp.cumsum(first_hot, axis=0) - first_hot) * first_hot, axis=1)
    second_before = (
        jnp.cumsum(second_hot, axis=0) - second_hot + jnp.sum(first_hot, axis=0, keepdims=True)
    )
    second_place = jnp.sum(second_before * second_hot, axis=1)
    first_slot = jnp.where(
        (live_mask == 1) & (first_place < capacity), routes[:, 0] * capacity + first_place, -1
    )
    second_slot = jnp.where(
        (live_mask == 1) & (second_place < capacity), routes[:, 1] * capacity + second_place, -1
    )
    slot_ids = jnp.arange(slots, dtype=jnp.int32)
    select_first = slot_ids[:, None] == first_slot[None, :]
    select_second = slot_ids[:, None] == second_slot[None, :]
    select_both = (select_first | select_second).astype(jnp.bfloat16)
    select_first_low = select_first.astype(jnp.bfloat16)
    select_second_low = select_second.astype(jnp.bfloat16)

    def to_experts(rows):
        return lax.all_to_all(rows, "dp", split_axis=0, concat_axis=0, tiled=True)

    grad_rows = jnp.dot(select_both, out_grad, preferred_element_type=jnp.float32)
    sent_grads = to_experts(grad_rows.astype(jnp.bfloat16).reshape(expert_count, capacity, width))
    sent_grads = sent_grads.reshape(slots, width)

    heads = qkv_full.shape[2] // DH
    inner = heads * DH
    table_local = lax.dynamic_slice_in_dim(rel_table, tensor_pos * heads, heads, 1)
    bucket_hot = (rel_bucket[:, None] == jnp.arange(NB, dtype=jnp.int32)[None, :]).astype(jnp.float32)
    line = line_of(jnp.dot(bucket_hot, table_local, precision=HIGHEST).T)
    segk, segq = mask_inputs(segments, padding)
    qkv_low, heads_low, lse = attend(line, segk, segq, seq_rows, qkv_full)
    heads_own = lax.all_to_all(heads_low, "tensor", split_axis=0, concat_axis=1, tiled=True)

    middle = x_float + jnp.dot(heads_own, out_full, preferred_element_type=jnp.float32)
    moe_low = norm_rows(middle, gain_moe).astype(jnp.bfloat16)
    rows_out = jnp.dot(select_both, moe_low, preferred_element_type=jnp.float32)
    sent_rows = to_experts(rows_out.astype(jnp.bfloat16).reshape(expert_count, capacity, width))
    sent_rows = sent_rows.reshape(slots, width)
    logits = jnp.dot(moe_low, w_router, preferred_element_type=jnp.float32)
    first_logit = jnp.sum(jnp.where(pick_first, logits, 0.0), axis=1)
    second_logit = jnp.sum(jnp.where(pick_second, logits, 0.0), axis=1)
    first_gate = jax.nn.sigmoid(first_logit - second_logit) * live_float
    second_gate = jax.nn.sigmoid(second_logit - first_logit) * live_float
    slot_gate = jnp.sum(
        jnp.where(select_first, first_gate[None, :], 0.0)
        + jnp.where(select_second, second_gate[None, :], 0.0),
        axis=1,
    )
    sent_gates = to_experts(slot_gate.reshape(expert_count, capacity)).reshape(slots, 1)

    act, pre_grad, back, dots = expert_first(sent_rows, sent_grads, up_full, down_full)
    returned_grad = to_experts(back.reshape(expert_count, capacity, width)).reshape(slots, width)
    slot_dots = to_experts(dots[0].reshape(expert_count, capacity)).reshape(slots)
    produced, up_part, down_part = expert_late(
        sent_rows, sent_grads, sent_gates, act, pre_grad, down_full
    )
    returned = to_experts(produced.reshape(expert_count, capacity, width)).reshape(slots, width)
    w_up_grad = lax.psum_scatter(up_part, "tensor", scatter_dimension=0, tiled=True)
    w_down_grad = lax.psum_scatter(down_part, "tensor", scatter_dimension=0, tiled=True)

    first_dot = jnp.sum(jnp.where(select_first, slot_dots[:, None], 0.0), axis=0)
    second_dot = jnp.sum(jnp.where(select_second, slot_dots[:, None], 0.0), axis=0)
    coefficient = first_gate * second_gate * (first_dot - second_dot)
    logit_grad = (
        jnp.where(pick_first, coefficient[:, None], 0.0)
        - jnp.where(pick_second, coefficient[:, None], 0.0)
    ).astype(jnp.bfloat16)
    router_grad = jnp.einsum("nd,ne->de", moe_low, logit_grad, preferred_element_type=jnp.float32)

    def gated(rows):
        first_rows = jnp.einsum("st,sd->td", select_first_low, rows, preferred_element_type=jnp.float32)
        second_rows = jnp.einsum("st,sd->td", select_second_low, rows, preferred_element_type=jnp.float32)
        return first_gate[:, None] * first_rows + second_gate[:, None] * second_rows

    moe_norm_grad = (
        jnp.einsum("ne,de->nd", logit_grad, w_router, preferred_element_type=jnp.float32)
        + gated(returned_grad)
    )
    middle_back, gain_moe_rows = norm_back(middle, gain_moe, moe_norm_grad)
    middle_grad = grad_float + middle_back
    gain_moe_grad = jnp.sum(gain_moe_rows, axis=0)
    attn_grad = middle_grad.astype(jnp.bfloat16)
    heads_grad = jnp.einsum("nd,fd->nf", attn_grad, out_full, preferred_element_type=jnp.float32)
    heads_grad = lax.all_to_all(
        heads_grad.astype(jnp.bfloat16), "tensor", split_axis=1, concat_axis=0, tiled=True
    )
    out_part = jnp.einsum("nf,nd->fd", heads_own, attn_grad, preferred_element_type=jnp.float32)
    out_part = lax.psum_scatter(out_part.astype(jnp.bfloat16), "tensor", scatter_dimension=0, tiled=True)
    w_out_grad = lax.psum_scatter(out_part.astype(jnp.float32), "dp", scatter_dimension=1, tiled=True)
    gain_moe_grad, router_grad = lax.psum((gain_moe_grad, router_grad), ("dp", "tensor"))

    norm_part, qkv_part, folded = attend_back(
        line, segk, segq, seq_rows, qkv_full, qkv_low, heads_grad, lse
    )
    attn_norm_grad = lax.psum_scatter(norm_part, "tensor", scatter_dimension=0, tiled=True)
    input_back, gain_attn_rows = norm_back(x_float, gain_attn, attn_norm_grad.astype(jnp.float32))
    input_grad = middle_grad + input_back
    gain_attn_grad = jnp.sum(gain_attn_rows, axis=0)
    w_qkv_grad = lax.psum_scatter(qkv_part, "dp", scatter_dimension=1, tiled=True)
    line_grad = lines_of(folded, heads, seq_len // QB)
    table_part = jnp.dot(bucket_hot.T, line_grad.T, precision=HIGHEST)
    table_whole = lax.dynamic_update_slice(
        jnp.zeros(rel_table.shape, jnp.float32), table_part, (0, tensor_pos * heads)
    )
    gain_attn_grad, table_whole = lax.psum((gain_attn_grad, table_whole), ("dp", "tensor"))
    block_output = middle + gated(returned)
    return (
        block_output,
        input_grad,
        w_qkv_grad,
        w_out_grad,
        table_whole,
        gain_attn_grad,
        gain_moe_grad,
        router_grad,
        w_up_grad.astype(jnp.float32)[None],
        w_down_grad.astype(jnp.float32)[None],
    )


def fused_body(
    block_input,
    out_grad,
    w_qkv,
    w_out,
    rel_table,
    gain_attn,
    gain_moe,
    w_router,
    w_up,
    w_down,
    routes,
    segments,
    padding,
    rel_bucket,
):
    dp_count, tensor_count = lax.axis_size("dp"), lax.axis_size("tensor")
    rows_local, width = block_input.shape
    seq_len = segments.shape[1]
    heads = w_qkv.shape[2] // DH
    capacity = slot_capacity(rows_local, w_router.shape[1])
    expert_count = w_router.shape[1]
    sizes = (dp_count, tensor_count, expert_count, capacity, capacity, heads, seq_len // QB, True)

    routes_t = routes.T
    gain_attn, gain_moe, bucket_row = gain_attn[None], gain_moe[None], rel_bucket[None]
    rows, w_all, outw, down_all, qkv, lse, heads_all, slot_rows, cot, line, segk = front(
        sizes, block_input, gain_attn, w_qkv, w_out, w_down[0], out_grad, routes_t, segments, padding,
        rel_table, bucket_row
    )
    (up_pair, up_own, down_own, down_land, produced, middle, middle_grad, heads_grad, out_part, early,
     gates) = middle_pass(
        sizes, block_input, out_grad, heads_all, outw, gain_moe, w_router.T, routes_t, padding,
        slot_rows, cot, w_up[0], w_down[0], down_all
    )
    block_output, input_grad, wgrad, early, late, up_land = last_pass(
        sizes, block_input, gain_attn, middle, middle_grad, heads_grad, rows, w_all, qkv, lse, line, segk, segments,
        produced, slot_rows, gates, early, bucket_row, out_part, up_pair
    )
    (block_output, input_grad, w_qkv_grad, w_out_grad, table_grad, gain_attn_grad, gain_moe_grad, router_grad,
     w_up_grad, w_down_grad) = finish(
        rel_table.shape[1], block_output, input_grad, wgrad, early, late, up_own, up_land, down_own, down_land
    )
    return (
        block_output,
        input_grad,
        w_qkv_grad,
        w_out_grad,
        table_grad,
        gain_attn_grad.reshape(width),
        gain_moe_grad.reshape(width),
        router_grad,
        w_up_grad[None],
        w_down_grad[None],
    )


def slot_capacity(tokens, experts):
    return (10 * tokens + 4 * experts - 1) // (4 * experts)


def body(*args):
    block_input, w_qkv, w_router = args[0], args[2], args[7]
    capacity = slot_capacity(block_input.shape[0], w_router.shape[1])
    fits = capacity % 16 == 0 and w_qkv.shape[1] % 16 == 0 and lax.axis_size("dp") == w_router.shape[1] == 8 and block_input.shape[1] <= 1024
    return fused_body(*args) if fits else plain_body(*args)


def solution(mesh):
    in_specs = (
        P(("dp", "tensor"), None),
        P(("dp", "tensor"), None),
        P(None, "dp", "tensor"),
        P("tensor", "dp"),
        P(),
        P(),
        P(),
        P(),
        P("dp", "tensor", None),
        P("dp", "tensor", None),
        P(("dp", "tensor"), None),
        P("dp", None),
        P("dp", None),
        P(),
    )
    out_specs = (
        P(("dp", "tensor"), None),
        P(("dp", "tensor"), None),
        P(None, "dp", "tensor"),
        P("tensor", "dp"),
        P(),
        P(),
        P(),
        P(),
        P("dp", "tensor", None),
        P("dp", "tensor", None),
    )
    return jax.shard_map(body, mesh=mesh, in_specs=in_specs, out_specs=out_specs, check_vma=False)
```

```python
import functools
import math

import jax
import jax.numpy as jnp
from jax import lax
from jax.experimental import pallas as pl
from jax.experimental.pallas import tpu as pltpu
from jax.sharding import PartitionSpec as P

NB = 32
EPSILON = 1e-06
HIGHEST = lax.Precision.HIGHEST
DH = 64
NEGATIVE = -1e30
QB = 256
NT = (((1,), (1,)), ((), ()))
TN = (((0,), (0,)), ((), ()))
NN = (((1,), (0,)), ((), ()))


def mm(a, b, dims):
    return lax.dot_general(a, b, dims, preferred_element_type=jnp.float32)


def build_bias(line_ref, tiles, heads, blocks):
    for h in range(heads):
        for d in range(blocks):
            piece = line_ref[h : h + 1, d * QB : d * QB + 2 * QB]
            wide = jnp.broadcast_to(piece, (QB, 2 * QB))
            turned = pltpu.roll(wide, 0, 1, stride=1, stride_axis=0)
            tiles[h, d] = turned[:, QB:]


def score_block(keys, query, tiles, h, qb, segk_ref, segq_ref):
    raw = mm(keys, query, NT)
    q_seg = segq_ref[:, qb * QB : (qb + 1) * QB]
    parts = []
    for kb in range(qb + 1):
        k_seg = segk_ref[kb * QB : (kb + 1) * QB, :]
        same = k_seg == q_seg
        if kb == qb:
            row = lax.broadcasted_iota(jnp.int32, (QB, QB), 0)
            col = lax.broadcasted_iota(jnp.int32, (QB, QB), 1)
            same = same | (row == col)
        parts.append(
            jnp.where(same, raw[kb * QB : (kb + 1) * QB] + tiles[h, qb - kb], NEGATIVE)
        )
    return parts


def attend_kernel(heads, blocks, line_ref, segk_ref, segq_ref, rows_ref, w_ref,
                  qkv_ref, out_ref, lse_ref, tiles):
    @pl.when(pl.program_id(0) == 0)
    def _():
        build_bias(line_ref, tiles, heads, blocks)

    for c in range(3):
        qkv_ref[c] = mm(rows_ref[...], w_ref[c], NN).astype(jnp.bfloat16)
    scale = 1.0 / math.sqrt(DH)
    for qb in range(blocks):
        nk = (qb + 1) * QB
        lower = qb * QB
        turned = []
        for h in range(heads):
            cols = slice(h * DH, (h + 1) * DH)
            query = (qkv_ref[0, lower : lower + QB, cols].astype(jnp.float32) * scale).astype(jnp.bfloat16)
            parts = score_block(qkv_ref[1, 0:nk, cols], query, tiles, h, qb, segk_ref.at[0], segq_ref.at[0])
            peak = functools.reduce(jnp.maximum, [jnp.max(x, axis=0, keepdims=True) for x in parts])
            probs = [jnp.exp(x - peak) for x in parts]
            total = functools.reduce(jnp.add, [jnp.sum(x, axis=0, keepdims=True) for x in probs])
            mixed = functools.reduce(jnp.add, [
                mm(qkv_ref[2, kb * QB : (kb + 1) * QB, cols], x.astype(jnp.bfloat16), TN)
                for kb, x in enumerate(probs)])
            turned.append(mixed / total)
            lse_ref[0, h : h + 1, lower : lower + QB] = peak + jnp.log(total)
        out_ref[lower : lower + QB, :] = jnp.concatenate(turned, axis=0).T.astype(jnp.bfloat16)


def attend(line, segk, segq, rows, w):
    seqs, _, seq_len = segq.shape
    heads = line.shape[0]
    inner = heads * DH
    blocks = seq_len // QB
    width = rows.shape[1]
    return pl.pallas_call(
        functools.partial(attend_kernel, heads, blocks),
        grid=(seqs,),
        in_specs=[
            pl.BlockSpec(line.shape, lambda s: (0, 0)),
            pl.BlockSpec((1, seq_len, 1), lambda s: (s, 0, 0)),
            pl.BlockSpec((1, 1, seq_len), lambda s: (s, 0, 0)),
            pl.BlockSpec((seq_len, width), lambda s: (s, 0)),
            pl.BlockSpec(w.shape, lambda s: (0, 0, 0)),
        ],
        out_specs=[
            pl.BlockSpec((3, seq_len, inner), lambda s: (0, s, 0)),
            pl.BlockSpec((seq_len, inner), lambda s: (s, 0)),
            pl.BlockSpec((1, heads, seq_len), lambda s: (s, 0, 0)),
        ],
        out_shape=[
            jax.ShapeDtypeStruct((3, seqs * seq_len, inner), jnp.bfloat16),
            jax.ShapeDtypeStruct((seqs * seq_len, inner), jnp.bfloat16),
            jax.ShapeDtypeStruct((seqs, heads, seq_len), jnp.float32),
        ],
        scratch_shapes=[pltpu.VMEM((heads, blocks, QB, QB), jnp.float32)],
        compiler_params=pltpu.CompilerParams(vmem_limit_bytes=48 << 20),
        cost_estimate=pl.CostEstimate(flops=10_000_000_000, bytes_accessed=10 << 20, transcendentals=4_000_000),
        name="attend",
    )(line, segk, segq, rows, w)


def attend_back_kernel(heads, blocks, seqs, line_ref, segk_ref, segq_ref, rows_ref, w_ref,
                       qkv_ref, og_ref, lse_ref,
                       norm_ref, wg_ref, lg_ref, tiles, sums, kg, vg, dq):
    step = pl.program_id(0)

    @pl.when(step == 0)
    def _():
        build_bias(line_ref, tiles, heads, blocks)
        sums[...] = jnp.zeros_like(sums)
        wg_ref[...] = jnp.zeros_like(wg_ref)

    scale = 1.0 / math.sqrt(DH)
    for h in range(heads):
        cols = slice(h * DH, (h + 1) * DH)
        kg[...] = jnp.zeros_like(kg)
        vg[...] = jnp.zeros_like(vg)
        for qb in range(blocks):
            nk = (qb + 1) * QB
            lower = qb * QB
            query = (qkv_ref[0, lower : lower + QB, cols].astype(jnp.float32) * scale).astype(jnp.bfloat16)
            grad = og_ref[lower : lower + QB, cols]
            lse = lse_ref[0, h : h + 1, lower : lower + QB]
            parts = score_block(qkv_ref[1, 0:nk, cols], query, tiles, h, qb, segk_ref.at[0], segq_ref.at[0])
            probs = [jnp.exp(x - lse) for x in parts]
            pg = mm(qkv_ref[2, 0:nk, cols], grad, NT)
            pgs = [pg[kb * QB : (kb + 1) * QB] for kb in range(qb + 1)]
            delta = functools.reduce(jnp.add, [jnp.sum(p * g, axis=0, keepdims=True) for p, g in zip(probs, pgs)])
            dqt = jnp.zeros((DH, QB), jnp.float32)
            for kb in range(qb + 1):
                rows = slice(kb * QB, (kb + 1) * QB)
                sg = (probs[kb] * (pgs[kb] - delta)).astype(jnp.bfloat16)
                sums[h, qb - kb] += sg.astype(jnp.float32)
                vg[rows] += mm(probs[kb].astype(jnp.bfloat16), grad, NN)
                kg[rows] += mm(sg, query, NN)
                dqt = dqt + mm(qkv_ref[1, rows, cols], sg, TN)
            dq[lower : lower + QB, h * DH : (h + 1) * DH] = (dqt * scale).T.astype(jnp.bfloat16)
        inner = heads * DH
        dq[:, inner + h * DH : inner + (h + 1) * DH] = kg[...].astype(jnp.bfloat16)
        dq[:, 2 * inner + h * DH : 2 * inner + (h + 1) * DH] = vg[...].astype(jnp.bfloat16)
    inner = heads * DH
    total = jnp.zeros(norm_ref.shape, jnp.float32)
    for c in range(3):
        piece = dq[:, c * inner : (c + 1) * inner]
        wg_ref[c] += mm(rows_ref[...], piece, TN)
        total = total + mm(piece, w_ref[c], NT)
    norm_ref[...] = total.astype(norm_ref.dtype)

    @pl.when(step == seqs - 1)
    def _():
        for h in range(heads):
            for d in range(blocks):
                lg_ref[h * blocks + d] = fold_tile(sums, h, d)


def fold_tile(sums, h, d):
    blank = jnp.zeros((8, QB), jnp.float32)
    total = jnp.zeros((8, 2 * QB), jnp.float32)
    for g in range(QB // 8):
        piece = jnp.concatenate([sums[h, d, 8 * g : 8 * g + 8, :], blank], axis=1)
        total = total + (piece if g == 0 else pltpu.roll(piece, 2 * QB - 8 * g, 1))
    return total


def lines_of(folded, heads, blocks):
    moved = sum(jnp.roll(folded[:, s, :], -s, axis=1) for s in range(8))
    moved = moved.reshape(heads, blocks, 2, QB)
    ahead = jnp.concatenate([moved[:, 1:, 1], jnp.zeros((heads, 1, QB), jnp.float32)], axis=1)
    return (moved[:, :, 0] + ahead).reshape(heads, blocks * QB)


def attend_back(line, segk, segq, rows, w, qkv, og, lse):
    seqs, _, seq_len = segq.shape
    heads = line.shape[0]
    inner = heads * DH
    blocks = seq_len // QB
    width = rows.shape[1]
    return pl.pallas_call(
        functools.partial(attend_back_kernel, heads, blocks, seqs),
        grid=(seqs,),
        in_specs=[
            pl.BlockSpec(line.shape, lambda s: (0, 0)),
            pl.BlockSpec((1, seq_len, 1), lambda s: (s, 0, 0)),
            pl.BlockSpec((1, 1, seq_len), lambda s: (s, 0, 0)),
            pl.BlockSpec((seq_len, width), lambda s: (s, 0)),
            pl.BlockSpec(w.shape, lambda s: (0, 0, 0)),
            pl.BlockSpec((3, seq_len, inner), lambda s: (0, s, 0)),
            pl.BlockSpec((seq_len, inner), lambda s: (s, 0)),
            pl.BlockSpec((1, heads, seq_len), lambda s: (s, 0, 0)),
        ],
        out_specs=[
            pl.BlockSpec((seq_len, width), lambda s: (s, 0)),
            pl.BlockSpec(w.shape, lambda s: (0, 0, 0)),
            pl.BlockSpec((heads * blocks, 8, 2 * QB), lambda s: (0, 0, 0)),
        ],
        out_shape=[
            jax.ShapeDtypeStruct((seqs * seq_len, width), jnp.bfloat16),
            jax.ShapeDtypeStruct(w.shape, jnp.float32),
            jax.ShapeDtypeStruct((heads * blocks, 8, 2 * QB), jnp.float32),
        ],
        scratch_shapes=[
            pltpu.VMEM((heads, blocks, QB, QB), jnp.float32),
            pltpu.VMEM((heads, blocks, QB, QB), jnp.float32),
            pltpu.VMEM((seq_len, DH), jnp.float32),
            pltpu.VMEM((seq_len, DH), jnp.float32),
            pltpu.VMEM((seq_len, 3 * inner), jnp.bfloat16),
        ],
        compiler_params=pltpu.CompilerParams(vmem_limit_bytes=48 << 20),
        cost_estimate=pl.CostEstimate(flops=20_000_000_000, bytes_accessed=16 << 20, transcendentals=4_000_000),
        name="attend_back",
    )(line, segk, segq, rows, w, qkv, og, lse)


def mask_inputs(segments, padding):
    keyed = jnp.where(padding == 1, segments, -1)
    return keyed[:, :, None], segments[:, None, :]


def line_of(by_distance):
    return jnp.concatenate([jnp.full((by_distance.shape[0], QB), NEGATIVE, jnp.float32), by_distance], axis=1)


FT = 512
ROOT_2_PI = math.sqrt(2.0 / math.pi)


def gelu_pair(x):
    square = x * x
    t = jnp.tanh(ROOT_2_PI * x * (1.0 + 0.044715 * square))
    half = 0.5 * (1.0 + t)
    slope = half + 0.5 * x * (1.0 - t * t) * (ROOT_2_PI * (1.0 + 3 * 0.044715 * square))
    return x * half, slope


def expert_kernel(steps, x_ref, g_ref, up_ref, down_ref, act_ref, pre_ref, back_ref, dot_ref, total, dots):
    step = pl.program_id(0)

    @pl.when(step == 0)
    def _():
        total[...] = jnp.zeros_like(total)
        dots[...] = jnp.zeros_like(dots)

    rows = x_ref.shape[0]
    chunk = 256
    for lower in range(0, rows, chunk):
        part = slice(lower, lower + chunk)
        pre = mm(x_ref[part], up_ref[...], NT)
        out_side = mm(g_ref[part], down_ref[...], NT)
        act, slope = gelu_pair(pre)
        low = act.astype(jnp.bfloat16)
        act_ref[part] = low
        product = low.astype(jnp.float32) * out_side
        dots[part] += sum(product[:, k : k + 128] for k in range(0, FT, 128))
        back = (out_side * slope).astype(jnp.bfloat16)
        pre_ref[part] = back
        total[part] += mm(back, up_ref[...], NN)

    @pl.when(step == steps - 1)
    def _():
        back_ref[...] = total[...].astype(jnp.bfloat16)
        dot_ref[...] = lax.dot_general(
            jnp.ones((8, 128), jnp.float32), dots[...], NT,
            precision=HIGHEST, preferred_element_type=jnp.float32)


def expert_first(x, g, up, down):
    rows, width = x.shape
    hidden = up.shape[0]
    steps = hidden // FT
    whole = lambda f: (0, 0)
    return pl.pallas_call(
        functools.partial(expert_kernel, steps),
        grid=(steps,),
        in_specs=[
            pl.BlockSpec((rows, width), whole),
            pl.BlockSpec((rows, width), whole),
            pl.BlockSpec((FT, width), lambda f: (f, 0)),
            pl.BlockSpec((FT, width), lambda f: (f, 0)),
        ],
        out_specs=[
            pl.BlockSpec((rows, FT), lambda f: (0, f)),
            pl.BlockSpec((rows, FT), lambda f: (0, f)),
            pl.BlockSpec((rows, width), whole),
            pl.BlockSpec((8, rows), whole),
        ],
        out_shape=[
            jax.ShapeDtypeStruct((rows, hidden), jnp.bfloat16),
            jax.ShapeDtypeStruct((rows, hidden), jnp.bfloat16),
            jax.ShapeDtypeStruct((rows, width), jnp.bfloat16),
            jax.ShapeDtypeStruct((8, rows), jnp.float32),
        ],
        scratch_shapes=[
            pltpu.VMEM((rows, width), jnp.float32),
            pltpu.VMEM((rows, 128), jnp.float32),
        ],
        compiler_params=pltpu.CompilerParams(vmem_limit_bytes=48 << 20),
        cost_estimate=pl.CostEstimate(
            flops=6 * rows * width * hidden, bytes_accessed=32 << 20, transcendentals=rows * hidden),
        name="expert_first",
    )(x, g, up, down)


def expert_late_kernel(steps, x_ref, g_ref, gate_ref, act_ref, pre_ref, down_ref,
                       out_ref, up_grad_ref, down_grad_ref, total, x_gated, g_gated):
    step = pl.program_id(0)

    @pl.when(step == 0)
    def _():
        total[...] = jnp.zeros_like(total)
        gate = gate_ref[...]
        x_gated[...] = (x_ref[...].astype(jnp.float32) * gate).astype(jnp.bfloat16)
        g_gated[...] = (g_ref[...].astype(jnp.float32) * gate).astype(jnp.bfloat16)

    up_grad_ref[...] = mm(pre_ref[...], x_gated[...], TN).astype(up_grad_ref.dtype)
    down_grad_ref[...] = mm(act_ref[...], g_gated[...], TN).astype(down_grad_ref.dtype)
    total[...] += mm(act_ref[...], down_ref[...], NN)

    @pl.when(step == steps - 1)
    def _():
        out_ref[...] = total[...].astype(jnp.bfloat16)


def expert_late(x, g, gate, act, pre, down):
    rows, width = x.shape
    hidden = down.shape[0]
    steps = hidden // FT
    whole = lambda f: (0, 0)
    tile = pl.BlockSpec((FT, width), lambda f: (f, 0))
    return pl.pallas_call(
        functools.partial(expert_late_kernel, steps),
        grid=(steps,),
        in_specs=[
            pl.BlockSpec((rows, width), whole),
            pl.BlockSpec((rows, width), whole),
            pl.BlockSpec((rows, 1), whole),
            pl.BlockSpec((rows, FT), lambda f: (0, f)),
            pl.BlockSpec((rows, FT), lambda f: (0, f)),
            tile,
        ],
        out_specs=[pl.BlockSpec((rows, width), whole), tile, tile],
        out_shape=[
            jax.ShapeDtypeStruct((rows, width), jnp.bfloat16),
            jax.ShapeDtypeStruct((hidden, width), jnp.bfloat16),
            jax.ShapeDtypeStruct((hidden, width), jnp.bfloat16),
        ],
        scratch_shapes=[
            pltpu.VMEM((rows, width), jnp.float32),
            pltpu.VMEM((rows, width), jnp.bfloat16),
            pltpu.VMEM((rows, width), jnp.bfloat16),
        ],
        compiler_params=pltpu.CompilerParams(vmem_limit_bytes=48 << 20),
        cost_estimate=pl.CostEstimate(
            flops=6 * rows * width * hidden, bytes_accessed=32 << 20, transcendentals=0),
        name="expert_late",
    )(x, g, gate, act, pre, down)


MESH = pl.DeviceIdType.MESH
VMEM_LIMIT = 61 << 20


def remote(src, dst, send, recv, axis, place):
    return pltpu.make_async_remote_copy(
        src_ref=src, dst_ref=dst, send_sem=send, recv_sem=recv, device_id={axis: place}, device_id_type=MESH
    )


def each_peer(count, step, start=1):
    if count <= 8:
        for r in range(start, count):
            step(r)
    else:
        def one(r, carry):
            step(r)
            return carry
        lax.fori_loop(start, count, one, 0)


def peer(r):
    return jnp.bitwise_xor(lax.axis_index("dp"), r)


def greet(dp_count, tensor_count):
    barrier = pltpu.get_barrier_semaphore()
    dp, tp = lax.axis_index("dp"), lax.axis_index("tensor")
    for r in range(1, tensor_count):
        pl.semaphore_signal(barrier, inc=1, device_id={"tensor": lax.rem(tp + r, tensor_count)}, device_id_type=MESH)

    def signal(r):
        pl.semaphore_signal(barrier, inc=1, device_id={"dp": peer(r)}, device_id_type=MESH)
    each_peer(dp_count, signal)
    return lambda: pl.semaphore_wait(barrier, tensor_count - 1 + dp_count - 1)


def partners(tensor_count):
    tp = lax.axis_index("tensor")
    sib = tp + 1 - 2 * lax.rem(tp, 2)
    return tp, sib, lax.rem(tp + 2, tensor_count), lax.rem(sib + 2, tensor_count)


def place_pairs(routes_ref, live, experts, capacity, cap_rows):
    tokens = live.shape[1]
    live = live == 1
    ids = lax.broadcasted_iota(jnp.int32, (experts, tokens), 0)
    row = lax.broadcasted_iota(jnp.int32, (tokens, tokens), 0)
    col = lax.broadcasted_iota(jnp.int32, (tokens, tokens), 1)
    before = (row < col).astype(jnp.float32).astype(jnp.bfloat16)
    slots = []
    base = jnp.zeros((experts, 1), jnp.float32)
    for k in range(2):
        route = routes_ref[k : k + 1, :]
        hot = jnp.where((ids == route) & live, 1.0, 0.0)
        count = mm(hot.astype(jnp.bfloat16), before, NN) + base
        place = jnp.sum(count * hot, axis=0, keepdims=True).astype(jnp.int32)
        slots.append(jnp.where(live & (place < capacity), route * cap_rows + place, -1))
        base = base + jnp.sum(hot, axis=1, keepdims=True)
    return slots


def chosen(first, second, expert, cap_rows):
    ids = lax.broadcasted_iota(jnp.int32, (cap_rows, first.shape[1]), 0) + expert * cap_rows
    return jnp.where((ids == first) | (ids == second), 1.0, 0.0).astype(jnp.bfloat16)


def attend_sequence(heads, blocks, seq, line_tiles, segk_ref, segq_ref, qkv, heads_out, lse_ref):
    scale = 1.0 / math.sqrt(DH)
    half = blocks // 2
    for qb in range(blocks):
        nk = (qb + 1) * QB
        lower = qb * QB
        for h in range(heads):
            cols = [slice((3 * h + c) * DH, (3 * h + c + 1) * DH) for c in range(3)]
            query = (qkv[seq, lower : lower + QB, cols[0]].astype(jnp.float32) * scale).astype(jnp.bfloat16)
            parts = score_block(qkv[seq, 0:nk, cols[1]], query, line_tiles, h, qb, segk_ref.at[seq], segq_ref.at[pl.ds(seq, 1)])
            peak = functools.reduce(jnp.maximum, [jnp.max(x, axis=0, keepdims=True) for x in parts])
            probs = [jnp.exp(x - peak) for x in parts]
            total = functools.reduce(jnp.add, [jnp.sum(x, axis=0, keepdims=True) for x in probs])
            mixed = functools.reduce(jnp.add, [
                mm(qkv[seq, kb * QB : (kb + 1) * QB, cols[2]], x.astype(jnp.bfloat16), TN)
                for kb, x in enumerate(probs)])
            heads_out[seq * 2 + qb // half, h * DH : (h + 1) * DH, (qb % half) * QB : (qb % half + 1) * QB] = (
                mixed / total).astype(jnp.bfloat16)
            lse_ref[seq, h : h + 1, lower : lower + QB] = peak + jnp.log(total)


def packed_gather(own_ref, all_ref, send, recv, dp_count):
    dp = lax.axis_index("dp")
    side = peer(1)
    columns = dp_count // 2
    near = remote(own_ref, all_ref.at[dp], send.at[0], recv.at[0], "dp", side)
    out = [remote(own_ref, all_ref.at[dp], send.at[k], recv.at[k], "dp", peer(2 * k))
           for k in range(1, columns)]
    onward = []
    for k in range(1, columns):
        src = peer(2 * k)
        n = columns - 1 + k
        onward.append(remote(all_ref.at[src], all_ref.at[src], send.at[n], recv.at[n], "dp", side))
    return near, out, onward


def prepare(heads, tp, table_ref, bucket_ref, segments_ref, padding_ref, line_ref, segk_ref):
    buckets, length = table_ref.shape[1], bucket_ref.shape[1]
    ids = lax.broadcasted_iota(jnp.int32, (buckets, length), 0)
    hot = ids == bucket_ref[...]
    for h in range(heads):
        column = to_column(table_ref[pl.ds(tp * heads + h, 1), :], buckets)
        line_ref[h : h + 1, :QB] = jnp.full((1, QB), NEGATIVE, jnp.float32)
        line_ref[h : h + 1, QB:] = jnp.sum(jnp.where(hot, column, 0.0), axis=0, keepdims=True)
    keyed = jnp.where(padding_ref[...] == 1, segments_ref[...], -1).astype(jnp.float32)
    for s in range(keyed.shape[0]):
        for k in range(length // QB):
            piece = keyed[s : s + 1, k * QB : (k + 1) * QB]
            segk_ref[s, k * QB : (k + 1) * QB, :] = to_column(piece, QB).astype(jnp.int32)


def front_kernel(sizes, x_ref, gain_ref, w_ref, outw_ref, down_ref, grad_ref, routes_ref, segments_ref, padding_ref,
                 table_ref, bucket_ref,
                 rows, w_all, outw_all, down_all, qkv, lse_ref, heads_all, slots_ref, cot, line_ref, segk_ref,
                 tiles, heads_out, cot_send, w_own,
                 far_send, far_recv, w_send, w_recv, ot_send, ot_recv,
                 dn_send, dn_recv, cot_s, cot_r, head_send, head_recv, local_sem):
    dp_count, tensor_count, experts, capacity, cap_rows, heads, blocks, gather_w = sizes
    dp = lax.axis_index("dp")
    tp, sib, opp, across = partners(tensor_count)
    wait_barrier = greet(dp_count, tensor_count)
    inner = heads * DH
    for h in range(heads):
        for c in range(3):
            n = (3 * h + c) * DH
            w_own[:, n : n + DH] = w_ref[c, :, h * DH : (h + 1) * DH]
    w_own[:, 3 * inner :] = outw_ref[...].T

    x = x_ref[...].astype(jnp.float32)
    r = lax.rsqrt(jnp.mean(x * x, axis=-1, keepdims=True) + EPSILON)
    rows[tp] = (x * r * gain_ref[...].reshape(1, x.shape[1])).astype(jnp.bfloat16)
    wait_barrier()

    half = rows.shape[1] // 2
    parts = [pl.ds(0, half), pl.ds(half, half)]
    far = [remote(rows.at[tp, p], rows.at[tp, p], far_send.at[k], far_recv.at[k], "tensor", opp) for k, p in enumerate(parts)]
    near = remote(rows.at[tp], rows.at[tp], far_send.at[2], far_recv.at[2], "tensor", sib)
    onward = [remote(rows.at[opp, p], rows.at[opp, p], far_send.at[3 + k], far_recv.at[3 + k], "tensor", sib) for k, p in enumerate(parts)]
    for c in far:
        c.start()
    near.start()

    w_near, w_out, w_on = packed_gather(w_own, w_all, w_send, w_recv, dp_count)
    for c in w_out:
        c.start()
    w_near.start()
    w_all[dp] = w_own[...]

    tokens = x_ref.shape[0]
    live = padding_ref[pl.ds(tp // 2, 1), pl.ds(pl.multiple_of(lax.rem(tp, 2) * tokens, 128), tokens)]
    first, second = place_pairs(routes_ref, live, experts, capacity, cap_rows)
    slots_ref[0:1, :] = first
    slots_ref[1:2, :] = second

    def cot_copy(r):
        to = peer(r)
        return remote(cot_send.at[to], cot.at[dp], cot_s.at[r], cot_r.at[r], "dp", to)

    def cot_fill(r):
        to = peer(r)
        cot_send[to] = mm(chosen(first, second, to, cap_rows), grad_ref[...], NN).astype(jnp.bfloat16)

    each_peer(dp_count, cot_fill)
    cot_fill(0)
    own_cot = pltpu.make_async_copy(cot_send.at[dp], cot.at[dp], local_sem.at[1])
    own_cot.start()

    each_peer(dp_count, lambda r: cot_copy(r).start())
    prepare(heads, tp, table_ref, bucket_ref, segments_ref, padding_ref, line_ref, segk_ref)
    build_bias(line_ref, tiles, heads, blocks)
    for c, on in zip(w_out, w_on):
        c.wait_recv()
        on.start()
    w_near.wait_recv()
    for c in w_on:
        c.wait_recv()
    near.wait_recv()

    width = rows.shape[2]
    own_seq = tp // 2
    packed = qkv.shape[2]

    def project(seq):
        tokens = rows[pl.ds(seq * 2, 2)].reshape(2 * rows.shape[1], width)
        weight = w_all[...].reshape(width, w_all.shape[2])[:, :packed]
        qkv[seq] = mm(tokens, weight, NN).astype(jnp.bfloat16)

    def head_copy(k, to):
        return remote(heads_out.at[to], heads_all.at[tp], head_send.at[k], head_recv.at[k], "tensor", to)

    part = pl.ds(0, 3 * down_ref.shape[0] // 4)
    down_far = remote(down_ref.at[part], down_all.at[tp, part], dn_send.at[0], dn_recv.at[0], "tensor", opp)
    down_near = remote(down_ref, down_all.at[tp], dn_send.at[1], dn_recv.at[1], "tensor", sib)
    down_on = remote(down_all.at[opp, part], down_all.at[opp, part], dn_send.at[2], dn_recv.at[2], "tensor", sib)

    project(own_seq)
    outw_all[tp] = w_all[...].reshape(width, w_all.shape[2])[:, 3 * inner :].T
    ot_far = remote(outw_all.at[tp], outw_all.at[tp], ot_send.at[0], ot_recv.at[0], "tensor", opp)
    ot_near = remote(outw_all.at[tp], outw_all.at[tp], ot_send.at[1], ot_recv.at[1], "tensor", sib)
    ot_on = remote(outw_all.at[opp], outw_all.at[opp], ot_send.at[2], ot_recv.at[2], "tensor", sib)
    for k in range(2):
        far[k].wait_recv()
        onward[k].start()
    ot_far.start()
    ot_near.start()
    down_far.start()
    down_near.start()
    attend_sequence(heads, blocks, own_seq, tiles, segk_ref, segments_ref, qkv, heads_out, lse_ref)
    head_copy(0, sib).start()
    heads_all[tp] = heads_out[tp]
    for k in range(2):
        onward[k].wait_recv()
    other = 1 - own_seq
    project(other)
    attend_sequence(heads, blocks, other, tiles, segk_ref, segments_ref, qkv, heads_out, lse_ref)
    ot_far.wait_recv()
    ot_on.start()
    head_copy(1, opp).start()
    head_copy(2, across).start()

    down_far.wait_recv()
    down_on.start()
    own_cot.wait()
    each_peer(dp_count, lambda r: cot_copy(r).wait())
    ot_on.wait()
    ot_near.wait()
    ot_far.wait_send()
    for c in [w_near] + w_out + w_on:
        c.wait_send()
    for c in far + [near] + onward:
        c.wait_send()
    head_copy(0, sib).wait()
    head_copy(1, opp).wait()
    head_copy(2, across).wait()
    down_far.wait_send()
    down_near.wait()
    down_on.wait()


def sems(*counts):
    out = []
    for n in counts:
        out += [pltpu.SemaphoreType.DMA((n,)), pltpu.SemaphoreType.DMA((n,))]
    return out


def front(sizes, x, gain, w, outw, down, grad, routes_t, segments, padding, table, bucket):
    dp_count, tensor_count, experts, capacity, cap_rows, heads, blocks, gather_w = sizes
    tokens, width = x.shape
    seq_len = blocks * QB
    seqs = tensor_count * tokens // seq_len
    inner = heads * DH
    packed = -(-3 * inner // 128) * 128
    vmem = pl.BlockSpec(memory_space=pltpu.VMEM)
    anywhere = pl.BlockSpec(memory_space=pl.ANY)
    shape = jax.ShapeDtypeStruct
    low = jnp.bfloat16
    return pl.pallas_call(
        functools.partial(front_kernel, sizes),
        in_specs=[vmem] * 4 + [anywhere] + [vmem] * 6,
        out_specs=[vmem] * 3 + [anywhere] + [vmem] * 4 + [anywhere] + [vmem] * 2,
        out_shape=[
            shape((tensor_count, tokens, width), low),
            shape((dp_count, w.shape[1], 4 * inner), low),
            shape((tensor_count, inner, width), low),
            shape((tensor_count,) + down.shape, low),
            shape((seqs, seq_len, packed), low),
            shape((seqs, heads, seq_len), jnp.float32),
            shape((tensor_count, inner, tokens), low),
            shape((8, tokens), jnp.int32),
            shape((experts, cap_rows, width), low),
            shape((heads, QB + seq_len), jnp.float32),
            shape((seqs, seq_len, 1), jnp.int32),
        ],
        scratch_shapes=[
            pltpu.VMEM((heads, blocks, QB, QB), jnp.float32),
            pltpu.VMEM((tensor_count, inner, tokens), low),
            pltpu.VMEM((experts, cap_rows, width), low),
            pltpu.VMEM((w.shape[1], 4 * inner), low),
        ] + sems(5, dp_count, 3, 3, dp_count, 3) + [pltpu.SemaphoreType.DMA((3,))],
        compiler_params=pltpu.CompilerParams(
            vmem_limit_bytes=VMEM_LIMIT, collective_id=1, has_side_effects=True),
        cost_estimate=pl.CostEstimate(flops=20_000_000_000, bytes_accessed=20 << 20, transcendentals=4_000_000),
        name="front",
    )(x, gain, w, outw, down, grad, routes_t, segments, padding, table, bucket)


def to_row(column, lanes):
    n = column.shape[0]
    row = lax.broadcasted_iota(jnp.int32, (n, lanes), 0)
    col = lax.broadcasted_iota(jnp.int32, (n, lanes), 1)
    return jnp.sum(jnp.where(row == col, column, 0.0), axis=0, keepdims=True)


def to_column(row_values, n):
    lanes = row_values.shape[1]
    row = lax.broadcasted_iota(jnp.int32, (n, lanes), 0)
    col = lax.broadcasted_iota(jnp.int32, (n, lanes), 1)
    return jnp.sum(jnp.where(row == col, row_values, 0.0), axis=1, keepdims=True)


def gate_map(first, second, gate_first, gate_second, expert, cap_rows):
    ids = lax.broadcasted_iota(jnp.int32, (cap_rows, first.shape[1]), 0) + expert * cap_rows
    return jnp.where(ids == first, gate_first, jnp.where(ids == second, gate_second, 0.0))


def gated_rows(weights, rows):
    high = weights.astype(jnp.bfloat16)
    low = (weights - high.astype(jnp.float32)).astype(jnp.bfloat16)
    return mm(high, rows, TN) + mm(low, rows, TN)


def middle_kernel(sizes, x_ref, grad_ref, heads_ref, outw_ref, gain_ref, router_ref, routes_ref, padding_ref,
                  slots_ref, cot_ref, up_ref, down_own_ref, down_ref,
                  up_pair, up_own, up_land, down_own, down_land, produced, landed_first, middle, middle_grad, heads_grad, out_part, stats, gates,
                  up, down, g_rows, x_rows, act, side, back_send, back, gate_send, gate_rows,
                  dot_send, dot_rows, moe_low, stage, down_pair,
                  up_s, up_r, x_s, x_r, b_s, b_r, g_s, g_r, d_s, d_r, a_s, a_r, p_s, p_r, load_sem):
    dp_count, tensor_count, experts, capacity, cap_rows, heads, blocks, gather_w = sizes
    dp = lax.axis_index("dp")
    tp, sib, opp, across = partners(tensor_count)
    hidden = up.shape[1]
    x_send = produced
    total = middle_grad
    tokens, width = x_ref.shape
    lanes = gate_send.shape[2]
    wait_barrier = greet(dp_count, tensor_count)

    load_g = pltpu.make_async_copy(cot_ref, g_rows, load_sem.at[0])
    early, late = pl.ds(0, 3 * hidden // 4), pl.ds(3 * hidden // 4, hidden // 4)
    load_down = [
        pltpu.make_async_copy(down_own_ref, down.at[tp], load_sem.at[1]),
        pltpu.make_async_copy(down_ref.at[sib], down.at[sib], load_sem.at[5]),
        pltpu.make_async_copy(down_ref.at[opp, early], down.at[opp, early], load_sem.at[6]),
        pltpu.make_async_copy(down_ref.at[across, early], down.at[across, early], load_sem.at[7]),
    ]
    load_up = pltpu.make_async_copy(up_ref, up.at[tp], load_sem.at[2])
    load_g.start()
    for c in load_down:
        c.start()
    load_up.start()

    mixed = x_ref[...].astype(jnp.float32)
    for t in range(tensor_count):
        mixed = mixed + mm(heads_ref[t], outw_ref[t], TN)
    middle[...] = mixed
    r = lax.rsqrt(jnp.mean(mixed * mixed, axis=-1, keepdims=True) + EPSILON)
    moe_low[...] = (mixed * r * gain_ref[...].reshape(1, width)).astype(jnp.bfloat16)
    first, second = slots_ref[0:1, :], slots_ref[1:2, :]
    wait_barrier()

    rest_far = remote(down_own_ref.at[late], down.at[tp, late], up_s.at[3], up_r.at[3], "tensor", opp)
    rest_on = remote(down.at[opp, late], down.at[opp, late], up_s.at[4], up_r.at[4], "tensor", sib)
    up_far = remote(up_ref, up.at[tp], up_s.at[0], up_r.at[0], "tensor", opp)
    up_near = remote(up_ref, up.at[tp], up_s.at[1], up_r.at[1], "tensor", sib)
    up_on = remote(up.at[opp], up.at[opp], up_s.at[2], up_r.at[2], "tensor", sib)
    rest_far.start()
    up_far.start()
    up_near.start()

    def x_copy(r):
        to = peer(r)
        return remote(x_send.at[to], x_rows.at[dp], x_s.at[r], x_r.at[r], "dp", to)

    held = dp_count - 2
    for r in list(range(dp_count // 2, dp_count)) + list(range(1, dp_count // 2)):
        to = peer(r)
        x_send[to] = mm(chosen(first, second, to, cap_rows), moe_low[...], NN).astype(jnp.bfloat16)
        if r < held:
            x_copy(r).start()
    x_rows[dp] = mm(chosen(first, second, dp, cap_rows), moe_low[...], NN).astype(jnp.bfloat16)


    ids = lax.broadcasted_iota(jnp.int32, (experts, tokens), 0)
    pick_first, pick_second = ids == routes_ref[0:1, :], ids == routes_ref[1:2, :]
    live = padding_ref[pl.ds(tp // 2, 1), pl.ds(pl.multiple_of(lax.rem(tp, 2) * tokens, 128), tokens)]
    live = (live == 1).astype(jnp.float32)
    logits = mm(router_ref[...], moe_low[...], NT)
    gap = jnp.sum(jnp.where(pick_first, logits, 0.0) - jnp.where(pick_second, logits, 0.0), axis=0, keepdims=True)
    gate_first = live / (1.0 + jnp.exp(-gap))
    gate_second = live / (1.0 + jnp.exp(gap))
    gates[0:1, :] = gate_first
    gates[1:2, :] = gate_second

    def gate_copy(r):
        to = peer(r)
        return remote(gate_send.at[to], gate_rows.at[dp], g_s.at[r], g_r.at[r], "dp", to)

    def gate_fill(r):
        to = peer(r)
        column = jnp.sum(gate_map(first, second, gate_first, gate_second, to, cap_rows), axis=1, keepdims=True)
        return jnp.broadcast_to(to_row(column, lanes), (8, lanes))

    def gate_go(r):
        gate_send[peer(r)] = gate_fill(r)
        gate_copy(r).start()
    each_peer(dp_count, gate_go)
    gate_rows[dp] = gate_fill(0)

    load_g.wait()
    rest_far.wait_recv()
    rest_on.start()
    for c in load_down:
        c.wait()
    rest_on.wait_recv()
    slots = experts * cap_rows
    block = slots // 4

    def side_block(k, carry):
        part = pl.ds(pl.multiple_of(k * block, 16), block)
        here = g_rows[pl.ds(k * (experts // 4), experts // 4)].reshape(block, width)
        for t in range(tensor_count):
            side[part, t * hidden : (t + 1) * hidden] = mm(here, down[t], NT).astype(jnp.bfloat16)
        return carry
    lax.fori_loop(0, 4, side_block, 0)

    for r in range(dp_count // 2, held):
        x_copy(r).wait_send()
    for r in range(held, dp_count):
        x_copy(r).start()
    load_up.wait()
    up_far.wait_recv()
    up_on.start()
    up_near.wait_recv()
    up_on.wait_recv()

    def back_copy(r):
        to = peer(r)
        return remote(back_send.at[to], back.at[dp], b_s.at[r], b_r.at[r], "dp", to)

    def dot_copy(r):
        to = peer(r)
        return remote(dot_send.at[to], dot_rows.at[dp], d_s.at[r], d_r.at[r], "dp", to)

    group = max(1, min(dp_count, 320 // cap_rows))

    def first_pass(step, carry):
        rounds = [step * group + k for k in range(group)]
        froms = [peer(r) for r in rounds]
        for k, r in enumerate(rounds):
            if k == 0:
                @pl.when(r > 0)
                def _():
                    x_copy(r).wait_recv()
            else:
                x_copy(r).wait_recv()
        here = jnp.concatenate([x_rows[s] for s in froms], axis=0)
        total_back = jnp.zeros((group * cap_rows, width), jnp.float32)
        dots = jnp.zeros((group * cap_rows, 128), jnp.float32)
        for t in range(tensor_count):
            cols = slice(t * hidden, (t + 1) * hidden)
            pre = mm(here, up[t], NT)
            value, slope = gelu_pair(pre)
            low = value.astype(jnp.bfloat16)
            places = [pl.ds(pl.multiple_of(s * cap_rows, 16), cap_rows) for s in froms]
            beside = jnp.concatenate([side[p, cols] for p in places], axis=0).astype(jnp.float32)
            product = low.astype(jnp.float32) * beside
            dots = dots + sum(product[:, k : k + 128] for k in range(0, hidden, 128))
            grad = (beside * slope).astype(jnp.bfloat16)
            for k, p in enumerate(places):
                piece = slice(k * cap_rows, (k + 1) * cap_rows)
                act[p, cols] = low[piece]
                side[p, cols] = grad[piece]
            total_back = total_back + mm(grad, up[t], NN)
        column = jnp.sum(dots, axis=1, keepdims=True)
        for k, (r, s) in enumerate(zip(rounds, froms)):
            piece = slice(k * cap_rows, (k + 1) * cap_rows)
            low = total_back[piece].astype(jnp.bfloat16)
            line = jnp.broadcast_to(to_row(column[piece], lanes), (8, lanes))

            def send():
                back_send[s] = low
                dot_send[s] = line
                back_copy(r).start()
                dot_copy(r).start()

            def keep():
                back[dp] = low
                dot_rows[dp] = line
            if k == 0:
                pl.when(r > 0)(send)
                pl.when(r == 0)(keep)
            else:
                send()
        return carry
    lax.fori_loop(0, dp_count // group, first_pass, 0)

    each_peer(dp_count, lambda r: gate_copy(r).wait_recv())

    def gate_rows_in(s, carry):
        column = to_column(gate_rows[s, 0:1, :], cap_rows)
        x_rows[s] = (x_rows[s].astype(jnp.float32) * column).astype(jnp.bfloat16)
        g_rows[s] = (g_rows[s].astype(jnp.float32) * column).astype(jnp.bfloat16)
        return carry
    lax.fori_loop(0, experts, gate_rows_in, 0)

    for r in list(range(1, dp_count // 2)) + list(range(held, dp_count)):
        x_copy(r).wait_send()
    lands = ((down_pair, down_own), (up_pair, up_own))
    aside = [remote(stage.at[k], lands[k][n], a_s.at[2 * k + n], a_r.at[2 * k + n], "tensor", sib)
             for k in range(2) for n in range(2)]
    across_out = [remote(down_pair, down_land, a_s.at[4], a_r.at[4], "tensor", opp),
                  remote(up_pair.at[pl.ds(0, hidden // 4)], up_land, a_s.at[5], a_r.at[5], "tensor", opp)]
    piece = hidden // 2
    shards = (across, sib, opp, tp)
    sources = ((act, g_rows), (side, x_rows))
    for k, n in ((0, 0), (0, 2), (1, 0), (1, 2), (0, 1), (1, 1), (0, 3), (1, 3)):
        left, right = sources[k]
        if n == 1:
            aside[2 * k].wait_send()
        if n >= 2:
            aside[2 * k + n - 2].wait_recv()
        for m in range(2):
            cols = pl.ds(pl.multiple_of(shards[n] * hidden + m * piece, 128), piece)
            part = pl.ds(m * piece, piece)
            tile = mm(left[:, cols], right[...].reshape(slots, width), TN)
            if n < 2:
                stage[k, part, :] = tile.astype(jnp.bfloat16)
            else:
                land = lands[k][n - 2]
                land[part, :] = (tile + land[part, :].astype(jnp.float32)).astype(jnp.bfloat16)
        if n < 2:
            aside[2 * k + n].start()
        elif n == 2:
            across_out[k].start()

    def produce(k, carry):
        part = pl.ds(pl.multiple_of(k * block, 16), block)
        out = jnp.zeros((block, width), jnp.float32)
        for t in range(tensor_count):
            out = out + mm(act[part, t * hidden : (t + 1) * hidden], down[t], NN)
        out = out.astype(jnp.bfloat16)
        for e in range(experts // 4):
            produced[k * (experts // 4) + e] = out[e * cap_rows : (e + 1) * cap_rows]
        return carry
    lax.fori_loop(0, 4, produce, 0)

    def p_copy(k):
        to = peer(dp_count // 2 + k)
        return remote(produced.at[to], landed_first.at[k], p_s.at[k], p_r.at[k], "dp", to)
    for k in range(landed_first.shape[0]):
        p_copy(k).start()

    total[...] = jnp.zeros_like(total)

    def combine(r, carry):
        dot_first, dot_second = carry
        e = peer(r)

        @pl.when(r > 0)
        def _():
            back_copy(r).wait_recv()
            dot_copy(r).wait_recv()
        weights = gate_map(first, second, gate_first, gate_second, e, cap_rows)
        total[...] += gated_rows(weights, back[e])
        column = to_column(dot_rows[e, 0:1, :], cap_rows)
        ids = lax.broadcasted_iota(jnp.int32, (cap_rows, tokens), 0) + e * cap_rows
        dot_first = dot_first + jnp.sum(jnp.where(ids == first, column, 0.0), axis=0, keepdims=True)
        dot_second = dot_second + jnp.sum(jnp.where(ids == second, column, 0.0), axis=0, keepdims=True)
        return dot_first, dot_second
    zero_row = jnp.zeros((1, tokens), jnp.float32)
    dot_first, dot_second = lax.fori_loop(0, dp_count, combine, (zero_row, zero_row))

    change = gate_first * gate_second * (dot_first - dot_second)
    logit_grad = (jnp.where(pick_first, change, 0.0) - jnp.where(pick_second, change, 0.0)).astype(jnp.bfloat16)
    norm_grad = total[...] + mm(logit_grad, router_ref[...], TN)
    mixed = middle[...]
    r = lax.rsqrt(jnp.mean(mixed * mixed, axis=-1, keepdims=True) + EPSILON)
    u = mixed * r
    du = norm_grad * gain_ref[...].reshape(1, width)
    grad = grad_ref[...].astype(jnp.float32) + r * (du - u * jnp.mean(du * u, axis=-1, keepdims=True))
    middle_grad[...] = grad
    low = grad.astype(jnp.bfloat16)
    for t in range(tensor_count):
        heads_grad[t] = mm(outw_ref[t], low, NT).astype(jnp.bfloat16)
        out_part[t] = mm(heads_ref[t], low, NN).astype(jnp.bfloat16)
    stats[0:8, :] = jnp.broadcast_to(jnp.sum(norm_grad * u, axis=0, keepdims=True), (8, width))
    stats[8:, :] = mm(logit_grad, moe_low[...], NN)

    for c in across_out:
        c.wait_recv()
    for c in across_out:
        c.wait_send()
    for k in range(2):
        aside[2 * k + 1].wait_send()
    up_far.wait_send()
    rest_far.wait_send()
    rest_on.wait_send()
    up_near.wait_send()
    up_on.wait_send()

    def drain(r):
        gate_copy(r).wait_send()
        back_copy(r).wait_send()
        dot_copy(r).wait_send()
    each_peer(dp_count, drain)
    for k in range(landed_first.shape[0]):
        p_copy(k).wait()


def middle_pass(sizes, x, grad, heads_all, outw, gain, router_t, routes_t, padding, slot_rows, cot, up, down, down_all):
    dp_count, tensor_count, experts, capacity, cap_rows, heads, blocks, gather_w = sizes
    tokens, width = x.shape
    inner = heads * DH
    hidden = up.shape[0]
    slots = experts * cap_rows
    lanes = -(-cap_rows // 128) * 128
    vmem = pl.BlockSpec(memory_space=pltpu.VMEM)
    anywhere = pl.BlockSpec(memory_space=pl.ANY)
    shape = jax.ShapeDtypeStruct
    low = jnp.bfloat16
    return pl.pallas_call(
        functools.partial(middle_kernel, sizes),
        in_specs=[vmem] * 9 + [anywhere] * 4,
        out_specs=[vmem] * 13,
        out_shape=[
            shape((hidden, width), low),
            shape((hidden, width), low),
            shape((hidden // 4, width), low),
            shape((hidden, width), low),
            shape((hidden, width), low),
            shape((experts, cap_rows, width), low),
            shape((1, cap_rows, width), low),
            shape((tokens, width), jnp.float32),
            shape((tokens, width), jnp.float32),
            shape((tensor_count, inner, tokens), low),
            shape((tensor_count, inner, width), low),
            shape((8 + experts, width), jnp.float32),
            shape((8, tokens), jnp.float32),
        ],
        scratch_shapes=[
            pltpu.VMEM((tensor_count, hidden, width), low),
            pltpu.VMEM((tensor_count, hidden, width), low),
            pltpu.VMEM((experts, cap_rows, width), low),
            pltpu.VMEM((experts, cap_rows, width), low),
            pltpu.VMEM((slots, tensor_count * hidden), low),
            pltpu.VMEM((slots, tensor_count * hidden), low),
            pltpu.VMEM((experts, cap_rows, width), low),
            pltpu.VMEM((experts, cap_rows, width), low),
            pltpu.VMEM((experts, 8, lanes), jnp.float32),
            pltpu.VMEM((experts, 8, lanes), jnp.float32),
            pltpu.VMEM((experts, 8, lanes), jnp.float32),
            pltpu.VMEM((experts, 8, lanes), jnp.float32),
            pltpu.VMEM((tokens, width), low),
            pltpu.VMEM((2, hidden, width), low),
            pltpu.VMEM((hidden, width), low),
        ] + sems(5, dp_count, dp_count, dp_count, dp_count, 6, 2) + [pltpu.SemaphoreType.DMA((8,))],
        compiler_params=pltpu.CompilerParams(
            vmem_limit_bytes=VMEM_LIMIT, collective_id=2, has_side_effects=True),
        cost_estimate=pl.CostEstimate(
            flops=12 * slots * width * hidden * tensor_count, bytes_accessed=40 << 20, transcendentals=4_000_000),
        name="middle_pass",
    )(x, grad, heads_all, outw, gain, router_t, routes_t, padding, slot_rows, cot, up, down, down_all)


def attend_back_sequence(heads, blocks, seq, tiles, sums, segk_ref, segq_ref, qkv, grads, lse_ref, kg, vg, dq, chosen_heads):
    scale = 1.0 / math.sqrt(DH)
    half = blocks // 2
    for h in chosen_heads:
        cols, kcols, vcols = [slice((3 * h + c) * DH, (3 * h + c + 1) * DH) for c in range(3)]
        gcols = slice(h * DH, (h + 1) * DH)
        kg[...] = jnp.zeros_like(kg)
        vg[...] = jnp.zeros_like(vg)
        for qb in range(blocks):
            nk = (qb + 1) * QB
            lower = qb * QB
            query = (qkv[seq, lower : lower + QB, cols].astype(jnp.float32) * scale).astype(jnp.bfloat16)
            grad = grads[seq * 2 + qb // half, gcols, (qb % half) * QB : (qb % half + 1) * QB]
            lse = lse_ref[seq, h : h + 1, lower : lower + QB]
            parts = score_block(qkv[seq, 0:nk, kcols], query, tiles, h, qb, segk_ref.at[seq], segq_ref.at[pl.ds(seq, 1)])
            probs = [jnp.exp(x - lse) for x in parts]
            pg = mm(qkv[seq, 0:nk, vcols], grad, NN)
            pgs = [pg[kb * QB : (kb + 1) * QB] for kb in range(qb + 1)]
            delta = functools.reduce(jnp.add, [jnp.sum(p * g, axis=0, keepdims=True) for p, g in zip(probs, pgs)])
            dqt = jnp.zeros((DH, QB), jnp.float32)
            for kb in range(qb + 1):
                rows = slice(kb * QB, (kb + 1) * QB)
                sg = (probs[kb] * (pgs[kb] - delta)).astype(jnp.bfloat16)
                sums[h, qb - kb] += sg.astype(jnp.float32)
                vg[rows] += mm(probs[kb].astype(jnp.bfloat16), grad, NT)
                kg[rows] += mm(sg, query, NN)
                dqt = dqt + mm(qkv[seq, rows, kcols], sg, TN)
            dq[lower : lower + QB, cols] = (dqt * scale).T.astype(jnp.bfloat16)
        dq[:, kcols] = kg[...].astype(jnp.bfloat16)
        dq[:, vcols] = vg[...].astype(jnp.bfloat16)


def fold_lines(sums, h, blocks):
    moved = []
    for d in range(blocks):
        folded = fold_tile(sums, h, d)
        line = folded[0:1, :]
        for s in range(1, 8):
            line = line + pltpu.roll(folded[s : s + 1, :], 2 * QB - s, 1)
        moved.append(line)
    out = []
    for d in range(blocks):
        piece = moved[d][:, :QB]
        if d + 1 < blocks:
            piece = piece + moved[d + 1][:, QB:]
        out.append(piece)
    return jnp.concatenate(out, axis=1)


def two_stage_start(send, land, s_sem, r_sem, tensor_count):
    tp = lax.axis_index("tensor")
    copies = []
    for r in range(1, tensor_count):
        copies.append(remote(send, land.at[r - 1], s_sem.at[r], r_sem.at[r], "tensor", lax.rem(tp + r, tensor_count)))
    for c in copies:
        c.start()
    return copies


def last_kernel(sizes, x_ref, gain_ref, middle_ref, mgrad_ref, hgrad_ref, rows, w_ref, qkv, lse_ref, line_ref,
                segk_ref, segq_ref, produced_ref, slots_ref, gates_ref, early_ref, bucket_ref,
                out_part, first_ref, up_pair,
                out_ref, input_grad_ref, wgrad_ref, early_out, late_out, up_land,
                tiles, sums, kg, vg, dq, grads, landed, npart, near_land, far_land, pair, wsum, wsend, wland,
                early_land, early_mid, early_dp, late, late_land, late_mid, late_dp, total,
                out_land, out_pair, out_far,
                h_s, h_r, p_s, p_r, n_s, n_r, w_s, w_r, et_s, et_r, ed_s, ed_r, lt_s, lt_r, ld_s, ld_r, o_s, o_r):
    dp_count, tensor_count, experts, capacity, cap_rows, heads, blocks, gather_w = sizes
    dp = lax.axis_index("dp")
    tp, sib, opp, across = partners(tensor_count)
    tokens, width = x_ref.shape
    inner = heads * DH
    wait_barrier = greet(dp_count, tensor_count)
    build_bias(line_ref, tiles, heads, blocks)
    sums[...] = jnp.zeros_like(sums)
    dq[:, :, 3 * inner :] = jnp.zeros((2, dq.shape[1], dq.shape[2] - 3 * inner), jnp.bfloat16)
    own_seq = tp // 2
    other = 1 - own_seq
    wait_barrier()

    def h_copy(k, to):
        return remote(hgrad_ref.at[to], grads.at[tp], h_s.at[k], h_r.at[k], "tensor", to)
    h_copy(0, opp).start()
    h_copy(1, across).start()
    h_copy(2, sib).start()
    grads[tp] = hgrad_ref[tp]

    def p_copy(r):
        to = peer(r)
        return remote(produced_ref.at[to], landed.at[dp], p_s.at[r], p_r.at[r], "dp", to)
    sent = [r for r in range(1, dp_count) if not dp_count // 2 <= r < dp_count // 2 + first_ref.shape[0]]
    for r in sent:
        p_copy(r).start()

    early = two_stage_start(early_ref.at[pl.ds(8, experts)], early_land, et_s, et_r, tensor_count)

    def early_copy(r):
        return remote(early_mid, early_dp.at[r], ed_s.at[r], ed_r.at[r], "dp", peer(r))

    out_near = [remote(out_part.at[t], out_land.at[k], o_s.at[k], o_r.at[k], "tensor", sib)
                for k, t in enumerate((across, sib))]
    out_across = remote(out_pair, out_far, o_s.at[2], o_r.at[2], "tensor", opp)
    for c in out_near:
        c.start()

    up_rest = remote(up_pair.at[pl.ds(up_pair.shape[0] // 4, up_land.shape[0])], up_land, o_s.at[3], o_r.at[3],
                     "tensor", opp)

    def n_copy(k, src, dst, to):
        return remote(src, dst, n_s.at[k], n_r.at[k], "tensor", to)
    pair_near = n_copy(0, npart.at[across], near_land.at[0], sib)
    pair_far = n_copy(1, pair, far_land, opp)
    own_near = n_copy(2, npart.at[sib], near_land.at[1], sib)
    packed = dq.shape[2]
    own_rows = rows[pl.ds(own_seq * 2, 2)].reshape(2 * tokens, width)

    def attend_part(seq, k, chosen_heads):
        attend_back_sequence(heads, blocks, seq, tiles, sums, segk_ref, segq_ref, qkv, grads, lse_ref, kg, vg,
                             dq.at[k], chosen_heads)

    def norm_part(seq, k):
        here = rows[pl.ds(seq * 2, 2)].reshape(2 * tokens, width)
        norm = mm(dq[k], w_ref[...].reshape(width, w_ref.shape[2])[:, :packed], NT)
        column = jnp.sum(norm * here.astype(jnp.float32), axis=0, keepdims=True)
        low = norm.astype(jnp.bfloat16)
        npart[seq * 2] = low[:tokens]
        npart[seq * 2 + 1] = low[tokens:]
        return column

    share = width // dp_count
    side = peer(1)
    columns = dp_count // 2
    lanes = wsum.shape[1] // 2

    def share_rows(d):
        return pl.ds(pl.multiple_of(d * share, 8), share)

    def side_copy(m, k):
        n = 2 * columns * m + k
        return remote(wsend.at[n], wland.at[n], w_s.at[n], w_r.at[n], "dp", side)

    def column_copy(m, k):
        n = 2 * columns * m + columns + k
        return remote(wsend.at[n], wland.at[n], w_s.at[n], w_r.at[n], "dp", peer(2 * k))

    def side_go(m):
        for k in list(range(1, columns)) + [0]:
            there = share_rows(jnp.bitwise_xor(side, 2 * k))
            wsend[2 * columns * m + k] = wsum[there, m * lanes : (m + 1) * lanes].astype(jnp.bfloat16)
            side_copy(m, k).start()

    def column_go(m):
        for k in range(1, columns):
            side_copy(m, k).wait_recv()
            mine = wsum[share_rows(peer(2 * k)), m * lanes : (m + 1) * lanes]
            n = 2 * columns * m + columns + k
            wsend[n] = (mine + wland[2 * columns * m + k].astype(jnp.float32)).astype(jnp.bfloat16)
            column_copy(m, k).start()

    out_near[0].wait_recv()
    out_pair[...] = (out_part[opp].astype(jnp.float32) + out_land[0].astype(jnp.float32)).astype(jnp.bfloat16)
    out_across.start()
    h_copy(2, sib).wait_recv()
    attend_part(own_seq, 0, range(1))
    up_rest.start()
    h_copy(0, opp).wait_recv()
    h_copy(1, across).wait_recv()
    attend_part(other, 1, range(heads))
    gain_row = norm_part(other, 1)
    pair_near.start()
    wsum[:, :packed] = mm(rows[pl.ds(other * 2, 2)].reshape(2 * tokens, width), dq[1], TN)
    out_across.wait_recv()
    out_near[1].wait_recv()
    out_whole = out_part[tp].astype(jnp.float32) + out_land[1].astype(jnp.float32) + out_far[...].astype(jnp.float32)
    wsum[:, 3 * inner :] = out_whole.T
    pair_near.wait_recv()
    pair[...] = (npart[opp].astype(jnp.float32) + near_land[0].astype(jnp.float32)).astype(jnp.bfloat16)
    pair_far.start()
    attend_part(own_seq, 0, range(1, 2))
    wsum[:, :lanes] += mm(own_rows, dq[0, :, :lanes], TN)
    side_go(0)
    for c in early:
        c.wait_recv()
    early_mid[...] = early_ref[8:, :] + early_land[0] + early_land[1] + early_land[2]
    each_peer(dp_count, lambda r: early_copy(r).start())
    attend_part(own_seq, 0, range(2, heads))
    column_go(0)
    wsum[:, lanes : 3 * inner] += mm(own_rows, dq[0, :, lanes:packed], TN)[:, : 3 * inner - lanes]
    side_go(1)
    gain_row = gain_row + norm_part(own_seq, 0)
    own_near.start()

    gain_row = gain_row / gain_ref[...].reshape(1, width)
    late[...] = jnp.zeros_like(late)
    for k in range(width // 128):
        late[k : k + 1, :] = gain_row[:, k * 128 : (k + 1) * 128]
        late[8 + k : 9 + k, :] = early_ref[0:1, k * 128 : (k + 1) * 128]
    buckets = late.shape[0] - 16
    ids = lax.broadcasted_iota(jnp.int32, (buckets, bucket_ref.shape[1]), 0)
    hot = ids == bucket_ref[...]
    lane = lax.broadcasted_iota(jnp.int32, (buckets, 128), 1)
    table = jnp.zeros((buckets, 128), jnp.float32)
    for h in range(heads):
        column = jnp.sum(jnp.where(hot, fold_lines(sums, h, blocks), 0.0), axis=1, keepdims=True)
        table = table + jnp.where(lane == tp * heads + h, column, 0.0)
    late[16:, :] = table
    late_first = two_stage_start(late, late_land, lt_s, lt_r, tensor_count)

    def late_copy(r):
        return remote(late_mid, late_dp.at[r], ld_s.at[r], ld_r.at[r], "dp", peer(r))

    column_go(1)

    each_peer(dp_count, lambda r: early_copy(r).wait_recv())
    summed = early_mid[...]
    for r in range(1, dp_count):
        summed = summed + early_dp[r]
    early_out[...] = summed

    for c in late_first:
        c.wait_recv()
    late_mid[...] = late[...] + late_land[0] + late_land[1] + late_land[2]
    each_peer(dp_count, lambda r: late_copy(r).start())

    first, second = slots_ref[0:1, :], slots_ref[1:2, :]
    gate_first, gate_second = gates_ref[0:1, :], gates_ref[1:2, :]
    total[...] = middle_ref[...]

    def combine(e, rows_here):
        total[...] += gated_rows(gate_map(first, second, gate_first, gate_second, e, cap_rows), rows_here)
    combine(dp, produced_ref[dp])
    for k in range(first_ref.shape[0]):
        combine(peer(dp_count // 2 + k), first_ref[k])
    for r in sent:
        p_copy(r).wait_recv()
        combine(peer(r), landed[peer(r)])
    out_ref[...] = total[...]

    own_near.wait_recv()
    pair_far.wait_recv()
    norm_grad = npart[tp].astype(jnp.float32) + near_land[1].astype(jnp.float32) + far_land[...].astype(jnp.float32)
    x = x_ref[...].astype(jnp.float32)
    r = lax.rsqrt(jnp.mean(x * x, axis=-1, keepdims=True) + EPSILON)
    u = x * r
    du = norm_grad * gain_ref[...].reshape(1, width)
    input_grad_ref[...] = mgrad_ref[...] + r * (du - u * jnp.mean(du * u, axis=-1, keepdims=True))

    for m in range(2):
        half = slice(m * lanes, (m + 1) * lanes)
        side_copy(m, 0).wait_recv()
        part = wsum[share_rows(dp), half] + wland[2 * columns * m].astype(jnp.float32)
        for k in range(1, columns):
            column_copy(m, k).wait_recv()
            part = part + wland[2 * columns * m + columns + k].astype(jnp.float32)
        wgrad_ref[:, half] = part
    up_rest.wait_recv()

    each_peer(dp_count, lambda r: late_copy(r).wait_recv())
    summed = late_mid[...]
    for r in range(1, dp_count):
        summed = summed + late_dp[r]
    late_out[...] = summed

    for c in early + late_first + out_near + [out_across, pair_near, pair_far, own_near, h_copy(0, opp), h_copy(1, across), h_copy(2, sib)]:
        c.wait_send()

    def drain(r):
        early_copy(r).wait_send()
        late_copy(r).wait_send()
    each_peer(dp_count, drain)
    for r in sent:
        p_copy(r).wait_send()
    for m in range(2):
        for k in range(columns):
            side_copy(m, k).wait_send()
            if k:
                column_copy(m, k).wait_send()
    up_rest.wait_send()


def last_pass(sizes, x, gain, middle, middle_grad, heads_grad, rows, w, qkv, lse, line, segk, segq, produced,
              slot_rows, gates, early, bucket_row, out_part, landed_first, up_pair):
    dp_count, tensor_count, experts, capacity, cap_rows, heads, blocks, gather_w = sizes
    tokens, width = x.shape
    inner = heads * DH
    seq_len = blocks * QB
    share = width // dp_count
    vmem = pl.BlockSpec(memory_space=pltpu.VMEM)
    shape = jax.ShapeDtypeStruct
    low, full = jnp.bfloat16, jnp.float32
    late = 16 + NB
    packed = qkv.shape[2]
    return pl.pallas_call(
        functools.partial(last_kernel, sizes),
        in_specs=[vmem] * 20,
        out_specs=[vmem] * 6,
        out_shape=[
            shape((tokens, width), full),
            shape((tokens, width), full),
            shape((share, w.shape[2]), full),
            shape((experts, width), full),
            shape((late, 128), full),
            shape((3 * up_pair.shape[0] // 4, width), low),
        ],
        scratch_shapes=[
            pltpu.VMEM((heads, blocks, QB, QB), full),
            pltpu.VMEM((heads, blocks, QB, QB), full),
            pltpu.VMEM((seq_len, DH), full),
            pltpu.VMEM((seq_len, DH), full),
            pltpu.VMEM((2, seq_len, packed), low),
            pltpu.VMEM((tensor_count, inner, tokens), low),
            pltpu.VMEM((experts, cap_rows, width), low),
            pltpu.VMEM((tensor_count, tokens, width), low),
            pltpu.VMEM((2, tokens, width), low),
            pltpu.VMEM((tokens, width), low),
            pltpu.VMEM((tokens, width), low),
            pltpu.VMEM((width, w.shape[2]), full),
            pltpu.VMEM((2 * dp_count, share, w.shape[2] // 2), low),
            pltpu.VMEM((2 * dp_count, share, w.shape[2] // 2), low),
            pltpu.VMEM((tensor_count - 1, experts, width), full),
            pltpu.VMEM((experts, width), full),
            pltpu.VMEM((dp_count, experts, width), full),
            pltpu.VMEM((late, 128), full),
            pltpu.VMEM((tensor_count - 1, late, 128), full),
            pltpu.VMEM((late, 128), full),
            pltpu.VMEM((dp_count, late, 128), full),
            pltpu.VMEM((tokens, width), full),
            pltpu.VMEM((2, inner, width), low),
            pltpu.VMEM((inner, width), low),
            pltpu.VMEM((inner, width), low),
        ] + sems(3, dp_count, 3, 2 * dp_count, tensor_count, dp_count, tensor_count, dp_count, 4),
        compiler_params=pltpu.CompilerParams(
            vmem_limit_bytes=VMEM_LIMIT, collective_id=3, has_side_effects=True),
        cost_estimate=pl.CostEstimate(flops=30_000_000_000, bytes_accessed=30 << 20, transcendentals=4_000_000),
        name="last_pass",
    )(x, gain, middle, middle_grad, heads_grad, rows, w, qkv, lse, line, segk, segq, produced, slot_rows, gates,
      early, bucket_row, out_part, landed_first, up_pair)


def finish_kernel(out_ref, input_grad_ref, wgrad_ref, early_ref, late_ref, up_own, up_first, up_rest, down_own, down_land,
                  out, input_grad, w_qkv_grad, w_out_grad, table, gain_attn, gain_moe, router, up_grad, down_grad):
    out[...] = out_ref[...]
    input_grad[...] = input_grad_ref[...]
    land = jnp.where(pl.program_id(0) == 0, up_first[...].astype(jnp.float32), up_rest[...].astype(jnp.float32))
    up_grad[...] = up_own[...].astype(jnp.float32) + land
    down_grad[...] = down_own[...].astype(jnp.float32) + down_land[...].astype(jnp.float32)

    @pl.when(pl.program_id(0) == 0)
    def _():
        inner = w_qkv_grad.shape[2]
        for h in range(inner // DH):
            for c in range(3):
                n = (3 * h + c) * DH
                w_qkv_grad[c, :, h * DH : (h + 1) * DH] = wgrad_ref[:, n : n + DH]
        w_out_grad[...] = wgrad_ref[:, 3 * inner :].T
        table[...] = late_ref[16:, :].T[: table.shape[0], :]
        pieces = gain_attn.shape[0] // 128
        for base, gain in ((0, gain_attn), (8, gain_moe)):
            row = jnp.concatenate([late_ref[base + k : base + k + 1, :] for k in range(pieces)], axis=1)
            gain[...] = row.reshape(gain.shape)
        router[...] = early_ref[...]


def finish(heads_total, out, input_grad, wgrad, early, late, up_own, up_first, up_rest, down_own, down_land):
    steps = 4
    tokens, width = out.shape
    share = wgrad.shape[0]
    inner = wgrad.shape[1] // 4
    hidden = up_own.shape[0]
    full = jnp.float32
    shape = jax.ShapeDtypeStruct

    def rows(n):
        return pl.BlockSpec((n // steps, width), lambda s: (s, 0))

    def whole(*dims):
        return pl.BlockSpec(dims, lambda s: (0,) * len(dims))
    return pl.pallas_call(
        finish_kernel,
        grid=(steps,),
        in_specs=[rows(tokens), rows(tokens), whole(*wgrad.shape), whole(*early.shape), whole(*late.shape)]
        + [rows(hidden), whole(*up_first.shape),
           pl.BlockSpec((hidden // steps, width), lambda s: (jnp.maximum(s - 1, 0), 0))] + [rows(hidden)] * 2,
        out_specs=[rows(tokens), rows(tokens), whole(3, share, inner), whole(inner, share), whole(heads_total, NB),
                   whole(width), whole(width), whole(*early.shape), rows(hidden), rows(hidden)],
        out_shape=[shape((tokens, width), full), shape((tokens, width), full), shape((3, share, inner), full),
                   shape((inner, share), full), shape((heads_total, NB), full), shape((width,), full),
                   shape((width,), full), shape(early.shape, full), shape((hidden, width), full),
                   shape((hidden, width), full)],
        compiler_params=pltpu.CompilerParams(vmem_limit_bytes=VMEM_LIMIT),
        cost_estimate=pl.CostEstimate(flops=0, bytes_accessed=16 << 20, transcendentals=0),
        name="finish",
    )(out, input_grad, wgrad, early, late, up_own, up_first, up_rest, down_own, down_land)


def norm_rows(values, gain):
    return values * lax.rsqrt(jnp.mean(values * values, axis=-1, keepdims=True) + EPSILON) * gain


def norm_back(values, gain, grad):
    r = lax.rsqrt(jnp.mean(values * values, axis=-1, keepdims=True) + EPSILON)
    u = values * r
    du = grad * gain
    return r * (du - u * jnp.mean(du * u, axis=-1, keepdims=True)), grad * u


def plain_body(
    block_input,
    out_grad,
    w_qkv,
    w_out,
    rel_table,
    gain_attn,
    gain_moe,
    w_router,
    w_up,
    w_down,
    routes,
    segments,
    padding,
    rel_bucket,
):
    tensor_pos = lax.axis_index("tensor")
    rows_local, width = block_input.shape
    seq_len = segments.shape[1]
    expert_count = w_router.shape[1]
    capacity = (10 * rows_local + 4 * expert_count - 1) // (4 * expert_count)
    slots = expert_count * capacity
    x_float = block_input.astype(jnp.float32)
    grad_float = out_grad.astype(jnp.float32)

    attn_norm = norm_rows(x_float, gain_attn).astype(jnp.bfloat16)
    seq_rows = lax.all_gather(attn_norm, "tensor", axis=0, tiled=True)
    qkv_full = lax.all_gather(w_qkv, "dp", axis=1, tiled=True)
    out_rows = lax.all_gather(w_out, "dp", axis=1, tiled=True)
    out_full = lax.all_gather(out_rows, "tensor", axis=0, tiled=True)
    up_full = lax.all_gather(w_up[0], "tensor", axis=0, tiled=True)
    down_full = lax.all_gather(w_down[0], "tensor", axis=0, tiled=True)

    live_mask = lax.dynamic_slice_in_dim(padding.reshape(-1), tensor_pos * rows_local, rows_local)
    live_float = live_mask.astype(jnp.float32)
    expert_ids = jnp.arange(expert_count, dtype=jnp.int32)
    pick_first = routes[:, 0:1] == expert_ids[None, :]
    pick_second = routes[:, 1:2] == expert_ids[None, :]
    usable = live_mask[:, None] == 1
    first_hot = (pick_first & usable).astype(jnp.int32)
    second_hot = (pick_second & usable).astype(jnp.int32)
    first_place = jnp.sum((jnp.cumsum(first_hot, axis=0) - first_hot) * first_hot, axis=1)
    second_before = (
        jnp.cumsum(second_hot, axis=0) - second_hot + jnp.sum(first_hot, axis=0, keepdims=True)
    )
    second_place = jnp.sum(second_before * second_hot, axis=1)
    first_slot = jnp.where(
        (live_mask == 1) & (first_place < capacity), routes[:, 0] * capacity + first_place, -1
    )
    second_slot = jnp.where(
        (live_mask == 1) & (second_place < capacity), routes[:, 1] * capacity + second_place, -1
    )
    slot_ids = jnp.arange(slots, dtype=jnp.int32)
    select_first = slot_ids[:, None] == first_slot[None, :]
    select_second = slot_ids[:, None] == second_slot[None, :]
    select_both = (select_first | select_second).astype(jnp.bfloat16)
    select_first_low = select_first.astype(jnp.bfloat16)
    select_second_low = select_second.astype(jnp.bfloat16)

    def to_experts(rows):
        return lax.all_to_all(rows, "dp", split_axis=0, concat_axis=0, tiled=True)

    grad_rows = jnp.dot(select_both, out_grad, preferred_element_type=jnp.float32)
    sent_grads = to_experts(grad_rows.astype(jnp.bfloat16).reshape(expert_count, capacity, width))
    sent_grads = sent_grads.reshape(slots, width)

    heads = qkv_full.shape[2] // DH
    inner = heads * DH
    table_local = lax.dynamic_slice_in_dim(rel_table, tensor_pos * heads, heads, 1)
    bucket_hot = (rel_bucket[:, None] == jnp.arange(NB, dtype=jnp.int32)[None, :]).astype(jnp.float32)
    line = line_of(jnp.dot(bucket_hot, table_local, precision=HIGHEST).T)
    segk, segq = mask_inputs(segments, padding)
    qkv_low, heads_low, lse = attend(line, segk, segq, seq_rows, qkv_full)
    heads_own = lax.all_to_all(heads_low, "tensor", split_axis=0, concat_axis=1, tiled=True)

    middle = x_float + jnp.dot(heads_own, out_full, preferred_element_type=jnp.float32)
    moe_low = norm_rows(middle, gain_moe).astype(jnp.bfloat16)
    rows_out = jnp.dot(select_both, moe_low, preferred_element_type=jnp.float32)
    sent_rows = to_experts(rows_out.astype(jnp.bfloat16).reshape(expert_count, capacity, width))
    sent_rows = sent_rows.reshape(slots, width)
    logits = jnp.dot(moe_low, w_router, preferred_element_type=jnp.float32)
    first_logit = jnp.sum(jnp.where(pick_first, logits, 0.0), axis=1)
    second_logit = jnp.sum(jnp.where(pick_second, logits, 0.0), axis=1)
    first_gate = jax.nn.sigmoid(first_logit - second_logit) * live_float
    second_gate = jax.nn.sigmoid(second_logit - first_logit) * live_float
    slot_gate = jnp.sum(
        jnp.where(select_first, first_gate[None, :], 0.0)
        + jnp.where(select_second, second_gate[None, :], 0.0),
        axis=1,
    )
    sent_gates = to_experts(slot_gate.reshape(expert_count, capacity)).reshape(slots, 1)

    act, pre_grad, back, dots = expert_first(sent_rows, sent_grads, up_full, down_full)
    returned_grad = to_experts(back.reshape(expert_count, capacity, width)).reshape(slots, width)
    slot_dots = to_experts(dots[0].reshape(expert_count, capacity)).reshape(slots)
    produced, up_part, down_part = expert_late(
        sent_rows, sent_grads, sent_gates, act, pre_grad, down_full
    )
    returned = to_experts(produced.reshape(expert_count, capacity, width)).reshape(slots, width)
    w_up_grad = lax.psum_scatter(up_part, "tensor", scatter_dimension=0, tiled=True)
    w_down_grad = lax.psum_scatter(down_part, "tensor", scatter_dimension=0, tiled=True)

    first_dot = jnp.sum(jnp.where(select_first, slot_dots[:, None], 0.0), axis=0)
    second_dot = jnp.sum(jnp.where(select_second, slot_dots[:, None], 0.0), axis=0)
    coefficient = first_gate * second_gate * (first_dot - second_dot)
    logit_grad = (
        jnp.where(pick_first, coefficient[:, None], 0.0)
        - jnp.where(pick_second, coefficient[:, None], 0.0)
    ).astype(jnp.bfloat16)
    router_grad = jnp.einsum("nd,ne->de", moe_low, logit_grad, preferred_element_type=jnp.float32)

    def gated(rows):
        first_rows = jnp.einsum("st,sd->td", select_first_low, rows, preferred_element_type=jnp.float32)
        second_rows = jnp.einsum("st,sd->td", select_second_low, rows, preferred_element_type=jnp.float32)
        return first_gate[:, None] * first_rows + second_gate[:, None] * second_rows

    moe_norm_grad = (
        jnp.einsum("ne,de->nd", logit_grad, w_router, preferred_element_type=jnp.float32)
        + gated(returned_grad)
    )
    middle_back, gain_moe_rows = norm_back(middle, gain_moe, moe_norm_grad)
    middle_grad = grad_float + middle_back
    gain_moe_grad = jnp.sum(gain_moe_rows, axis=0)
    attn_grad = middle_grad.astype(jnp.bfloat16)
    heads_grad = jnp.einsum("nd,fd->nf", attn_grad, out_full, preferred_element_type=jnp.float32)
    heads_grad = lax.all_to_all(
        heads_grad.astype(jnp.bfloat16), "tensor", split_axis=1, concat_axis=0, tiled=True
    )
    out_part = jnp.einsum("nf,nd->fd", heads_own, attn_grad, preferred_element_type=jnp.float32)
    out_part = lax.psum_scatter(out_part.astype(jnp.bfloat16), "tensor", scatter_dimension=0, tiled=True)
    w_out_grad = lax.psum_scatter(out_part.astype(jnp.float32), "dp", scatter_dimension=1, tiled=True)
    gain_moe_grad, router_grad = lax.psum((gain_moe_grad, router_grad), ("dp", "tensor"))

    norm_part, qkv_part, folded = attend_back(
        line, segk, segq, seq_rows, qkv_full, qkv_low, heads_grad, lse
    )
    attn_norm_grad = lax.psum_scatter(norm_part, "tensor", scatter_dimension=0, tiled=True)
    input_back, gain_attn_rows = norm_back(x_float, gain_attn, attn_norm_grad.astype(jnp.float32))
    input_grad = middle_grad + input_back
    gain_attn_grad = jnp.sum(gain_attn_rows, axis=0)
    w_qkv_grad = lax.psum_scatter(qkv_part, "dp", scatter_dimension=1, tiled=True)
    line_grad = lines_of(folded, heads, seq_len // QB)
    table_part = jnp.dot(bucket_hot.T, line_grad.T, precision=HIGHEST)
    table_whole = lax.dynamic_update_slice(
        jnp.zeros(rel_table.shape, jnp.float32), table_part, (0, tensor_pos * heads)
    )
    gain_attn_grad, table_whole = lax.psum((gain_attn_grad, table_whole), ("dp", "tensor"))
    block_output = middle + gated(returned)
    return (
        block_output,
        input_grad,
        w_qkv_grad,
        w_out_grad,
        table_whole,
        gain_attn_grad,
        gain_moe_grad,
        router_grad,
        w_up_grad.astype(jnp.float32)[None],
        w_down_grad.astype(jnp.float32)[None],
    )


def fused_body(
    block_input,
    out_grad,
    w_qkv,
    w_out,
    rel_table,
    gain_attn,
    gain_moe,
    w_router,
    w_up,
    w_down,
    routes,
    segments,
    padding,
    rel_bucket,
):
    dp_count, tensor_count = lax.axis_size("dp"), lax.axis_size("tensor")
    rows_local, width = block_input.shape
    seq_len = segments.shape[1]
    heads = w_qkv.shape[2] // DH
    capacity = slot_capacity(rows_local, w_router.shape[1])
    expert_count = w_router.shape[1]
    sizes = (dp_count, tensor_count, expert_count, capacity, capacity, heads, seq_len // QB, True)

    routes_t = routes.T
    bucket_row = rel_bucket[None]
    rows, w_all, outw, down_all, qkv, lse, heads_all, slot_rows, cot, line, segk = front(
        sizes, block_input, gain_attn, w_qkv, w_out, w_down[0], out_grad, routes_t, segments, padding,
        rel_table.T, bucket_row
    )
    (up_pair, up_own, up_first, down_own, down_land, produced, landed_first, middle, middle_grad, heads_grad, out_part, early,
     gates) = middle_pass(
        sizes, block_input, out_grad, heads_all, outw, gain_moe, w_router.T, routes_t, padding,
        slot_rows, cot, w_up[0], w_down[0], down_all
    )
    block_output, input_grad, wgrad, early, late, up_rest = last_pass(
        sizes, block_input, gain_attn, middle, middle_grad, heads_grad, rows, w_all, qkv, lse, line, segk, segments,
        produced, slot_rows, gates, early, bucket_row, out_part, landed_first, up_pair
    )
    (block_output, input_grad, w_qkv_grad, w_out_grad, table_grad, gain_attn_grad, gain_moe_grad, router_grad,
     w_up_grad, w_down_grad) = finish(
        rel_table.shape[1], block_output, input_grad, wgrad, early, late, up_own, up_first, up_rest, down_own, down_land
    )
    return (
        block_output,
        input_grad,
        w_qkv_grad,
        w_out_grad,
        table_grad.T,
        gain_attn_grad,
        gain_moe_grad,
        router_grad.T,
        w_up_grad[None],
        w_down_grad[None],
    )


def slot_capacity(tokens, experts):
    return (10 * tokens + 4 * experts - 1) // (4 * experts)


def body(*args):
    block_input, w_qkv, w_router = args[0], args[2], args[7]
    capacity = slot_capacity(block_input.shape[0], w_router.shape[1])
    fits = capacity % 16 == 0 and w_qkv.shape[1] % 16 == 0 and lax.axis_size("dp") == w_router.shape[1] == 8 and block_input.shape[1] <= 1024
    return fused_body(*args) if fits else plain_body(*args)


def solution(mesh):
    in_specs = (
        P(("dp", "tensor"), None),
        P(("dp", "tensor"), None),
        P(None, "dp", "tensor"),
        P("tensor", "dp"),
        P(),
        P(),
        P(),
        P(),
        P("dp", "tensor", None),
        P("dp", "tensor", None),
        P(("dp", "tensor"), None),
        P("dp", None),
        P("dp", None),
        P(),
    )
    out_specs = (
        P(("dp", "tensor"), None),
        P(("dp", "tensor"), None),
        P(None, "dp", "tensor"),
        P("tensor", "dp"),
        P(),
        P(),
        P(),
        P(),
        P("dp", "tensor", None),
        P("dp", "tensor", None),
    )
    return jax.shard_map(body, mesh=mesh, in_specs=in_specs, out_specs=out_specs, check_vma=False)
```

```python
import functools
import math

import jax
import jax.numpy as jnp
from jax import lax
from jax.experimental import pallas as pl
from jax.experimental.pallas import tpu as pltpu
from jax.sharding import PartitionSpec as P

NB = 32
EPSILON = 1e-06
HIGHEST = lax.Precision.HIGHEST
DH = 64
NEGATIVE = -1e30
QB = 256
NT = (((1,), (1,)), ((), ()))
TN = (((0,), (0,)), ((), ()))
NN = (((1,), (0,)), ((), ()))


def mm(a, b, dims):
    return lax.dot_general(a, b, dims, preferred_element_type=jnp.float32)


def build_bias(line_ref, tiles, heads, blocks):
    for h in range(heads):
        for d in range(blocks):
            piece = line_ref[h : h + 1, d * QB : d * QB + 2 * QB]
            wide = jnp.broadcast_to(piece, (QB, 2 * QB))
            turned = pltpu.roll(wide, 0, 1, stride=1, stride_axis=0)
            tiles[h, d] = turned[:, QB:]


def score_block(keys, query, tiles, h, qb, segk_ref, segq_ref):
    raw = mm(keys, query, NT)
    q_seg = segq_ref[:, qb * QB : (qb + 1) * QB]
    parts = []
    for kb in range(qb + 1):
        k_seg = segk_ref[kb * QB : (kb + 1) * QB, :]
        same = k_seg == q_seg
        if kb == qb:
            row = lax.broadcasted_iota(jnp.int32, (QB, QB), 0)
            col = lax.broadcasted_iota(jnp.int32, (QB, QB), 1)
            same = same | (row == col)
        parts.append(
            jnp.where(same, raw[kb * QB : (kb + 1) * QB] + tiles[h, qb - kb], NEGATIVE)
        )
    return parts


def attend_kernel(heads, blocks, line_ref, segk_ref, segq_ref, rows_ref, w_ref,
                  qkv_ref, out_ref, lse_ref, tiles):
    @pl.when(pl.program_id(0) == 0)
    def _():
        build_bias(line_ref, tiles, heads, blocks)

    for c in range(3):
        qkv_ref[c] = mm(rows_ref[...], w_ref[c], NN).astype(jnp.bfloat16)
    scale = 1.0 / math.sqrt(DH)
    for qb in range(blocks):
        nk = (qb + 1) * QB
        lower = qb * QB
        turned = []
        for h in range(heads):
            cols = slice(h * DH, (h + 1) * DH)
            query = (qkv_ref[0, lower : lower + QB, cols].astype(jnp.float32) * scale).astype(jnp.bfloat16)
            parts = score_block(qkv_ref[1, 0:nk, cols], query, tiles, h, qb, segk_ref.at[0], segq_ref.at[0])
            peak = functools.reduce(jnp.maximum, [jnp.max(x, axis=0, keepdims=True) for x in parts])
            probs = [jnp.exp(x - peak) for x in parts]
            total = functools.reduce(jnp.add, [jnp.sum(x, axis=0, keepdims=True) for x in probs])
            mixed = functools.reduce(jnp.add, [
                mm(qkv_ref[2, kb * QB : (kb + 1) * QB, cols], x.astype(jnp.bfloat16), TN)
                for kb, x in enumerate(probs)])
            turned.append(mixed / total)
            lse_ref[0, h : h + 1, lower : lower + QB] = peak + jnp.log(total)
        out_ref[lower : lower + QB, :] = jnp.concatenate(turned, axis=0).T.astype(jnp.bfloat16)


def attend(line, segk, segq, rows, w):
    seqs, _, seq_len = segq.shape
    heads = line.shape[0]
    inner = heads * DH
    blocks = seq_len // QB
    width = rows.shape[1]
    return pl.pallas_call(
        functools.partial(attend_kernel, heads, blocks),
        grid=(seqs,),
        in_specs=[
            pl.BlockSpec(line.shape, lambda s: (0, 0)),
            pl.BlockSpec((1, seq_len, 1), lambda s: (s, 0, 0)),
            pl.BlockSpec((1, 1, seq_len), lambda s: (s, 0, 0)),
            pl.BlockSpec((seq_len, width), lambda s: (s, 0)),
            pl.BlockSpec(w.shape, lambda s: (0, 0, 0)),
        ],
        out_specs=[
            pl.BlockSpec((3, seq_len, inner), lambda s: (0, s, 0)),
            pl.BlockSpec((seq_len, inner), lambda s: (s, 0)),
            pl.BlockSpec((1, heads, seq_len), lambda s: (s, 0, 0)),
        ],
        out_shape=[
            jax.ShapeDtypeStruct((3, seqs * seq_len, inner), jnp.bfloat16),
            jax.ShapeDtypeStruct((seqs * seq_len, inner), jnp.bfloat16),
            jax.ShapeDtypeStruct((seqs, heads, seq_len), jnp.float32),
        ],
        scratch_shapes=[pltpu.VMEM((heads, blocks, QB, QB), jnp.float32)],
        compiler_params=pltpu.CompilerParams(vmem_limit_bytes=48 << 20),
        cost_estimate=pl.CostEstimate(flops=10_000_000_000, bytes_accessed=10 << 20, transcendentals=4_000_000),
        name="attend",
    )(line, segk, segq, rows, w)


def attend_back_kernel(heads, blocks, seqs, line_ref, segk_ref, segq_ref, rows_ref, w_ref,
                       qkv_ref, og_ref, lse_ref,
                       norm_ref, wg_ref, lg_ref, tiles, sums, kg, vg, dq):
    step = pl.program_id(0)

    @pl.when(step == 0)
    def _():
        build_bias(line_ref, tiles, heads, blocks)
        sums[...] = jnp.zeros_like(sums)
        wg_ref[...] = jnp.zeros_like(wg_ref)

    scale = 1.0 / math.sqrt(DH)
    for h in range(heads):
        cols = slice(h * DH, (h + 1) * DH)
        kg[...] = jnp.zeros_like(kg)
        vg[...] = jnp.zeros_like(vg)
        for qb in range(blocks):
            nk = (qb + 1) * QB
            lower = qb * QB
            query = (qkv_ref[0, lower : lower + QB, cols].astype(jnp.float32) * scale).astype(jnp.bfloat16)
            grad = og_ref[lower : lower + QB, cols]
            lse = lse_ref[0, h : h + 1, lower : lower + QB]
            parts = score_block(qkv_ref[1, 0:nk, cols], query, tiles, h, qb, segk_ref.at[0], segq_ref.at[0])
            probs = [jnp.exp(x - lse) for x in parts]
            pg = mm(qkv_ref[2, 0:nk, cols], grad, NT)
            pgs = [pg[kb * QB : (kb + 1) * QB] for kb in range(qb + 1)]
            delta = functools.reduce(jnp.add, [jnp.sum(p * g, axis=0, keepdims=True) for p, g in zip(probs, pgs)])
            dqt = jnp.zeros((DH, QB), jnp.float32)
            for kb in range(qb + 1):
                rows = slice(kb * QB, (kb + 1) * QB)
                sg = (probs[kb] * (pgs[kb] - delta)).astype(jnp.bfloat16)
                sums[h, qb - kb] += sg.astype(jnp.float32)
                vg[rows] += mm(probs[kb].astype(jnp.bfloat16), grad, NN)
                kg[rows] += mm(sg, query, NN)
                dqt = dqt + mm(qkv_ref[1, rows, cols], sg, TN)
            dq[lower : lower + QB, h * DH : (h + 1) * DH] = (dqt * scale).T.astype(jnp.bfloat16)
        inner = heads * DH
        dq[:, inner + h * DH : inner + (h + 1) * DH] = kg[...].astype(jnp.bfloat16)
        dq[:, 2 * inner + h * DH : 2 * inner + (h + 1) * DH] = vg[...].astype(jnp.bfloat16)
    inner = heads * DH
    total = jnp.zeros(norm_ref.shape, jnp.float32)
    for c in range(3):
        piece = dq[:, c * inner : (c + 1) * inner]
        wg_ref[c] += mm(rows_ref[...], piece, TN)
        total = total + mm(piece, w_ref[c], NT)
    norm_ref[...] = total.astype(norm_ref.dtype)

    @pl.when(step == seqs - 1)
    def _():
        for h in range(heads):
            for d in range(blocks):
                lg_ref[h * blocks + d] = fold_tile(sums, h, d)


def fold_tile(sums, h, d):
    blank = jnp.zeros((8, QB), jnp.float32)
    total = jnp.zeros((8, 2 * QB), jnp.float32)
    for g in range(QB // 8):
        piece = jnp.concatenate([sums[h, d, 8 * g : 8 * g + 8, :], blank], axis=1)
        total = total + (piece if g == 0 else pltpu.roll(piece, 2 * QB - 8 * g, 1))
    return total


def lines_of(folded, heads, blocks):
    moved = sum(jnp.roll(folded[:, s, :], -s, axis=1) for s in range(8))
    moved = moved.reshape(heads, blocks, 2, QB)
    ahead = jnp.concatenate([moved[:, 1:, 1], jnp.zeros((heads, 1, QB), jnp.float32)], axis=1)
    return (moved[:, :, 0] + ahead).reshape(heads, blocks * QB)


def attend_back(line, segk, segq, rows, w, qkv, og, lse):
    seqs, _, seq_len = segq.shape
    heads = line.shape[0]
    inner = heads * DH
    blocks = seq_len // QB
    width = rows.shape[1]
    return pl.pallas_call(
        functools.partial(attend_back_kernel, heads, blocks, seqs),
        grid=(seqs,),
        in_specs=[
            pl.BlockSpec(line.shape, lambda s: (0, 0)),
            pl.BlockSpec((1, seq_len, 1), lambda s: (s, 0, 0)),
            pl.BlockSpec((1, 1, seq_len), lambda s: (s, 0, 0)),
            pl.BlockSpec((seq_len, width), lambda s: (s, 0)),
            pl.BlockSpec(w.shape, lambda s: (0, 0, 0)),
            pl.BlockSpec((3, seq_len, inner), lambda s: (0, s, 0)),
            pl.BlockSpec((seq_len, inner), lambda s: (s, 0)),
            pl.BlockSpec((1, heads, seq_len), lambda s: (s, 0, 0)),
        ],
        out_specs=[
            pl.BlockSpec((seq_len, width), lambda s: (s, 0)),
            pl.BlockSpec(w.shape, lambda s: (0, 0, 0)),
            pl.BlockSpec((heads * blocks, 8, 2 * QB), lambda s: (0, 0, 0)),
        ],
        out_shape=[
            jax.ShapeDtypeStruct((seqs * seq_len, width), jnp.bfloat16),
            jax.ShapeDtypeStruct(w.shape, jnp.float32),
            jax.ShapeDtypeStruct((heads * blocks, 8, 2 * QB), jnp.float32),
        ],
        scratch_shapes=[
            pltpu.VMEM((heads, blocks, QB, QB), jnp.float32),
            pltpu.VMEM((heads, blocks, QB, QB), jnp.float32),
            pltpu.VMEM((seq_len, DH), jnp.float32),
            pltpu.VMEM((seq_len, DH), jnp.float32),
            pltpu.VMEM((seq_len, 3 * inner), jnp.bfloat16),
        ],
        compiler_params=pltpu.CompilerParams(vmem_limit_bytes=48 << 20),
        cost_estimate=pl.CostEstimate(flops=20_000_000_000, bytes_accessed=16 << 20, transcendentals=4_000_000),
        name="attend_back",
    )(line, segk, segq, rows, w, qkv, og, lse)


def mask_inputs(segments, padding):
    keyed = jnp.where(padding == 1, segments, -1)
    return keyed[:, :, None], segments[:, None, :]


def line_of(by_distance):
    return jnp.concatenate([jnp.full((by_distance.shape[0], QB), NEGATIVE, jnp.float32), by_distance], axis=1)


FT = 512
ROOT_2_PI = math.sqrt(2.0 / math.pi)


def gelu_pair(x):
    square = x * x
    t = jnp.tanh(ROOT_2_PI * x * (1.0 + 0.044715 * square))
    half = 0.5 * (1.0 + t)
    slope = half + 0.5 * x * (1.0 - t * t) * (ROOT_2_PI * (1.0 + 3 * 0.044715 * square))
    return x * half, slope


def expert_kernel(steps, x_ref, g_ref, up_ref, down_ref, act_ref, pre_ref, back_ref, dot_ref, total, dots):
    step = pl.program_id(0)

    @pl.when(step == 0)
    def _():
        total[...] = jnp.zeros_like(total)
        dots[...] = jnp.zeros_like(dots)

    rows = x_ref.shape[0]
    chunk = 256
    for lower in range(0, rows, chunk):
        part = slice(lower, lower + chunk)
        pre = mm(x_ref[part], up_ref[...], NT)
        out_side = mm(g_ref[part], down_ref[...], NT)
        act, slope = gelu_pair(pre)
        low = act.astype(jnp.bfloat16)
        act_ref[part] = low
        product = low.astype(jnp.float32) * out_side
        dots[part] += sum(product[:, k : k + 128] for k in range(0, FT, 128))
        back = (out_side * slope).astype(jnp.bfloat16)
        pre_ref[part] = back
        total[part] += mm(back, up_ref[...], NN)

    @pl.when(step == steps - 1)
    def _():
        back_ref[...] = total[...].astype(jnp.bfloat16)
        dot_ref[...] = lax.dot_general(
            jnp.ones((8, 128), jnp.float32), dots[...], NT,
            precision=HIGHEST, preferred_element_type=jnp.float32)


def expert_first(x, g, up, down):
    rows, width = x.shape
    hidden = up.shape[0]
    steps = hidden // FT
    whole = lambda f: (0, 0)
    return pl.pallas_call(
        functools.partial(expert_kernel, steps),
        grid=(steps,),
        in_specs=[
            pl.BlockSpec((rows, width), whole),
            pl.BlockSpec((rows, width), whole),
            pl.BlockSpec((FT, width), lambda f: (f, 0)),
            pl.BlockSpec((FT, width), lambda f: (f, 0)),
        ],
        out_specs=[
            pl.BlockSpec((rows, FT), lambda f: (0, f)),
            pl.BlockSpec((rows, FT), lambda f: (0, f)),
            pl.BlockSpec((rows, width), whole),
            pl.BlockSpec((8, rows), whole),
        ],
        out_shape=[
            jax.ShapeDtypeStruct((rows, hidden), jnp.bfloat16),
            jax.ShapeDtypeStruct((rows, hidden), jnp.bfloat16),
            jax.ShapeDtypeStruct((rows, width), jnp.bfloat16),
            jax.ShapeDtypeStruct((8, rows), jnp.float32),
        ],
        scratch_shapes=[
            pltpu.VMEM((rows, width), jnp.float32),
            pltpu.VMEM((rows, 128), jnp.float32),
        ],
        compiler_params=pltpu.CompilerParams(vmem_limit_bytes=48 << 20),
        cost_estimate=pl.CostEstimate(
            flops=6 * rows * width * hidden, bytes_accessed=32 << 20, transcendentals=rows * hidden),
        name="expert_first",
    )(x, g, up, down)


def expert_late_kernel(steps, x_ref, g_ref, gate_ref, act_ref, pre_ref, down_ref,
                       out_ref, up_grad_ref, down_grad_ref, total, x_gated, g_gated):
    step = pl.program_id(0)

    @pl.when(step == 0)
    def _():
        total[...] = jnp.zeros_like(total)
        gate = gate_ref[...]
        x_gated[...] = (x_ref[...].astype(jnp.float32) * gate).astype(jnp.bfloat16)
        g_gated[...] = (g_ref[...].astype(jnp.float32) * gate).astype(jnp.bfloat16)

    up_grad_ref[...] = mm(pre_ref[...], x_gated[...], TN).astype(up_grad_ref.dtype)
    down_grad_ref[...] = mm(act_ref[...], g_gated[...], TN).astype(down_grad_ref.dtype)
    total[...] += mm(act_ref[...], down_ref[...], NN)

    @pl.when(step == steps - 1)
    def _():
        out_ref[...] = total[...].astype(jnp.bfloat16)


def expert_late(x, g, gate, act, pre, down):
    rows, width = x.shape
    hidden = down.shape[0]
    steps = hidden // FT
    whole = lambda f: (0, 0)
    tile = pl.BlockSpec((FT, width), lambda f: (f, 0))
    return pl.pallas_call(
        functools.partial(expert_late_kernel, steps),
        grid=(steps,),
        in_specs=[
            pl.BlockSpec((rows, width), whole),
            pl.BlockSpec((rows, width), whole),
            pl.BlockSpec((rows, 1), whole),
            pl.BlockSpec((rows, FT), lambda f: (0, f)),
            pl.BlockSpec((rows, FT), lambda f: (0, f)),
            tile,
        ],
        out_specs=[pl.BlockSpec((rows, width), whole), tile, tile],
        out_shape=[
            jax.ShapeDtypeStruct((rows, width), jnp.bfloat16),
            jax.ShapeDtypeStruct((hidden, width), jnp.bfloat16),
            jax.ShapeDtypeStruct((hidden, width), jnp.bfloat16),
        ],
        scratch_shapes=[
            pltpu.VMEM((rows, width), jnp.float32),
            pltpu.VMEM((rows, width), jnp.bfloat16),
            pltpu.VMEM((rows, width), jnp.bfloat16),
        ],
        compiler_params=pltpu.CompilerParams(vmem_limit_bytes=48 << 20),
        cost_estimate=pl.CostEstimate(
            flops=6 * rows * width * hidden, bytes_accessed=32 << 20, transcendentals=0),
        name="expert_late",
    )(x, g, gate, act, pre, down)


MESH = pl.DeviceIdType.MESH
VMEM_LIMIT = 61 << 20


def remote(src, dst, send, recv, axis, place):
    return pltpu.make_async_remote_copy(
        src_ref=src, dst_ref=dst, send_sem=send, recv_sem=recv, device_id={axis: place}, device_id_type=MESH
    )


def each_peer(count, step, start=1):
    if count <= 8:
        for r in range(start, count):
            step(r)
    else:
        def one(r, carry):
            step(r)
            return carry
        lax.fori_loop(start, count, one, 0)


def peer(r):
    return jnp.bitwise_xor(lax.axis_index("dp"), r)


def greet(dp_count, tensor_count):
    barrier = pltpu.get_barrier_semaphore()
    dp, tp = lax.axis_index("dp"), lax.axis_index("tensor")
    for r in range(1, tensor_count):
        pl.semaphore_signal(barrier, inc=1, device_id={"tensor": lax.rem(tp + r, tensor_count)}, device_id_type=MESH)

    def signal(r):
        pl.semaphore_signal(barrier, inc=1, device_id={"dp": peer(r)}, device_id_type=MESH)
    each_peer(dp_count, signal)
    return lambda: pl.semaphore_wait(barrier, tensor_count - 1 + dp_count - 1)


def partners(tensor_count):
    tp = lax.axis_index("tensor")
    sib = tp + 1 - 2 * lax.rem(tp, 2)
    return tp, sib, lax.rem(tp + 2, tensor_count), lax.rem(sib + 2, tensor_count)


def place_pairs(routes_ref, live, experts, capacity, cap_rows):
    tokens = live.shape[1]
    live = live == 1
    ids = lax.broadcasted_iota(jnp.int32, (experts, tokens), 0)
    row = lax.broadcasted_iota(jnp.int32, (tokens, tokens), 0)
    col = lax.broadcasted_iota(jnp.int32, (tokens, tokens), 1)
    before = (row < col).astype(jnp.float32).astype(jnp.bfloat16)
    slots = []
    base = jnp.zeros((experts, 1), jnp.float32)
    for k in range(2):
        route = routes_ref[k : k + 1, :]
        hot = jnp.where((ids == route) & live, 1.0, 0.0)
        count = mm(hot.astype(jnp.bfloat16), before, NN) + base
        place = jnp.sum(count * hot, axis=0, keepdims=True).astype(jnp.int32)
        slots.append(jnp.where(live & (place < capacity), route * cap_rows + place, -1))
        base = base + jnp.sum(hot, axis=1, keepdims=True)
    return slots


def chosen(first, second, expert, cap_rows):
    ids = lax.broadcasted_iota(jnp.int32, (cap_rows, first.shape[1]), 0) + expert * cap_rows
    return jnp.where((ids == first) | (ids == second), 1.0, 0.0).astype(jnp.bfloat16)


def attend_sequence(heads, blocks, seq, line_tiles, segk_ref, segq_ref, qkv, heads_out, lse_ref):
    scale = 1.0 / math.sqrt(DH)
    half = blocks // 2
    for qb in range(blocks):
        nk = (qb + 1) * QB
        lower = qb * QB
        for h in range(heads):
            cols = [slice((3 * h + c) * DH, (3 * h + c + 1) * DH) for c in range(3)]
            query = (qkv[seq, lower : lower + QB, cols[0]].astype(jnp.float32) * scale).astype(jnp.bfloat16)
            parts = score_block(qkv[seq, 0:nk, cols[1]], query, line_tiles, h, qb, segk_ref.at[seq], segq_ref.at[pl.ds(seq, 1)])
            peak = functools.reduce(jnp.maximum, [jnp.max(x, axis=0, keepdims=True) for x in parts])
            probs = [jnp.exp(x - peak) for x in parts]
            total = functools.reduce(jnp.add, [jnp.sum(x, axis=0, keepdims=True) for x in probs])
            mixed = functools.reduce(jnp.add, [
                mm(qkv[seq, kb * QB : (kb + 1) * QB, cols[2]], x.astype(jnp.bfloat16), TN)
                for kb, x in enumerate(probs)])
            heads_out[seq * 2 + qb // half, h * DH : (h + 1) * DH, (qb % half) * QB : (qb % half + 1) * QB] = (
                mixed / total).astype(jnp.bfloat16)
            lse_ref[seq, h : h + 1, lower : lower + QB] = peak + jnp.log(total)


def packed_gather(own_ref, all_ref, send, recv, dp_count):
    dp = lax.axis_index("dp")
    side = peer(1)
    columns = dp_count // 2
    near = remote(own_ref, all_ref.at[dp], send.at[0], recv.at[0], "dp", side)
    out = [remote(own_ref, all_ref.at[dp], send.at[k], recv.at[k], "dp", peer(2 * k))
           for k in range(1, columns)]
    onward = []
    for k in range(1, columns):
        src = peer(2 * k)
        n = columns - 1 + k
        onward.append(remote(all_ref.at[src], all_ref.at[src], send.at[n], recv.at[n], "dp", side))
    return near, out, onward


def prepare(heads, tp, table_ref, bucket_ref, segments_ref, padding_ref, line_ref, segk_ref):
    buckets, length = table_ref.shape[1], bucket_ref.shape[1]
    ids = lax.broadcasted_iota(jnp.int32, (buckets, length), 0)
    hot = ids == bucket_ref[...]
    for h in range(heads):
        column = to_column(table_ref[pl.ds(tp * heads + h, 1), :], buckets)
        line_ref[h : h + 1, :QB] = jnp.full((1, QB), NEGATIVE, jnp.float32)
        line_ref[h : h + 1, QB:] = jnp.sum(jnp.where(hot, column, 0.0), axis=0, keepdims=True)
    keyed = jnp.where(padding_ref[...] == 1, segments_ref[...], -1).astype(jnp.float32)
    for s in range(keyed.shape[0]):
        for k in range(length // QB):
            piece = keyed[s : s + 1, k * QB : (k + 1) * QB]
            segk_ref[s, k * QB : (k + 1) * QB, :] = to_column(piece, QB).astype(jnp.int32)


def front_kernel(sizes, x_ref, gain_ref, w_ref, outw_ref, down_ref, grad_ref, routes_ref, segments_ref, padding_ref,
                 table_ref, bucket_ref, gain_moe_ref,
                 rows_out, w_out_all, outw_all, down_all, qkv_out, lse_ref, heads_all, slots_ref, cot, line_ref, segk_ref,
                 middle_out, moe_out, x_out,
                 tiles, heads_out, cot_send, w_own, rows, w_all, qkv, middle, moe_low, x_send,
                 far_send, far_recv, w_send, w_recv, ot_send, ot_recv,
                 dn_send, dn_recv, cot_s, cot_r, head_send, head_recv, local_sem, out_sem):
    dp_count, tensor_count, experts, capacity, cap_rows, heads, blocks, gather_w = sizes
    dp = lax.axis_index("dp")
    tp, sib, opp, across = partners(tensor_count)
    wait_barrier = greet(dp_count, tensor_count)
    inner = heads * DH
    for h in range(heads):
        for c in range(3):
            n = (3 * h + c) * DH
            w_own[:, n : n + DH] = w_ref[c, :, h * DH : (h + 1) * DH]
    w_own[:, 3 * inner :] = outw_ref[...].T

    x = x_ref[...].astype(jnp.float32)
    r = lax.rsqrt(jnp.mean(x * x, axis=-1, keepdims=True) + EPSILON)
    rows[tp] = (x * r * gain_ref[...].reshape(1, x.shape[1])).astype(jnp.bfloat16)
    wait_barrier()

    half = rows.shape[1] // 2
    parts = [pl.ds(0, half), pl.ds(half, half)]
    far = [remote(rows.at[tp, p], rows.at[tp, p], far_send.at[k], far_recv.at[k], "tensor", opp) for k, p in enumerate(parts)]
    near = remote(rows.at[tp], rows.at[tp], far_send.at[2], far_recv.at[2], "tensor", sib)
    onward = [remote(rows.at[opp, p], rows.at[opp, p], far_send.at[3 + k], far_recv.at[3 + k], "tensor", sib) for k, p in enumerate(parts)]
    for c in far:
        c.start()
    near.start()

    w_near, w_out, w_on = packed_gather(w_own, w_all, w_send, w_recv, dp_count)
    for c in w_out:
        c.start()
    w_near.start()
    w_all[dp] = w_own[...]

    tokens = x_ref.shape[0]
    live = padding_ref[pl.ds(tp // 2, 1), pl.ds(pl.multiple_of(lax.rem(tp, 2) * tokens, 128), tokens)]
    first, second = place_pairs(routes_ref, live, experts, capacity, cap_rows)
    slots_ref[0:1, :] = first
    slots_ref[1:2, :] = second

    def cot_copy(r):
        to = peer(r)
        return remote(cot_send.at[to], cot.at[dp], cot_s.at[r], cot_r.at[r], "dp", to)

    def cot_fill(r):
        to = peer(r)
        cot_send[to] = mm(chosen(first, second, to, cap_rows), grad_ref[...], NN).astype(jnp.bfloat16)

    each_peer(dp_count, cot_fill)
    cot_fill(0)
    own_cot = pltpu.make_async_copy(cot_send.at[dp], cot.at[dp], local_sem.at[1])
    own_cot.start()

    prepare(heads, tp, table_ref, bucket_ref, segments_ref, padding_ref, line_ref, segk_ref)
    build_bias(line_ref, tiles, heads, blocks)
    for c, on in zip(w_out, w_on):
        c.wait_recv()
        on.start()
    each_peer(dp_count, lambda r: cot_copy(r).start())
    w_near.wait_recv()
    for c in w_on:
        c.wait_recv()
    near.wait_recv()

    width = rows.shape[2]
    own_seq = tp // 2
    packed = qkv.shape[2]

    def project(seq):
        tokens = rows[pl.ds(seq * 2, 2)].reshape(2 * rows.shape[1], width)
        weight = w_all[...].reshape(width, w_all.shape[2])[:, :packed]
        qkv[seq] = mm(tokens, weight, NN).astype(jnp.bfloat16)

    def head_copy(k, to):
        return remote(heads_out.at[to], heads_all.at[tp], head_send.at[k], head_recv.at[k], "tensor", to)

    down_far = remote(down_ref, down_all.at[tp], dn_send.at[0], dn_recv.at[0], "tensor", opp)
    down_near = remote(down_ref, down_all.at[tp], dn_send.at[1], dn_recv.at[1], "tensor", sib)
    down_on = remote(down_all.at[opp], down_all.at[opp], dn_send.at[2], dn_recv.at[2], "tensor", sib)

    put_w = pltpu.make_async_copy(w_all, w_out_all, out_sem.at[0])
    put_w.start()
    project(own_seq)
    put_own = pltpu.make_async_copy(qkv.at[own_seq], qkv_out.at[own_seq], out_sem.at[1])
    put_own.start()
    outw_all[tp] = w_all[...].reshape(width, w_all.shape[2])[:, 3 * inner :].T
    ot_far = remote(outw_all.at[tp], outw_all.at[tp], ot_send.at[0], ot_recv.at[0], "tensor", opp)
    ot_near = remote(outw_all.at[tp], outw_all.at[tp], ot_send.at[1], ot_recv.at[1], "tensor", sib)
    ot_on = remote(outw_all.at[opp], outw_all.at[opp], ot_send.at[2], ot_recv.at[2], "tensor", sib)
    for k in range(2):
        far[k].wait_recv()
        onward[k].start()
    ot_far.start()
    ot_near.start()
    down_far.start()
    down_near.start()
    attend_sequence(heads, blocks, own_seq, tiles, segk_ref, segments_ref, qkv, heads_out, lse_ref)
    head_copy(0, sib).start()
    heads_all[tp] = heads_out[tp]
    for k in range(2):
        onward[k].wait_recv()
    other = 1 - own_seq
    put_rows = pltpu.make_async_copy(rows, rows_out, out_sem.at[2])
    put_rows.start()
    project(other)
    put_other = pltpu.make_async_copy(qkv.at[other], qkv_out.at[other], out_sem.at[3])
    put_other.start()
    attend_sequence(heads, blocks, other, tiles, segk_ref, segments_ref, qkv, heads_out, lse_ref)
    ot_far.wait_recv()
    ot_on.start()
    head_copy(1, opp).start()
    head_copy(2, across).start()

    head_copy(0, sib).wait_recv()
    head_copy(1, opp).wait_recv()
    head_copy(2, across).wait_recv()
    ot_near.wait_recv()
    ot_on.wait_recv()
    mixed = x_ref[...].astype(jnp.float32)
    for t in range(tensor_count):
        mixed = mixed + mm(heads_all[t], outw_all[t], TN)
    middle[...] = mixed
    r = lax.rsqrt(jnp.mean(mixed * mixed, axis=-1, keepdims=True) + EPSILON)
    moe_low[...] = (mixed * r * gain_moe_ref[...].reshape(1, width)).astype(jnp.bfloat16)
    for e in range(experts):
        x_send[e] = mm(chosen(first, second, e, cap_rows), moe_low[...], NN).astype(jnp.bfloat16)
    puts = [pltpu.make_async_copy(src, dst, out_sem.at[4 + k]) for k, (src, dst) in enumerate((
        (x_send, x_out), (moe_low, moe_out), (middle, middle_out)))]
    for c in puts:
        c.start()

    for c in [put_w, put_own, put_rows, put_other] + puts:
        c.wait()
    down_far.wait_recv()
    down_on.start()
    own_cot.wait()
    each_peer(dp_count, lambda r: cot_copy(r).wait())
    ot_on.wait_send()
    ot_near.wait_send()
    ot_far.wait_send()
    for c in [w_near] + w_out + w_on:
        c.wait_send()
    for c in far + [near] + onward:
        c.wait_send()
    head_copy(0, sib).wait_send()
    head_copy(1, opp).wait_send()
    head_copy(2, across).wait_send()
    down_far.wait_send()
    down_near.wait()
    down_on.wait()


def sems(*counts):
    out = []
    for n in counts:
        out += [pltpu.SemaphoreType.DMA((n,)), pltpu.SemaphoreType.DMA((n,))]
    return out


def front(sizes, x, gain, w, outw, down, grad, routes_t, segments, padding, table, bucket, gain_moe):
    dp_count, tensor_count, experts, capacity, cap_rows, heads, blocks, gather_w = sizes
    tokens, width = x.shape
    seq_len = blocks * QB
    seqs = tensor_count * tokens // seq_len
    inner = heads * DH
    packed = -(-3 * inner // 128) * 128
    vmem = pl.BlockSpec(memory_space=pltpu.VMEM)
    anywhere = pl.BlockSpec(memory_space=pl.ANY)
    shape = jax.ShapeDtypeStruct
    low = jnp.bfloat16
    return pl.pallas_call(
        functools.partial(front_kernel, sizes),
        in_specs=[vmem] * 4 + [anywhere] + [vmem] * 7,
        out_specs=[anywhere] * 2 + [vmem] + [anywhere] * 2 + [vmem] * 3 + [anywhere] + [vmem] * 2 + [anywhere] * 3,
        out_shape=[
            shape((tensor_count, tokens, width), low),
            shape((dp_count, w.shape[1], 4 * inner), low),
            shape((tensor_count, inner, width), low),
            shape((tensor_count,) + down.shape, low),
            shape((seqs, seq_len, packed), low),
            shape((seqs, heads, seq_len), jnp.float32),
            shape((tensor_count, inner, tokens), low),
            shape((8, tokens), jnp.int32),
            shape((experts, cap_rows, width), low),
            shape((heads, QB + seq_len), jnp.float32),
            shape((seqs, seq_len, 1), jnp.int32),
            shape((tokens, width), jnp.float32),
            shape((tokens, width), low),
            shape((experts, cap_rows, width), low),
        ],
        scratch_shapes=[
            pltpu.VMEM((heads, blocks, QB, QB), jnp.float32),
            pltpu.VMEM((tensor_count, inner, tokens), low),
            pltpu.VMEM((experts, cap_rows, width), low),
            pltpu.VMEM((w.shape[1], 4 * inner), low),
            pltpu.VMEM((tensor_count, tokens, width), low),
            pltpu.VMEM((dp_count, w.shape[1], 4 * inner), low),
            pltpu.VMEM((seqs, seq_len, packed), low),
            pltpu.VMEM((tokens, width), jnp.float32),
            pltpu.VMEM((tokens, width), low),
            pltpu.VMEM((experts, cap_rows, width), low),
        ] + sems(5, dp_count, 3, 3, dp_count, 3) + [pltpu.SemaphoreType.DMA((3,)), pltpu.SemaphoreType.DMA((7,))],
        compiler_params=pltpu.CompilerParams(
            vmem_limit_bytes=VMEM_LIMIT, collective_id=1, has_side_effects=True),
        cost_estimate=pl.CostEstimate(flops=20_000_000_000, bytes_accessed=20 << 20, transcendentals=4_000_000),
        name="front",
    )(x, gain, w, outw, down, grad, routes_t, segments, padding, table, bucket, gain_moe)


def to_row(column, lanes):
    n = column.shape[0]
    row = lax.broadcasted_iota(jnp.int32, (n, lanes), 0)
    col = lax.broadcasted_iota(jnp.int32, (n, lanes), 1)
    return jnp.sum(jnp.where(row == col, column, 0.0), axis=0, keepdims=True)


def to_column(row_values, n):
    lanes = row_values.shape[1]
    row = lax.broadcasted_iota(jnp.int32, (n, lanes), 0)
    col = lax.broadcasted_iota(jnp.int32, (n, lanes), 1)
    return jnp.sum(jnp.where(row == col, row_values, 0.0), axis=1, keepdims=True)


def gate_map(first, second, gate_first, gate_second, expert, cap_rows):
    ids = lax.broadcasted_iota(jnp.int32, (cap_rows, first.shape[1]), 0) + expert * cap_rows
    return jnp.where(ids == first, gate_first, jnp.where(ids == second, gate_second, 0.0))


def gated_rows(weights, rows):
    high = weights.astype(jnp.bfloat16)
    low = (weights - high.astype(jnp.float32)).astype(jnp.bfloat16)
    return mm(high, rows, TN) + mm(low, rows, TN)


def middle_kernel(sizes, x_send, moe_in, middle_in, grad_ref, heads_ref, outw_ref, gain_ref, router_ref, routes_ref, padding_ref,
                  slots_ref, cot_ref, up_ref, down_own_ref, down_ref,
                  up_pair_out, up_own_out, up_land, down_own_out, down_land, produced_out, middle_grad, heads_grad, out_part, stats, gates,
                  up, down, g_rows, x_rows, act, side, back_send, back, gate_send, gate_rows,
                  dot_send, dot_rows, moe_low, stage, up_pair, up_own, down_own, produced, middle, down_pair,
                  up_s, up_r, x_s, x_r, b_s, b_r, g_s, g_r, d_s, d_r, a_s, a_r, load_sem, out_sem):
    dp_count, tensor_count, experts, capacity, cap_rows, heads, blocks, gather_w = sizes
    dp = lax.axis_index("dp")
    tp, sib, opp, across = partners(tensor_count)
    hidden = up.shape[1]
    total = middle_grad
    tokens, width = grad_ref.shape
    lanes = gate_send.shape[2]
    wait_barrier = greet(dp_count, tensor_count)

    load_g = pltpu.make_async_copy(cot_ref, g_rows, load_sem.at[0])
    load_down = [
        pltpu.make_async_copy(down_own_ref, down.at[tp], load_sem.at[1]),
        pltpu.make_async_copy(down_ref.at[sib], down.at[sib], load_sem.at[5]),
        pltpu.make_async_copy(down_ref.at[opp], down.at[opp], load_sem.at[6]),
        pltpu.make_async_copy(down_ref.at[across], down.at[across], load_sem.at[7]),
    ]
    load_up = pltpu.make_async_copy(up_ref, up.at[tp], load_sem.at[2])
    load_g.start()
    for c in load_down:
        c.start()
    load_up.start()

    loads = [pltpu.make_async_copy(src, dst, load_sem.at[n]) for n, src, dst in (
        (3, moe_in, moe_low), (4, middle_in, middle), (8, x_send.at[dp], x_rows.at[dp]))]
    for c in loads:
        c.start()
    puts = [pltpu.make_async_copy(src, dst, out_sem.at[k]) for k, (src, dst) in enumerate((
        (produced, produced_out), (up_pair, up_pair_out), (up_own, up_own_out), (down_own, down_own_out)))]
    first, second = slots_ref[0:1, :], slots_ref[1:2, :]
    wait_barrier()

    up_far = remote(up_ref, up.at[tp], up_s.at[0], up_r.at[0], "tensor", opp)
    up_near = remote(up_ref, up.at[tp], up_s.at[1], up_r.at[1], "tensor", sib)
    up_on = remote(up.at[opp], up.at[opp], up_s.at[2], up_r.at[2], "tensor", sib)
    up_far.start()
    up_near.start()

    def x_copy(r):
        to = peer(r)
        return remote(x_send.at[to], x_rows.at[dp], x_s.at[r], x_r.at[r], "dp", to)

    held = dp_count - 2
    for r in list(range(dp_count // 2, held)) + list(range(1, dp_count // 2)):
        x_copy(r).start()
    loads[0].wait()
    loads[2].wait()


    ids = lax.broadcasted_iota(jnp.int32, (experts, tokens), 0)
    pick_first, pick_second = ids == routes_ref[0:1, :], ids == routes_ref[1:2, :]
    live = padding_ref[pl.ds(tp // 2, 1), pl.ds(pl.multiple_of(lax.rem(tp, 2) * tokens, 128), tokens)]
    live = (live == 1).astype(jnp.float32)
    logits = mm(router_ref[...], moe_low[...], NT)
    gap = jnp.sum(jnp.where(pick_first, logits, 0.0) - jnp.where(pick_second, logits, 0.0), axis=0, keepdims=True)
    gate_first = live / (1.0 + jnp.exp(-gap))
    gate_second = live / (1.0 + jnp.exp(gap))
    gates[0:1, :] = gate_first
    gates[1:2, :] = gate_second

    def gate_copy(r):
        to = peer(r)
        return remote(gate_send.at[to], gate_rows.at[dp], g_s.at[r], g_r.at[r], "dp", to)

    def gate_fill(r):
        to = peer(r)
        column = jnp.sum(gate_map(first, second, gate_first, gate_second, to, cap_rows), axis=1, keepdims=True)
        return jnp.broadcast_to(to_row(column, lanes), (8, lanes))

    def gate_go(r):
        gate_send[peer(r)] = gate_fill(r)
        gate_copy(r).start()
    each_peer(dp_count, gate_go)
    gate_rows[dp] = gate_fill(0)

    load_g.wait()
    for c in load_down:
        c.wait()
    slots = experts * cap_rows
    block = slots // 4

    def side_block(k, carry):
        part = pl.ds(pl.multiple_of(k * block, 16), block)
        here = g_rows[pl.ds(k * (experts // 4), experts // 4)].reshape(block, width)
        for t in range(tensor_count):
            side[part, t * hidden : (t + 1) * hidden] = mm(here, down[t], NT).astype(jnp.bfloat16)
        return carry
    lax.fori_loop(0, 4, side_block, 0)

    for r in range(dp_count // 2, held):
        x_copy(r).wait_send()
    for r in range(held, dp_count):
        x_copy(r).start()
    load_up.wait()
    up_far.wait_recv()
    up_on.start()
    up_near.wait_recv()
    up_on.wait_recv()

    def back_copy(r):
        to = peer(r)
        return remote(back_send.at[to], back.at[dp], b_s.at[r], b_r.at[r], "dp", to)

    def dot_copy(r):
        to = peer(r)
        return remote(dot_send.at[to], dot_rows.at[dp], d_s.at[r], d_r.at[r], "dp", to)

    group = max(1, min(dp_count, 320 // cap_rows))

    def first_pass(step, carry):
        rounds = [step * group + k for k in range(group)]
        froms = [peer(r) for r in rounds]
        for k, r in enumerate(rounds):
            if k == 0:
                @pl.when(r > 0)
                def _():
                    x_copy(r).wait_recv()
            else:
                x_copy(r).wait_recv()
        here = jnp.concatenate([x_rows[s] for s in froms], axis=0)
        total_back = jnp.zeros((group * cap_rows, width), jnp.float32)
        dots = jnp.zeros((group * cap_rows, 128), jnp.float32)
        for t in range(tensor_count):
            cols = slice(t * hidden, (t + 1) * hidden)
            pre = mm(here, up[t], NT)
            value, slope = gelu_pair(pre)
            low = value.astype(jnp.bfloat16)
            places = [pl.ds(pl.multiple_of(s * cap_rows, 16), cap_rows) for s in froms]
            beside = jnp.concatenate([side[p, cols] for p in places], axis=0).astype(jnp.float32)
            product = low.astype(jnp.float32) * beside
            dots = dots + sum(product[:, k : k + 128] for k in range(0, hidden, 128))
            grad = (beside * slope).astype(jnp.bfloat16)
            for k, p in enumerate(places):
                piece = slice(k * cap_rows, (k + 1) * cap_rows)
                act[p, cols] = low[piece]
                side[p, cols] = grad[piece]
            total_back = total_back + mm(grad, up[t], NN)
        column = jnp.sum(dots, axis=1, keepdims=True)
        for k, (r, s) in enumerate(zip(rounds, froms)):
            piece = slice(k * cap_rows, (k + 1) * cap_rows)
            low = total_back[piece].astype(jnp.bfloat16)
            line = jnp.broadcast_to(to_row(column[piece], lanes), (8, lanes))

            def send():
                back_send[s] = low
                dot_send[s] = line
                back_copy(r).start()
                dot_copy(r).start()

            def keep():
                back[dp] = low
                dot_rows[dp] = line
            if k == 0:
                pl.when(r > 0)(send)
                pl.when(r == 0)(keep)
            else:
                send()
        return carry
    lax.fori_loop(0, dp_count // group, first_pass, 0)

    each_peer(dp_count, lambda r: gate_copy(r).wait_recv())

    def gate_rows_in(s, carry):
        column = to_column(gate_rows[s, 0:1, :], cap_rows)
        x_rows[s] = (x_rows[s].astype(jnp.float32) * column).astype(jnp.bfloat16)
        g_rows[s] = (g_rows[s].astype(jnp.float32) * column).astype(jnp.bfloat16)
        return carry
    lax.fori_loop(0, experts, gate_rows_in, 0)

    for r in list(range(1, dp_count // 2)) + list(range(held, dp_count)):
        x_copy(r).wait_send()
    lands = ((down_pair, down_own), (up_pair, up_own))
    aside = [remote(stage.at[k], lands[k][n], a_s.at[2 * k + n], a_r.at[2 * k + n], "tensor", sib)
             for k in range(2) for n in range(2)]
    up_far_part = remote(up_pair.at[pl.ds(0, hidden // 4)], up_land, a_s.at[5], a_r.at[5], "tensor", opp)
    down_far = remote(down_pair, down_land, a_s.at[4], a_r.at[4], "tensor", opp)
    piece = hidden // 2
    shards = (across, sib, opp, tp)
    sources = ((act, g_rows), (side, x_rows))
    for k, n in ((0, 0), (0, 2), (1, 0), (1, 2), (0, 1), (1, 1), (0, 3), (1, 3)):
        left, right = sources[k]
        if n == 1:
            aside[2 * k].wait_send()
        if n >= 2:
            aside[2 * k + n - 2].wait_recv()
        for m in range(2):
            cols = pl.ds(pl.multiple_of(shards[n] * hidden + m * piece, 128), piece)
            part = pl.ds(m * piece, piece)
            tile = mm(left[:, cols], right[...].reshape(slots, width), TN)
            if n < 2:
                stage[k, part, :] = tile.astype(jnp.bfloat16)
            else:
                land = lands[k][n - 2]
                land[part, :] = (tile + land[part, :].astype(jnp.float32)).astype(jnp.bfloat16)
        if n < 2:
            aside[2 * k + n].start()
        elif n == 2 and k == 0:
            down_far.start()
        elif n == 2:
            up_far_part.start()
            puts[1].start()
        elif k == 0:
            puts[3].start()
        else:
            puts[2].start()

    def produce(k, carry):
        part = pl.ds(pl.multiple_of(k * block, 16), block)
        out = jnp.zeros((block, width), jnp.float32)
        for t in range(tensor_count):
            out = out + mm(act[part, t * hidden : (t + 1) * hidden], down[t], NN)
        out = out.astype(jnp.bfloat16)
        for e in range(experts // 4):
            produced[k * (experts // 4) + e] = out[e * cap_rows : (e + 1) * cap_rows]
        return carry
    lax.fori_loop(0, 4, produce, 0)

    puts[0].start()

    total[...] = jnp.zeros_like(total)

    def combine(r, carry):
        dot_first, dot_second = carry
        e = peer(r)

        @pl.when(r > 0)
        def _():
            back_copy(r).wait_recv()
            dot_copy(r).wait_recv()
        weights = gate_map(first, second, gate_first, gate_second, e, cap_rows)
        total[...] += gated_rows(weights, back[e])
        column = to_column(dot_rows[e, 0:1, :], cap_rows)
        ids = lax.broadcasted_iota(jnp.int32, (cap_rows, tokens), 0) + e * cap_rows
        dot_first = dot_first + jnp.sum(jnp.where(ids == first, column, 0.0), axis=0, keepdims=True)
        dot_second = dot_second + jnp.sum(jnp.where(ids == second, column, 0.0), axis=0, keepdims=True)
        return dot_first, dot_second
    zero_row = jnp.zeros((1, tokens), jnp.float32)
    dot_first, dot_second = lax.fori_loop(0, dp_count, combine, (zero_row, zero_row))

    change = gate_first * gate_second * (dot_first - dot_second)
    logit_grad = (jnp.where(pick_first, change, 0.0) - jnp.where(pick_second, change, 0.0)).astype(jnp.bfloat16)
    norm_grad = total[...] + mm(logit_grad, router_ref[...], TN)
    loads[1].wait()
    mixed = middle[...]
    r = lax.rsqrt(jnp.mean(mixed * mixed, axis=-1, keepdims=True) + EPSILON)
    u = mixed * r
    du = norm_grad * gain_ref[...].reshape(1, width)
    grad = grad_ref[...].astype(jnp.float32) + r * (du - u * jnp.mean(du * u, axis=-1, keepdims=True))
    middle_grad[...] = grad
    low = grad.astype(jnp.bfloat16)
    for t in range(tensor_count):
        heads_grad[t] = mm(outw_ref[t], low, NT).astype(jnp.bfloat16)
        out_part[t] = mm(heads_ref[t], low, NN).astype(jnp.bfloat16)
    stats[0:8, :] = jnp.broadcast_to(jnp.sum(norm_grad * u, axis=0, keepdims=True), (8, width))
    stats[8:, :] = mm(logit_grad, moe_low[...], NN)

    down_far.wait_recv()
    up_far_part.wait_recv()
    down_far.wait_send()
    up_far_part.wait_send()
    for c in puts:
        c.wait()
    for k in range(2):
        aside[2 * k + 1].wait_send()
    up_far.wait_send()
    up_near.wait_send()
    up_on.wait_send()

    def drain(r):
        gate_copy(r).wait_send()
        back_copy(r).wait_send()
        dot_copy(r).wait_send()
    each_peer(dp_count, drain)


def middle_pass(sizes, x_send, moe_low, middle, grad, heads_all, outw, gain, router_t, routes_t, padding, slot_rows, cot, up, down, down_all):
    dp_count, tensor_count, experts, capacity, cap_rows, heads, blocks, gather_w = sizes
    tokens, width = grad.shape
    inner = heads * DH
    hidden = up.shape[0]
    slots = experts * cap_rows
    lanes = -(-cap_rows // 128) * 128
    vmem = pl.BlockSpec(memory_space=pltpu.VMEM)
    anywhere = pl.BlockSpec(memory_space=pl.ANY)
    shape = jax.ShapeDtypeStruct
    low = jnp.bfloat16
    return pl.pallas_call(
        functools.partial(middle_kernel, sizes),
        in_specs=[anywhere] * 3 + [vmem] * 8 + [anywhere] * 4,
        out_specs=[anywhere] * 2 + [vmem] + [anywhere] + [vmem] + [anywhere] + [vmem] * 5,
        out_shape=[
            shape((hidden, width), low),
            shape((hidden, width), low),
            shape((hidden // 4, width), low),
            shape((hidden, width), low),
            shape((hidden, width), low),
            shape((experts, cap_rows, width), low),
            shape((tokens, width), jnp.float32),
            shape((tensor_count, inner, tokens), low),
            shape((tensor_count, inner, width), low),
            shape((8 + experts, width), jnp.float32),
            shape((8, tokens), jnp.float32),
        ],
        scratch_shapes=[
            pltpu.VMEM((tensor_count, hidden, width), low),
            pltpu.VMEM((tensor_count, hidden, width), low),
            pltpu.VMEM((experts, cap_rows, width), low),
            pltpu.VMEM((experts, cap_rows, width), low),
            pltpu.VMEM((slots, tensor_count * hidden), low),
            pltpu.VMEM((slots, tensor_count * hidden), low),
            pltpu.VMEM((experts, cap_rows, width), low),
            pltpu.VMEM((experts, cap_rows, width), low),
            pltpu.VMEM((experts, 8, lanes), jnp.float32),
            pltpu.VMEM((experts, 8, lanes), jnp.float32),
            pltpu.VMEM((experts, 8, lanes), jnp.float32),
            pltpu.VMEM((experts, 8, lanes), jnp.float32),
            pltpu.VMEM((tokens, width), low),
            pltpu.VMEM((2, hidden, width), low),
            pltpu.VMEM((hidden, width), low),
            pltpu.VMEM((hidden, width), low),
            pltpu.VMEM((hidden, width), low),
            pltpu.VMEM((experts, cap_rows, width), low),
            pltpu.VMEM((tokens, width), jnp.float32),
            pltpu.VMEM((hidden, width), low),
        ] + sems(5, dp_count, dp_count, dp_count, dp_count, 6) + [pltpu.SemaphoreType.DMA((9,)), pltpu.SemaphoreType.DMA((4,))],
        compiler_params=pltpu.CompilerParams(
            vmem_limit_bytes=VMEM_LIMIT, collective_id=2, has_side_effects=True),
        cost_estimate=pl.CostEstimate(
            flops=12 * slots * width * hidden * tensor_count, bytes_accessed=40 << 20, transcendentals=4_000_000),
        name="middle_pass",
    )(x_send, moe_low, middle, grad, heads_all, outw, gain, router_t, routes_t, padding, slot_rows, cot, up, down, down_all)


def attend_back_sequence(heads, blocks, seq, tiles, sums, segk_ref, segq_ref, qkv, grads, lse_ref, kg, vg, dq, chosen_heads):
    scale = 1.0 / math.sqrt(DH)
    half = blocks // 2
    for h in chosen_heads:
        cols, kcols, vcols = [slice((3 * h + c) * DH, (3 * h + c + 1) * DH) for c in range(3)]
        gcols = slice(h * DH, (h + 1) * DH)
        kg[...] = jnp.zeros_like(kg)
        vg[...] = jnp.zeros_like(vg)
        for qb in range(blocks):
            nk = (qb + 1) * QB
            lower = qb * QB
            query = (qkv[seq, lower : lower + QB, cols].astype(jnp.float32) * scale).astype(jnp.bfloat16)
            grad = grads[seq * 2 + qb // half, gcols, (qb % half) * QB : (qb % half + 1) * QB]
            lse = lse_ref[seq, h : h + 1, lower : lower + QB]
            parts = score_block(qkv[seq, 0:nk, kcols], query, tiles, h, qb, segk_ref.at[seq], segq_ref.at[pl.ds(seq, 1)])
            probs = [jnp.exp(x - lse) for x in parts]
            pg = mm(qkv[seq, 0:nk, vcols], grad, NN)
            pgs = [pg[kb * QB : (kb + 1) * QB] for kb in range(qb + 1)]
            delta = functools.reduce(jnp.add, [jnp.sum(p * g, axis=0, keepdims=True) for p, g in zip(probs, pgs)])
            dqt = jnp.zeros((DH, QB), jnp.float32)
            for kb in range(qb + 1):
                rows = slice(kb * QB, (kb + 1) * QB)
                sg = (probs[kb] * (pgs[kb] - delta)).astype(jnp.bfloat16)
                sums[h, qb - kb] += sg.astype(jnp.float32)
                vg[rows] += mm(probs[kb].astype(jnp.bfloat16), grad, NT)
                kg[rows] += mm(sg, query, NN)
                dqt = dqt + mm(qkv[seq, rows, kcols], sg, TN)
            dq[lower : lower + QB, cols] = (dqt * scale).T.astype(jnp.bfloat16)
        dq[:, kcols] = kg[...].astype(jnp.bfloat16)
        dq[:, vcols] = vg[...].astype(jnp.bfloat16)


def fold_lines(sums, h, blocks):
    moved = []
    for d in range(blocks):
        folded = fold_tile(sums, h, d)
        line = folded[0:1, :]
        for s in range(1, 8):
            line = line + pltpu.roll(folded[s : s + 1, :], 2 * QB - s, 1)
        moved.append(line)
    out = []
    for d in range(blocks):
        piece = moved[d][:, :QB]
        if d + 1 < blocks:
            piece = piece + moved[d + 1][:, QB:]
        out.append(piece)
    return jnp.concatenate(out, axis=1)


def two_stage_start(send, land, s_sem, r_sem, tensor_count):
    tp = lax.axis_index("tensor")
    copies = []
    for r in range(1, tensor_count):
        copies.append(remote(send, land.at[r - 1], s_sem.at[r], r_sem.at[r], "tensor", lax.rem(tp + r, tensor_count)))
    for c in copies:
        c.start()
    return copies


def last_kernel(sizes, x_ref, gain_ref, middle_ref, mgrad_in, hgrad_ref, rows_in, w_in, qkv_in, lse_ref, line_ref,
                segk_ref, segq_ref, produced_ref, slots_ref, gates_ref, early_ref, bucket_ref,
                out_part, up_pair,
                out_ref, input_grad_ref, wgrad_ref, early_out, late_out, up_land,
                tiles, sums, kg, vg, dq, grads, landed, npart, near_land, far_land, pair, wsum, wsend, wland,
                early_land, early_mid, early_dp, late, late_land, late_mid, late_dp, total, mgrad_ref, rows, w_ref, qkv,
                out_land, out_pair, out_far,
                h_s, h_r, p_s, p_r, n_s, n_r, w_s, w_r, et_s, et_r, ed_s, ed_r, lt_s, lt_r, ld_s, ld_r, o_s, o_r, load_sem):
    dp_count, tensor_count, experts, capacity, cap_rows, heads, blocks, gather_w = sizes
    dp = lax.axis_index("dp")
    tp, sib, opp, across = partners(tensor_count)
    tokens, width = x_ref.shape
    inner = heads * DH
    wait_barrier = greet(dp_count, tensor_count)
    loads = [pltpu.make_async_copy(src, dst, load_sem.at[k]) for k, (src, dst) in enumerate((
        (qkv_in, qkv), (rows_in, rows), (w_in, w_ref), (produced_ref.at[dp], landed.at[dp]), (middle_ref, total),
        (mgrad_in, mgrad_ref)))]
    for c in loads:
        c.start()
    build_bias(line_ref, tiles, heads, blocks)
    sums[...] = jnp.zeros_like(sums)
    dq[:, :, 3 * inner :] = jnp.zeros((2, dq.shape[1], dq.shape[2] - 3 * inner), jnp.bfloat16)
    own_seq = tp // 2
    other = 1 - own_seq
    wait_barrier()

    def h_copy(k, to):
        return remote(hgrad_ref.at[to], grads.at[tp], h_s.at[k], h_r.at[k], "tensor", to)
    h_copy(0, opp).start()
    h_copy(1, across).start()
    h_copy(2, sib).start()
    grads[tp] = hgrad_ref[tp]

    def p_copy(r):
        to = peer(r)
        return remote(produced_ref.at[to], landed.at[dp], p_s.at[r], p_r.at[r], "dp", to)
    sent = list(range(dp_count // 2, dp_count)) + list(range(1, dp_count // 2))
    for r in sent:
        p_copy(r).start()

    early = two_stage_start(early_ref.at[pl.ds(8, experts)], early_land, et_s, et_r, tensor_count)

    def early_copy(r):
        return remote(early_mid, early_dp.at[r], ed_s.at[r], ed_r.at[r], "dp", peer(r))

    out_near = [remote(out_part.at[t], out_land.at[k], o_s.at[k], o_r.at[k], "tensor", sib)
                for k, t in enumerate((across, sib))]
    out_across = remote(out_pair, out_far, o_s.at[2], o_r.at[2], "tensor", opp)
    for c in out_near:
        c.start()

    up_rest = remote(up_pair.at[pl.ds(up_pair.shape[0] // 4, up_land.shape[0])], up_land, o_s.at[3], o_r.at[3],
                     "tensor", opp)

    def n_copy(k, src, dst, to):
        return remote(src, dst, n_s.at[k], n_r.at[k], "tensor", to)
    pair_near = n_copy(0, npart.at[across], near_land.at[0], sib)
    pair_far = n_copy(1, pair, far_land, opp)
    own_near = n_copy(2, npart.at[sib], near_land.at[1], sib)
    packed = dq.shape[2]

    def attend_part(seq, k, chosen_heads):
        attend_back_sequence(heads, blocks, seq, tiles, sums, segk_ref, segq_ref, qkv, grads, lse_ref, kg, vg,
                             dq.at[k], chosen_heads)

    def norm_part(seq, k):
        here = rows[pl.ds(seq * 2, 2)].reshape(2 * tokens, width)
        norm = mm(dq[k], w_ref[...].reshape(width, w_ref.shape[2])[:, :packed], NT)
        column = jnp.sum(norm * here.astype(jnp.float32), axis=0, keepdims=True)
        low = norm.astype(jnp.bfloat16)
        npart[seq * 2] = low[:tokens]
        npart[seq * 2 + 1] = low[tokens:]
        return column

    share = width // dp_count
    side = peer(1)
    columns = dp_count // 2
    lanes = wsum.shape[1] // 2

    def share_rows(d):
        return pl.ds(pl.multiple_of(d * share, 8), share)

    def side_copy(m, k):
        n = 2 * columns * m + k
        return remote(wsend.at[n], wland.at[n], w_s.at[n], w_r.at[n], "dp", side)

    def column_copy(m, k):
        n = 2 * columns * m + columns + k
        return remote(wsend.at[n], wland.at[n], w_s.at[n], w_r.at[n], "dp", peer(2 * k))

    def side_go(m):
        for k in list(range(1, columns)) + [0]:
            there = share_rows(jnp.bitwise_xor(side, 2 * k))
            wsend[2 * columns * m + k] = wsum[there, m * lanes : (m + 1) * lanes].astype(jnp.bfloat16)
            side_copy(m, k).start()

    def column_go(m):
        for k in range(1, columns):
            side_copy(m, k).wait_recv()
            mine = wsum[share_rows(peer(2 * k)), m * lanes : (m + 1) * lanes]
            n = 2 * columns * m + columns + k
            wsend[n] = (mine + wland[2 * columns * m + k].astype(jnp.float32)).astype(jnp.bfloat16)
            column_copy(m, k).start()

    out_near[0].wait_recv()
    out_pair[...] = (out_part[opp].astype(jnp.float32) + out_land[0].astype(jnp.float32)).astype(jnp.bfloat16)
    out_across.start()
    loads[0].wait()
    h_copy(2, sib).wait_recv()
    attend_part(own_seq, 0, range(1))
    loads[1].wait()
    loads[2].wait()
    up_rest.start()
    h_copy(0, opp).wait_recv()
    h_copy(1, across).wait_recv()
    attend_part(other, 1, range(heads))
    gain_row = norm_part(other, 1)
    pair_near.start()
    wsum[:, :packed] = mm(rows[pl.ds(other * 2, 2)].reshape(2 * tokens, width), dq[1], TN)
    out_across.wait_recv()
    out_near[1].wait_recv()
    out_whole = out_part[tp].astype(jnp.float32) + out_land[1].astype(jnp.float32) + out_far[...].astype(jnp.float32)
    wsum[:, 3 * inner :] = out_whole.T
    pair_near.wait_recv()
    pair[...] = (npart[opp].astype(jnp.float32) + near_land[0].astype(jnp.float32)).astype(jnp.bfloat16)
    pair_far.start()
    attend_part(own_seq, 0, range(1, 2))
    wsum[:, :lanes] += mm(rows[pl.ds(own_seq * 2, 2)].reshape(2 * tokens, width), dq[0, :, :lanes], TN)
    side_go(0)
    for c in early:
        c.wait_recv()
    early_mid[...] = early_ref[8:, :] + early_land[0] + early_land[1] + early_land[2]
    each_peer(dp_count, lambda r: early_copy(r).start())
    attend_part(own_seq, 0, range(2, heads))
    column_go(0)
    wsum[:, lanes : 3 * inner] += mm(rows[pl.ds(own_seq * 2, 2)].reshape(2 * tokens, width), dq[0, :, lanes:packed], TN)[:, : 3 * inner - lanes]
    side_go(1)
    gain_row = gain_row + norm_part(own_seq, 0)
    own_near.start()

    gain_row = gain_row / gain_ref[...].reshape(1, width)
    late[...] = jnp.zeros_like(late)
    pieces = width // 128
    for k in range(pieces):
        late[k : k + 1, :] = gain_row[:, k * 128 : (k + 1) * 128]
        late[pieces + k : pieces + k + 1, :] = early_ref[0:1, k * 128 : (k + 1) * 128]
    ids = lax.broadcasted_iota(jnp.int32, (NB, bucket_ref.shape[1]), 0)
    hot = ids == bucket_ref[...]
    place = lax.broadcasted_iota(jnp.int32, (NB, 128), 1) - lax.broadcasted_iota(jnp.int32, (NB, 128), 0)
    table = jnp.zeros((1, 128), jnp.float32)
    for h in range(heads):
        column = jnp.sum(jnp.where(hot, fold_lines(sums, h, blocks), 0.0), axis=1, keepdims=True)
        table = table + jnp.sum(jnp.where(place == h * NB, column, 0.0), axis=0, keepdims=True)
    late[pl.ds(2 * pieces + tp, 1), :] = table
    late_first = two_stage_start(late, late_land, lt_s, lt_r, tensor_count)

    def late_copy(r):
        return remote(late_mid, late_dp.at[r], ld_s.at[r], ld_r.at[r], "dp", peer(r))

    first, second = slots_ref[0:1, :], slots_ref[1:2, :]
    gate_first, gate_second = gates_ref[0:1, :], gates_ref[1:2, :]
    loads[3].wait()
    loads[4].wait()

    def combine(e):
        total[...] += gated_rows(gate_map(first, second, gate_first, gate_second, e, cap_rows), landed[e])
    combine(dp)
    for r in range(1, dp_count // 2):
        p_copy(r).wait_recv()
        combine(peer(r))

    for c in late_first:
        c.wait_recv()
    late_mid[...] = late[...] + late_land[0] + late_land[1] + late_land[2]
    each_peer(dp_count, lambda r: late_copy(r).start())
    column_go(1)
    for r in range(dp_count // 2, dp_count):
        p_copy(r).wait_recv()
        combine(peer(r))
    out_ref[...] = total[...]

    each_peer(dp_count, lambda r: early_copy(r).wait_recv())
    summed = early_mid[...]
    for r in range(1, dp_count):
        summed = summed + early_dp[r]
    early_out[...] = summed
    loads[5].wait()

    own_near.wait_recv()
    pair_far.wait_recv()
    norm_grad = npart[tp].astype(jnp.float32) + near_land[1].astype(jnp.float32) + far_land[...].astype(jnp.float32)
    x = x_ref[...].astype(jnp.float32)
    r = lax.rsqrt(jnp.mean(x * x, axis=-1, keepdims=True) + EPSILON)
    u = x * r
    du = norm_grad * gain_ref[...].reshape(1, width)
    input_grad_ref[...] = mgrad_ref[...] + r * (du - u * jnp.mean(du * u, axis=-1, keepdims=True))

    for m in range(2):
        half = slice(m * lanes, (m + 1) * lanes)
        side_copy(m, 0).wait_recv()
        part = wsum[share_rows(dp), half] + wland[2 * columns * m].astype(jnp.float32)
        for k in range(1, columns):
            column_copy(m, k).wait_recv()
            part = part + wland[2 * columns * m + columns + k].astype(jnp.float32)
        wgrad_ref[:, half] = part
    up_rest.wait_recv()

    each_peer(dp_count, lambda r: late_copy(r).wait_recv())
    summed = late_mid[...]
    for r in range(1, dp_count):
        summed = summed + late_dp[r]
    late_out[...] = summed

    for c in early + late_first + out_near + [out_across, pair_near, pair_far, own_near, h_copy(0, opp), h_copy(1, across), h_copy(2, sib)]:
        c.wait_send()

    def drain(r):
        early_copy(r).wait_send()
        late_copy(r).wait_send()
    each_peer(dp_count, drain)
    for r in sent:
        p_copy(r).wait_send()
    for m in range(2):
        for k in range(columns):
            side_copy(m, k).wait_send()
            if k:
                column_copy(m, k).wait_send()
    up_rest.wait_send()


def last_pass(sizes, x, gain, middle, middle_grad, heads_grad, rows, w, qkv, lse, line, segk, segq, produced,
              slot_rows, gates, early, bucket_row, out_part, up_pair):
    dp_count, tensor_count, experts, capacity, cap_rows, heads, blocks, gather_w = sizes
    tokens, width = x.shape
    inner = heads * DH
    seq_len = blocks * QB
    share = width // dp_count
    vmem = pl.BlockSpec(memory_space=pltpu.VMEM)
    anywhere = pl.BlockSpec(memory_space=pl.ANY)
    shape = jax.ShapeDtypeStruct
    low, full = jnp.bfloat16, jnp.float32
    late = 16
    packed = qkv.shape[2]
    return pl.pallas_call(
        functools.partial(last_kernel, sizes),
        in_specs=[vmem] * 2 + [anywhere] * 2 + [vmem] + [anywhere] * 3 + [vmem] * 4 + [anywhere] + [vmem] * 5 + [anywhere],
        out_specs=[vmem] * 5 + [anywhere],
        out_shape=[
            shape((tokens, width), full),
            shape((tokens, width), full),
            shape((share, w.shape[2]), full),
            shape((experts, width), full),
            shape((late, 128), full),
            shape((3 * up_pair.shape[0] // 4, width), low),
        ],
        scratch_shapes=[
            pltpu.VMEM((heads, blocks, QB, QB), full),
            pltpu.VMEM((heads, blocks, QB, QB), full),
            pltpu.VMEM((seq_len, DH), full),
            pltpu.VMEM((seq_len, DH), full),
            pltpu.VMEM((2, seq_len, packed), low),
            pltpu.VMEM((tensor_count, inner, tokens), low),
            pltpu.VMEM((experts, cap_rows, width), low),
            pltpu.VMEM((tensor_count, tokens, width), low),
            pltpu.VMEM((2, tokens, width), low),
            pltpu.VMEM((tokens, width), low),
            pltpu.VMEM((tokens, width), low),
            pltpu.VMEM((width, w.shape[2]), full),
            pltpu.VMEM((2 * dp_count, share, w.shape[2] // 2), low),
            pltpu.VMEM((2 * dp_count, share, w.shape[2] // 2), low),
            pltpu.VMEM((tensor_count - 1, experts, width), full),
            pltpu.VMEM((experts, width), full),
            pltpu.VMEM((dp_count, experts, width), full),
            pltpu.VMEM((late, 128), full),
            pltpu.VMEM((tensor_count - 1, late, 128), full),
            pltpu.VMEM((late, 128), full),
            pltpu.VMEM((dp_count, late, 128), full),
            pltpu.VMEM((tokens, width), full),
            pltpu.VMEM((tokens, width), full),
            pltpu.VMEM(rows.shape, low),
            pltpu.VMEM(w.shape, low),
            pltpu.VMEM(qkv.shape, low),
            pltpu.VMEM((2, inner, width), low),
            pltpu.VMEM((inner, width), low),
            pltpu.VMEM((inner, width), low),
        ] + sems(3, dp_count, 3, 2 * dp_count, tensor_count, dp_count, tensor_count, dp_count, 4) + [pltpu.SemaphoreType.DMA((6,))],
        compiler_params=pltpu.CompilerParams(
            vmem_limit_bytes=VMEM_LIMIT, collective_id=3, has_side_effects=True),
        cost_estimate=pl.CostEstimate(flops=30_000_000_000, bytes_accessed=30 << 20, transcendentals=4_000_000),
        name="last_pass",
    )(x, gain, middle, middle_grad, heads_grad, rows, w, qkv, lse, line, segk, segq, produced, slot_rows, gates,
      early, bucket_row, out_part, up_pair)


def finish_kernel(out_ref, input_grad_ref, wgrad_ref, early_ref, late_ref, up_own, up_first, up_rest, down_own, down_land,
                  out, input_grad, w_qkv_grad, w_out_grad, table, gain_attn, gain_moe, router, up_grad, down_grad):
    out[...] = out_ref[...]
    input_grad[...] = input_grad_ref[...]
    land = jnp.where(pl.program_id(0) == 0, up_first[...].astype(jnp.float32), up_rest[...].astype(jnp.float32))
    up_grad[...] = up_own[...].astype(jnp.float32) + land
    down_grad[...] = down_own[...].astype(jnp.float32) + down_land[...].astype(jnp.float32)

    @pl.when(pl.program_id(0) == 0)
    def _():
        inner = w_qkv_grad.shape[2]
        for h in range(inner // DH):
            for c in range(3):
                n = (3 * h + c) * DH
                w_qkv_grad[c, :, h * DH : (h + 1) * DH] = wgrad_ref[:, n : n + DH]
        w_out_grad[...] = wgrad_ref[:, 3 * inner :].T
        pieces = gain_attn.shape[0] // 128
        heads = inner // DH
        for h in range(table.shape[0]):
            place = (h % heads) * NB
            table[h : h + 1, :] = late_ref[2 * pieces + h // heads : 2 * pieces + h // heads + 1, place : place + NB]
        for base, gain in ((0, gain_attn), (pieces, gain_moe)):
            row = jnp.concatenate([late_ref[base + k : base + k + 1, :] for k in range(pieces)], axis=1)
            gain[...] = row.reshape(gain.shape)
        router[...] = early_ref[...]


def finish(heads_total, out, input_grad, wgrad, early, late, up_own, up_first, up_rest, down_own, down_land):
    steps = 4
    tokens, width = out.shape
    share = wgrad.shape[0]
    inner = wgrad.shape[1] // 4
    hidden = up_own.shape[0]
    full = jnp.float32
    shape = jax.ShapeDtypeStruct

    def rows(n):
        return pl.BlockSpec((n // steps, width), lambda s: (s, 0))

    def whole(*dims):
        return pl.BlockSpec(dims, lambda s: (0,) * len(dims))
    return pl.pallas_call(
        finish_kernel,
        grid=(steps,),
        in_specs=[rows(tokens), rows(tokens), whole(*wgrad.shape), whole(*early.shape), whole(*late.shape)]
        + [rows(hidden), whole(*up_first.shape),
           pl.BlockSpec((hidden // steps, width), lambda s: (jnp.maximum(s - 1, 0), 0))] + [rows(hidden)] * 2,
        out_specs=[rows(tokens), rows(tokens), whole(3, share, inner), whole(inner, share), whole(heads_total, NB),
                   whole(width), whole(width), whole(*early.shape), rows(hidden), rows(hidden)],
        out_shape=[shape((tokens, width), full), shape((tokens, width), full), shape((3, share, inner), full),
                   shape((inner, share), full), shape((heads_total, NB), full), shape((width,), full),
                   shape((width,), full), shape(early.shape, full), shape((hidden, width), full),
                   shape((hidden, width), full)],
        compiler_params=pltpu.CompilerParams(vmem_limit_bytes=VMEM_LIMIT),
        cost_estimate=pl.CostEstimate(flops=0, bytes_accessed=16 << 20, transcendentals=0),
        name="finish",
    )(out, input_grad, wgrad, early, late, up_own, up_first, up_rest, down_own, down_land)


def norm_rows(values, gain):
    return values * lax.rsqrt(jnp.mean(values * values, axis=-1, keepdims=True) + EPSILON) * gain


def norm_back(values, gain, grad):
    r = lax.rsqrt(jnp.mean(values * values, axis=-1, keepdims=True) + EPSILON)
    u = values * r
    du = grad * gain
    return r * (du - u * jnp.mean(du * u, axis=-1, keepdims=True)), grad * u


def plain_body(
    block_input,
    out_grad,
    w_qkv,
    w_out,
    rel_table,
    gain_attn,
    gain_moe,
    w_router,
    w_up,
    w_down,
    routes,
    segments,
    padding,
    rel_bucket,
):
    tensor_pos = lax.axis_index("tensor")
    rows_local, width = block_input.shape
    seq_len = segments.shape[1]
    expert_count = w_router.shape[1]
    capacity = (10 * rows_local + 4 * expert_count - 1) // (4 * expert_count)
    slots = expert_count * capacity
    x_float = block_input.astype(jnp.float32)
    grad_float = out_grad.astype(jnp.float32)

    attn_norm = norm_rows(x_float, gain_attn).astype(jnp.bfloat16)
    seq_rows = lax.all_gather(attn_norm, "tensor", axis=0, tiled=True)
    qkv_full = lax.all_gather(w_qkv, "dp", axis=1, tiled=True)
    out_rows = lax.all_gather(w_out, "dp", axis=1, tiled=True)
    out_full = lax.all_gather(out_rows, "tensor", axis=0, tiled=True)
    up_full = lax.all_gather(w_up[0], "tensor", axis=0, tiled=True)
    down_full = lax.all_gather(w_down[0], "tensor", axis=0, tiled=True)

    live_mask = lax.dynamic_slice_in_dim(padding.reshape(-1), tensor_pos * rows_local, rows_local)
    live_float = live_mask.astype(jnp.float32)
    expert_ids = jnp.arange(expert_count, dtype=jnp.int32)
    pick_first = routes[:, 0:1] == expert_ids[None, :]
    pick_second = routes[:, 1:2] == expert_ids[None, :]
    usable = live_mask[:, None] == 1
    first_hot = (pick_first & usable).astype(jnp.int32)
    second_hot = (pick_second & usable).astype(jnp.int32)
    first_place = jnp.sum((jnp.cumsum(first_hot, axis=0) - first_hot) * first_hot, axis=1)
    second_before = (
        jnp.cumsum(second_hot, axis=0) - second_hot + jnp.sum(first_hot, axis=0, keepdims=True)
    )
    second_place = jnp.sum(second_before * second_hot, axis=1)
    first_slot = jnp.where(
        (live_mask == 1) & (first_place < capacity), routes[:, 0] * capacity + first_place, -1
    )
    second_slot = jnp.where(
        (live_mask == 1) & (second_place < capacity), routes[:, 1] * capacity + second_place, -1
    )
    slot_ids = jnp.arange(slots, dtype=jnp.int32)
    select_first = slot_ids[:, None] == first_slot[None, :]
    select_second = slot_ids[:, None] == second_slot[None, :]
    select_both = (select_first | select_second).astype(jnp.bfloat16)
    select_first_low = select_first.astype(jnp.bfloat16)
    select_second_low = select_second.astype(jnp.bfloat16)

    def to_experts(rows):
        return lax.all_to_all(rows, "dp", split_axis=0, concat_axis=0, tiled=True)

    grad_rows = jnp.dot(select_both, out_grad, preferred_element_type=jnp.float32)
    sent_grads = to_experts(grad_rows.astype(jnp.bfloat16).reshape(expert_count, capacity, width))
    sent_grads = sent_grads.reshape(slots, width)

    heads = qkv_full.shape[2] // DH
    inner = heads * DH
    table_local = lax.dynamic_slice_in_dim(rel_table, tensor_pos * heads, heads, 1)
    bucket_hot = (rel_bucket[:, None] == jnp.arange(NB, dtype=jnp.int32)[None, :]).astype(jnp.float32)
    line = line_of(jnp.dot(bucket_hot, table_local, precision=HIGHEST).T)
    segk, segq = mask_inputs(segments, padding)
    qkv_low, heads_low, lse = attend(line, segk, segq, seq_rows, qkv_full)
    heads_own = lax.all_to_all(heads_low, "tensor", split_axis=0, concat_axis=1, tiled=True)

    middle = x_float + jnp.dot(heads_own, out_full, preferred_element_type=jnp.float32)
    moe_low = norm_rows(middle, gain_moe).astype(jnp.bfloat16)
    rows_out = jnp.dot(select_both, moe_low, preferred_element_type=jnp.float32)
    sent_rows = to_experts(rows_out.astype(jnp.bfloat16).reshape(expert_count, capacity, width))
    sent_rows = sent_rows.reshape(slots, width)
    logits = jnp.dot(moe_low, w_router, preferred_element_type=jnp.float32)
    first_logit = jnp.sum(jnp.where(pick_first, logits, 0.0), axis=1)
    second_logit = jnp.sum(jnp.where(pick_second, logits, 0.0), axis=1)
    first_gate = jax.nn.sigmoid(first_logit - second_logit) * live_float
    second_gate = jax.nn.sigmoid(second_logit - first_logit) * live_float
    slot_gate = jnp.sum(
        jnp.where(select_first, first_gate[None, :], 0.0)
        + jnp.where(select_second, second_gate[None, :], 0.0),
        axis=1,
    )
    sent_gates = to_experts(slot_gate.reshape(expert_count, capacity)).reshape(slots, 1)

    act, pre_grad, back, dots = expert_first(sent_rows, sent_grads, up_full, down_full)
    returned_grad = to_experts(back.reshape(expert_count, capacity, width)).reshape(slots, width)
    slot_dots = to_experts(dots[0].reshape(expert_count, capacity)).reshape(slots)
    produced, up_part, down_part = expert_late(
        sent_rows, sent_grads, sent_gates, act, pre_grad, down_full
    )
    returned = to_experts(produced.reshape(expert_count, capacity, width)).reshape(slots, width)
    w_up_grad = lax.psum_scatter(up_part, "tensor", scatter_dimension=0, tiled=True)
    w_down_grad = lax.psum_scatter(down_part, "tensor", scatter_dimension=0, tiled=True)

    first_dot = jnp.sum(jnp.where(select_first, slot_dots[:, None], 0.0), axis=0)
    second_dot = jnp.sum(jnp.where(select_second, slot_dots[:, None], 0.0), axis=0)
    coefficient = first_gate * second_gate * (first_dot - second_dot)
    logit_grad = (
        jnp.where(pick_first, coefficient[:, None], 0.0)
        - jnp.where(pick_second, coefficient[:, None], 0.0)
    ).astype(jnp.bfloat16)
    router_grad = jnp.einsum("nd,ne->de", moe_low, logit_grad, preferred_element_type=jnp.float32)

    def gated(rows):
        first_rows = jnp.einsum("st,sd->td", select_first_low, rows, preferred_element_type=jnp.float32)
        second_rows = jnp.einsum("st,sd->td", select_second_low, rows, preferred_element_type=jnp.float32)
        return first_gate[:, None] * first_rows + second_gate[:, None] * second_rows

    moe_norm_grad = (
        jnp.einsum("ne,de->nd", logit_grad, w_router, preferred_element_type=jnp.float32)
        + gated(returned_grad)
    )
    middle_back, gain_moe_rows = norm_back(middle, gain_moe, moe_norm_grad)
    middle_grad = grad_float + middle_back
    gain_moe_grad = jnp.sum(gain_moe_rows, axis=0)
    attn_grad = middle_grad.astype(jnp.bfloat16)
    heads_grad = jnp.einsum("nd,fd->nf", attn_grad, out_full, preferred_element_type=jnp.float32)
    heads_grad = lax.all_to_all(
        heads_grad.astype(jnp.bfloat16), "tensor", split_axis=1, concat_axis=0, tiled=True
    )
    out_part = jnp.einsum("nf,nd->fd", heads_own, attn_grad, preferred_element_type=jnp.float32)
    out_part = lax.psum_scatter(out_part.astype(jnp.bfloat16), "tensor", scatter_dimension=0, tiled=True)
    w_out_grad = lax.psum_scatter(out_part.astype(jnp.float32), "dp", scatter_dimension=1, tiled=True)
    gain_moe_grad, router_grad = lax.psum((gain_moe_grad, router_grad), ("dp", "tensor"))

    norm_part, qkv_part, folded = attend_back(
        line, segk, segq, seq_rows, qkv_full, qkv_low, heads_grad, lse
    )
    attn_norm_grad = lax.psum_scatter(norm_part, "tensor", scatter_dimension=0, tiled=True)
    input_back, gain_attn_rows = norm_back(x_float, gain_attn, attn_norm_grad.astype(jnp.float32))
    input_grad = middle_grad + input_back
    gain_attn_grad = jnp.sum(gain_attn_rows, axis=0)
    w_qkv_grad = lax.psum_scatter(qkv_part, "dp", scatter_dimension=1, tiled=True)
    line_grad = lines_of(folded, heads, seq_len // QB)
    table_part = jnp.dot(bucket_hot.T, line_grad.T, precision=HIGHEST)
    table_whole = lax.dynamic_update_slice(
        jnp.zeros(rel_table.shape, jnp.float32), table_part, (0, tensor_pos * heads)
    )
    gain_attn_grad, table_whole = lax.psum((gain_attn_grad, table_whole), ("dp", "tensor"))
    block_output = middle + gated(returned)
    return (
        block_output,
        input_grad,
        w_qkv_grad,
        w_out_grad,
        table_whole,
        gain_attn_grad,
        gain_moe_grad,
        router_grad,
        w_up_grad.astype(jnp.float32)[None],
        w_down_grad.astype(jnp.float32)[None],
    )


def fused_body(
    block_input,
    out_grad,
    w_qkv,
    w_out,
    rel_table,
    gain_attn,
    gain_moe,
    w_router,
    w_up,
    w_down,
    routes,
    segments,
    padding,
    rel_bucket,
):
    dp_count, tensor_count = lax.axis_size("dp"), lax.axis_size("tensor")
    rows_local, width = block_input.shape
    seq_len = segments.shape[1]
    heads = w_qkv.shape[2] // DH
    capacity = slot_capacity(rows_local, w_router.shape[1])
    expert_count = w_router.shape[1]
    sizes = (dp_count, tensor_count, expert_count, capacity, capacity, heads, seq_len // QB, True)

    routes_t = routes.T
    bucket_row = rel_bucket[None]
    rows, w_all, outw, down_all, qkv, lse, heads_all, slot_rows, cot, line, segk, middle, moe_low, x_send = front(
        sizes, block_input, gain_attn, w_qkv, w_out, w_down[0], out_grad, routes_t, segments, padding,
        rel_table.T, bucket_row, gain_moe
    )
    (up_pair, up_own, up_first, down_own, down_land, produced, middle_grad, heads_grad, out_part, early,
     gates) = middle_pass(
        sizes, x_send, moe_low, middle, out_grad, heads_all, outw, gain_moe, w_router.T, routes_t, padding,
        slot_rows, cot, w_up[0], w_down[0], down_all
    )
    block_output, input_grad, wgrad, early, late, up_rest = last_pass(
        sizes, block_input, gain_attn, middle, middle_grad, heads_grad, rows, w_all, qkv, lse, line, segk, segments,
        produced, slot_rows, gates, early, bucket_row, out_part, up_pair
    )
    (block_output, input_grad, w_qkv_grad, w_out_grad, table_grad, gain_attn_grad, gain_moe_grad, router_grad,
     w_up_grad, w_down_grad) = finish(
        rel_table.shape[1], block_output, input_grad, wgrad, early, late, up_own, up_first, up_rest, down_own, down_land
    )
    return (
        block_output,
        input_grad,
        w_qkv_grad,
        w_out_grad,
        table_grad.T,
        gain_attn_grad,
        gain_moe_grad,
        router_grad.T,
        w_up_grad[None],
        w_down_grad[None],
    )


def slot_capacity(tokens, experts):
    return (10 * tokens + 4 * experts - 1) // (4 * experts)


def body(*args):
    block_input, w_qkv, w_router = args[0], args[2], args[7]
    capacity = slot_capacity(block_input.shape[0], w_router.shape[1])
    fits = capacity % 16 == 0 and w_qkv.shape[1] % 16 == 0 and lax.axis_size("dp") == w_router.shape[1] == 8 and block_input.shape[1] <= 1024
    return fused_body(*args) if fits else plain_body(*args)


def solution(mesh):
    in_specs = (
        P(("dp", "tensor"), None),
        P(("dp", "tensor"), None),
        P(None, "dp", "tensor"),
        P("tensor", "dp"),
        P(),
        P(),
        P(),
        P(),
        P("dp", "tensor", None),
        P("dp", "tensor", None),
        P(("dp", "tensor"), None),
        P("dp", None),
        P("dp", None),
        P(),
    )
    out_specs = (
        P(("dp", "tensor"), None),
        P(("dp", "tensor"), None),
        P(None, "dp", "tensor"),
        P("tensor", "dp"),
        P(),
        P(),
        P(),
        P(),
        P("dp", "tensor", None),
        P("dp", "tensor", None),
    )
    return jax.shard_map(body, mesh=mesh, in_specs=in_specs, out_specs=out_specs, check_vma=False)
```

```python
import functools
import math

import jax
import jax.numpy as jnp
from jax import lax
from jax.experimental import pallas as pl
from jax.experimental.pallas import tpu as pltpu
from jax.sharding import PartitionSpec as P

NB = 32
EPSILON = 1e-06
HIGHEST = lax.Precision.HIGHEST
DH = 64
NEGATIVE = -1e30
QB = 256
NT = (((1,), (1,)), ((), ()))
TN = (((0,), (0,)), ((), ()))
NN = (((1,), (0,)), ((), ()))


def mm(a, b, dims):
    return lax.dot_general(a, b, dims, preferred_element_type=jnp.float32)


def build_bias(line_ref, tiles, heads, blocks):
    for h in range(heads):
        for d in range(blocks):
            piece = line_ref[h : h + 1, d * QB : d * QB + 2 * QB]
            wide = jnp.broadcast_to(piece, (QB, 2 * QB))
            turned = pltpu.roll(wide, 0, 1, stride=1, stride_axis=0)
            tiles[h, d] = turned[:, QB:]


def score_block(keys, query, tiles, h, qb, segk_ref, segq_ref):
    raw = mm(keys, query, NT)
    q_seg = segq_ref[:, qb * QB : (qb + 1) * QB]
    parts = []
    for kb in range(qb + 1):
        k_seg = segk_ref[kb * QB : (kb + 1) * QB, :]
        same = k_seg == q_seg
        if kb == qb:
            row = lax.broadcasted_iota(jnp.int32, (QB, QB), 0)
            col = lax.broadcasted_iota(jnp.int32, (QB, QB), 1)
            same = same | (row == col)
        parts.append(
            jnp.where(same, raw[kb * QB : (kb + 1) * QB] + tiles[h, qb - kb], NEGATIVE)
        )
    return parts


def attend_kernel(heads, blocks, line_ref, segk_ref, segq_ref, rows_ref, w_ref,
                  qkv_ref, out_ref, lse_ref, tiles):
    @pl.when(pl.program_id(0) == 0)
    def _():
        build_bias(line_ref, tiles, heads, blocks)

    for c in range(3):
        qkv_ref[c] = mm(rows_ref[...], w_ref[c], NN).astype(jnp.bfloat16)
    scale = 1.0 / math.sqrt(DH)
    for qb in range(blocks):
        nk = (qb + 1) * QB
        lower = qb * QB
        turned = []
        for h in range(heads):
            cols = slice(h * DH, (h + 1) * DH)
            query = (qkv_ref[0, lower : lower + QB, cols].astype(jnp.float32) * scale).astype(jnp.bfloat16)
            parts = score_block(qkv_ref[1, 0:nk, cols], query, tiles, h, qb, segk_ref.at[0], segq_ref.at[0])
            peak = functools.reduce(jnp.maximum, [jnp.max(x, axis=0, keepdims=True) for x in parts])
            probs = [jnp.exp(x - peak) for x in parts]
            total = functools.reduce(jnp.add, [jnp.sum(x, axis=0, keepdims=True) for x in probs])
            mixed = functools.reduce(jnp.add, [
                mm(qkv_ref[2, kb * QB : (kb + 1) * QB, cols], x.astype(jnp.bfloat16), TN)
                for kb, x in enumerate(probs)])
            turned.append(mixed / total)
            lse_ref[0, h : h + 1, lower : lower + QB] = peak + jnp.log(total)
        out_ref[lower : lower + QB, :] = jnp.concatenate(turned, axis=0).T.astype(jnp.bfloat16)


def attend(line, segk, segq, rows, w):
    seqs, _, seq_len = segq.shape
    heads = line.shape[0]
    inner = heads * DH
    blocks = seq_len // QB
    width = rows.shape[1]
    return pl.pallas_call(
        functools.partial(attend_kernel, heads, blocks),
        grid=(seqs,),
        in_specs=[
            pl.BlockSpec(line.shape, lambda s: (0, 0)),
            pl.BlockSpec((1, seq_len, 1), lambda s: (s, 0, 0)),
            pl.BlockSpec((1, 1, seq_len), lambda s: (s, 0, 0)),
            pl.BlockSpec((seq_len, width), lambda s: (s, 0)),
            pl.BlockSpec(w.shape, lambda s: (0, 0, 0)),
        ],
        out_specs=[
            pl.BlockSpec((3, seq_len, inner), lambda s: (0, s, 0)),
            pl.BlockSpec((seq_len, inner), lambda s: (s, 0)),
            pl.BlockSpec((1, heads, seq_len), lambda s: (s, 0, 0)),
        ],
        out_shape=[
            jax.ShapeDtypeStruct((3, seqs * seq_len, inner), jnp.bfloat16),
            jax.ShapeDtypeStruct((seqs * seq_len, inner), jnp.bfloat16),
            jax.ShapeDtypeStruct((seqs, heads, seq_len), jnp.float32),
        ],
        scratch_shapes=[pltpu.VMEM((heads, blocks, QB, QB), jnp.float32)],
        compiler_params=pltpu.CompilerParams(vmem_limit_bytes=48 << 20),
        cost_estimate=pl.CostEstimate(flops=10_000_000_000, bytes_accessed=10 << 20, transcendentals=4_000_000),
        name="attend",
    )(line, segk, segq, rows, w)


def attend_back_kernel(heads, blocks, seqs, line_ref, segk_ref, segq_ref, rows_ref, w_ref,
                       qkv_ref, og_ref, lse_ref,
                       norm_ref, wg_ref, lg_ref, tiles, sums, kg, vg, dq):
    step = pl.program_id(0)

    @pl.when(step == 0)
    def _():
        build_bias(line_ref, tiles, heads, blocks)
        sums[...] = jnp.zeros_like(sums)
        wg_ref[...] = jnp.zeros_like(wg_ref)

    scale = 1.0 / math.sqrt(DH)
    for h in range(heads):
        cols = slice(h * DH, (h + 1) * DH)
        kg[...] = jnp.zeros_like(kg)
        vg[...] = jnp.zeros_like(vg)
        for qb in range(blocks):
            nk = (qb + 1) * QB
            lower = qb * QB
            query = (qkv_ref[0, lower : lower + QB, cols].astype(jnp.float32) * scale).astype(jnp.bfloat16)
            grad = og_ref[lower : lower + QB, cols]
            lse = lse_ref[0, h : h + 1, lower : lower + QB]
            parts = score_block(qkv_ref[1, 0:nk, cols], query, tiles, h, qb, segk_ref.at[0], segq_ref.at[0])
            probs = [jnp.exp(x - lse) for x in parts]
            pg = mm(qkv_ref[2, 0:nk, cols], grad, NT)
            pgs = [pg[kb * QB : (kb + 1) * QB] for kb in range(qb + 1)]
            delta = functools.reduce(jnp.add, [jnp.sum(p * g, axis=0, keepdims=True) for p, g in zip(probs, pgs)])
            dqt = jnp.zeros((DH, QB), jnp.float32)
            for kb in range(qb + 1):
                rows = slice(kb * QB, (kb + 1) * QB)
                sg = (probs[kb] * (pgs[kb] - delta)).astype(jnp.bfloat16)
                sums[h, qb - kb] += sg.astype(jnp.float32)
                vg[rows] += mm(probs[kb].astype(jnp.bfloat16), grad, NN)
                kg[rows] += mm(sg, query, NN)
                dqt = dqt + mm(qkv_ref[1, rows, cols], sg, TN)
            dq[lower : lower + QB, h * DH : (h + 1) * DH] = (dqt * scale).T.astype(jnp.bfloat16)
        inner = heads * DH
        dq[:, inner + h * DH : inner + (h + 1) * DH] = kg[...].astype(jnp.bfloat16)
        dq[:, 2 * inner + h * DH : 2 * inner + (h + 1) * DH] = vg[...].astype(jnp.bfloat16)
    inner = heads * DH
    total = jnp.zeros(norm_ref.shape, jnp.float32)
    for c in range(3):
        piece = dq[:, c * inner : (c + 1) * inner]
        wg_ref[c] += mm(rows_ref[...], piece, TN)
        total = total + mm(piece, w_ref[c], NT)
    norm_ref[...] = total.astype(norm_ref.dtype)

    @pl.when(step == seqs - 1)
    def _():
        for h in range(heads):
            for d in range(blocks):
                lg_ref[h * blocks + d] = fold_tile(sums, h, d)


def fold_tile(sums, h, d):
    blank = jnp.zeros((8, QB), jnp.float32)
    total = jnp.zeros((8, 2 * QB), jnp.float32)
    for g in range(QB // 8):
        piece = jnp.concatenate([sums[h, d, 8 * g : 8 * g + 8, :], blank], axis=1)
        total = total + (piece if g == 0 else pltpu.roll(piece, 2 * QB - 8 * g, 1))
    return total


def lines_of(folded, heads, blocks):
    moved = sum(jnp.roll(folded[:, s, :], -s, axis=1) for s in range(8))
    moved = moved.reshape(heads, blocks, 2, QB)
    ahead = jnp.concatenate([moved[:, 1:, 1], jnp.zeros((heads, 1, QB), jnp.float32)], axis=1)
    return (moved[:, :, 0] + ahead).reshape(heads, blocks * QB)


def attend_back(line, segk, segq, rows, w, qkv, og, lse):
    seqs, _, seq_len = segq.shape
    heads = line.shape[0]
    inner = heads * DH
    blocks = seq_len // QB
    width = rows.shape[1]
    return pl.pallas_call(
        functools.partial(attend_back_kernel, heads, blocks, seqs),
        grid=(seqs,),
        in_specs=[
            pl.BlockSpec(line.shape, lambda s: (0, 0)),
            pl.BlockSpec((1, seq_len, 1), lambda s: (s, 0, 0)),
            pl.BlockSpec((1, 1, seq_len), lambda s: (s, 0, 0)),
            pl.BlockSpec((seq_len, width), lambda s: (s, 0)),
            pl.BlockSpec(w.shape, lambda s: (0, 0, 0)),
            pl.BlockSpec((3, seq_len, inner), lambda s: (0, s, 0)),
            pl.BlockSpec((seq_len, inner), lambda s: (s, 0)),
            pl.BlockSpec((1, heads, seq_len), lambda s: (s, 0, 0)),
        ],
        out_specs=[
            pl.BlockSpec((seq_len, width), lambda s: (s, 0)),
            pl.BlockSpec(w.shape, lambda s: (0, 0, 0)),
            pl.BlockSpec((heads * blocks, 8, 2 * QB), lambda s: (0, 0, 0)),
        ],
        out_shape=[
            jax.ShapeDtypeStruct((seqs * seq_len, width), jnp.bfloat16),
            jax.ShapeDtypeStruct(w.shape, jnp.float32),
            jax.ShapeDtypeStruct((heads * blocks, 8, 2 * QB), jnp.float32),
        ],
        scratch_shapes=[
            pltpu.VMEM((heads, blocks, QB, QB), jnp.float32),
            pltpu.VMEM((heads, blocks, QB, QB), jnp.float32),
            pltpu.VMEM((seq_len, DH), jnp.float32),
            pltpu.VMEM((seq_len, DH), jnp.float32),
            pltpu.VMEM((seq_len, 3 * inner), jnp.bfloat16),
        ],
        compiler_params=pltpu.CompilerParams(vmem_limit_bytes=48 << 20),
        cost_estimate=pl.CostEstimate(flops=20_000_000_000, bytes_accessed=16 << 20, transcendentals=4_000_000),
        name="attend_back",
    )(line, segk, segq, rows, w, qkv, og, lse)


def mask_inputs(segments, padding):
    keyed = jnp.where(padding == 1, segments, -1)
    return keyed[:, :, None], segments[:, None, :]


def line_of(by_distance):
    return jnp.concatenate([jnp.full((by_distance.shape[0], QB), NEGATIVE, jnp.float32), by_distance], axis=1)


FT = 512
ROOT_2_PI = math.sqrt(2.0 / math.pi)


def gelu_pair(x):
    square = x * x
    t = jnp.tanh(ROOT_2_PI * x * (1.0 + 0.044715 * square))
    half = 0.5 * (1.0 + t)
    slope = half + 0.5 * x * (1.0 - t * t) * (ROOT_2_PI * (1.0 + 3 * 0.044715 * square))
    return x * half, slope


def expert_kernel(steps, x_ref, g_ref, up_ref, down_ref, act_ref, pre_ref, back_ref, dot_ref, total, dots):
    step = pl.program_id(0)

    @pl.when(step == 0)
    def _():
        total[...] = jnp.zeros_like(total)
        dots[...] = jnp.zeros_like(dots)

    rows = x_ref.shape[0]
    chunk = 256
    for lower in range(0, rows, chunk):
        part = slice(lower, lower + chunk)
        pre = mm(x_ref[part], up_ref[...], NT)
        out_side = mm(g_ref[part], down_ref[...], NT)
        act, slope = gelu_pair(pre)
        low = act.astype(jnp.bfloat16)
        act_ref[part] = low
        product = low.astype(jnp.float32) * out_side
        dots[part] += sum(product[:, k : k + 128] for k in range(0, FT, 128))
        back = (out_side * slope).astype(jnp.bfloat16)
        pre_ref[part] = back
        total[part] += mm(back, up_ref[...], NN)

    @pl.when(step == steps - 1)
    def _():
        back_ref[...] = total[...].astype(jnp.bfloat16)
        dot_ref[...] = lax.dot_general(
            jnp.ones((8, 128), jnp.float32), dots[...], NT,
            precision=HIGHEST, preferred_element_type=jnp.float32)


def expert_first(x, g, up, down):
    rows, width = x.shape
    hidden = up.shape[0]
    steps = hidden // FT
    whole = lambda f: (0, 0)
    return pl.pallas_call(
        functools.partial(expert_kernel, steps),
        grid=(steps,),
        in_specs=[
            pl.BlockSpec((rows, width), whole),
            pl.BlockSpec((rows, width), whole),
            pl.BlockSpec((FT, width), lambda f: (f, 0)),
            pl.BlockSpec((FT, width), lambda f: (f, 0)),
        ],
        out_specs=[
            pl.BlockSpec((rows, FT), lambda f: (0, f)),
            pl.BlockSpec((rows, FT), lambda f: (0, f)),
            pl.BlockSpec((rows, width), whole),
            pl.BlockSpec((8, rows), whole),
        ],
        out_shape=[
            jax.ShapeDtypeStruct((rows, hidden), jnp.bfloat16),
            jax.ShapeDtypeStruct((rows, hidden), jnp.bfloat16),
            jax.ShapeDtypeStruct((rows, width), jnp.bfloat16),
            jax.ShapeDtypeStruct((8, rows), jnp.float32),
        ],
        scratch_shapes=[
            pltpu.VMEM((rows, width), jnp.float32),
            pltpu.VMEM((rows, 128), jnp.float32),
        ],
        compiler_params=pltpu.CompilerParams(vmem_limit_bytes=48 << 20),
        cost_estimate=pl.CostEstimate(
            flops=6 * rows * width * hidden, bytes_accessed=32 << 20, transcendentals=rows * hidden),
        name="expert_first",
    )(x, g, up, down)


def expert_late_kernel(steps, x_ref, g_ref, gate_ref, act_ref, pre_ref, down_ref,
                       out_ref, up_grad_ref, down_grad_ref, total, x_gated, g_gated):
    step = pl.program_id(0)

    @pl.when(step == 0)
    def _():
        total[...] = jnp.zeros_like(total)
        gate = gate_ref[...]
        x_gated[...] = (x_ref[...].astype(jnp.float32) * gate).astype(jnp.bfloat16)
        g_gated[...] = (g_ref[...].astype(jnp.float32) * gate).astype(jnp.bfloat16)

    up_grad_ref[...] = mm(pre_ref[...], x_gated[...], TN).astype(up_grad_ref.dtype)
    down_grad_ref[...] = mm(act_ref[...], g_gated[...], TN).astype(down_grad_ref.dtype)
    total[...] += mm(act_ref[...], down_ref[...], NN)

    @pl.when(step == steps - 1)
    def _():
        out_ref[...] = total[...].astype(jnp.bfloat16)


def expert_late(x, g, gate, act, pre, down):
    rows, width = x.shape
    hidden = down.shape[0]
    steps = hidden // FT
    whole = lambda f: (0, 0)
    tile = pl.BlockSpec((FT, width), lambda f: (f, 0))
    return pl.pallas_call(
        functools.partial(expert_late_kernel, steps),
        grid=(steps,),
        in_specs=[
            pl.BlockSpec((rows, width), whole),
            pl.BlockSpec((rows, width), whole),
            pl.BlockSpec((rows, 1), whole),
            pl.BlockSpec((rows, FT), lambda f: (0, f)),
            pl.BlockSpec((rows, FT), lambda f: (0, f)),
            tile,
        ],
        out_specs=[pl.BlockSpec((rows, width), whole), tile, tile],
        out_shape=[
            jax.ShapeDtypeStruct((rows, width), jnp.bfloat16),
            jax.ShapeDtypeStruct((hidden, width), jnp.bfloat16),
            jax.ShapeDtypeStruct((hidden, width), jnp.bfloat16),
        ],
        scratch_shapes=[
            pltpu.VMEM((rows, width), jnp.float32),
            pltpu.VMEM((rows, width), jnp.bfloat16),
            pltpu.VMEM((rows, width), jnp.bfloat16),
        ],
        compiler_params=pltpu.CompilerParams(vmem_limit_bytes=48 << 20),
        cost_estimate=pl.CostEstimate(
            flops=6 * rows * width * hidden, bytes_accessed=32 << 20, transcendentals=0),
        name="expert_late",
    )(x, g, gate, act, pre, down)


MESH = pl.DeviceIdType.MESH
VMEM_LIMIT = 61 << 20


def remote(src, dst, send, recv, axis, place):
    return pltpu.make_async_remote_copy(
        src_ref=src, dst_ref=dst, send_sem=send, recv_sem=recv, device_id={axis: place}, device_id_type=MESH
    )


def each_peer(count, step, start=1):
    if count <= 8:
        for r in range(start, count):
            step(r)
    else:
        def one(r, carry):
            step(r)
            return carry
        lax.fori_loop(start, count, one, 0)


def peer(r):
    return jnp.bitwise_xor(lax.axis_index("dp"), r)


def greet(dp_count, tensor_count):
    barrier = pltpu.get_barrier_semaphore()
    dp, tp = lax.axis_index("dp"), lax.axis_index("tensor")
    for r in range(1, tensor_count):
        pl.semaphore_signal(barrier, inc=1, device_id={"tensor": lax.rem(tp + r, tensor_count)}, device_id_type=MESH)

    def signal(r):
        pl.semaphore_signal(barrier, inc=1, device_id={"dp": peer(r)}, device_id_type=MESH)
    each_peer(dp_count, signal)
    return lambda: pl.semaphore_wait(barrier, tensor_count - 1 + dp_count - 1)


def partners(tensor_count):
    tp = lax.axis_index("tensor")
    sib = tp + 1 - 2 * lax.rem(tp, 2)
    return tp, sib, lax.rem(tp + 2, tensor_count), lax.rem(sib + 2, tensor_count)


def place_pairs(routes_ref, live, experts, capacity, cap_rows):
    tokens = live.shape[1]
    live = live == 1
    ids = lax.broadcasted_iota(jnp.int32, (experts, tokens), 0)
    row = lax.broadcasted_iota(jnp.int32, (tokens, tokens), 0)
    col = lax.broadcasted_iota(jnp.int32, (tokens, tokens), 1)
    before = (row < col).astype(jnp.float32).astype(jnp.bfloat16)
    slots = []
    base = jnp.zeros((experts, 1), jnp.float32)
    for k in range(2):
        route = routes_ref[k : k + 1, :]
        hot = jnp.where((ids == route) & live, 1.0, 0.0)
        count = mm(hot.astype(jnp.bfloat16), before, NN) + base
        place = jnp.sum(count * hot, axis=0, keepdims=True).astype(jnp.int32)
        slots.append(jnp.where(live & (place < capacity), route * cap_rows + place, -1))
        base = base + jnp.sum(hot, axis=1, keepdims=True)
    return slots


def chosen(first, second, expert, cap_rows):
    ids = lax.broadcasted_iota(jnp.int32, (cap_rows, first.shape[1]), 0) + expert * cap_rows
    return jnp.where((ids == first) | (ids == second), 1.0, 0.0).astype(jnp.bfloat16)


def attend_sequence(heads, blocks, seq, line_tiles, segk_ref, segq_ref, qkv, heads_out, lse_ref):
    scale = 1.0 / math.sqrt(DH)
    half = blocks // 2
    for qb in range(blocks):
        nk = (qb + 1) * QB
        lower = qb * QB
        for h in range(heads):
            cols = [slice((3 * h + c) * DH, (3 * h + c + 1) * DH) for c in range(3)]
            query = (qkv[seq, lower : lower + QB, cols[0]].astype(jnp.float32) * scale).astype(jnp.bfloat16)
            parts = score_block(qkv[seq, 0:nk, cols[1]], query, line_tiles, h, qb, segk_ref.at[seq], segq_ref.at[pl.ds(seq, 1)])
            peak = functools.reduce(jnp.maximum, [jnp.max(x, axis=0, keepdims=True) for x in parts])
            probs = [jnp.exp(x - peak) for x in parts]
            total = functools.reduce(jnp.add, [jnp.sum(x, axis=0, keepdims=True) for x in probs])
            mixed = functools.reduce(jnp.add, [
                mm(qkv[seq, kb * QB : (kb + 1) * QB, cols[2]], x.astype(jnp.bfloat16), TN)
                for kb, x in enumerate(probs)])
            heads_out[seq * 2 + qb // half, h * DH : (h + 1) * DH, (qb % half) * QB : (qb % half + 1) * QB] = (
                mixed / total).astype(jnp.bfloat16)
            lse_ref[seq, h : h + 1, lower : lower + QB] = peak + jnp.log(total)


def packed_gather(own_ref, all_ref, send, recv, dp_count):
    dp = lax.axis_index("dp")
    side = peer(1)
    columns = dp_count // 2
    near = remote(own_ref, all_ref.at[dp], send.at[0], recv.at[0], "dp", side)
    out = [remote(own_ref, all_ref.at[dp], send.at[k], recv.at[k], "dp", peer(2 * k))
           for k in range(1, columns)]
    onward = []
    for k in range(1, columns):
        src = peer(2 * k)
        n = columns - 1 + k
        onward.append(remote(all_ref.at[src], all_ref.at[src], send.at[n], recv.at[n], "dp", side))
    return near, out, onward


def prepare(heads, tp, table_ref, bucket_ref, segments_ref, padding_ref, line_ref, segk_ref):
    buckets, length = table_ref.shape[1], bucket_ref.shape[1]
    ids = lax.broadcasted_iota(jnp.int32, (buckets, length), 0)
    hot = ids == bucket_ref[...]
    for h in range(heads):
        column = to_column(table_ref[pl.ds(tp * heads + h, 1), :], buckets)
        line_ref[h : h + 1, :QB] = jnp.full((1, QB), NEGATIVE, jnp.float32)
        line_ref[h : h + 1, QB:] = jnp.sum(jnp.where(hot, column, 0.0), axis=0, keepdims=True)
    keyed = jnp.where(padding_ref[...] == 1, segments_ref[...], -1).astype(jnp.float32)
    for s in range(keyed.shape[0]):
        for k in range(length // QB):
            piece = keyed[s : s + 1, k * QB : (k + 1) * QB]
            segk_ref[s, k * QB : (k + 1) * QB, :] = to_column(piece, QB).astype(jnp.int32)


def front_kernel(sizes, x_ref, gain_ref, w_ref, outw_ref, down_ref, grad_ref, routes_ref, segments_ref, padding_ref,
                 table_ref, bucket_ref, gain_moe_ref,
                 rows_out, w_out_all, outw_all, down_all, qkv_out, lse_ref, heads_all, slots_ref, cot, line_ref, segk_ref,
                 middle_out, moe_out, x_out,
                 tiles, heads_out, cot_send, w_own, rows, w_all, qkv, middle, moe_low, x_send,
                 far_send, far_recv, w_send, w_recv, ot_send, ot_recv,
                 dn_send, dn_recv, cot_s, cot_r, head_send, head_recv, local_sem, out_sem):
    dp_count, tensor_count, experts, capacity, cap_rows, heads, blocks, gather_w = sizes
    dp = lax.axis_index("dp")
    tp, sib, opp, across = partners(tensor_count)
    wait_barrier = greet(dp_count, tensor_count)
    inner = heads * DH
    for h in range(heads):
        for c in range(3):
            n = (3 * h + c) * DH
            w_own[:, n : n + DH] = w_ref[c, :, h * DH : (h + 1) * DH]
    w_own[:, 3 * inner :] = outw_ref[...].T

    x = x_ref[...].astype(jnp.float32)
    r = lax.rsqrt(jnp.mean(x * x, axis=-1, keepdims=True) + EPSILON)
    rows[tp] = (x * r * gain_ref[...].reshape(1, x.shape[1])).astype(jnp.bfloat16)
    wait_barrier()

    half = rows.shape[1] // 2
    parts = [pl.ds(0, half), pl.ds(half, half)]
    far = [remote(rows.at[tp, p], rows.at[tp, p], far_send.at[k], far_recv.at[k], "tensor", opp) for k, p in enumerate(parts)]
    near = remote(rows.at[tp], rows.at[tp], far_send.at[2], far_recv.at[2], "tensor", sib)
    onward = [remote(rows.at[opp, p], rows.at[opp, p], far_send.at[3 + k], far_recv.at[3 + k], "tensor", sib) for k, p in enumerate(parts)]
    for c in far:
        c.start()
    near.start()

    w_near, w_out, w_on = packed_gather(w_own, w_all, w_send, w_recv, dp_count)
    for c in w_out:
        c.start()
    w_near.start()
    w_all[dp] = w_own[...]

    tokens = x_ref.shape[0]
    live = padding_ref[pl.ds(tp // 2, 1), pl.ds(pl.multiple_of(lax.rem(tp, 2) * tokens, 128), tokens)]
    first, second = place_pairs(routes_ref, live, experts, capacity, cap_rows)
    slots_ref[0:1, :] = first
    slots_ref[1:2, :] = second

    def cot_copy(r):
        to = peer(r)
        return remote(cot_send.at[to], cot.at[dp], cot_s.at[r], cot_r.at[r], "dp", to)

    def cot_fill(r):
        to = peer(r)
        cot_send[to] = mm(chosen(first, second, to, cap_rows), grad_ref[...], NN).astype(jnp.bfloat16)

    each_peer(dp_count, cot_fill)
    cot_fill(0)
    own_cot = pltpu.make_async_copy(cot_send.at[dp], cot.at[dp], local_sem.at[1])
    own_cot.start()

    prepare(heads, tp, table_ref, bucket_ref, segments_ref, padding_ref, line_ref, segk_ref)
    build_bias(line_ref, tiles, heads, blocks)
    for c, on in zip(w_out, w_on):
        c.wait_recv()
        on.start()
    each_peer(dp_count, lambda r: cot_copy(r).start())
    w_near.wait_recv()
    for c in w_on:
        c.wait_recv()
    near.wait_recv()

    width = rows.shape[2]
    own_seq = tp // 2
    packed = qkv.shape[2]

    def project(seq):
        tokens = rows[pl.ds(seq * 2, 2)].reshape(2 * rows.shape[1], width)
        weight = w_all[...].reshape(width, w_all.shape[2])[:, :packed]
        qkv[seq] = mm(tokens, weight, NN).astype(jnp.bfloat16)

    def head_copy(k, to):
        return remote(heads_out.at[to], heads_all.at[tp], head_send.at[k], head_recv.at[k], "tensor", to)

    cut = down_ref.shape[0] // 2
    strips = [pl.ds(0, cut), pl.ds(cut, cut)]
    down_far = [remote(down_ref.at[p], down_all.at[tp, p], dn_send.at[k], dn_recv.at[k], "tensor", opp)
                for k, p in enumerate(strips)]
    down_near = remote(down_ref, down_all.at[tp], dn_send.at[2], dn_recv.at[2], "tensor", sib)
    down_on = [remote(down_all.at[opp, p], down_all.at[opp, p], dn_send.at[3 + k], dn_recv.at[3 + k], "tensor", sib)
               for k, p in enumerate(strips)]

    put_w = pltpu.make_async_copy(w_all, w_out_all, out_sem.at[0])
    put_w.start()
    project(own_seq)
    put_own = pltpu.make_async_copy(qkv.at[own_seq], qkv_out.at[own_seq], out_sem.at[1])
    put_own.start()
    outw_all[tp] = w_all[...].reshape(width, w_all.shape[2])[:, 3 * inner :].T
    ot_far = remote(outw_all.at[tp], outw_all.at[tp], ot_send.at[0], ot_recv.at[0], "tensor", opp)
    ot_near = remote(outw_all.at[tp], outw_all.at[tp], ot_send.at[1], ot_recv.at[1], "tensor", sib)
    ot_on = remote(outw_all.at[opp], outw_all.at[opp], ot_send.at[2], ot_recv.at[2], "tensor", sib)
    for k in range(2):
        far[k].wait_recv()
        onward[k].start()
    ot_far.start()
    ot_near.start()
    down_far[0].start()
    down_near.start()
    attend_sequence(heads, blocks, own_seq, tiles, segk_ref, segments_ref, qkv, heads_out, lse_ref)
    head_copy(0, sib).start()
    heads_all[tp] = heads_out[tp]
    for k in range(2):
        onward[k].wait_recv()
    other = 1 - own_seq
    put_rows = pltpu.make_async_copy(rows, rows_out, out_sem.at[2])
    put_rows.start()
    project(other)
    put_other = pltpu.make_async_copy(qkv.at[other], qkv_out.at[other], out_sem.at[3])
    put_other.start()
    attend_sequence(heads, blocks, other, tiles, segk_ref, segments_ref, qkv, heads_out, lse_ref)
    ot_far.wait_recv()
    ot_on.start()
    head_copy(1, opp).start()
    head_copy(2, across).start()
    down_far[1].start()
    down_far[0].wait_recv()
    down_on[0].start()

    head_copy(0, sib).wait_recv()
    head_copy(1, opp).wait_recv()
    head_copy(2, across).wait_recv()
    ot_near.wait_recv()
    ot_on.wait_recv()
    mixed = x_ref[...].astype(jnp.float32)
    for t in range(tensor_count):
        mixed = mixed + mm(heads_all[t], outw_all[t], TN)
    middle[...] = mixed
    r = lax.rsqrt(jnp.mean(mixed * mixed, axis=-1, keepdims=True) + EPSILON)
    moe_low[...] = (mixed * r * gain_moe_ref[...].reshape(1, width)).astype(jnp.bfloat16)
    for e in range(experts):
        x_send[e] = mm(chosen(first, second, e, cap_rows), moe_low[...], NN).astype(jnp.bfloat16)
    puts = [pltpu.make_async_copy(src, dst, out_sem.at[4 + k]) for k, (src, dst) in enumerate((
        (x_send, x_out), (moe_low, moe_out), (middle, middle_out)))]
    for c in puts:
        c.start()

    down_far[1].wait_recv()
    down_on[1].start()
    for c in [put_w, put_own, put_rows, put_other] + puts:
        c.wait()
    own_cot.wait()
    each_peer(dp_count, lambda r: cot_copy(r).wait())
    ot_on.wait_send()
    ot_near.wait_send()
    ot_far.wait_send()
    for c in [w_near] + w_out + w_on:
        c.wait_send()
    for c in far + [near] + onward:
        c.wait_send()
    head_copy(0, sib).wait_send()
    head_copy(1, opp).wait_send()
    head_copy(2, across).wait_send()
    for k in range(2):
        down_far[k].wait_send()
        down_on[k].wait()
    down_near.wait()


def sems(*counts):
    out = []
    for n in counts:
        out += [pltpu.SemaphoreType.DMA((n,)), pltpu.SemaphoreType.DMA((n,))]
    return out


def front(sizes, x, gain, w, outw, down, grad, routes_t, segments, padding, table, bucket, gain_moe):
    dp_count, tensor_count, experts, capacity, cap_rows, heads, blocks, gather_w = sizes
    tokens, width = x.shape
    seq_len = blocks * QB
    seqs = tensor_count * tokens // seq_len
    inner = heads * DH
    packed = -(-3 * inner // 128) * 128
    vmem = pl.BlockSpec(memory_space=pltpu.VMEM)
    anywhere = pl.BlockSpec(memory_space=pl.ANY)
    shape = jax.ShapeDtypeStruct
    low = jnp.bfloat16
    return pl.pallas_call(
        functools.partial(front_kernel, sizes),
        in_specs=[vmem] * 4 + [anywhere] + [vmem] * 7,
        out_specs=[anywhere] * 2 + [vmem] + [anywhere] * 2 + [vmem] * 3 + [anywhere] + [vmem] * 2 + [anywhere] * 3,
        out_shape=[
            shape((tensor_count, tokens, width), low),
            shape((dp_count, w.shape[1], 4 * inner), low),
            shape((tensor_count, inner, width), low),
            shape((tensor_count,) + down.shape, low),
            shape((seqs, seq_len, packed), low),
            shape((seqs, heads, seq_len), jnp.float32),
            shape((tensor_count, inner, tokens), low),
            shape((8, tokens), jnp.int32),
            shape((experts, cap_rows, width), low),
            shape((heads, QB + seq_len), jnp.float32),
            shape((seqs, seq_len, 1), jnp.int32),
            shape((tokens, width), jnp.float32),
            shape((tokens, width), low),
            shape((experts, cap_rows, width), low),
        ],
        scratch_shapes=[
            pltpu.VMEM((heads, blocks, QB, QB), jnp.float32),
            pltpu.VMEM((tensor_count, inner, tokens), low),
            pltpu.VMEM((experts, cap_rows, width), low),
            pltpu.VMEM((w.shape[1], 4 * inner), low),
            pltpu.VMEM((tensor_count, tokens, width), low),
            pltpu.VMEM((dp_count, w.shape[1], 4 * inner), low),
            pltpu.VMEM((seqs, seq_len, packed), low),
            pltpu.VMEM((tokens, width), jnp.float32),
            pltpu.VMEM((tokens, width), low),
            pltpu.VMEM((experts, cap_rows, width), low),
        ] + sems(5, dp_count, 3, 5, dp_count, 3) + [pltpu.SemaphoreType.DMA((3,)), pltpu.SemaphoreType.DMA((7,))],
        compiler_params=pltpu.CompilerParams(
            vmem_limit_bytes=VMEM_LIMIT, collective_id=1, has_side_effects=True),
        cost_estimate=pl.CostEstimate(flops=20_000_000_000, bytes_accessed=20 << 20, transcendentals=4_000_000),
        name="front",
    )(x, gain, w, outw, down, grad, routes_t, segments, padding, table, bucket, gain_moe)


def to_row(column, lanes):
    n = column.shape[0]
    row = lax.broadcasted_iota(jnp.int32, (n, lanes), 0)
    col = lax.broadcasted_iota(jnp.int32, (n, lanes), 1)
    return jnp.sum(jnp.where(row == col, column, 0.0), axis=0, keepdims=True)


def to_column(row_values, n):
    lanes = row_values.shape[1]
    row = lax.broadcasted_iota(jnp.int32, (n, lanes), 0)
    col = lax.broadcasted_iota(jnp.int32, (n, lanes), 1)
    return jnp.sum(jnp.where(row == col, row_values, 0.0), axis=1, keepdims=True)


def gate_map(first, second, gate_first, gate_second, expert, cap_rows):
    ids = lax.broadcasted_iota(jnp.int32, (cap_rows, first.shape[1]), 0) + expert * cap_rows
    return jnp.where(ids == first, gate_first, jnp.where(ids == second, gate_second, 0.0))


def gated_rows(weights, rows):
    high = weights.astype(jnp.bfloat16)
    low = (weights - high.astype(jnp.float32)).astype(jnp.bfloat16)
    return mm(high, rows, TN) + mm(low, rows, TN)


def middle_kernel(sizes, x_send, moe_in, middle_in, grad_ref, heads_ref, outw_ref, gain_ref, router_ref, routes_ref, padding_ref,
                  slots_ref, cot_ref, up_ref, down_own_ref, down_ref,
                  up_pair_out, up_own_out, up_land, down_own_out, down_land, produced_out, middle_grad, heads_grad, out_part, stats, gates,
                  up, down, g_rows, x_rows, act, side, back_send, back, gate_send, gate_rows,
                  dot_send, dot_rows, moe_low, stage, up_pair, up_own, down_own, produced, middle, down_pair,
                  up_s, up_r, x_s, x_r, b_s, b_r, g_s, g_r, d_s, d_r, a_s, a_r, load_sem, out_sem):
    dp_count, tensor_count, experts, capacity, cap_rows, heads, blocks, gather_w = sizes
    dp = lax.axis_index("dp")
    tp, sib, opp, across = partners(tensor_count)
    hidden = up.shape[1]
    total = middle_grad
    tokens, width = grad_ref.shape
    lanes = gate_send.shape[2]
    wait_barrier = greet(dp_count, tensor_count)

    load_g = pltpu.make_async_copy(cot_ref, g_rows, load_sem.at[0])
    load_down = [
        pltpu.make_async_copy(down_own_ref, down.at[tp], load_sem.at[1]),
        pltpu.make_async_copy(down_ref.at[sib], down.at[sib], load_sem.at[5]),
        pltpu.make_async_copy(down_ref.at[opp], down.at[opp], load_sem.at[6]),
        pltpu.make_async_copy(down_ref.at[across], down.at[across], load_sem.at[7]),
    ]
    load_up = pltpu.make_async_copy(up_ref, up.at[tp], load_sem.at[2])
    load_g.start()
    for c in load_down:
        c.start()
    load_up.start()

    loads = [pltpu.make_async_copy(src, dst, load_sem.at[n]) for n, src, dst in (
        (3, moe_in, moe_low), (4, middle_in, middle), (8, x_send.at[dp], x_rows.at[dp]))]
    for c in loads:
        c.start()
    puts = [pltpu.make_async_copy(src, dst, out_sem.at[k]) for k, (src, dst) in enumerate((
        (produced, produced_out), (up_pair, up_pair_out), (up_own, up_own_out), (down_own, down_own_out)))]
    first, second = slots_ref[0:1, :], slots_ref[1:2, :]
    wait_barrier()

    up_far = remote(up_ref, up.at[tp], up_s.at[0], up_r.at[0], "tensor", opp)
    up_near = remote(up_ref, up.at[tp], up_s.at[1], up_r.at[1], "tensor", sib)
    up_on = remote(up.at[opp], up.at[opp], up_s.at[2], up_r.at[2], "tensor", sib)
    up_far.start()
    up_near.start()

    def x_copy(r):
        to = peer(r)
        return remote(x_send.at[to], x_rows.at[dp], x_s.at[r], x_r.at[r], "dp", to)

    held = dp_count - 2
    for r in list(range(dp_count // 2, held)) + list(range(1, dp_count // 2)):
        x_copy(r).start()
    loads[0].wait()
    loads[2].wait()


    ids = lax.broadcasted_iota(jnp.int32, (experts, tokens), 0)
    pick_first, pick_second = ids == routes_ref[0:1, :], ids == routes_ref[1:2, :]
    live = padding_ref[pl.ds(tp // 2, 1), pl.ds(pl.multiple_of(lax.rem(tp, 2) * tokens, 128), tokens)]
    live = (live == 1).astype(jnp.float32)
    logits = mm(router_ref[...], moe_low[...], NT)
    gap = jnp.sum(jnp.where(pick_first, logits, 0.0) - jnp.where(pick_second, logits, 0.0), axis=0, keepdims=True)
    gate_first = live / (1.0 + jnp.exp(-gap))
    gate_second = live / (1.0 + jnp.exp(gap))
    gates[0:1, :] = gate_first
    gates[1:2, :] = gate_second

    def gate_copy(r):
        to = peer(r)
        return remote(gate_send.at[to], gate_rows.at[dp], g_s.at[r], g_r.at[r], "dp", to)

    def gate_fill(r):
        to = peer(r)
        column = jnp.sum(gate_map(first, second, gate_first, gate_second, to, cap_rows), axis=1, keepdims=True)
        return jnp.broadcast_to(to_row(column, lanes), (8, lanes))

    def gate_go(r):
        gate_send[peer(r)] = gate_fill(r)
        gate_copy(r).start()
    each_peer(dp_count, gate_go)
    gate_rows[dp] = gate_fill(0)

    load_g.wait()
    for c in load_down:
        c.wait()
    slots = experts * cap_rows
    block = slots // 4

    def side_block(k, carry):
        part = pl.ds(pl.multiple_of(k * block, 16), block)
        here = g_rows[pl.ds(k * (experts // 4), experts // 4)].reshape(block, width)
        for t in range(tensor_count):
            side[part, t * hidden : (t + 1) * hidden] = mm(here, down[t], NT).astype(jnp.bfloat16)
        return carry
    lax.fori_loop(0, 4, side_block, 0)

    for r in range(dp_count // 2, held):
        x_copy(r).wait_send()
    for r in range(held, dp_count):
        x_copy(r).start()
    load_up.wait()
    up_far.wait_recv()
    up_on.start()
    up_near.wait_recv()
    up_on.wait_recv()

    def back_copy(r):
        to = peer(r)
        return remote(back_send.at[to], back.at[dp], b_s.at[r], b_r.at[r], "dp", to)

    def dot_copy(r):
        to = peer(r)
        return remote(dot_send.at[to], dot_rows.at[dp], d_s.at[r], d_r.at[r], "dp", to)

    group = max(1, min(dp_count, 320 // cap_rows))

    def first_pass(step, carry):
        rounds = [step * group + k for k in range(group)]
        froms = [peer(r) for r in rounds]
        for k, r in enumerate(rounds):
            if k == 0:
                @pl.when(r > 0)
                def _():
                    x_copy(r).wait_recv()
            else:
                x_copy(r).wait_recv()
        here = jnp.concatenate([x_rows[s] for s in froms], axis=0)
        total_back = jnp.zeros((group * cap_rows, width), jnp.float32)
        dots = jnp.zeros((group * cap_rows, 128), jnp.float32)
        for t in range(tensor_count):
            cols = slice(t * hidden, (t + 1) * hidden)
            pre = mm(here, up[t], NT)
            value, slope = gelu_pair(pre)
            low = value.astype(jnp.bfloat16)
            places = [pl.ds(pl.multiple_of(s * cap_rows, 16), cap_rows) for s in froms]
            beside = jnp.concatenate([side[p, cols] for p in places], axis=0).astype(jnp.float32)
            product = low.astype(jnp.float32) * beside
            dots = dots + sum(product[:, k : k + 128] for k in range(0, hidden, 128))
            grad = (beside * slope).astype(jnp.bfloat16)
            for k, p in enumerate(places):
                piece = slice(k * cap_rows, (k + 1) * cap_rows)
                act[p, cols] = low[piece]
                side[p, cols] = grad[piece]
            total_back = total_back + mm(grad, up[t], NN)
        column = jnp.sum(dots, axis=1, keepdims=True)
        for k, (r, s) in enumerate(zip(rounds, froms)):
            piece = slice(k * cap_rows, (k + 1) * cap_rows)
            low = total_back[piece].astype(jnp.bfloat16)
            line = jnp.broadcast_to(to_row(column[piece], lanes), (8, lanes))

            def send():
                back_send[s] = low
                dot_send[s] = line
                back_copy(r).start()
                dot_copy(r).start()

            def keep():
                back[dp] = low
                dot_rows[dp] = line
            if k == 0:
                pl.when(r > 0)(send)
                pl.when(r == 0)(keep)
            else:
                send()
        return carry
    lax.fori_loop(0, dp_count // group, first_pass, 0)

    each_peer(dp_count, lambda r: gate_copy(r).wait_recv())

    def gate_rows_in(s, carry):
        column = to_column(gate_rows[s, 0:1, :], cap_rows)
        x_rows[s] = (x_rows[s].astype(jnp.float32) * column).astype(jnp.bfloat16)
        g_rows[s] = (g_rows[s].astype(jnp.float32) * column).astype(jnp.bfloat16)
        return carry
    lax.fori_loop(0, experts, gate_rows_in, 0)

    for r in list(range(1, dp_count // 2)) + list(range(held, dp_count)):
        x_copy(r).wait_send()
    lands = ((down_pair, down_own), (up_pair, up_own))
    aside = [remote(stage.at[k], lands[k][n], a_s.at[2 * k + n], a_r.at[2 * k + n], "tensor", sib)
             for k in range(2) for n in range(2)]
    up_far_part = remote(up_pair.at[pl.ds(0, hidden // 4)], up_land, a_s.at[5], a_r.at[5], "tensor", opp)
    down_far = remote(down_pair, down_land, a_s.at[4], a_r.at[4], "tensor", opp)
    piece = hidden // 2
    shards = (across, sib, opp, tp)
    sources = ((act, g_rows), (side, x_rows))
    for k, n in ((0, 0), (0, 2), (1, 0), (1, 2), (0, 1), (1, 1), (0, 3), (1, 3)):
        left, right = sources[k]
        if n == 1:
            aside[2 * k].wait_send()
        if n >= 2:
            aside[2 * k + n - 2].wait_recv()
        for m in range(2):
            cols = pl.ds(pl.multiple_of(shards[n] * hidden + m * piece, 128), piece)
            part = pl.ds(m * piece, piece)
            tile = mm(left[:, cols], right[...].reshape(slots, width), TN)
            if n < 2:
                stage[k, part, :] = tile.astype(jnp.bfloat16)
            else:
                land = lands[k][n - 2]
                land[part, :] = (tile + land[part, :].astype(jnp.float32)).astype(jnp.bfloat16)
        if n < 2:
            aside[2 * k + n].start()
        elif n == 2 and k == 0:
            down_far.start()
        elif n == 2:
            up_far_part.start()
            puts[1].start()
        elif k == 0:
            puts[3].start()
        else:
            puts[2].start()

    def produce(k, carry):
        part = pl.ds(pl.multiple_of(k * block, 16), block)
        out = jnp.zeros((block, width), jnp.float32)
        for t in range(tensor_count):
            out = out + mm(act[part, t * hidden : (t + 1) * hidden], down[t], NN)
        out = out.astype(jnp.bfloat16)
        for e in range(experts // 4):
            produced[k * (experts // 4) + e] = out[e * cap_rows : (e + 1) * cap_rows]
        return carry
    lax.fori_loop(0, 4, produce, 0)

    puts[0].start()

    total[...] = jnp.zeros_like(total)

    def combine(r, carry):
        dot_first, dot_second = carry
        e = peer(r)

        @pl.when(r > 0)
        def _():
            back_copy(r).wait_recv()
            dot_copy(r).wait_recv()
        weights = gate_map(first, second, gate_first, gate_second, e, cap_rows)
        total[...] += gated_rows(weights, back[e])
        column = to_column(dot_rows[e, 0:1, :], cap_rows)
        ids = lax.broadcasted_iota(jnp.int32, (cap_rows, tokens), 0) + e * cap_rows
        dot_first = dot_first + jnp.sum(jnp.where(ids == first, column, 0.0), axis=0, keepdims=True)
        dot_second = dot_second + jnp.sum(jnp.where(ids == second, column, 0.0), axis=0, keepdims=True)
        return dot_first, dot_second
    zero_row = jnp.zeros((1, tokens), jnp.float32)
    dot_first, dot_second = lax.fori_loop(0, dp_count, combine, (zero_row, zero_row))

    change = gate_first * gate_second * (dot_first - dot_second)
    logit_grad = (jnp.where(pick_first, change, 0.0) - jnp.where(pick_second, change, 0.0)).astype(jnp.bfloat16)
    norm_grad = total[...] + mm(logit_grad, router_ref[...], TN)
    loads[1].wait()
    mixed = middle[...]
    r = lax.rsqrt(jnp.mean(mixed * mixed, axis=-1, keepdims=True) + EPSILON)
    u = mixed * r
    du = norm_grad * gain_ref[...].reshape(1, width)
    grad = grad_ref[...].astype(jnp.float32) + r * (du - u * jnp.mean(du * u, axis=-1, keepdims=True))
    middle_grad[...] = grad
    low = grad.astype(jnp.bfloat16)
    for t in range(tensor_count):
        heads_grad[t] = mm(outw_ref[t], low, NT).astype(jnp.bfloat16)
        out_part[t] = mm(heads_ref[t], low, NN).astype(jnp.bfloat16)
    stats[0:8, :] = jnp.broadcast_to(jnp.sum(norm_grad * u, axis=0, keepdims=True), (8, width))
    stats[8:, :] = mm(logit_grad, moe_low[...], NN)

    down_far.wait_recv()
    up_far_part.wait_recv()
    down_far.wait_send()
    up_far_part.wait_send()
    for c in puts:
        c.wait()
    for k in range(2):
        aside[2 * k + 1].wait_send()
    up_far.wait_send()
    up_near.wait_send()
    up_on.wait_send()

    def drain(r):
        gate_copy(r).wait_send()
        back_copy(r).wait_send()
        dot_copy(r).wait_send()
    each_peer(dp_count, drain)


def middle_pass(sizes, x_send, moe_low, middle, grad, heads_all, outw, gain, router_t, routes_t, padding, slot_rows, cot, up, down, down_all):
    dp_count, tensor_count, experts, capacity, cap_rows, heads, blocks, gather_w = sizes
    tokens, width = grad.shape
    inner = heads * DH
    hidden = up.shape[0]
    slots = experts * cap_rows
    lanes = -(-cap_rows // 128) * 128
    vmem = pl.BlockSpec(memory_space=pltpu.VMEM)
    anywhere = pl.BlockSpec(memory_space=pl.ANY)
    shape = jax.ShapeDtypeStruct
    low = jnp.bfloat16
    return pl.pallas_call(
        functools.partial(middle_kernel, sizes),
        in_specs=[anywhere] * 3 + [vmem] * 8 + [anywhere] * 4,
        out_specs=[anywhere] * 2 + [vmem] + [anywhere] + [vmem] + [anywhere] + [vmem] * 5,
        out_shape=[
            shape((hidden, width), low),
            shape((hidden, width), low),
            shape((hidden // 4, width), low),
            shape((hidden, width), low),
            shape((hidden, width), low),
            shape((experts, cap_rows, width), low),
            shape((tokens, width), jnp.float32),
            shape((tensor_count, inner, tokens), low),
            shape((tensor_count, inner, width), low),
            shape((8 + experts, width), jnp.float32),
            shape((8, tokens), jnp.float32),
        ],
        scratch_shapes=[
            pltpu.VMEM((tensor_count, hidden, width), low),
            pltpu.VMEM((tensor_count, hidden, width), low),
            pltpu.VMEM((experts, cap_rows, width), low),
            pltpu.VMEM((experts, cap_rows, width), low),
            pltpu.VMEM((slots, tensor_count * hidden), low),
            pltpu.VMEM((slots, tensor_count * hidden), low),
            pltpu.VMEM((experts, cap_rows, width), low),
            pltpu.VMEM((experts, cap_rows, width), low),
            pltpu.VMEM((experts, 8, lanes), jnp.float32),
            pltpu.VMEM((experts, 8, lanes), jnp.float32),
            pltpu.VMEM((experts, 8, lanes), jnp.float32),
            pltpu.VMEM((experts, 8, lanes), jnp.float32),
            pltpu.VMEM((tokens, width), low),
            pltpu.VMEM((2, hidden, width), low),
            pltpu.VMEM((hidden, width), low),
            pltpu.VMEM((hidden, width), low),
            pltpu.VMEM((hidden, width), low),
            pltpu.VMEM((experts, cap_rows, width), low),
            pltpu.VMEM((tokens, width), jnp.float32),
            pltpu.VMEM((hidden, width), low),
        ] + sems(5, dp_count, dp_count, dp_count, dp_count, 6) + [pltpu.SemaphoreType.DMA((9,)), pltpu.SemaphoreType.DMA((4,))],
        compiler_params=pltpu.CompilerParams(
            vmem_limit_bytes=VMEM_LIMIT, collective_id=2, has_side_effects=True),
        cost_estimate=pl.CostEstimate(
            flops=12 * slots * width * hidden * tensor_count, bytes_accessed=40 << 20, transcendentals=4_000_000),
        name="middle_pass",
    )(x_send, moe_low, middle, grad, heads_all, outw, gain, router_t, routes_t, padding, slot_rows, cot, up, down, down_all)


def attend_back_sequence(heads, blocks, seq, tiles, sums, segk_ref, segq_ref, qkv, grads, lse_ref, kg, vg, dq, chosen_heads):
    scale = 1.0 / math.sqrt(DH)
    half = blocks // 2
    for h in chosen_heads:
        cols, kcols, vcols = [slice((3 * h + c) * DH, (3 * h + c + 1) * DH) for c in range(3)]
        gcols = slice(h * DH, (h + 1) * DH)
        kg[...] = jnp.zeros_like(kg)
        vg[...] = jnp.zeros_like(vg)
        for qb in range(blocks):
            nk = (qb + 1) * QB
            lower = qb * QB
            query = (qkv[seq, lower : lower + QB, cols].astype(jnp.float32) * scale).astype(jnp.bfloat16)
            grad = grads[seq * 2 + qb // half, gcols, (qb % half) * QB : (qb % half + 1) * QB]
            lse = lse_ref[seq, h : h + 1, lower : lower + QB]
            parts = score_block(qkv[seq, 0:nk, kcols], query, tiles, h, qb, segk_ref.at[seq], segq_ref.at[pl.ds(seq, 1)])
            probs = [jnp.exp(x - lse) for x in parts]
            pg = mm(qkv[seq, 0:nk, vcols], grad, NN)
            pgs = [pg[kb * QB : (kb + 1) * QB] for kb in range(qb + 1)]
            delta = functools.reduce(jnp.add, [jnp.sum(p * g, axis=0, keepdims=True) for p, g in zip(probs, pgs)])
            dqt = jnp.zeros((DH, QB), jnp.float32)
            for kb in range(qb + 1):
                rows = slice(kb * QB, (kb + 1) * QB)
                sg = (probs[kb] * (pgs[kb] - delta)).astype(jnp.bfloat16)
                sums[h, qb - kb] += sg.astype(jnp.float32)
                vg[rows] += mm(probs[kb].astype(jnp.bfloat16), grad, NT)
                kg[rows] += mm(sg, query, NN)
                dqt = dqt + mm(qkv[seq, rows, kcols], sg, TN)
            dq[lower : lower + QB, cols] = (dqt * scale).T.astype(jnp.bfloat16)
        dq[:, kcols] = kg[...].astype(jnp.bfloat16)
        dq[:, vcols] = vg[...].astype(jnp.bfloat16)


def fold_lines(sums, h, blocks):
    moved = []
    for d in range(blocks):
        folded = fold_tile(sums, h, d)
        line = folded[0:1, :]
        for s in range(1, 8):
            line = line + pltpu.roll(folded[s : s + 1, :], 2 * QB - s, 1)
        moved.append(line)
    out = []
    for d in range(blocks):
        piece = moved[d][:, :QB]
        if d + 1 < blocks:
            piece = piece + moved[d + 1][:, QB:]
        out.append(piece)
    return jnp.concatenate(out, axis=1)


def two_stage_start(send, land, s_sem, r_sem, tensor_count):
    tp = lax.axis_index("tensor")
    copies = []
    for r in range(1, tensor_count):
        copies.append(remote(send, land.at[r - 1], s_sem.at[r], r_sem.at[r], "tensor", lax.rem(tp + r, tensor_count)))
    for c in copies:
        c.start()
    return copies


def last_kernel(sizes, x_ref, gain_ref, middle_ref, mgrad_in, hgrad_ref, rows_in, w_in, qkv_in, lse_ref, line_ref,
                segk_ref, segq_ref, produced_ref, slots_ref, gates_ref, early_ref, bucket_ref,
                out_part, up_pair,
                out_ref, input_grad_ref, wgrad_ref, early_out, late_out, up_land,
                tiles, sums, kg, vg, dq, grads, landed, npart, near_land, far_land, pair, wsum, wsend, wland,
                early_land, early_mid, early_dp, late, late_land, late_mid, late_dp, total, mgrad_ref, rows, w_ref, qkv,
                out_land, out_pair, out_far,
                h_s, h_r, p_s, p_r, n_s, n_r, w_s, w_r, et_s, et_r, ed_s, ed_r, lt_s, lt_r, ld_s, ld_r, o_s, o_r, load_sem):
    dp_count, tensor_count, experts, capacity, cap_rows, heads, blocks, gather_w = sizes
    dp = lax.axis_index("dp")
    tp, sib, opp, across = partners(tensor_count)
    tokens, width = x_ref.shape
    inner = heads * DH
    wait_barrier = greet(dp_count, tensor_count)
    loads = [pltpu.make_async_copy(src, dst, load_sem.at[k]) for k, (src, dst) in enumerate((
        (qkv_in, qkv), (rows_in, rows), (w_in, w_ref), (produced_ref.at[dp], landed.at[dp]), (middle_ref, total),
        (mgrad_in, mgrad_ref)))]
    for c in loads:
        c.start()
    build_bias(line_ref, tiles, heads, blocks)
    sums[...] = jnp.zeros_like(sums)
    dq[:, :, 3 * inner :] = jnp.zeros((2, dq.shape[1], dq.shape[2] - 3 * inner), jnp.bfloat16)
    own_seq = tp // 2
    other = 1 - own_seq
    wait_barrier()

    def h_copy(k, to):
        return remote(hgrad_ref.at[to], grads.at[tp], h_s.at[k], h_r.at[k], "tensor", to)
    h_copy(0, opp).start()
    h_copy(1, across).start()
    h_copy(2, sib).start()
    grads[tp] = hgrad_ref[tp]

    def p_copy(r):
        to = peer(r)
        return remote(produced_ref.at[to], landed.at[dp], p_s.at[r], p_r.at[r], "dp", to)
    sent = list(range(dp_count // 2, dp_count)) + list(range(1, dp_count // 2))
    for r in sent:
        p_copy(r).start()

    early = two_stage_start(early_ref.at[pl.ds(8, experts)], early_land, et_s, et_r, tensor_count)

    def early_copy(r):
        return remote(early_mid, early_dp.at[r], ed_s.at[r], ed_r.at[r], "dp", peer(r))

    out_near = [remote(out_part.at[t], out_land.at[k], o_s.at[k], o_r.at[k], "tensor", sib)
                for k, t in enumerate((across, sib))]
    out_across = remote(out_pair, out_far, o_s.at[2], o_r.at[2], "tensor", opp)
    for c in out_near:
        c.start()

    up_rest = remote(up_pair.at[pl.ds(up_pair.shape[0] // 4, up_land.shape[0])], up_land, o_s.at[3], o_r.at[3],
                     "tensor", opp)

    def n_copy(k, src, dst, to):
        return remote(src, dst, n_s.at[k], n_r.at[k], "tensor", to)
    pair_near = n_copy(0, npart.at[across], near_land.at[0], sib)
    pair_far = n_copy(1, pair, far_land, opp)
    own_near = n_copy(2, npart.at[sib], near_land.at[1], sib)
    packed = dq.shape[2]

    def attend_part(seq, k, chosen_heads):
        attend_back_sequence(heads, blocks, seq, tiles, sums, segk_ref, segq_ref, qkv, grads, lse_ref, kg, vg,
                             dq.at[k], chosen_heads)

    def norm_part(seq, k):
        here = rows[pl.ds(seq * 2, 2)].reshape(2 * tokens, width)
        norm = mm(dq[k], w_ref[...].reshape(width, w_ref.shape[2])[:, :packed], NT)
        column = jnp.sum(norm * here.astype(jnp.float32), axis=0, keepdims=True)
        low = norm.astype(jnp.bfloat16)
        npart[seq * 2] = low[:tokens]
        npart[seq * 2 + 1] = low[tokens:]
        return column

    share = width // dp_count
    side = peer(1)
    columns = dp_count // 2
    lanes = wsum.shape[1] // 2

    def share_rows(d):
        return pl.ds(pl.multiple_of(d * share, 8), share)

    def side_copy(m, k):
        n = 2 * columns * m + k
        return remote(wsend.at[n], wland.at[n], w_s.at[n], w_r.at[n], "dp", side)

    def column_copy(m, k):
        n = 2 * columns * m + columns + k
        return remote(wsend.at[n], wland.at[n], w_s.at[n], w_r.at[n], "dp", peer(2 * k))

    def side_go(m):
        for k in list(range(1, columns)) + [0]:
            there = share_rows(jnp.bitwise_xor(side, 2 * k))
            wsend[2 * columns * m + k] = wsum[there, m * lanes : (m + 1) * lanes].astype(jnp.bfloat16)
            side_copy(m, k).start()

    def column_go(m):
        for k in range(1, columns):
            side_copy(m, k).wait_recv()
            mine = wsum[share_rows(peer(2 * k)), m * lanes : (m + 1) * lanes]
            n = 2 * columns * m + columns + k
            wsend[n] = (mine + wland[2 * columns * m + k].astype(jnp.float32)).astype(jnp.bfloat16)
            column_copy(m, k).start()

    out_near[0].wait_recv()
    out_pair[...] = (out_part[opp].astype(jnp.float32) + out_land[0].astype(jnp.float32)).astype(jnp.bfloat16)
    out_across.start()
    loads[0].wait()
    h_copy(2, sib).wait_recv()
    attend_part(own_seq, 0, range(1))
    loads[1].wait()
    loads[2].wait()
    up_rest.start()
    h_copy(0, opp).wait_recv()
    h_copy(1, across).wait_recv()
    attend_part(other, 1, range(heads))
    gain_row = norm_part(other, 1)
    pair_near.start()
    wsum[:, :packed] = mm(rows[pl.ds(other * 2, 2)].reshape(2 * tokens, width), dq[1], TN)
    out_across.wait_recv()
    out_near[1].wait_recv()
    out_whole = out_part[tp].astype(jnp.float32) + out_land[1].astype(jnp.float32) + out_far[...].astype(jnp.float32)
    wsum[:, 3 * inner :] = out_whole.T
    pair_near.wait_recv()
    pair[...] = (npart[opp].astype(jnp.float32) + near_land[0].astype(jnp.float32)).astype(jnp.bfloat16)
    pair_far.start()
    attend_part(own_seq, 0, range(1, 2))
    wsum[:, :lanes] += mm(rows[pl.ds(own_seq * 2, 2)].reshape(2 * tokens, width), dq[0, :, :lanes], TN)
    side_go(0)
    for c in early:
        c.wait_recv()
    early_mid[...] = early_ref[8:, :] + early_land[0] + early_land[1] + early_land[2]
    each_peer(dp_count, lambda r: early_copy(r).start())
    attend_part(own_seq, 0, range(2, heads))
    column_go(0)
    wsum[:, lanes : 3 * inner] += mm(rows[pl.ds(own_seq * 2, 2)].reshape(2 * tokens, width), dq[0, :, lanes:packed], TN)[:, : 3 * inner - lanes]
    side_go(1)
    gain_row = gain_row + norm_part(own_seq, 0)
    own_near.start()

    gain_row = gain_row / gain_ref[...].reshape(1, width)
    late[...] = jnp.zeros_like(late)
    pieces = width // 128
    for k in range(pieces):
        late[k : k + 1, :] = gain_row[:, k * 128 : (k + 1) * 128]
        late[pieces + k : pieces + k + 1, :] = early_ref[0:1, k * 128 : (k + 1) * 128]
    ids = lax.broadcasted_iota(jnp.int32, (NB, bucket_ref.shape[1]), 0)
    hot = ids == bucket_ref[...]
    place = lax.broadcasted_iota(jnp.int32, (NB, 128), 1) - lax.broadcasted_iota(jnp.int32, (NB, 128), 0)
    table = jnp.zeros((1, 128), jnp.float32)
    for h in range(heads):
        column = jnp.sum(jnp.where(hot, fold_lines(sums, h, blocks), 0.0), axis=1, keepdims=True)
        table = table + jnp.sum(jnp.where(place == h * NB, column, 0.0), axis=0, keepdims=True)
    late[pl.ds(2 * pieces + tp, 1), :] = table
    late_first = two_stage_start(late, late_land, lt_s, lt_r, tensor_count)

    def late_copy(r):
        return remote(late_mid, late_dp.at[r], ld_s.at[r], ld_r.at[r], "dp", peer(r))

    first, second = slots_ref[0:1, :], slots_ref[1:2, :]
    gate_first, gate_second = gates_ref[0:1, :], gates_ref[1:2, :]
    loads[3].wait()
    loads[4].wait()

    def combine(e):
        total[...] += gated_rows(gate_map(first, second, gate_first, gate_second, e, cap_rows), landed[e])
    combine(dp)
    for r in range(1, dp_count // 2):
        p_copy(r).wait_recv()
        combine(peer(r))

    for c in late_first:
        c.wait_recv()
    late_mid[...] = late[...] + late_land[0] + late_land[1] + late_land[2]
    each_peer(dp_count, lambda r: late_copy(r).start())
    column_go(1)
    for r in range(dp_count // 2, dp_count):
        p_copy(r).wait_recv()
        combine(peer(r))
    out_ref[...] = total[...]

    each_peer(dp_count, lambda r: early_copy(r).wait_recv())
    summed = early_mid[...]
    for r in range(1, dp_count):
        summed = summed + early_dp[r]
    early_out[...] = summed
    loads[5].wait()

    own_near.wait_recv()
    pair_far.wait_recv()
    norm_grad = npart[tp].astype(jnp.float32) + near_land[1].astype(jnp.float32) + far_land[...].astype(jnp.float32)
    x = x_ref[...].astype(jnp.float32)
    r = lax.rsqrt(jnp.mean(x * x, axis=-1, keepdims=True) + EPSILON)
    u = x * r
    du = norm_grad * gain_ref[...].reshape(1, width)
    input_grad_ref[...] = mgrad_ref[...] + r * (du - u * jnp.mean(du * u, axis=-1, keepdims=True))

    for m in range(2):
        half = slice(m * lanes, (m + 1) * lanes)
        side_copy(m, 0).wait_recv()
        part = wsum[share_rows(dp), half] + wland[2 * columns * m].astype(jnp.float32)
        for k in range(1, columns):
            column_copy(m, k).wait_recv()
            part = part + wland[2 * columns * m + columns + k].astype(jnp.float32)
        wgrad_ref[:, half] = part
    up_rest.wait_recv()

    each_peer(dp_count, lambda r: late_copy(r).wait_recv())
    summed = late_mid[...]
    for r in range(1, dp_count):
        summed = summed + late_dp[r]
    late_out[...] = summed

    for c in early + late_first + out_near + [out_across, pair_near, pair_far, own_near, h_copy(0, opp), h_copy(1, across), h_copy(2, sib)]:
        c.wait_send()

    def drain(r):
        early_copy(r).wait_send()
        late_copy(r).wait_send()
    each_peer(dp_count, drain)
    for r in sent:
        p_copy(r).wait_send()
    for m in range(2):
        for k in range(columns):
            side_copy(m, k).wait_send()
            if k:
                column_copy(m, k).wait_send()
    up_rest.wait_send()


def last_pass(sizes, x, gain, middle, middle_grad, heads_grad, rows, w, qkv, lse, line, segk, segq, produced,
              slot_rows, gates, early, bucket_row, out_part, up_pair):
    dp_count, tensor_count, experts, capacity, cap_rows, heads, blocks, gather_w = sizes
    tokens, width = x.shape
    inner = heads * DH
    seq_len = blocks * QB
    share = width // dp_count
    vmem = pl.BlockSpec(memory_space=pltpu.VMEM)
    anywhere = pl.BlockSpec(memory_space=pl.ANY)
    shape = jax.ShapeDtypeStruct
    low, full = jnp.bfloat16, jnp.float32
    late = 16
    packed = qkv.shape[2]
    return pl.pallas_call(
        functools.partial(last_kernel, sizes),
        in_specs=[vmem] * 2 + [anywhere] * 2 + [vmem] + [anywhere] * 3 + [vmem] * 4 + [anywhere] + [vmem] * 5 + [anywhere],
        out_specs=[vmem] * 5 + [anywhere],
        out_shape=[
            shape((tokens, width), full),
            shape((tokens, width), full),
            shape((share, w.shape[2]), full),
            shape((experts, width), full),
            shape((late, 128), full),
            shape((3 * up_pair.shape[0] // 4, width), low),
        ],
        scratch_shapes=[
            pltpu.VMEM((heads, blocks, QB, QB), full),
            pltpu.VMEM((heads, blocks, QB, QB), full),
            pltpu.VMEM((seq_len, DH), full),
            pltpu.VMEM((seq_len, DH), full),
            pltpu.VMEM((2, seq_len, packed), low),
            pltpu.VMEM((tensor_count, inner, tokens), low),
            pltpu.VMEM((experts, cap_rows, width), low),
            pltpu.VMEM((tensor_count, tokens, width), low),
            pltpu.VMEM((2, tokens, width), low),
            pltpu.VMEM((tokens, width), low),
            pltpu.VMEM((tokens, width), low),
            pltpu.VMEM((width, w.shape[2]), full),
            pltpu.VMEM((2 * dp_count, share, w.shape[2] // 2), low),
            pltpu.VMEM((2 * dp_count, share, w.shape[2] // 2), low),
            pltpu.VMEM((tensor_count - 1, experts, width), full),
            pltpu.VMEM((experts, width), full),
            pltpu.VMEM((dp_count, experts, width), full),
            pltpu.VMEM((late, 128), full),
            pltpu.VMEM((tensor_count - 1, late, 128), full),
            pltpu.VMEM((late, 128), full),
            pltpu.VMEM((dp_count, late, 128), full),
            pltpu.VMEM((tokens, width), full),
            pltpu.VMEM((tokens, width), full),
            pltpu.VMEM(rows.shape, low),
            pltpu.VMEM(w.shape, low),
            pltpu.VMEM(qkv.shape, low),
            pltpu.VMEM((2, inner, width), low),
            pltpu.VMEM((inner, width), low),
            pltpu.VMEM((inner, width), low),
        ] + sems(3, dp_count, 3, 2 * dp_count, tensor_count, dp_count, tensor_count, dp_count, 4) + [pltpu.SemaphoreType.DMA((6,))],
        compiler_params=pltpu.CompilerParams(
            vmem_limit_bytes=VMEM_LIMIT, collective_id=3, has_side_effects=True),
        cost_estimate=pl.CostEstimate(flops=30_000_000_000, bytes_accessed=30 << 20, transcendentals=4_000_000),
        name="last_pass",
    )(x, gain, middle, middle_grad, heads_grad, rows, w, qkv, lse, line, segk, segq, produced, slot_rows, gates,
      early, bucket_row, out_part, up_pair)


def finish_kernel(out_ref, input_grad_ref, wgrad_ref, early_ref, late_ref, up_own, up_first, up_rest, down_own, down_land,
                  out, input_grad, w_qkv_grad, w_out_grad, table, gain_attn, gain_moe, router, up_grad, down_grad):
    out[...] = out_ref[...]
    input_grad[...] = input_grad_ref[...]
    land = jnp.where(pl.program_id(0) == 0, up_first[...].astype(jnp.float32), up_rest[...].astype(jnp.float32))
    up_grad[...] = up_own[...].astype(jnp.float32) + land
    down_grad[...] = down_own[...].astype(jnp.float32) + down_land[...].astype(jnp.float32)

    @pl.when(pl.program_id(0) == 0)
    def _():
        inner = w_qkv_grad.shape[2]
        for h in range(inner // DH):
            for c in range(3):
                n = (3 * h + c) * DH
                w_qkv_grad[c, :, h * DH : (h + 1) * DH] = wgrad_ref[:, n : n + DH]
        w_out_grad[...] = wgrad_ref[:, 3 * inner :].T
        pieces = gain_attn.shape[0] // 128
        heads = inner // DH
        for h in range(table.shape[0]):
            place = (h % heads) * NB
            table[h : h + 1, :] = late_ref[2 * pieces + h // heads : 2 * pieces + h // heads + 1, place : place + NB]
        for base, gain in ((0, gain_attn), (pieces, gain_moe)):
            row = jnp.concatenate([late_ref[base + k : base + k + 1, :] for k in range(pieces)], axis=1)
            gain[...] = row.reshape(gain.shape)
        router[...] = early_ref[...]


def finish(heads_total, out, input_grad, wgrad, early, late, up_own, up_first, up_rest, down_own, down_land):
    steps = 4
    tokens, width = out.shape
    share = wgrad.shape[0]
    inner = wgrad.shape[1] // 4
    hidden = up_own.shape[0]
    full = jnp.float32
    shape = jax.ShapeDtypeStruct

    def rows(n):
        return pl.BlockSpec((n // steps, width), lambda s: (s, 0))

    def whole(*dims):
        return pl.BlockSpec(dims, lambda s: (0,) * len(dims))
    return pl.pallas_call(
        finish_kernel,
        grid=(steps,),
        in_specs=[rows(tokens), rows(tokens), whole(*wgrad.shape), whole(*early.shape), whole(*late.shape)]
        + [rows(hidden), whole(*up_first.shape),
           pl.BlockSpec((hidden // steps, width), lambda s: (jnp.maximum(s - 1, 0), 0))] + [rows(hidden)] * 2,
        out_specs=[rows(tokens), rows(tokens), whole(3, share, inner), whole(inner, share), whole(heads_total, NB),
                   whole(width), whole(width), whole(*early.shape), rows(hidden), rows(hidden)],
        out_shape=[shape((tokens, width), full), shape((tokens, width), full), shape((3, share, inner), full),
                   shape((inner, share), full), shape((heads_total, NB), full), shape((width,), full),
                   shape((width,), full), shape(early.shape, full), shape((hidden, width), full),
                   shape((hidden, width), full)],
        compiler_params=pltpu.CompilerParams(vmem_limit_bytes=VMEM_LIMIT),
        cost_estimate=pl.CostEstimate(flops=0, bytes_accessed=16 << 20, transcendentals=0),
        name="finish",
    )(out, input_grad, wgrad, early, late, up_own, up_first, up_rest, down_own, down_land)


def norm_rows(values, gain):
    return values * lax.rsqrt(jnp.mean(values * values, axis=-1, keepdims=True) + EPSILON) * gain


def norm_back(values, gain, grad):
    r = lax.rsqrt(jnp.mean(values * values, axis=-1, keepdims=True) + EPSILON)
    u = values * r
    du = grad * gain
    return r * (du - u * jnp.mean(du * u, axis=-1, keepdims=True)), grad * u


def plain_body(
    block_input,
    out_grad,
    w_qkv,
    w_out,
    rel_table,
    gain_attn,
    gain_moe,
    w_router,
    w_up,
    w_down,
    routes,
    segments,
    padding,
    rel_bucket,
):
    tensor_pos = lax.axis_index("tensor")
    rows_local, width = block_input.shape
    seq_len = segments.shape[1]
    expert_count = w_router.shape[1]
    capacity = (10 * rows_local + 4 * expert_count - 1) // (4 * expert_count)
    slots = expert_count * capacity
    x_float = block_input.astype(jnp.float32)
    grad_float = out_grad.astype(jnp.float32)

    attn_norm = norm_rows(x_float, gain_attn).astype(jnp.bfloat16)
    seq_rows = lax.all_gather(attn_norm, "tensor", axis=0, tiled=True)
    qkv_full = lax.all_gather(w_qkv, "dp", axis=1, tiled=True)
    out_rows = lax.all_gather(w_out, "dp", axis=1, tiled=True)
    out_full = lax.all_gather(out_rows, "tensor", axis=0, tiled=True)
    up_full = lax.all_gather(w_up[0], "tensor", axis=0, tiled=True)
    down_full = lax.all_gather(w_down[0], "tensor", axis=0, tiled=True)

    live_mask = lax.dynamic_slice_in_dim(padding.reshape(-1), tensor_pos * rows_local, rows_local)
    live_float = live_mask.astype(jnp.float32)
    expert_ids = jnp.arange(expert_count, dtype=jnp.int32)
    pick_first = routes[:, 0:1] == expert_ids[None, :]
    pick_second = routes[:, 1:2] == expert_ids[None, :]
    usable = live_mask[:, None] == 1
    first_hot = (pick_first & usable).astype(jnp.int32)
    second_hot = (pick_second & usable).astype(jnp.int32)
    first_place = jnp.sum((jnp.cumsum(first_hot, axis=0) - first_hot) * first_hot, axis=1)
    second_before = (
        jnp.cumsum(second_hot, axis=0) - second_hot + jnp.sum(first_hot, axis=0, keepdims=True)
    )
    second_place = jnp.sum(second_before * second_hot, axis=1)
    first_slot = jnp.where(
        (live_mask == 1) & (first_place < capacity), routes[:, 0] * capacity + first_place, -1
    )
    second_slot = jnp.where(
        (live_mask == 1) & (second_place < capacity), routes[:, 1] * capacity + second_place, -1
    )
    slot_ids = jnp.arange(slots, dtype=jnp.int32)
    select_first = slot_ids[:, None] == first_slot[None, :]
    select_second = slot_ids[:, None] == second_slot[None, :]
    select_both = (select_first | select_second).astype(jnp.bfloat16)
    select_first_low = select_first.astype(jnp.bfloat16)
    select_second_low = select_second.astype(jnp.bfloat16)

    def to_experts(rows):
        return lax.all_to_all(rows, "dp", split_axis=0, concat_axis=0, tiled=True)

    grad_rows = jnp.dot(select_both, out_grad, preferred_element_type=jnp.float32)
    sent_grads = to_experts(grad_rows.astype(jnp.bfloat16).reshape(expert_count, capacity, width))
    sent_grads = sent_grads.reshape(slots, width)

    heads = qkv_full.shape[2] // DH
    inner = heads * DH
    table_local = lax.dynamic_slice_in_dim(rel_table, tensor_pos * heads, heads, 1)
    bucket_hot = (rel_bucket[:, None] == jnp.arange(NB, dtype=jnp.int32)[None, :]).astype(jnp.float32)
    line = line_of(jnp.dot(bucket_hot, table_local, precision=HIGHEST).T)
    segk, segq = mask_inputs(segments, padding)
    qkv_low, heads_low, lse = attend(line, segk, segq, seq_rows, qkv_full)
    heads_own = lax.all_to_all(heads_low, "tensor", split_axis=0, concat_axis=1, tiled=True)

    middle = x_float + jnp.dot(heads_own, out_full, preferred_element_type=jnp.float32)
    moe_low = norm_rows(middle, gain_moe).astype(jnp.bfloat16)
    rows_out = jnp.dot(select_both, moe_low, preferred_element_type=jnp.float32)
    sent_rows = to_experts(rows_out.astype(jnp.bfloat16).reshape(expert_count, capacity, width))
    sent_rows = sent_rows.reshape(slots, width)
    logits = jnp.dot(moe_low, w_router, preferred_element_type=jnp.float32)
    first_logit = jnp.sum(jnp.where(pick_first, logits, 0.0), axis=1)
    second_logit = jnp.sum(jnp.where(pick_second, logits, 0.0), axis=1)
    first_gate = jax.nn.sigmoid(first_logit - second_logit) * live_float
    second_gate = jax.nn.sigmoid(second_logit - first_logit) * live_float
    slot_gate = jnp.sum(
        jnp.where(select_first, first_gate[None, :], 0.0)
        + jnp.where(select_second, second_gate[None, :], 0.0),
        axis=1,
    )
    sent_gates = to_experts(slot_gate.reshape(expert_count, capacity)).reshape(slots, 1)

    act, pre_grad, back, dots = expert_first(sent_rows, sent_grads, up_full, down_full)
    returned_grad = to_experts(back.reshape(expert_count, capacity, width)).reshape(slots, width)
    slot_dots = to_experts(dots[0].reshape(expert_count, capacity)).reshape(slots)
    produced, up_part, down_part = expert_late(
        sent_rows, sent_grads, sent_gates, act, pre_grad, down_full
    )
    returned = to_experts(produced.reshape(expert_count, capacity, width)).reshape(slots, width)
    w_up_grad = lax.psum_scatter(up_part, "tensor", scatter_dimension=0, tiled=True)
    w_down_grad = lax.psum_scatter(down_part, "tensor", scatter_dimension=0, tiled=True)

    first_dot = jnp.sum(jnp.where(select_first, slot_dots[:, None], 0.0), axis=0)
    second_dot = jnp.sum(jnp.where(select_second, slot_dots[:, None], 0.0), axis=0)
    coefficient = first_gate * second_gate * (first_dot - second_dot)
    logit_grad = (
        jnp.where(pick_first, coefficient[:, None], 0.0)
        - jnp.where(pick_second, coefficient[:, None], 0.0)
    ).astype(jnp.bfloat16)
    router_grad = jnp.einsum("nd,ne->de", moe_low, logit_grad, preferred_element_type=jnp.float32)

    def gated(rows):
        first_rows = jnp.einsum("st,sd->td", select_first_low, rows, preferred_element_type=jnp.float32)
        second_rows = jnp.einsum("st,sd->td", select_second_low, rows, preferred_element_type=jnp.float32)
        return first_gate[:, None] * first_rows + second_gate[:, None] * second_rows

    moe_norm_grad = (
        jnp.einsum("ne,de->nd", logit_grad, w_router, preferred_element_type=jnp.float32)
        + gated(returned_grad)
    )
    middle_back, gain_moe_rows = norm_back(middle, gain_moe, moe_norm_grad)
    middle_grad = grad_float + middle_back
    gain_moe_grad = jnp.sum(gain_moe_rows, axis=0)
    attn_grad = middle_grad.astype(jnp.bfloat16)
    heads_grad = jnp.einsum("nd,fd->nf", attn_grad, out_full, preferred_element_type=jnp.float32)
    heads_grad = lax.all_to_all(
        heads_grad.astype(jnp.bfloat16), "tensor", split_axis=1, concat_axis=0, tiled=True
    )
    out_part = jnp.einsum("nf,nd->fd", heads_own, attn_grad, preferred_element_type=jnp.float32)
    out_part = lax.psum_scatter(out_part.astype(jnp.bfloat16), "tensor", scatter_dimension=0, tiled=True)
    w_out_grad = lax.psum_scatter(out_part.astype(jnp.float32), "dp", scatter_dimension=1, tiled=True)
    gain_moe_grad, router_grad = lax.psum((gain_moe_grad, router_grad), ("dp", "tensor"))

    norm_part, qkv_part, folded = attend_back(
        line, segk, segq, seq_rows, qkv_full, qkv_low, heads_grad, lse
    )
    attn_norm_grad = lax.psum_scatter(norm_part, "tensor", scatter_dimension=0, tiled=True)
    input_back, gain_attn_rows = norm_back(x_float, gain_attn, attn_norm_grad.astype(jnp.float32))
    input_grad = middle_grad + input_back
    gain_attn_grad = jnp.sum(gain_attn_rows, axis=0)
    w_qkv_grad = lax.psum_scatter(qkv_part, "dp", scatter_dimension=1, tiled=True)
    line_grad = lines_of(folded, heads, seq_len // QB)
    table_part = jnp.dot(bucket_hot.T, line_grad.T, precision=HIGHEST)
    table_whole = lax.dynamic_update_slice(
        jnp.zeros(rel_table.shape, jnp.float32), table_part, (0, tensor_pos * heads)
    )
    gain_attn_grad, table_whole = lax.psum((gain_attn_grad, table_whole), ("dp", "tensor"))
    block_output = middle + gated(returned)
    return (
        block_output,
        input_grad,
        w_qkv_grad,
        w_out_grad,
        table_whole,
        gain_attn_grad,
        gain_moe_grad,
        router_grad,
        w_up_grad.astype(jnp.float32)[None],
        w_down_grad.astype(jnp.float32)[None],
    )


def fused_body(
    block_input,
    out_grad,
    w_qkv,
    w_out,
    rel_table,
    gain_attn,
    gain_moe,
    w_router,
    w_up,
    w_down,
    routes,
    segments,
    padding,
    rel_bucket,
):
    dp_count, tensor_count = lax.axis_size("dp"), lax.axis_size("tensor")
    rows_local, width = block_input.shape
    seq_len = segments.shape[1]
    heads = w_qkv.shape[2] // DH
    capacity = slot_capacity(rows_local, w_router.shape[1])
    expert_count = w_router.shape[1]
    sizes = (dp_count, tensor_count, expert_count, capacity, capacity, heads, seq_len // QB, True)

    routes_t = routes.T
    bucket_row = rel_bucket[None]
    rows, w_all, outw, down_all, qkv, lse, heads_all, slot_rows, cot, line, segk, middle, moe_low, x_send = front(
        sizes, block_input, gain_attn, w_qkv, w_out, w_down[0], out_grad, routes_t, segments, padding,
        rel_table.T, bucket_row, gain_moe
    )
    (up_pair, up_own, up_first, down_own, down_land, produced, middle_grad, heads_grad, out_part, early,
     gates) = middle_pass(
        sizes, x_send, moe_low, middle, out_grad, heads_all, outw, gain_moe, w_router.T, routes_t, padding,
        slot_rows, cot, w_up[0], w_down[0], down_all
    )
    block_output, input_grad, wgrad, early, late, up_rest = last_pass(
        sizes, block_input, gain_attn, middle, middle_grad, heads_grad, rows, w_all, qkv, lse, line, segk, segments,
        produced, slot_rows, gates, early, bucket_row, out_part, up_pair
    )
    (block_output, input_grad, w_qkv_grad, w_out_grad, table_grad, gain_attn_grad, gain_moe_grad, router_grad,
     w_up_grad, w_down_grad) = finish(
        rel_table.shape[1], block_output, input_grad, wgrad, early, late, up_own, up_first, up_rest, down_own, down_land
    )
    return (
        block_output,
        input_grad,
        w_qkv_grad,
        w_out_grad,
        table_grad.T,
        gain_attn_grad,
        gain_moe_grad,
        router_grad.T,
        w_up_grad[None],
        w_down_grad[None],
    )


def slot_capacity(tokens, experts):
    return (10 * tokens + 4 * experts - 1) // (4 * experts)


def body(*args):
    block_input, w_qkv, w_router = args[0], args[2], args[7]
    capacity = slot_capacity(block_input.shape[0], w_router.shape[1])
    fits = capacity % 16 == 0 and w_qkv.shape[1] % 16 == 0 and lax.axis_size("dp") == w_router.shape[1] == 8 and block_input.shape[1] <= 1024
    return fused_body(*args) if fits else plain_body(*args)


def solution(mesh):
    in_specs = (
        P(("dp", "tensor"), None),
        P(("dp", "tensor"), None),
        P(None, "dp", "tensor"),
        P("tensor", "dp"),
        P(),
        P(),
        P(),
        P(),
        P("dp", "tensor", None),
        P("dp", "tensor", None),
        P(("dp", "tensor"), None),
        P("dp", None),
        P("dp", None),
        P(),
    )
    out_specs = (
        P(("dp", "tensor"), None),
        P(("dp", "tensor"), None),
        P(None, "dp", "tensor"),
        P("tensor", "dp"),
        P(),
        P(),
        P(),
        P(),
        P("dp", "tensor", None),
        P("dp", "tensor", None),
    )
    return jax.shard_map(body, mesh=mesh, in_specs=in_specs, out_specs=out_specs, check_vma=False)
```

```python
import functools
import math

import jax
import jax.numpy as jnp
from jax import lax
from jax.experimental import pallas as pl
from jax.experimental.pallas import tpu as pltpu
from jax.sharding import PartitionSpec as P

NB = 32
EPSILON = 1e-06
HIGHEST = lax.Precision.HIGHEST
DH = 64
NEGATIVE = -1e30
QB = 256
NT = (((1,), (1,)), ((), ()))
TN = (((0,), (0,)), ((), ()))
NN = (((1,), (0,)), ((), ()))


def mm(a, b, dims):
    return lax.dot_general(a, b, dims, preferred_element_type=jnp.float32)


def build_bias(line_ref, tiles, heads, blocks):
    for h in range(heads):
        for d in range(blocks):
            piece = line_ref[h : h + 1, d * QB : d * QB + 2 * QB]
            wide = jnp.broadcast_to(piece, (QB, 2 * QB))
            turned = pltpu.roll(wide, 0, 1, stride=1, stride_axis=0)
            tiles[h, d] = turned[:, QB:]


def score_block(keys, query, tiles, h, qb, segk_ref, segq_ref):
    raw = mm(keys, query, NT)
    q_seg = segq_ref[:, qb * QB : (qb + 1) * QB]
    parts = []
    for kb in range(qb + 1):
        k_seg = segk_ref[kb * QB : (kb + 1) * QB, :]
        same = k_seg == q_seg
        if kb == qb:
            row = lax.broadcasted_iota(jnp.int32, (QB, QB), 0)
            col = lax.broadcasted_iota(jnp.int32, (QB, QB), 1)
            same = same | (row == col)
        parts.append(
            jnp.where(same, raw[kb * QB : (kb + 1) * QB] + tiles[h, qb - kb], NEGATIVE)
        )
    return parts


def attend_kernel(heads, blocks, line_ref, segk_ref, segq_ref, rows_ref, w_ref,
                  qkv_ref, out_ref, lse_ref, tiles):
    @pl.when(pl.program_id(0) == 0)
    def _():
        build_bias(line_ref, tiles, heads, blocks)

    for c in range(3):
        qkv_ref[c] = mm(rows_ref[...], w_ref[c], NN).astype(jnp.bfloat16)
    scale = 1.0 / math.sqrt(DH)
    for qb in range(blocks):
        nk = (qb + 1) * QB
        lower = qb * QB
        turned = []
        for h in range(heads):
            cols = slice(h * DH, (h + 1) * DH)
            query = (qkv_ref[0, lower : lower + QB, cols].astype(jnp.float32) * scale).astype(jnp.bfloat16)
            parts = score_block(qkv_ref[1, 0:nk, cols], query, tiles, h, qb, segk_ref.at[0], segq_ref.at[0])
            peak = functools.reduce(jnp.maximum, [jnp.max(x, axis=0, keepdims=True) for x in parts])
            probs = [jnp.exp(x - peak) for x in parts]
            total = functools.reduce(jnp.add, [jnp.sum(x, axis=0, keepdims=True) for x in probs])
            mixed = functools.reduce(jnp.add, [
                mm(qkv_ref[2, kb * QB : (kb + 1) * QB, cols], x.astype(jnp.bfloat16), TN)
                for kb, x in enumerate(probs)])
            turned.append(mixed / total)
            lse_ref[0, h : h + 1, lower : lower + QB] = peak + jnp.log(total)
        out_ref[lower : lower + QB, :] = jnp.concatenate(turned, axis=0).T.astype(jnp.bfloat16)


def attend(line, segk, segq, rows, w):
    seqs, _, seq_len = segq.shape
    heads = line.shape[0]
    inner = heads * DH
    blocks = seq_len // QB
    width = rows.shape[1]
    return pl.pallas_call(
        functools.partial(attend_kernel, heads, blocks),
        grid=(seqs,),
        in_specs=[
            pl.BlockSpec(line.shape, lambda s: (0, 0)),
            pl.BlockSpec((1, seq_len, 1), lambda s: (s, 0, 0)),
            pl.BlockSpec((1, 1, seq_len), lambda s: (s, 0, 0)),
            pl.BlockSpec((seq_len, width), lambda s: (s, 0)),
            pl.BlockSpec(w.shape, lambda s: (0, 0, 0)),
        ],
        out_specs=[
            pl.BlockSpec((3, seq_len, inner), lambda s: (0, s, 0)),
            pl.BlockSpec((seq_len, inner), lambda s: (s, 0)),
            pl.BlockSpec((1, heads, seq_len), lambda s: (s, 0, 0)),
        ],
        out_shape=[
            jax.ShapeDtypeStruct((3, seqs * seq_len, inner), jnp.bfloat16),
            jax.ShapeDtypeStruct((seqs * seq_len, inner), jnp.bfloat16),
            jax.ShapeDtypeStruct((seqs, heads, seq_len), jnp.float32),
        ],
        scratch_shapes=[pltpu.VMEM((heads, blocks, QB, QB), jnp.float32)],
        compiler_params=pltpu.CompilerParams(vmem_limit_bytes=48 << 20),
        cost_estimate=pl.CostEstimate(flops=10_000_000_000, bytes_accessed=10 << 20, transcendentals=4_000_000),
        name="attend",
    )(line, segk, segq, rows, w)


def attend_back_kernel(heads, blocks, seqs, line_ref, segk_ref, segq_ref, rows_ref, w_ref,
                       qkv_ref, og_ref, lse_ref,
                       norm_ref, wg_ref, lg_ref, tiles, sums, kg, vg, dq):
    step = pl.program_id(0)

    @pl.when(step == 0)
    def _():
        build_bias(line_ref, tiles, heads, blocks)
        sums[...] = jnp.zeros_like(sums)
        wg_ref[...] = jnp.zeros_like(wg_ref)

    scale = 1.0 / math.sqrt(DH)
    for h in range(heads):
        cols = slice(h * DH, (h + 1) * DH)
        kg[...] = jnp.zeros_like(kg)
        vg[...] = jnp.zeros_like(vg)
        for qb in range(blocks):
            nk = (qb + 1) * QB
            lower = qb * QB
            query = (qkv_ref[0, lower : lower + QB, cols].astype(jnp.float32) * scale).astype(jnp.bfloat16)
            grad = og_ref[lower : lower + QB, cols]
            lse = lse_ref[0, h : h + 1, lower : lower + QB]
            parts = score_block(qkv_ref[1, 0:nk, cols], query, tiles, h, qb, segk_ref.at[0], segq_ref.at[0])
            probs = [jnp.exp(x - lse) for x in parts]
            pg = mm(qkv_ref[2, 0:nk, cols], grad, NT)
            pgs = [pg[kb * QB : (kb + 1) * QB] for kb in range(qb + 1)]
            delta = functools.reduce(jnp.add, [jnp.sum(p * g, axis=0, keepdims=True) for p, g in zip(probs, pgs)])
            dqt = jnp.zeros((DH, QB), jnp.float32)
            for kb in range(qb + 1):
                rows = slice(kb * QB, (kb + 1) * QB)
                sg = (probs[kb] * (pgs[kb] - delta)).astype(jnp.bfloat16)
                sums[h, qb - kb] += sg.astype(jnp.float32)
                vg[rows] += mm(probs[kb].astype(jnp.bfloat16), grad, NN)
                kg[rows] += mm(sg, query, NN)
                dqt = dqt + mm(qkv_ref[1, rows, cols], sg, TN)
            dq[lower : lower + QB, h * DH : (h + 1) * DH] = (dqt * scale).T.astype(jnp.bfloat16)
        inner = heads * DH
        dq[:, inner + h * DH : inner + (h + 1) * DH] = kg[...].astype(jnp.bfloat16)
        dq[:, 2 * inner + h * DH : 2 * inner + (h + 1) * DH] = vg[...].astype(jnp.bfloat16)
    inner = heads * DH
    total = jnp.zeros(norm_ref.shape, jnp.float32)
    for c in range(3):
        piece = dq[:, c * inner : (c + 1) * inner]
        wg_ref[c] += mm(rows_ref[...], piece, TN)
        total = total + mm(piece, w_ref[c], NT)
    norm_ref[...] = total.astype(norm_ref.dtype)

    @pl.when(step == seqs - 1)
    def _():
        for h in range(heads):
            for d in range(blocks):
                lg_ref[h * blocks + d] = fold_tile(sums, h, d)


def fold_tile(sums, h, d):
    blank = jnp.zeros((8, QB), jnp.float32)
    total = jnp.zeros((8, 2 * QB), jnp.float32)
    for g in range(QB // 8):
        piece = jnp.concatenate([sums[h, d, 8 * g : 8 * g + 8, :], blank], axis=1)
        total = total + (piece if g == 0 else pltpu.roll(piece, 2 * QB - 8 * g, 1))
    return total


def lines_of(folded, heads, blocks):
    moved = sum(jnp.roll(folded[:, s, :], -s, axis=1) for s in range(8))
    moved = moved.reshape(heads, blocks, 2, QB)
    ahead = jnp.concatenate([moved[:, 1:, 1], jnp.zeros((heads, 1, QB), jnp.float32)], axis=1)
    return (moved[:, :, 0] + ahead).reshape(heads, blocks * QB)


def attend_back(line, segk, segq, rows, w, qkv, og, lse):
    seqs, _, seq_len = segq.shape
    heads = line.shape[0]
    inner = heads * DH
    blocks = seq_len // QB
    width = rows.shape[1]
    return pl.pallas_call(
        functools.partial(attend_back_kernel, heads, blocks, seqs),
        grid=(seqs,),
        in_specs=[
            pl.BlockSpec(line.shape, lambda s: (0, 0)),
            pl.BlockSpec((1, seq_len, 1), lambda s: (s, 0, 0)),
            pl.BlockSpec((1, 1, seq_len), lambda s: (s, 0, 0)),
            pl.BlockSpec((seq_len, width), lambda s: (s, 0)),
            pl.BlockSpec(w.shape, lambda s: (0, 0, 0)),
            pl.BlockSpec((3, seq_len, inner), lambda s: (0, s, 0)),
            pl.BlockSpec((seq_len, inner), lambda s: (s, 0)),
            pl.BlockSpec((1, heads, seq_len), lambda s: (s, 0, 0)),
        ],
        out_specs=[
            pl.BlockSpec((seq_len, width), lambda s: (s, 0)),
            pl.BlockSpec(w.shape, lambda s: (0, 0, 0)),
            pl.BlockSpec((heads * blocks, 8, 2 * QB), lambda s: (0, 0, 0)),
        ],
        out_shape=[
            jax.ShapeDtypeStruct((seqs * seq_len, width), jnp.bfloat16),
            jax.ShapeDtypeStruct(w.shape, jnp.float32),
            jax.ShapeDtypeStruct((heads * blocks, 8, 2 * QB), jnp.float32),
        ],
        scratch_shapes=[
            pltpu.VMEM((heads, blocks, QB, QB), jnp.float32),
            pltpu.VMEM((heads, blocks, QB, QB), jnp.float32),
            pltpu.VMEM((seq_len, DH), jnp.float32),
            pltpu.VMEM((seq_len, DH), jnp.float32),
            pltpu.VMEM((seq_len, 3 * inner), jnp.bfloat16),
        ],
        compiler_params=pltpu.CompilerParams(vmem_limit_bytes=48 << 20),
        cost_estimate=pl.CostEstimate(flops=20_000_000_000, bytes_accessed=16 << 20, transcendentals=4_000_000),
        name="attend_back",
    )(line, segk, segq, rows, w, qkv, og, lse)


def mask_inputs(segments, padding):
    keyed = jnp.where(padding == 1, segments, -1)
    return keyed[:, :, None], segments[:, None, :]


def line_of(by_distance):
    return jnp.concatenate([jnp.full((by_distance.shape[0], QB), NEGATIVE, jnp.float32), by_distance], axis=1)


FT = 512
ROOT_2_PI = math.sqrt(2.0 / math.pi)


def gelu_pair(x):
    square = x * x
    t = jnp.tanh(ROOT_2_PI * x * (1.0 + 0.044715 * square))
    half = 0.5 * (1.0 + t)
    slope = half + 0.5 * x * (1.0 - t * t) * (ROOT_2_PI * (1.0 + 3 * 0.044715 * square))
    return x * half, slope


def expert_kernel(steps, x_ref, g_ref, up_ref, down_ref, act_ref, pre_ref, back_ref, dot_ref, total, dots):
    step = pl.program_id(0)

    @pl.when(step == 0)
    def _():
        total[...] = jnp.zeros_like(total)
        dots[...] = jnp.zeros_like(dots)

    rows = x_ref.shape[0]
    chunk = 256
    for lower in range(0, rows, chunk):
        part = slice(lower, lower + chunk)
        pre = mm(x_ref[part], up_ref[...], NT)
        out_side = mm(g_ref[part], down_ref[...], NT)
        act, slope = gelu_pair(pre)
        low = act.astype(jnp.bfloat16)
        act_ref[part] = low
        product = low.astype(jnp.float32) * out_side
        dots[part] += sum(product[:, k : k + 128] for k in range(0, FT, 128))
        back = (out_side * slope).astype(jnp.bfloat16)
        pre_ref[part] = back
        total[part] += mm(back, up_ref[...], NN)

    @pl.when(step == steps - 1)
    def _():
        back_ref[...] = total[...].astype(jnp.bfloat16)
        dot_ref[...] = lax.dot_general(
            jnp.ones((8, 128), jnp.float32), dots[...], NT,
            precision=HIGHEST, preferred_element_type=jnp.float32)


def expert_first(x, g, up, down):
    rows, width = x.shape
    hidden = up.shape[0]
    steps = hidden // FT
    whole = lambda f: (0, 0)
    return pl.pallas_call(
        functools.partial(expert_kernel, steps),
        grid=(steps,),
        in_specs=[
            pl.BlockSpec((rows, width), whole),
            pl.BlockSpec((rows, width), whole),
            pl.BlockSpec((FT, width), lambda f: (f, 0)),
            pl.BlockSpec((FT, width), lambda f: (f, 0)),
        ],
        out_specs=[
            pl.BlockSpec((rows, FT), lambda f: (0, f)),
            pl.BlockSpec((rows, FT), lambda f: (0, f)),
            pl.BlockSpec((rows, width), whole),
            pl.BlockSpec((8, rows), whole),
        ],
        out_shape=[
            jax.ShapeDtypeStruct((rows, hidden), jnp.bfloat16),
            jax.ShapeDtypeStruct((rows, hidden), jnp.bfloat16),
            jax.ShapeDtypeStruct((rows, width), jnp.bfloat16),
            jax.ShapeDtypeStruct((8, rows), jnp.float32),
        ],
        scratch_shapes=[
            pltpu.VMEM((rows, width), jnp.float32),
            pltpu.VMEM((rows, 128), jnp.float32),
        ],
        compiler_params=pltpu.CompilerParams(vmem_limit_bytes=48 << 20),
        cost_estimate=pl.CostEstimate(
            flops=6 * rows * width * hidden, bytes_accessed=32 << 20, transcendentals=rows * hidden),
        name="expert_first",
    )(x, g, up, down)


def expert_late_kernel(steps, x_ref, g_ref, gate_ref, act_ref, pre_ref, down_ref,
                       out_ref, up_grad_ref, down_grad_ref, total, x_gated, g_gated):
    step = pl.program_id(0)

    @pl.when(step == 0)
    def _():
        total[...] = jnp.zeros_like(total)
        gate = gate_ref[...]
        x_gated[...] = (x_ref[...].astype(jnp.float32) * gate).astype(jnp.bfloat16)
        g_gated[...] = (g_ref[...].astype(jnp.float32) * gate).astype(jnp.bfloat16)

    up_grad_ref[...] = mm(pre_ref[...], x_gated[...], TN).astype(up_grad_ref.dtype)
    down_grad_ref[...] = mm(act_ref[...], g_gated[...], TN).astype(down_grad_ref.dtype)
    total[...] += mm(act_ref[...], down_ref[...], NN)

    @pl.when(step == steps - 1)
    def _():
        out_ref[...] = total[...].astype(jnp.bfloat16)


def expert_late(x, g, gate, act, pre, down):
    rows, width = x.shape
    hidden = down.shape[0]
    steps = hidden // FT
    whole = lambda f: (0, 0)
    tile = pl.BlockSpec((FT, width), lambda f: (f, 0))
    return pl.pallas_call(
        functools.partial(expert_late_kernel, steps),
        grid=(steps,),
        in_specs=[
            pl.BlockSpec((rows, width), whole),
            pl.BlockSpec((rows, width), whole),
            pl.BlockSpec((rows, 1), whole),
            pl.BlockSpec((rows, FT), lambda f: (0, f)),
            pl.BlockSpec((rows, FT), lambda f: (0, f)),
            tile,
        ],
        out_specs=[pl.BlockSpec((rows, width), whole), tile, tile],
        out_shape=[
            jax.ShapeDtypeStruct((rows, width), jnp.bfloat16),
            jax.ShapeDtypeStruct((hidden, width), jnp.bfloat16),
            jax.ShapeDtypeStruct((hidden, width), jnp.bfloat16),
        ],
        scratch_shapes=[
            pltpu.VMEM((rows, width), jnp.float32),
            pltpu.VMEM((rows, width), jnp.bfloat16),
            pltpu.VMEM((rows, width), jnp.bfloat16),
        ],
        compiler_params=pltpu.CompilerParams(vmem_limit_bytes=48 << 20),
        cost_estimate=pl.CostEstimate(
            flops=6 * rows * width * hidden, bytes_accessed=32 << 20, transcendentals=0),
        name="expert_late",
    )(x, g, gate, act, pre, down)


MESH = pl.DeviceIdType.MESH
VMEM_LIMIT = 61 << 20


def remote(src, dst, send, recv, axis, place):
    return pltpu.make_async_remote_copy(
        src_ref=src, dst_ref=dst, send_sem=send, recv_sem=recv, device_id={axis: place}, device_id_type=MESH
    )


def each_peer(count, step, start=1):
    if count <= 8:
        for r in range(start, count):
            step(r)
    else:
        def one(r, carry):
            step(r)
            return carry
        lax.fori_loop(start, count, one, 0)


def peer(r):
    return jnp.bitwise_xor(lax.axis_index("dp"), r)


def greet(dp_count, tensor_count):
    barrier = pltpu.get_barrier_semaphore()
    dp, tp = lax.axis_index("dp"), lax.axis_index("tensor")
    for r in range(1, tensor_count):
        pl.semaphore_signal(barrier, inc=1, device_id={"tensor": lax.rem(tp + r, tensor_count)}, device_id_type=MESH)

    def signal(r):
        pl.semaphore_signal(barrier, inc=1, device_id={"dp": peer(r)}, device_id_type=MESH)
    each_peer(dp_count, signal)
    return lambda: pl.semaphore_wait(barrier, tensor_count - 1 + dp_count - 1)


def partners(tensor_count):
    tp = lax.axis_index("tensor")
    sib = tp + 1 - 2 * lax.rem(tp, 2)
    return tp, sib, lax.rem(tp + 2, tensor_count), lax.rem(sib + 2, tensor_count)


def place_pairs(routes_ref, live, experts, capacity, cap_rows):
    tokens = live.shape[1]
    live = live == 1
    ids = lax.broadcasted_iota(jnp.int32, (experts, tokens), 0)
    row = lax.broadcasted_iota(jnp.int32, (tokens, tokens), 0)
    col = lax.broadcasted_iota(jnp.int32, (tokens, tokens), 1)
    before = (row < col).astype(jnp.float32).astype(jnp.bfloat16)
    slots = []
    base = jnp.zeros((experts, 1), jnp.float32)
    for k in range(2):
        route = routes_ref[k : k + 1, :]
        hot = jnp.where((ids == route) & live, 1.0, 0.0)
        count = mm(hot.astype(jnp.bfloat16), before, NN) + base
        place = jnp.sum(count * hot, axis=0, keepdims=True).astype(jnp.int32)
        slots.append(jnp.where(live & (place < capacity), route * cap_rows + place, -1))
        base = base + jnp.sum(hot, axis=1, keepdims=True)
    return slots


def chosen(first, second, expert, cap_rows):
    ids = lax.broadcasted_iota(jnp.int32, (cap_rows, first.shape[1]), 0) + expert * cap_rows
    return jnp.where((ids == first) | (ids == second), 1.0, 0.0).astype(jnp.bfloat16)


def attend_sequence(heads, blocks, seq, line_tiles, segk_ref, segq_ref, qkv, heads_out, lse_ref):
    scale = 1.0 / math.sqrt(DH)
    half = blocks // 2
    for qb in range(blocks):
        nk = (qb + 1) * QB
        lower = qb * QB
        for h in range(heads):
            cols = [slice((3 * h + c) * DH, (3 * h + c + 1) * DH) for c in range(3)]
            query = (qkv[seq, lower : lower + QB, cols[0]].astype(jnp.float32) * scale).astype(jnp.bfloat16)
            parts = score_block(qkv[seq, 0:nk, cols[1]], query, line_tiles, h, qb, segk_ref.at[seq], segq_ref.at[pl.ds(seq, 1)])
            peak = functools.reduce(jnp.maximum, [jnp.max(x, axis=0, keepdims=True) for x in parts])
            probs = [jnp.exp(x - peak) for x in parts]
            total = functools.reduce(jnp.add, [jnp.sum(x, axis=0, keepdims=True) for x in probs])
            mixed = functools.reduce(jnp.add, [
                mm(qkv[seq, kb * QB : (kb + 1) * QB, cols[2]], x.astype(jnp.bfloat16), TN)
                for kb, x in enumerate(probs)])
            heads_out[seq * 2 + qb // half, h * DH : (h + 1) * DH, (qb % half) * QB : (qb % half + 1) * QB] = (
                mixed / total).astype(jnp.bfloat16)
            lse_ref[seq, h : h + 1, lower : lower + QB] = peak + jnp.log(total)


def packed_gather(own_ref, all_ref, send, recv, dp_count):
    dp = lax.axis_index("dp")
    side = peer(1)
    columns = dp_count // 2
    near = remote(own_ref, all_ref.at[dp], send.at[0], recv.at[0], "dp", side)
    out = [remote(own_ref, all_ref.at[dp], send.at[k], recv.at[k], "dp", peer(2 * k))
           for k in range(1, columns)]
    onward = []
    for k in range(1, columns):
        src = peer(2 * k)
        n = columns - 1 + k
        onward.append(remote(all_ref.at[src], all_ref.at[src], send.at[n], recv.at[n], "dp", side))
    return near, out, onward


def prepare(heads, tp, table_ref, bucket_ref, segments_ref, padding_ref, line_ref, segk_ref):
    buckets, length = table_ref.shape[1], bucket_ref.shape[1]
    ids = lax.broadcasted_iota(jnp.int32, (buckets, length), 0)
    hot = ids == bucket_ref[...]
    for h in range(heads):
        column = to_column(table_ref[pl.ds(tp * heads + h, 1), :], buckets)
        line_ref[h : h + 1, :QB] = jnp.full((1, QB), NEGATIVE, jnp.float32)
        line_ref[h : h + 1, QB:] = jnp.sum(jnp.where(hot, column, 0.0), axis=0, keepdims=True)
    keyed = jnp.where(padding_ref[...] == 1, segments_ref[...], -1).astype(jnp.float32)
    for s in range(keyed.shape[0]):
        for k in range(length // QB):
            piece = keyed[s : s + 1, k * QB : (k + 1) * QB]
            segk_ref[s, k * QB : (k + 1) * QB, :] = to_column(piece, QB).astype(jnp.int32)


def front_kernel(sizes, x_ref, gain_ref, w_ref, outw_ref, down_ref, grad_ref, routes_ref, segments_ref, padding_ref,
                 table_ref, bucket_ref, gain_moe_ref,
                 rows_out, w_out_all, outw_all, down_all, qkv_out, lse_ref, heads_all, slots_ref, cot, line_ref, segk_ref,
                 middle_out, moe_out, x_out,
                 tiles, heads_out, cot_send, w_own, rows, w_all, qkv, middle, moe_low, x_send,
                 far_send, far_recv, w_send, w_recv, ot_send, ot_recv,
                 dn_send, dn_recv, cot_s, cot_r, head_send, head_recv, local_sem, out_sem):
    dp_count, tensor_count, experts, capacity, cap_rows, heads, blocks, gather_w = sizes
    dp = lax.axis_index("dp")
    tp, sib, opp, across = partners(tensor_count)
    wait_barrier = greet(dp_count, tensor_count)
    inner = heads * DH
    for h in range(heads):
        for c in range(3):
            n = (3 * h + c) * DH
            w_own[:, n : n + DH] = w_ref[c, :, h * DH : (h + 1) * DH]
    w_own[:, 3 * inner :] = outw_ref[...].T

    x = x_ref[...].astype(jnp.float32)
    r = lax.rsqrt(jnp.mean(x * x, axis=-1, keepdims=True) + EPSILON)
    rows[tp] = (x * r * gain_ref[...].reshape(1, x.shape[1])).astype(jnp.bfloat16)
    wait_barrier()

    half = rows.shape[1] // 2
    parts = [pl.ds(0, half), pl.ds(half, half)]
    far = [remote(rows.at[tp, p], rows.at[tp, p], far_send.at[k], far_recv.at[k], "tensor", opp) for k, p in enumerate(parts)]
    near = remote(rows.at[tp], rows.at[tp], far_send.at[2], far_recv.at[2], "tensor", sib)
    onward = [remote(rows.at[opp, p], rows.at[opp, p], far_send.at[3 + k], far_recv.at[3 + k], "tensor", sib) for k, p in enumerate(parts)]
    for c in far:
        c.start()
    near.start()

    w_near, w_out, w_on = packed_gather(w_own, w_all, w_send, w_recv, dp_count)
    for c in w_out:
        c.start()
    w_near.start()
    w_all[dp] = w_own[...]

    tokens = x_ref.shape[0]
    live = padding_ref[pl.ds(tp // 2, 1), pl.ds(pl.multiple_of(lax.rem(tp, 2) * tokens, 128), tokens)]
    first, second = place_pairs(routes_ref, live, experts, capacity, cap_rows)
    slots_ref[0:1, :] = first
    slots_ref[1:2, :] = second

    def cot_copy(r):
        to = peer(r)
        return remote(cot_send.at[to], cot.at[dp], cot_s.at[r], cot_r.at[r], "dp", to)

    def cot_fill(r):
        to = peer(r)
        cot_send[to] = mm(chosen(first, second, to, cap_rows), grad_ref[...], NN).astype(jnp.bfloat16)

    each_peer(dp_count, cot_fill)
    cot_fill(0)
    own_cot = pltpu.make_async_copy(cot_send.at[dp], cot.at[dp], local_sem.at[1])
    own_cot.start()

    prepare(heads, tp, table_ref, bucket_ref, segments_ref, padding_ref, line_ref, segk_ref)
    build_bias(line_ref, tiles, heads, blocks)
    for c, on in zip(w_out, w_on):
        c.wait_recv()
        on.start()
    each_peer(dp_count, lambda r: cot_copy(r).start())
    w_near.wait_recv()
    for c in w_on:
        c.wait_recv()
    near.wait_recv()

    width = rows.shape[2]
    own_seq = tp // 2
    packed = qkv.shape[2]

    def project(seq):
        tokens = rows[pl.ds(seq * 2, 2)].reshape(2 * rows.shape[1], width)
        weight = w_all[...].reshape(width, w_all.shape[2])[:, :packed]
        qkv[seq] = mm(tokens, weight, NN).astype(jnp.bfloat16)

    def head_copy(k, to):
        return remote(heads_out.at[to], heads_all.at[tp], head_send.at[k], head_recv.at[k], "tensor", to)

    cut = 5 * down_ref.shape[0] // 8
    strips = [pl.ds(0, cut), pl.ds(cut, down_ref.shape[0] - cut)]
    down_far = [remote(down_ref.at[p], down_all.at[tp, p], dn_send.at[k], dn_recv.at[k], "tensor", opp)
                for k, p in enumerate(strips)]
    down_near = remote(down_ref, down_all.at[tp], dn_send.at[2], dn_recv.at[2], "tensor", sib)
    down_on = [remote(down_all.at[opp, p], down_all.at[opp, p], dn_send.at[3 + k], dn_recv.at[3 + k], "tensor", sib)
               for k, p in enumerate(strips)]

    put_w = pltpu.make_async_copy(w_all, w_out_all, out_sem.at[0])
    put_w.start()
    project(own_seq)
    put_own = pltpu.make_async_copy(qkv.at[own_seq], qkv_out.at[own_seq], out_sem.at[1])
    put_own.start()
    outw_all[tp] = w_all[...].reshape(width, w_all.shape[2])[:, 3 * inner :].T
    ot_far = remote(outw_all.at[tp], outw_all.at[tp], ot_send.at[0], ot_recv.at[0], "tensor", opp)
    ot_near = remote(outw_all.at[tp], outw_all.at[tp], ot_send.at[1], ot_recv.at[1], "tensor", sib)
    ot_on = remote(outw_all.at[opp], outw_all.at[opp], ot_send.at[2], ot_recv.at[2], "tensor", sib)
    for k in range(2):
        far[k].wait_recv()
        onward[k].start()
    ot_far.start()
    ot_near.start()
    down_far[0].start()
    down_near.start()
    attend_sequence(heads, blocks, own_seq, tiles, segk_ref, segments_ref, qkv, heads_out, lse_ref)
    head_copy(0, sib).start()
    heads_all[tp] = heads_out[tp]
    for k in range(2):
        onward[k].wait_recv()
    other = 1 - own_seq
    put_rows = pltpu.make_async_copy(rows, rows_out, out_sem.at[2])
    put_rows.start()
    project(other)
    put_other = pltpu.make_async_copy(qkv.at[other], qkv_out.at[other], out_sem.at[3])
    put_other.start()
    attend_sequence(heads, blocks, other, tiles, segk_ref, segments_ref, qkv, heads_out, lse_ref)
    ot_far.wait_recv()
    ot_on.start()
    head_copy(1, opp).start()
    head_copy(2, across).start()
    down_far[1].start()
    down_far[0].wait_recv()
    down_on[0].start()

    head_copy(0, sib).wait_recv()
    head_copy(1, opp).wait_recv()
    head_copy(2, across).wait_recv()
    ot_near.wait_recv()
    ot_on.wait_recv()
    mixed = x_ref[...].astype(jnp.float32)
    for t in range(tensor_count):
        mixed = mixed + mm(heads_all[t], outw_all[t], TN)
    middle[...] = mixed
    r = lax.rsqrt(jnp.mean(mixed * mixed, axis=-1, keepdims=True) + EPSILON)
    moe_low[...] = (mixed * r * gain_moe_ref[...].reshape(1, width)).astype(jnp.bfloat16)
    for e in range(experts):
        x_send[e] = mm(chosen(first, second, e, cap_rows), moe_low[...], NN).astype(jnp.bfloat16)
    puts = [pltpu.make_async_copy(src, dst, out_sem.at[4 + k]) for k, (src, dst) in enumerate((
        (x_send, x_out), (moe_low, moe_out), (middle, middle_out)))]
    for c in puts:
        c.start()

    down_far[1].wait_recv()
    down_on[1].start()
    for c in [put_w, put_own, put_rows, put_other] + puts:
        c.wait()
    own_cot.wait()
    each_peer(dp_count, lambda r: cot_copy(r).wait())
    ot_on.wait_send()
    ot_near.wait_send()
    ot_far.wait_send()
    for c in [w_near] + w_out + w_on:
        c.wait_send()
    for c in far + [near] + onward:
        c.wait_send()
    head_copy(0, sib).wait_send()
    head_copy(1, opp).wait_send()
    head_copy(2, across).wait_send()
    for k in range(2):
        down_far[k].wait_send()
        down_on[k].wait()
    down_near.wait()


def sems(*counts):
    out = []
    for n in counts:
        out += [pltpu.SemaphoreType.DMA((n,)), pltpu.SemaphoreType.DMA((n,))]
    return out


def front(sizes, x, gain, w, outw, down, grad, routes_t, segments, padding, table, bucket, gain_moe):
    dp_count, tensor_count, experts, capacity, cap_rows, heads, blocks, gather_w = sizes
    tokens, width = x.shape
    seq_len = blocks * QB
    seqs = tensor_count * tokens // seq_len
    inner = heads * DH
    packed = -(-3 * inner // 128) * 128
    vmem = pl.BlockSpec(memory_space=pltpu.VMEM)
    anywhere = pl.BlockSpec(memory_space=pl.ANY)
    shape = jax.ShapeDtypeStruct
    low = jnp.bfloat16
    return pl.pallas_call(
        functools.partial(front_kernel, sizes),
        in_specs=[vmem] * 4 + [anywhere] + [vmem] * 7,
        out_specs=[anywhere] * 2 + [vmem] + [anywhere] * 2 + [vmem] * 3 + [anywhere] + [vmem] * 2 + [anywhere] * 3,
        out_shape=[
            shape((tensor_count, tokens, width), low),
            shape((dp_count, w.shape[1], 4 * inner), low),
            shape((tensor_count, inner, width), low),
            shape((tensor_count,) + down.shape, low),
            shape((seqs, seq_len, packed), low),
            shape((seqs, heads, seq_len), jnp.float32),
            shape((tensor_count, inner, tokens), low),
            shape((8, tokens), jnp.int32),
            shape((experts, cap_rows, width), low),
            shape((heads, QB + seq_len), jnp.float32),
            shape((seqs, seq_len, 1), jnp.int32),
            shape((tokens, width), jnp.float32),
            shape((tokens, width), low),
            shape((experts, cap_rows, width), low),
        ],
        scratch_shapes=[
            pltpu.VMEM((heads, blocks, QB, QB), jnp.float32),
            pltpu.VMEM((tensor_count, inner, tokens), low),
            pltpu.VMEM((experts, cap_rows, width), low),
            pltpu.VMEM((w.shape[1], 4 * inner), low),
            pltpu.VMEM((tensor_count, tokens, width), low),
            pltpu.VMEM((dp_count, w.shape[1], 4 * inner), low),
            pltpu.VMEM((seqs, seq_len, packed), low),
            pltpu.VMEM((tokens, width), jnp.float32),
            pltpu.VMEM((tokens, width), low),
            pltpu.VMEM((experts, cap_rows, width), low),
        ] + sems(5, dp_count, 3, 5, dp_count, 3) + [pltpu.SemaphoreType.DMA((3,)), pltpu.SemaphoreType.DMA((7,))],
        compiler_params=pltpu.CompilerParams(
            vmem_limit_bytes=VMEM_LIMIT, collective_id=1, has_side_effects=True),
        cost_estimate=pl.CostEstimate(flops=20_000_000_000, bytes_accessed=20 << 20, transcendentals=4_000_000),
        name="front",
    )(x, gain, w, outw, down, grad, routes_t, segments, padding, table, bucket, gain_moe)


def to_row(column, lanes):
    n = column.shape[0]
    row = lax.broadcasted_iota(jnp.int32, (n, lanes), 0)
    col = lax.broadcasted_iota(jnp.int32, (n, lanes), 1)
    return jnp.sum(jnp.where(row == col, column, 0.0), axis=0, keepdims=True)


def to_column(row_values, n):
    lanes = row_values.shape[1]
    row = lax.broadcasted_iota(jnp.int32, (n, lanes), 0)
    col = lax.broadcasted_iota(jnp.int32, (n, lanes), 1)
    return jnp.sum(jnp.where(row == col, row_values, 0.0), axis=1, keepdims=True)


def gate_map(first, second, gate_first, gate_second, expert, cap_rows):
    ids = lax.broadcasted_iota(jnp.int32, (cap_rows, first.shape[1]), 0) + expert * cap_rows
    return jnp.where(ids == first, gate_first, jnp.where(ids == second, gate_second, 0.0))


def gated_rows(weights, rows):
    high = weights.astype(jnp.bfloat16)
    low = (weights - high.astype(jnp.float32)).astype(jnp.bfloat16)
    return mm(high, rows, TN) + mm(low, rows, TN)


def middle_kernel(sizes, x_send, moe_in, middle_in, grad_ref, heads_ref, outw_ref, gain_ref, router_ref, routes_ref, padding_ref,
                  slots_ref, cot_ref, up_ref, down_own_ref, down_ref,
                  up_pair_out, up_own_out, up_land, down_own_out, down_land, produced_out, middle_grad, heads_grad, out_part, stats, gates,
                  up, down, g_rows, x_rows, act, side, back_send, back, gate_send, gate_rows,
                  dot_send, dot_rows, moe_low, stage, up_pair, up_own, down_own, produced, middle, down_pair,
                  up_s, up_r, x_s, x_r, b_s, b_r, g_s, g_r, d_s, d_r, a_s, a_r, load_sem, out_sem):
    dp_count, tensor_count, experts, capacity, cap_rows, heads, blocks, gather_w = sizes
    dp = lax.axis_index("dp")
    tp, sib, opp, across = partners(tensor_count)
    hidden = up.shape[1]
    total = middle_grad
    tokens, width = grad_ref.shape
    lanes = gate_send.shape[2]
    wait_barrier = greet(dp_count, tensor_count)

    load_g = pltpu.make_async_copy(cot_ref, g_rows, load_sem.at[0])
    load_down = [
        pltpu.make_async_copy(down_own_ref, down.at[tp], load_sem.at[1]),
        pltpu.make_async_copy(down_ref.at[sib], down.at[sib], load_sem.at[5]),
        pltpu.make_async_copy(down_ref.at[opp], down.at[opp], load_sem.at[6]),
        pltpu.make_async_copy(down_ref.at[across], down.at[across], load_sem.at[7]),
    ]
    load_up = pltpu.make_async_copy(up_ref, up.at[tp], load_sem.at[2])
    load_g.start()
    for c in load_down:
        c.start()
    load_up.start()

    loads = [pltpu.make_async_copy(src, dst, load_sem.at[n]) for n, src, dst in (
        (3, moe_in, moe_low), (4, middle_in, middle), (8, x_send.at[dp], x_rows.at[dp]))]
    for c in loads:
        c.start()
    puts = [pltpu.make_async_copy(src, dst, out_sem.at[k]) for k, (src, dst) in enumerate((
        (produced, produced_out), (up_pair, up_pair_out), (up_own, up_own_out), (down_own, down_own_out)))]
    first, second = slots_ref[0:1, :], slots_ref[1:2, :]
    wait_barrier()

    up_far = remote(up_ref, up.at[tp], up_s.at[0], up_r.at[0], "tensor", opp)
    up_near = remote(up_ref, up.at[tp], up_s.at[1], up_r.at[1], "tensor", sib)
    up_on = remote(up.at[opp], up.at[opp], up_s.at[2], up_r.at[2], "tensor", sib)
    up_far.start()
    up_near.start()

    def x_copy(r):
        to = peer(r)
        return remote(x_send.at[to], x_rows.at[dp], x_s.at[r], x_r.at[r], "dp", to)

    held = dp_count - 2
    for r in list(range(dp_count // 2, held)) + list(range(1, dp_count // 2)):
        x_copy(r).start()
    loads[0].wait()
    loads[2].wait()


    ids = lax.broadcasted_iota(jnp.int32, (experts, tokens), 0)
    pick_first, pick_second = ids == routes_ref[0:1, :], ids == routes_ref[1:2, :]
    live = padding_ref[pl.ds(tp // 2, 1), pl.ds(pl.multiple_of(lax.rem(tp, 2) * tokens, 128), tokens)]
    live = (live == 1).astype(jnp.float32)
    logits = mm(router_ref[...], moe_low[...], NT)
    gap = jnp.sum(jnp.where(pick_first, logits, 0.0) - jnp.where(pick_second, logits, 0.0), axis=0, keepdims=True)
    gate_first = live / (1.0 + jnp.exp(-gap))
    gate_second = live / (1.0 + jnp.exp(gap))
    gates[0:1, :] = gate_first
    gates[1:2, :] = gate_second

    def gate_copy(r):
        to = peer(r)
        return remote(gate_send.at[to], gate_rows.at[dp], g_s.at[r], g_r.at[r], "dp", to)

    def gate_fill(r):
        to = peer(r)
        column = jnp.sum(gate_map(first, second, gate_first, gate_second, to, cap_rows), axis=1, keepdims=True)
        return jnp.broadcast_to(to_row(column, lanes), (8, lanes))

    def gate_go(r):
        gate_send[peer(r)] = gate_fill(r)
        gate_copy(r).start()
    each_peer(dp_count, gate_go)
    gate_rows[dp] = gate_fill(0)

    load_g.wait()
    for c in load_down:
        c.wait()
    slots = experts * cap_rows
    block = slots // 4

    def side_block(k, carry):
        part = pl.ds(pl.multiple_of(k * block, 16), block)
        here = g_rows[pl.ds(k * (experts // 4), experts // 4)].reshape(block, width)
        for t in range(tensor_count):
            side[part, t * hidden : (t + 1) * hidden] = mm(here, down[t], NT).astype(jnp.bfloat16)
        return carry
    lax.fori_loop(0, 4, side_block, 0)

    for r in range(dp_count // 2, held):
        x_copy(r).wait_send()
    for r in range(held, dp_count):
        x_copy(r).start()
    load_up.wait()
    up_far.wait_recv()
    up_on.start()
    up_near.wait_recv()
    up_on.wait_recv()

    def back_copy(r):
        to = peer(r)
        return remote(back_send.at[to], back.at[dp], b_s.at[r], b_r.at[r], "dp", to)

    def dot_copy(r):
        to = peer(r)
        return remote(dot_send.at[to], dot_rows.at[dp], d_s.at[r], d_r.at[r], "dp", to)

    group = max(1, min(dp_count, 320 // cap_rows))

    def first_pass(step, carry):
        rounds = [step * group + k for k in range(group)]
        froms = [peer(r) for r in rounds]
        for k, r in enumerate(rounds):
            if k == 0:
                @pl.when(r > 0)
                def _():
                    x_copy(r).wait_recv()
            else:
                x_copy(r).wait_recv()
        here = jnp.concatenate([x_rows[s] for s in froms], axis=0)
        total_back = jnp.zeros((group * cap_rows, width), jnp.float32)
        dots = jnp.zeros((group * cap_rows, 128), jnp.float32)
        for t in range(tensor_count):
            cols = slice(t * hidden, (t + 1) * hidden)
            pre = mm(here, up[t], NT)
            value, slope = gelu_pair(pre)
            low = value.astype(jnp.bfloat16)
            places = [pl.ds(pl.multiple_of(s * cap_rows, 16), cap_rows) for s in froms]
            beside = jnp.concatenate([side[p, cols] for p in places], axis=0).astype(jnp.float32)
            product = low.astype(jnp.float32) * beside
            dots = dots + sum(product[:, k : k + 128] for k in range(0, hidden, 128))
            grad = (beside * slope).astype(jnp.bfloat16)
            for k, p in enumerate(places):
                piece = slice(k * cap_rows, (k + 1) * cap_rows)
                act[p, cols] = low[piece]
                side[p, cols] = grad[piece]
            total_back = total_back + mm(grad, up[t], NN)
        column = jnp.sum(dots, axis=1, keepdims=True)
        for k, (r, s) in enumerate(zip(rounds, froms)):
            piece = slice(k * cap_rows, (k + 1) * cap_rows)
            low = total_back[piece].astype(jnp.bfloat16)
            line = jnp.broadcast_to(to_row(column[piece], lanes), (8, lanes))

            def send():
                back_send[s] = low
                dot_send[s] = line
                back_copy(r).start()
                dot_copy(r).start()

            def keep():
                back[dp] = low
                dot_rows[dp] = line
            if k == 0:
                pl.when(r > 0)(send)
                pl.when(r == 0)(keep)
            else:
                send()
        return carry
    lax.fori_loop(0, dp_count // group, first_pass, 0)

    each_peer(dp_count, lambda r: gate_copy(r).wait_recv())

    def gate_rows_in(s, carry):
        column = to_column(gate_rows[s, 0:1, :], cap_rows)
        x_rows[s] = (x_rows[s].astype(jnp.float32) * column).astype(jnp.bfloat16)
        g_rows[s] = (g_rows[s].astype(jnp.float32) * column).astype(jnp.bfloat16)
        return carry
    lax.fori_loop(0, experts, gate_rows_in, 0)

    for r in list(range(1, dp_count // 2)) + list(range(held, dp_count)):
        x_copy(r).wait_send()
    lands = ((down_pair, down_own), (up_pair, up_own))
    aside = [remote(stage.at[k], lands[k][n], a_s.at[2 * k + n], a_r.at[2 * k + n], "tensor", sib)
             for k in range(2) for n in range(2)]
    up_far_part = remote(up_pair.at[pl.ds(0, hidden // 4)], up_land, a_s.at[5], a_r.at[5], "tensor", opp)
    down_far = remote(down_pair, down_land, a_s.at[4], a_r.at[4], "tensor", opp)
    piece = hidden // 2
    shards = (across, sib, opp, tp)
    sources = ((act, g_rows), (side, x_rows))
    for k, n in ((0, 0), (0, 2), (1, 0), (1, 2), (0, 1), (1, 1), (0, 3), (1, 3)):
        left, right = sources[k]
        if n == 1:
            aside[2 * k].wait_send()
        if n >= 2:
            aside[2 * k + n - 2].wait_recv()
        for m in range(2):
            cols = pl.ds(pl.multiple_of(shards[n] * hidden + m * piece, 128), piece)
            part = pl.ds(m * piece, piece)
            tile = mm(left[:, cols], right[...].reshape(slots, width), TN)
            if n < 2:
                stage[k, part, :] = tile.astype(jnp.bfloat16)
            else:
                land = lands[k][n - 2]
                land[part, :] = (tile + land[part, :].astype(jnp.float32)).astype(jnp.bfloat16)
        if n < 2:
            aside[2 * k + n].start()
        elif n == 2 and k == 0:
            down_far.start()
        elif n == 2:
            up_far_part.start()
            puts[1].start()
        elif k == 0:
            puts[3].start()
        else:
            puts[2].start()

    def produce(k, carry):
        part = pl.ds(pl.multiple_of(k * block, 16), block)
        out = jnp.zeros((block, width), jnp.float32)
        for t in range(tensor_count):
            out = out + mm(act[part, t * hidden : (t + 1) * hidden], down[t], NN)
        out = out.astype(jnp.bfloat16)
        for e in range(experts // 4):
            produced[k * (experts // 4) + e] = out[e * cap_rows : (e + 1) * cap_rows]
        return carry
    lax.fori_loop(0, 4, produce, 0)

    puts[0].start()

    total[...] = jnp.zeros_like(total)

    def combine(r, carry):
        dot_first, dot_second = carry
        e = peer(r)

        @pl.when(r > 0)
        def _():
            back_copy(r).wait_recv()
            dot_copy(r).wait_recv()
        weights = gate_map(first, second, gate_first, gate_second, e, cap_rows)
        total[...] += gated_rows(weights, back[e])
        column = to_column(dot_rows[e, 0:1, :], cap_rows)
        ids = lax.broadcasted_iota(jnp.int32, (cap_rows, tokens), 0) + e * cap_rows
        dot_first = dot_first + jnp.sum(jnp.where(ids == first, column, 0.0), axis=0, keepdims=True)
        dot_second = dot_second + jnp.sum(jnp.where(ids == second, column, 0.0), axis=0, keepdims=True)
        return dot_first, dot_second
    zero_row = jnp.zeros((1, tokens), jnp.float32)
    dot_first, dot_second = lax.fori_loop(0, dp_count, combine, (zero_row, zero_row))

    change = gate_first * gate_second * (dot_first - dot_second)
    logit_grad = (jnp.where(pick_first, change, 0.0) - jnp.where(pick_second, change, 0.0)).astype(jnp.bfloat16)
    norm_grad = total[...] + mm(logit_grad, router_ref[...], TN)
    loads[1].wait()
    mixed = middle[...]
    r = lax.rsqrt(jnp.mean(mixed * mixed, axis=-1, keepdims=True) + EPSILON)
    u = mixed * r
    du = norm_grad * gain_ref[...].reshape(1, width)
    grad = grad_ref[...].astype(jnp.float32) + r * (du - u * jnp.mean(du * u, axis=-1, keepdims=True))
    middle_grad[...] = grad
    low = grad.astype(jnp.bfloat16)
    for t in range(tensor_count):
        heads_grad[t] = mm(outw_ref[t], low, NT).astype(jnp.bfloat16)
        out_part[t] = mm(heads_ref[t], low, NN).astype(jnp.bfloat16)
    stats[0:8, :] = jnp.broadcast_to(jnp.sum(norm_grad * u, axis=0, keepdims=True), (8, width))
    stats[8:, :] = mm(logit_grad, moe_low[...], NN)

    down_far.wait_recv()
    up_far_part.wait_recv()
    down_far.wait_send()
    up_far_part.wait_send()
    for c in puts:
        c.wait()
    for k in range(2):
        aside[2 * k + 1].wait_send()
    up_far.wait_send()
    up_near.wait_send()
    up_on.wait_send()

    def drain(r):
        gate_copy(r).wait_send()
        back_copy(r).wait_send()
        dot_copy(r).wait_send()
    each_peer(dp_count, drain)


def middle_pass(sizes, x_send, moe_low, middle, grad, heads_all, outw, gain, router_t, routes_t, padding, slot_rows, cot, up, down, down_all):
    dp_count, tensor_count, experts, capacity, cap_rows, heads, blocks, gather_w = sizes
    tokens, width = grad.shape
    inner = heads * DH
    hidden = up.shape[0]
    slots = experts * cap_rows
    lanes = -(-cap_rows // 128) * 128
    vmem = pl.BlockSpec(memory_space=pltpu.VMEM)
    anywhere = pl.BlockSpec(memory_space=pl.ANY)
    shape = jax.ShapeDtypeStruct
    low = jnp.bfloat16
    return pl.pallas_call(
        functools.partial(middle_kernel, sizes),
        in_specs=[anywhere] * 3 + [vmem] * 8 + [anywhere] * 4,
        out_specs=[anywhere] * 2 + [vmem] + [anywhere] + [vmem] + [anywhere] + [vmem] * 5,
        out_shape=[
            shape((hidden, width), low),
            shape((hidden, width), low),
            shape((hidden // 4, width), low),
            shape((hidden, width), low),
            shape((hidden, width), low),
            shape((experts, cap_rows, width), low),
            shape((tokens, width), jnp.float32),
            shape((tensor_count, inner, tokens), low),
            shape((tensor_count, inner, width), low),
            shape((8 + experts, width), jnp.float32),
            shape((8, tokens), jnp.float32),
        ],
        scratch_shapes=[
            pltpu.VMEM((tensor_count, hidden, width), low),
            pltpu.VMEM((tensor_count, hidden, width), low),
            pltpu.VMEM((experts, cap_rows, width), low),
            pltpu.VMEM((experts, cap_rows, width), low),
            pltpu.VMEM((slots, tensor_count * hidden), low),
            pltpu.VMEM((slots, tensor_count * hidden), low),
            pltpu.VMEM((experts, cap_rows, width), low),
            pltpu.VMEM((experts, cap_rows, width), low),
            pltpu.VMEM((experts, 8, lanes), jnp.float32),
            pltpu.VMEM((experts, 8, lanes), jnp.float32),
            pltpu.VMEM((experts, 8, lanes), jnp.float32),
            pltpu.VMEM((experts, 8, lanes), jnp.float32),
            pltpu.VMEM((tokens, width), low),
            pltpu.VMEM((2, hidden, width), low),
            pltpu.VMEM((hidden, width), low),
            pltpu.VMEM((hidden, width), low),
            pltpu.VMEM((hidden, width), low),
            pltpu.VMEM((experts, cap_rows, width), low),
            pltpu.VMEM((tokens, width), jnp.float32),
            pltpu.VMEM((hidden, width), low),
        ] + sems(5, dp_count, dp_count, dp_count, dp_count, 6) + [pltpu.SemaphoreType.DMA((9,)), pltpu.SemaphoreType.DMA((4,))],
        compiler_params=pltpu.CompilerParams(
            vmem_limit_bytes=VMEM_LIMIT, collective_id=2, has_side_effects=True),
        cost_estimate=pl.CostEstimate(
            flops=12 * slots * width * hidden * tensor_count, bytes_accessed=40 << 20, transcendentals=4_000_000),
        name="middle_pass",
    )(x_send, moe_low, middle, grad, heads_all, outw, gain, router_t, routes_t, padding, slot_rows, cot, up, down, down_all)


def attend_back_sequence(heads, blocks, seq, tiles, sums, segk_ref, segq_ref, qkv, grads, lse_ref, kg, vg, dq, chosen_heads):
    scale = 1.0 / math.sqrt(DH)
    half = blocks // 2
    for h in chosen_heads:
        cols, kcols, vcols = [slice((3 * h + c) * DH, (3 * h + c + 1) * DH) for c in range(3)]
        gcols = slice(h * DH, (h + 1) * DH)
        kg[...] = jnp.zeros_like(kg)
        vg[...] = jnp.zeros_like(vg)
        for qb in range(blocks):
            nk = (qb + 1) * QB
            lower = qb * QB
            query = (qkv[seq, lower : lower + QB, cols].astype(jnp.float32) * scale).astype(jnp.bfloat16)
            grad = grads[seq * 2 + qb // half, gcols, (qb % half) * QB : (qb % half + 1) * QB]
            lse = lse_ref[seq, h : h + 1, lower : lower + QB]
            parts = score_block(qkv[seq, 0:nk, kcols], query, tiles, h, qb, segk_ref.at[seq], segq_ref.at[pl.ds(seq, 1)])
            probs = [jnp.exp(x - lse) for x in parts]
            pg = mm(qkv[seq, 0:nk, vcols], grad, NN)
            pgs = [pg[kb * QB : (kb + 1) * QB] for kb in range(qb + 1)]
            delta = functools.reduce(jnp.add, [jnp.sum(p * g, axis=0, keepdims=True) for p, g in zip(probs, pgs)])
            dqt = jnp.zeros((DH, QB), jnp.float32)
            for kb in range(qb + 1):
                rows = slice(kb * QB, (kb + 1) * QB)
                sg = (probs[kb] * (pgs[kb] - delta)).astype(jnp.bfloat16)
                sums[h, qb - kb] += sg.astype(jnp.float32)
                vg[rows] += mm(probs[kb].astype(jnp.bfloat16), grad, NT)
                kg[rows] += mm(sg, query, NN)
                dqt = dqt + mm(qkv[seq, rows, kcols], sg, TN)
            dq[lower : lower + QB, cols] = (dqt * scale).T.astype(jnp.bfloat16)
        dq[:, kcols] = kg[...].astype(jnp.bfloat16)
        dq[:, vcols] = vg[...].astype(jnp.bfloat16)


def fold_lines(sums, h, blocks):
    moved = []
    for d in range(blocks):
        folded = fold_tile(sums, h, d)
        line = folded[0:1, :]
        for s in range(1, 8):
            line = line + pltpu.roll(folded[s : s + 1, :], 2 * QB - s, 1)
        moved.append(line)
    out = []
    for d in range(blocks):
        piece = moved[d][:, :QB]
        if d + 1 < blocks:
            piece = piece + moved[d + 1][:, QB:]
        out.append(piece)
    return jnp.concatenate(out, axis=1)


def two_stage_start(send, land, s_sem, r_sem, tensor_count):
    tp = lax.axis_index("tensor")
    copies = []
    for r in range(1, tensor_count):
        copies.append(remote(send, land.at[r - 1], s_sem.at[r], r_sem.at[r], "tensor", lax.rem(tp + r, tensor_count)))
    for c in copies:
        c.start()
    return copies


def last_kernel(sizes, x_ref, gain_ref, middle_ref, mgrad_in, hgrad_ref, rows_in, w_in, qkv_in, lse_ref, line_ref,
                segk_ref, segq_ref, produced_ref, slots_ref, gates_ref, early_ref, bucket_ref,
                out_part, up_pair,
                out_ref, input_grad_ref, wgrad_ref, early_out, late_out, up_land,
                tiles, sums, kg, vg, dq, grads, landed, npart, near_land, far_land, pair, wsum, wsend, wland,
                early_land, early_mid, early_dp, late, late_land, late_mid, late_dp, total, mgrad_ref, rows, w_ref, qkv,
                out_land, out_pair, out_far,
                h_s, h_r, p_s, p_r, n_s, n_r, w_s, w_r, et_s, et_r, ed_s, ed_r, lt_s, lt_r, ld_s, ld_r, o_s, o_r, load_sem):
    dp_count, tensor_count, experts, capacity, cap_rows, heads, blocks, gather_w = sizes
    dp = lax.axis_index("dp")
    tp, sib, opp, across = partners(tensor_count)
    tokens, width = x_ref.shape
    inner = heads * DH
    wait_barrier = greet(dp_count, tensor_count)
    loads = [pltpu.make_async_copy(src, dst, load_sem.at[k]) for k, (src, dst) in enumerate((
        (qkv_in, qkv), (rows_in, rows), (w_in, w_ref), (produced_ref.at[dp], landed.at[dp]), (middle_ref, total),
        (mgrad_in, mgrad_ref)))]
    for c in loads:
        c.start()
    build_bias(line_ref, tiles, heads, blocks)
    sums[...] = jnp.zeros_like(sums)
    dq[:, :, 3 * inner :] = jnp.zeros((2, dq.shape[1], dq.shape[2] - 3 * inner), jnp.bfloat16)
    own_seq = tp // 2
    other = 1 - own_seq
    wait_barrier()

    def h_copy(k, to):
        return remote(hgrad_ref.at[to], grads.at[tp], h_s.at[k], h_r.at[k], "tensor", to)
    h_copy(0, opp).start()
    h_copy(1, across).start()
    h_copy(2, sib).start()
    grads[tp] = hgrad_ref[tp]

    def p_copy(r):
        to = peer(r)
        return remote(produced_ref.at[to], landed.at[dp], p_s.at[r], p_r.at[r], "dp", to)
    sent = list(range(dp_count // 2, dp_count)) + list(range(1, dp_count // 2))
    for r in sent:
        p_copy(r).start()

    early = two_stage_start(early_ref.at[pl.ds(8, experts)], early_land, et_s, et_r, tensor_count)

    def early_copy(r):
        return remote(early_mid, early_dp.at[r], ed_s.at[r], ed_r.at[r], "dp", peer(r))

    out_near = [remote(out_part.at[t], out_land.at[k], o_s.at[k], o_r.at[k], "tensor", sib)
                for k, t in enumerate((across, sib))]
    out_across = remote(out_pair, out_far, o_s.at[2], o_r.at[2], "tensor", opp)
    for c in out_near:
        c.start()

    up_rest = remote(up_pair.at[pl.ds(up_pair.shape[0] // 4, up_land.shape[0])], up_land, o_s.at[3], o_r.at[3],
                     "tensor", opp)

    def n_copy(k, src, dst, to):
        return remote(src, dst, n_s.at[k], n_r.at[k], "tensor", to)
    pair_near = n_copy(0, npart.at[across], near_land.at[0], sib)
    pair_far = n_copy(1, pair, far_land, opp)
    own_near = n_copy(2, npart.at[sib], near_land.at[1], sib)
    packed = dq.shape[2]

    def attend_part(seq, k, chosen_heads):
        attend_back_sequence(heads, blocks, seq, tiles, sums, segk_ref, segq_ref, qkv, grads, lse_ref, kg, vg,
                             dq.at[k], chosen_heads)

    def norm_part(seq, k):
        here = rows[pl.ds(seq * 2, 2)].reshape(2 * tokens, width)
        norm = mm(dq[k], w_ref[...].reshape(width, w_ref.shape[2])[:, :packed], NT)
        column = jnp.sum(norm * here.astype(jnp.float32), axis=0, keepdims=True)
        low = norm.astype(jnp.bfloat16)
        npart[seq * 2] = low[:tokens]
        npart[seq * 2 + 1] = low[tokens:]
        return column

    share = width // dp_count
    side = peer(1)
    columns = dp_count // 2
    lanes = wsum.shape[1] // 2

    def share_rows(d):
        return pl.ds(pl.multiple_of(d * share, 8), share)

    def side_copy(m, k):
        n = 2 * columns * m + k
        return remote(wsend.at[n], wland.at[n], w_s.at[n], w_r.at[n], "dp", side)

    def column_copy(m, k):
        n = 2 * columns * m + columns + k
        return remote(wsend.at[n], wland.at[n], w_s.at[n], w_r.at[n], "dp", peer(2 * k))

    def side_go(m):
        for k in list(range(1, columns)) + [0]:
            there = share_rows(jnp.bitwise_xor(side, 2 * k))
            wsend[2 * columns * m + k] = wsum[there, m * lanes : (m + 1) * lanes].astype(jnp.bfloat16)
            side_copy(m, k).start()

    def column_go(m):
        for k in range(1, columns):
            side_copy(m, k).wait_recv()
            mine = wsum[share_rows(peer(2 * k)), m * lanes : (m + 1) * lanes]
            n = 2 * columns * m + columns + k
            wsend[n] = (mine + wland[2 * columns * m + k].astype(jnp.float32)).astype(jnp.bfloat16)
            column_copy(m, k).start()

    out_near[0].wait_recv()
    out_pair[...] = (out_part[opp].astype(jnp.float32) + out_land[0].astype(jnp.float32)).astype(jnp.bfloat16)
    out_across.start()
    loads[0].wait()
    h_copy(2, sib).wait_recv()
    attend_part(own_seq, 0, range(1))
    loads[1].wait()
    loads[2].wait()
    up_rest.start()
    h_copy(0, opp).wait_recv()
    h_copy(1, across).wait_recv()
    attend_part(other, 1, range(heads))
    gain_row = norm_part(other, 1)
    pair_near.start()
    wsum[:, :packed] = mm(rows[pl.ds(other * 2, 2)].reshape(2 * tokens, width), dq[1], TN)
    out_across.wait_recv()
    out_near[1].wait_recv()
    out_whole = out_part[tp].astype(jnp.float32) + out_land[1].astype(jnp.float32) + out_far[...].astype(jnp.float32)
    wsum[:, 3 * inner :] = out_whole.T
    pair_near.wait_recv()
    pair[...] = (npart[opp].astype(jnp.float32) + near_land[0].astype(jnp.float32)).astype(jnp.bfloat16)
    pair_far.start()
    attend_part(own_seq, 0, range(1, 2))
    wsum[:, :lanes] += mm(rows[pl.ds(own_seq * 2, 2)].reshape(2 * tokens, width), dq[0, :, :lanes], TN)
    side_go(0)
    attend_part(own_seq, 0, range(2, heads))
    column_go(0)
    wsum[:, lanes : 3 * inner] += mm(rows[pl.ds(own_seq * 2, 2)].reshape(2 * tokens, width), dq[0, :, lanes:packed], TN)[:, : 3 * inner - lanes]
    side_go(1)
    gain_row = gain_row + norm_part(own_seq, 0)
    own_near.start()
    for c in early:
        c.wait_recv()
    early_mid[...] = early_ref[8:, :] + early_land[0] + early_land[1] + early_land[2]
    each_peer(dp_count, lambda r: early_copy(r).start())

    gain_row = gain_row / gain_ref[...].reshape(1, width)
    late[...] = jnp.zeros_like(late)
    pieces = width // 128
    for k in range(pieces):
        late[k : k + 1, :] = gain_row[:, k * 128 : (k + 1) * 128]
        late[pieces + k : pieces + k + 1, :] = early_ref[0:1, k * 128 : (k + 1) * 128]
    ids = lax.broadcasted_iota(jnp.int32, (NB, bucket_ref.shape[1]), 0)
    hot = ids == bucket_ref[...]
    place = lax.broadcasted_iota(jnp.int32, (NB, 128), 1) - lax.broadcasted_iota(jnp.int32, (NB, 128), 0)
    table = jnp.zeros((1, 128), jnp.float32)
    for h in range(heads):
        column = jnp.sum(jnp.where(hot, fold_lines(sums, h, blocks), 0.0), axis=1, keepdims=True)
        table = table + jnp.sum(jnp.where(place == h * NB, column, 0.0), axis=0, keepdims=True)
    late[pl.ds(2 * pieces + tp, 1), :] = table
    late_first = two_stage_start(late, late_land, lt_s, lt_r, tensor_count)

    def late_copy(r):
        return remote(late_mid, late_dp.at[r], ld_s.at[r], ld_r.at[r], "dp", peer(r))

    first, second = slots_ref[0:1, :], slots_ref[1:2, :]
    gate_first, gate_second = gates_ref[0:1, :], gates_ref[1:2, :]
    loads[3].wait()
    loads[4].wait()

    def combine(e):
        total[...] += gated_rows(gate_map(first, second, gate_first, gate_second, e, cap_rows), landed[e])
    combine(dp)
    for r in range(1, dp_count // 2):
        p_copy(r).wait_recv()
        combine(peer(r))

    column_go(1)
    for r in range(dp_count // 2, dp_count):
        p_copy(r).wait_recv()
        combine(peer(r))
    out_ref[...] = total[...]
    for c in late_first:
        c.wait_recv()
    late_mid[...] = late[...] + late_land[0] + late_land[1] + late_land[2]
    each_peer(dp_count, lambda r: late_copy(r).start())

    each_peer(dp_count, lambda r: early_copy(r).wait_recv())
    summed = early_mid[...]
    for r in range(1, dp_count):
        summed = summed + early_dp[r]
    early_out[...] = summed
    loads[5].wait()

    own_near.wait_recv()
    pair_far.wait_recv()
    norm_grad = npart[tp].astype(jnp.float32) + near_land[1].astype(jnp.float32) + far_land[...].astype(jnp.float32)
    x = x_ref[...].astype(jnp.float32)
    r = lax.rsqrt(jnp.mean(x * x, axis=-1, keepdims=True) + EPSILON)
    u = x * r
    du = norm_grad * gain_ref[...].reshape(1, width)
    input_grad_ref[...] = mgrad_ref[...] + r * (du - u * jnp.mean(du * u, axis=-1, keepdims=True))

    for m in range(2):
        half = slice(m * lanes, (m + 1) * lanes)
        side_copy(m, 0).wait_recv()
        part = wsum[share_rows(dp), half] + wland[2 * columns * m].astype(jnp.float32)
        for k in range(1, columns):
            column_copy(m, k).wait_recv()
            part = part + wland[2 * columns * m + columns + k].astype(jnp.float32)
        wgrad_ref[:, half] = part
    up_rest.wait_recv()

    each_peer(dp_count, lambda r: late_copy(r).wait_recv())
    summed = late_mid[...]
    for r in range(1, dp_count):
        summed = summed + late_dp[r]
    late_out[...] = summed

    for c in early + late_first + out_near + [out_across, pair_near, pair_far, own_near, h_copy(0, opp), h_copy(1, across), h_copy(2, sib)]:
        c.wait_send()

    def drain(r):
        early_copy(r).wait_send()
        late_copy(r).wait_send()
    each_peer(dp_count, drain)
    for r in sent:
        p_copy(r).wait_send()
    for m in range(2):
        for k in range(columns):
            side_copy(m, k).wait_send()
            if k:
                column_copy(m, k).wait_send()
    up_rest.wait_send()


def last_pass(sizes, x, gain, middle, middle_grad, heads_grad, rows, w, qkv, lse, line, segk, segq, produced,
              slot_rows, gates, early, bucket_row, out_part, up_pair):
    dp_count, tensor_count, experts, capacity, cap_rows, heads, blocks, gather_w = sizes
    tokens, width = x.shape
    inner = heads * DH
    seq_len = blocks * QB
    share = width // dp_count
    vmem = pl.BlockSpec(memory_space=pltpu.VMEM)
    anywhere = pl.BlockSpec(memory_space=pl.ANY)
    shape = jax.ShapeDtypeStruct
    low, full = jnp.bfloat16, jnp.float32
    late = 16
    packed = qkv.shape[2]
    return pl.pallas_call(
        functools.partial(last_kernel, sizes),
        in_specs=[vmem] * 2 + [anywhere] * 2 + [vmem] + [anywhere] * 3 + [vmem] * 4 + [anywhere] + [vmem] * 5 + [anywhere],
        out_specs=[vmem] * 5 + [anywhere],
        out_shape=[
            shape((tokens, width), full),
            shape((tokens, width), full),
            shape((share, w.shape[2]), full),
            shape((experts, width), full),
            shape((late, 128), full),
            shape((3 * up_pair.shape[0] // 4, width), low),
        ],
        scratch_shapes=[
            pltpu.VMEM((heads, blocks, QB, QB), full),
            pltpu.VMEM((heads, blocks, QB, QB), full),
            pltpu.VMEM((seq_len, DH), full),
            pltpu.VMEM((seq_len, DH), full),
            pltpu.VMEM((2, seq_len, packed), low),
            pltpu.VMEM((tensor_count, inner, tokens), low),
            pltpu.VMEM((experts, cap_rows, width), low),
            pltpu.VMEM((tensor_count, tokens, width), low),
            pltpu.VMEM((2, tokens, width), low),
            pltpu.VMEM((tokens, width), low),
            pltpu.VMEM((tokens, width), low),
            pltpu.VMEM((width, w.shape[2]), full),
            pltpu.VMEM((2 * dp_count, share, w.shape[2] // 2), low),
            pltpu.VMEM((2 * dp_count, share, w.shape[2] // 2), low),
            pltpu.VMEM((tensor_count - 1, experts, width), full),
            pltpu.VMEM((experts, width), full),
            pltpu.VMEM((dp_count, experts, width), full),
            pltpu.VMEM((late, 128), full),
            pltpu.VMEM((tensor_count - 1, late, 128), full),
            pltpu.VMEM((late, 128), full),
            pltpu.VMEM((dp_count, late, 128), full),
            pltpu.VMEM((tokens, width), full),
            pltpu.VMEM((tokens, width), full),
            pltpu.VMEM(rows.shape, low),
            pltpu.VMEM(w.shape, low),
            pltpu.VMEM(qkv.shape, low),
            pltpu.VMEM((2, inner, width), low),
            pltpu.VMEM((inner, width), low),
            pltpu.VMEM((inner, width), low),
        ] + sems(3, dp_count, 3, 2 * dp_count, tensor_count, dp_count, tensor_count, dp_count, 4) + [pltpu.SemaphoreType.DMA((6,))],
        compiler_params=pltpu.CompilerParams(
            vmem_limit_bytes=VMEM_LIMIT, collective_id=3, has_side_effects=True),
        cost_estimate=pl.CostEstimate(flops=30_000_000_000, bytes_accessed=30 << 20, transcendentals=4_000_000),
        name="last_pass",
    )(x, gain, middle, middle_grad, heads_grad, rows, w, qkv, lse, line, segk, segq, produced, slot_rows, gates,
      early, bucket_row, out_part, up_pair)


def finish_kernel(out_ref, input_grad_ref, wgrad_ref, early_ref, late_ref, up_own, up_first, up_rest, down_own, down_land,
                  out, input_grad, w_qkv_grad, w_out_grad, table, gain_attn, gain_moe, router, up_grad, down_grad):
    out[...] = out_ref[...]
    input_grad[...] = input_grad_ref[...]
    land = jnp.where(pl.program_id(0) == 0, up_first[...].astype(jnp.float32), up_rest[...].astype(jnp.float32))
    up_grad[...] = up_own[...].astype(jnp.float32) + land
    down_grad[...] = down_own[...].astype(jnp.float32) + down_land[...].astype(jnp.float32)

    @pl.when(pl.program_id(0) == 0)
    def _():
        inner = w_qkv_grad.shape[2]
        for h in range(inner // DH):
            for c in range(3):
                n = (3 * h + c) * DH
                w_qkv_grad[c, :, h * DH : (h + 1) * DH] = wgrad_ref[:, n : n + DH]
        w_out_grad[...] = wgrad_ref[:, 3 * inner :].T
        pieces = gain_attn.shape[0] // 128
        heads = inner // DH
        for h in range(table.shape[0]):
            place = (h % heads) * NB
            table[h : h + 1, :] = late_ref[2 * pieces + h // heads : 2 * pieces + h // heads + 1, place : place + NB]
        for base, gain in ((0, gain_attn), (pieces, gain_moe)):
            row = jnp.concatenate([late_ref[base + k : base + k + 1, :] for k in range(pieces)], axis=1)
            gain[...] = row.reshape(gain.shape)
        router[...] = early_ref[...]


def finish(heads_total, out, input_grad, wgrad, early, late, up_own, up_first, up_rest, down_own, down_land):
    steps = 4
    tokens, width = out.shape
    share = wgrad.shape[0]
    inner = wgrad.shape[1] // 4
    hidden = up_own.shape[0]
    full = jnp.float32
    shape = jax.ShapeDtypeStruct

    def rows(n):
        return pl.BlockSpec((n // steps, width), lambda s: (s, 0))

    def whole(*dims):
        return pl.BlockSpec(dims, lambda s: (0,) * len(dims))
    return pl.pallas_call(
        finish_kernel,
        grid=(steps,),
        in_specs=[rows(tokens), rows(tokens), whole(*wgrad.shape), whole(*early.shape), whole(*late.shape)]
        + [rows(hidden), whole(*up_first.shape),
           pl.BlockSpec((hidden // steps, width), lambda s: (jnp.maximum(s - 1, 0), 0))] + [rows(hidden)] * 2,
        out_specs=[rows(tokens), rows(tokens), whole(3, share, inner), whole(inner, share), whole(heads_total, NB),
                   whole(width), whole(width), whole(*early.shape), rows(hidden), rows(hidden)],
        out_shape=[shape((tokens, width), full), shape((tokens, width), full), shape((3, share, inner), full),
                   shape((inner, share), full), shape((heads_total, NB), full), shape((width,), full),
                   shape((width,), full), shape(early.shape, full), shape((hidden, width), full),
                   shape((hidden, width), full)],
        compiler_params=pltpu.CompilerParams(vmem_limit_bytes=VMEM_LIMIT),
        cost_estimate=pl.CostEstimate(flops=0, bytes_accessed=16 << 20, transcendentals=0),
        name="finish",
    )(out, input_grad, wgrad, early, late, up_own, up_first, up_rest, down_own, down_land)


def norm_rows(values, gain):
    return values * lax.rsqrt(jnp.mean(values * values, axis=-1, keepdims=True) + EPSILON) * gain


def norm_back(values, gain, grad):
    r = lax.rsqrt(jnp.mean(values * values, axis=-1, keepdims=True) + EPSILON)
    u = values * r
    du = grad * gain
    return r * (du - u * jnp.mean(du * u, axis=-1, keepdims=True)), grad * u


def plain_body(
    block_input,
    out_grad,
    w_qkv,
    w_out,
    rel_table,
    gain_attn,
    gain_moe,
    w_router,
    w_up,
    w_down,
    routes,
    segments,
    padding,
    rel_bucket,
):
    tensor_pos = lax.axis_index("tensor")
    rows_local, width = block_input.shape
    seq_len = segments.shape[1]
    expert_count = w_router.shape[1]
    capacity = (10 * rows_local + 4 * expert_count - 1) // (4 * expert_count)
    slots = expert_count * capacity
    x_float = block_input.astype(jnp.float32)
    grad_float = out_grad.astype(jnp.float32)

    attn_norm = norm_rows(x_float, gain_attn).astype(jnp.bfloat16)
    seq_rows = lax.all_gather(attn_norm, "tensor", axis=0, tiled=True)
    qkv_full = lax.all_gather(w_qkv, "dp", axis=1, tiled=True)
    out_rows = lax.all_gather(w_out, "dp", axis=1, tiled=True)
    out_full = lax.all_gather(out_rows, "tensor", axis=0, tiled=True)
    up_full = lax.all_gather(w_up[0], "tensor", axis=0, tiled=True)
    down_full = lax.all_gather(w_down[0], "tensor", axis=0, tiled=True)

    live_mask = lax.dynamic_slice_in_dim(padding.reshape(-1), tensor_pos * rows_local, rows_local)
    live_float = live_mask.astype(jnp.float32)
    expert_ids = jnp.arange(expert_count, dtype=jnp.int32)
    pick_first = routes[:, 0:1] == expert_ids[None, :]
    pick_second = routes[:, 1:2] == expert_ids[None, :]
    usable = live_mask[:, None] == 1
    first_hot = (pick_first & usable).astype(jnp.int32)
    second_hot = (pick_second & usable).astype(jnp.int32)
    first_place = jnp.sum((jnp.cumsum(first_hot, axis=0) - first_hot) * first_hot, axis=1)
    second_before = (
        jnp.cumsum(second_hot, axis=0) - second_hot + jnp.sum(first_hot, axis=0, keepdims=True)
    )
    second_place = jnp.sum(second_before * second_hot, axis=1)
    first_slot = jnp.where(
        (live_mask == 1) & (first_place < capacity), routes[:, 0] * capacity + first_place, -1
    )
    second_slot = jnp.where(
        (live_mask == 1) & (second_place < capacity), routes[:, 1] * capacity + second_place, -1
    )
    slot_ids = jnp.arange(slots, dtype=jnp.int32)
    select_first = slot_ids[:, None] == first_slot[None, :]
    select_second = slot_ids[:, None] == second_slot[None, :]
    select_both = (select_first | select_second).astype(jnp.bfloat16)
    select_first_low = select_first.astype(jnp.bfloat16)
    select_second_low = select_second.astype(jnp.bfloat16)

    def to_experts(rows):
        return lax.all_to_all(rows, "dp", split_axis=0, concat_axis=0, tiled=True)

    grad_rows = jnp.dot(select_both, out_grad, preferred_element_type=jnp.float32)
    sent_grads = to_experts(grad_rows.astype(jnp.bfloat16).reshape(expert_count, capacity, width))
    sent_grads = sent_grads.reshape(slots, width)

    heads = qkv_full.shape[2] // DH
    inner = heads * DH
    table_local = lax.dynamic_slice_in_dim(rel_table, tensor_pos * heads, heads, 1)
    bucket_hot = (rel_bucket[:, None] == jnp.arange(NB, dtype=jnp.int32)[None, :]).astype(jnp.float32)
    line = line_of(jnp.dot(bucket_hot, table_local, precision=HIGHEST).T)
    segk, segq = mask_inputs(segments, padding)
    qkv_low, heads_low, lse = attend(line, segk, segq, seq_rows, qkv_full)
    heads_own = lax.all_to_all(heads_low, "tensor", split_axis=0, concat_axis=1, tiled=True)

    middle = x_float + jnp.dot(heads_own, out_full, preferred_element_type=jnp.float32)
    moe_low = norm_rows(middle, gain_moe).astype(jnp.bfloat16)
    rows_out = jnp.dot(select_both, moe_low, preferred_element_type=jnp.float32)
    sent_rows = to_experts(rows_out.astype(jnp.bfloat16).reshape(expert_count, capacity, width))
    sent_rows = sent_rows.reshape(slots, width)
    logits = jnp.dot(moe_low, w_router, preferred_element_type=jnp.float32)
    first_logit = jnp.sum(jnp.where(pick_first, logits, 0.0), axis=1)
    second_logit = jnp.sum(jnp.where(pick_second, logits, 0.0), axis=1)
    first_gate = jax.nn.sigmoid(first_logit - second_logit) * live_float
    second_gate = jax.nn.sigmoid(second_logit - first_logit) * live_float
    slot_gate = jnp.sum(
        jnp.where(select_first, first_gate[None, :], 0.0)
        + jnp.where(select_second, second_gate[None, :], 0.0),
        axis=1,
    )
    sent_gates = to_experts(slot_gate.reshape(expert_count, capacity)).reshape(slots, 1)

    act, pre_grad, back, dots = expert_first(sent_rows, sent_grads, up_full, down_full)
    returned_grad = to_experts(back.reshape(expert_count, capacity, width)).reshape(slots, width)
    slot_dots = to_experts(dots[0].reshape(expert_count, capacity)).reshape(slots)
    produced, up_part, down_part = expert_late(
        sent_rows, sent_grads, sent_gates, act, pre_grad, down_full
    )
    returned = to_experts(produced.reshape(expert_count, capacity, width)).reshape(slots, width)
    w_up_grad = lax.psum_scatter(up_part, "tensor", scatter_dimension=0, tiled=True)
    w_down_grad = lax.psum_scatter(down_part, "tensor", scatter_dimension=0, tiled=True)

    first_dot = jnp.sum(jnp.where(select_first, slot_dots[:, None], 0.0), axis=0)
    second_dot = jnp.sum(jnp.where(select_second, slot_dots[:, None], 0.0), axis=0)
    coefficient = first_gate * second_gate * (first_dot - second_dot)
    logit_grad = (
        jnp.where(pick_first, coefficient[:, None], 0.0)
        - jnp.where(pick_second, coefficient[:, None], 0.0)
    ).astype(jnp.bfloat16)
    router_grad = jnp.einsum("nd,ne->de", moe_low, logit_grad, preferred_element_type=jnp.float32)

    def gated(rows):
        first_rows = jnp.einsum("st,sd->td", select_first_low, rows, preferred_element_type=jnp.float32)
        second_rows = jnp.einsum("st,sd->td", select_second_low, rows, preferred_element_type=jnp.float32)
        return first_gate[:, None] * first_rows + second_gate[:, None] * second_rows

    moe_norm_grad = (
        jnp.einsum("ne,de->nd", logit_grad, w_router, preferred_element_type=jnp.float32)
        + gated(returned_grad)
    )
    middle_back, gain_moe_rows = norm_back(middle, gain_moe, moe_norm_grad)
    middle_grad = grad_float + middle_back
    gain_moe_grad = jnp.sum(gain_moe_rows, axis=0)
    attn_grad = middle_grad.astype(jnp.bfloat16)
    heads_grad = jnp.einsum("nd,fd->nf", attn_grad, out_full, preferred_element_type=jnp.float32)
    heads_grad = lax.all_to_all(
        heads_grad.astype(jnp.bfloat16), "tensor", split_axis=1, concat_axis=0, tiled=True
    )
    out_part = jnp.einsum("nf,nd->fd", heads_own, attn_grad, preferred_element_type=jnp.float32)
    out_part = lax.psum_scatter(out_part.astype(jnp.bfloat16), "tensor", scatter_dimension=0, tiled=True)
    w_out_grad = lax.psum_scatter(out_part.astype(jnp.float32), "dp", scatter_dimension=1, tiled=True)
    gain_moe_grad, router_grad = lax.psum((gain_moe_grad, router_grad), ("dp", "tensor"))

    norm_part, qkv_part, folded = attend_back(
        line, segk, segq, seq_rows, qkv_full, qkv_low, heads_grad, lse
    )
    attn_norm_grad = lax.psum_scatter(norm_part, "tensor", scatter_dimension=0, tiled=True)
    input_back, gain_attn_rows = norm_back(x_float, gain_attn, attn_norm_grad.astype(jnp.float32))
    input_grad = middle_grad + input_back
    gain_attn_grad = jnp.sum(gain_attn_rows, axis=0)
    w_qkv_grad = lax.psum_scatter(qkv_part, "dp", scatter_dimension=1, tiled=True)
    line_grad = lines_of(folded, heads, seq_len // QB)
    table_part = jnp.dot(bucket_hot.T, line_grad.T, precision=HIGHEST)
    table_whole = lax.dynamic_update_slice(
        jnp.zeros(rel_table.shape, jnp.float32), table_part, (0, tensor_pos * heads)
    )
    gain_attn_grad, table_whole = lax.psum((gain_attn_grad, table_whole), ("dp", "tensor"))
    block_output = middle + gated(returned)
    return (
        block_output,
        input_grad,
        w_qkv_grad,
        w_out_grad,
        table_whole,
        gain_attn_grad,
        gain_moe_grad,
        router_grad,
        w_up_grad.astype(jnp.float32)[None],
        w_down_grad.astype(jnp.float32)[None],
    )


def fused_body(
    block_input,
    out_grad,
    w_qkv,
    w_out,
    rel_table,
    gain_attn,
    gain_moe,
    w_router,
    w_up,
    w_down,
    routes,
    segments,
    padding,
    rel_bucket,
):
    dp_count, tensor_count = lax.axis_size("dp"), lax.axis_size("tensor")
    rows_local, width = block_input.shape
    seq_len = segments.shape[1]
    heads = w_qkv.shape[2] // DH
    capacity = slot_capacity(rows_local, w_router.shape[1])
    expert_count = w_router.shape[1]
    sizes = (dp_count, tensor_count, expert_count, capacity, capacity, heads, seq_len // QB, True)

    routes_t = routes.T
    bucket_row = rel_bucket[None]
    rows, w_all, outw, down_all, qkv, lse, heads_all, slot_rows, cot, line, segk, middle, moe_low, x_send = front(
        sizes, block_input, gain_attn, w_qkv, w_out, w_down[0], out_grad, routes_t, segments, padding,
        rel_table.T, bucket_row, gain_moe
    )
    (up_pair, up_own, up_first, down_own, down_land, produced, middle_grad, heads_grad, out_part, early,
     gates) = middle_pass(
        sizes, x_send, moe_low, middle, out_grad, heads_all, outw, gain_moe, w_router.T, routes_t, padding,
        slot_rows, cot, w_up[0], w_down[0], down_all
    )
    block_output, input_grad, wgrad, early, late, up_rest = last_pass(
        sizes, block_input, gain_attn, middle, middle_grad, heads_grad, rows, w_all, qkv, lse, line, segk, segments,
        produced, slot_rows, gates, early, bucket_row, out_part, up_pair
    )
    (block_output, input_grad, w_qkv_grad, w_out_grad, table_grad, gain_attn_grad, gain_moe_grad, router_grad,
     w_up_grad, w_down_grad) = finish(
        rel_table.shape[1], block_output, input_grad, wgrad, early, late, up_own, up_first, up_rest, down_own, down_land
    )
    return (
        block_output,
        input_grad,
        w_qkv_grad,
        w_out_grad,
        table_grad.T,
        gain_attn_grad,
        gain_moe_grad,
        router_grad.T,
        w_up_grad[None],
        w_down_grad[None],
    )


def slot_capacity(tokens, experts):
    return (10 * tokens + 4 * experts - 1) // (4 * experts)


def body(*args):
    block_input, w_qkv, w_router = args[0], args[2], args[7]
    capacity = slot_capacity(block_input.shape[0], w_router.shape[1])
    fits = capacity % 16 == 0 and w_qkv.shape[1] % 16 == 0 and lax.axis_size("dp") == w_router.shape[1] == 8 and block_input.shape[1] <= 1024
    return fused_body(*args) if fits else plain_body(*args)


def solution(mesh):
    in_specs = (
        P(("dp", "tensor"), None),
        P(("dp", "tensor"), None),
        P(None, "dp", "tensor"),
        P("tensor", "dp"),
        P(),
        P(),
        P(),
        P(),
        P("dp", "tensor", None),
        P("dp", "tensor", None),
        P(("dp", "tensor"), None),
        P("dp", None),
        P("dp", None),
        P(),
    )
    out_specs = (
        P(("dp", "tensor"), None),
        P(("dp", "tensor"), None),
        P(None, "dp", "tensor"),
        P("tensor", "dp"),
        P(),
        P(),
        P(),
        P(),
        P("dp", "tensor", None),
        P("dp", "tensor", None),
    )
    return jax.shard_map(body, mesh=mesh, in_specs=in_specs, out_specs=out_specs, check_vma=False)
```
